32 devices in a mesh: section: 4 (over y, x), group: 2 (over core), dp: 4 (over z).
Axes of the slice: x: 2, y: 2, z: 4, core: 2. Of those that a mesh axis runs over, the one named last changes fastest.
Arguments:
- activations: bfloat16 [16384, 768], P(('group', 'dp')), may hold values from -6 to 6
- weight_in: bfloat16 [4, 768, 3072], P('section', 'group'), may hold values from -0.21875 to 0.21875
- weight_out: bfloat16 [4, 3072, 768], P('section', 'group'), may hold values from -0.8660254 to 0.8660254
- bias_in: bfloat16 [4, 3072], P('section', 'group'), may hold values from -4 to 4
- bias_out: bfloat16 [4, 768], P('section', 'group'), may hold values from -4 to 4
- norm_gain: bfloat16 [4, 768], P('section', 'group'), may hold values from 0.25 to 1.75
- norm_shift: bfloat16 [4, 768], P('section', 'group'), may hold values from -4 to 4
- rope_freq: bfloat16 [4, 2, 384], P('section', None, 'group'), may hold values from -1 to 1
- image_sides: int32 [16, 5], P(('group', 'dp')), may hold values from 0 to 24, as said below
- cotangent: bfloat16 [16384, 768], P(('group', 'dp')), may hold values from -6 to 6
Outputs:
- section_out: bfloat16 [4, 16384, 768], P('section', ('group', 'dp'))
- section_grad: bfloat16 [4, 16384, 768], P('section', ('group', 'dp'))
- grad_weight_in: float32 [4, 768, 3072], P('section', 'group')
- grad_weight_out: float32 [4, 3072, 768], P('section', 'group')
- grad_bias_in: float32 [4, 3072], P('section', 'group')
- grad_bias_out: float32 [4, 768], P('section', 'group')
- grad_norm_gain: float32 [4, 768], P('section', 'group')
- grad_norm_shift: float32 [4, 768], P('section', 'group')
- grad_rope_freq: float32 [4, 2, 384], P('section', None, 'group')
The draws below stay inside these ranges and needn't reach their ends.
Inputs may be any that keep to these rules, and one draw needn't show every extreme that they name: `image_sides`: each entry is 0 (empty slot) or one of 14, 20, 24; the squares of a row sum to at most 1024; slot 0 of every row holds an image, and some row holds an image of side 24.
All inputs are finite; a program needn't handle non-finite values.
Results may differ from the reference program's by a relative error of at most 0.018.
Values may be sent and summed in bfloat16 or wider, within the bound.
A program may use at most 320 MiB of HBM per device.

```python
import jax
import jax.numpy as jnp
from jax import lax

D = 768
HEADS = 12
HD = 64
FF = 3072
CAP = 1024
IMGS = 5
SIDE = 24
BATCHES = 16
TOKENS = 16384
N_SECTION = 4


def draw_weight_out(key, part):
    key = jax.random.fold_in(key, 5)
    noise = jnp.clip(jax.random.normal(key, (N_SECTION, FF, D), jnp.float32), -6.0, 6.0)
    section_ids = jnp.arange(N_SECTION)[:, None, None]
    row_ids = jnp.arange(FF)[None, :, None]
    attends = (section_ids % 2 == 0) & (row_ids < D)
    scaling = jnp.where(attends, (D // 16) ** (-0.5), FF ** (-0.5))
    return (noise * scaling).astype(jnp.bfloat16)


def draw_image_sides(key, part):
    key = jax.random.fold_in(key, 11)
    picks = jax.random.randint(key, (BATCHES, IMGS), 0, 3)
    table = jnp.array([SIDE * 7 // 12, SIDE * 10 // 12, SIDE], jnp.int32)
    chosen = table[picks]
    chosen = chosen.at[0, 0].set(SIDE)
    used = jnp.zeros((BATCHES,), jnp.int32)
    columns = []
    for slot_index in range(IMGS):
        area = chosen[:, slot_index] * chosen[:, slot_index]
        fits = used + area <= CAP
        columns.append(jnp.where(fits, chosen[:, slot_index], 0))
        used = used + jnp.where(fits, area, 0)
    return jnp.stack(columns, axis=1).astype(jnp.int32)


def levels(stream_key, extent, shards, low, largest):
    def one(position, shards_of):
        draws = jax.random.uniform(jax.random.fold_in(jax.random.fold_in(stream_key, 6), position), (shards_of,), jnp.float32, low / len(shards), largest / len(shards))
        return jnp.repeat(jnp.exp(draws), extent[position] // shards_of).reshape((-1,) + (1,) * (len(extent) - position - 1))

    level = one(*shards[0])
    for cut in shards[1:]:
        level = level * one(*cut)
    return level


def gaussian(own_key, shape, scale, limit, split=(), kind=jnp.bfloat16):
    gain = levels(own_key, shape, split, -0.22, 0.18) if split else 1.0
    entries = jax.random.normal(own_key, shape, jnp.float32) * scale * gain
    return jnp.minimum(jnp.maximum(entries, -limit), limit).astype(kind)


def setup_inputs(seed: int = 0) -> dict:
    splits = jax.random.split(jax.random.key(seed), 11)
    return {
        "activations": gaussian(splits[0], (TOKENS, D), 1.0, 6.0, ((0, 8),)),
        "weight_in": gaussian(splits[1], (N_SECTION, D, FF), D ** -0.5, 0.21875, ((0, 4), (1, 2))),
        "weight_out": draw_weight_out(jax.random.fold_in(splits[10], 71), 0),
        "bias_in": gaussian(splits[3], (N_SECTION, FF), 0.3, 4.0, ((0, 4), (1, 2))),
        "bias_out": gaussian(splits[4], (N_SECTION, D), 0.3, 4.0, ((0, 4), (1, 2))),
        "norm_gain": jnp.clip(1.0 + 0.15 * jax.random.normal(splits[5], (N_SECTION, D), jnp.float32), 0.25, 1.75).astype(jnp.bfloat16),
        "norm_shift": gaussian(splits[6], (N_SECTION, D), 0.3, 4.0, ((0, 4), (1, 2))),
        "rope_freq": jnp.clip(jax.random.uniform(splits[7], (N_SECTION, 2, D // 2), jnp.float32, -1.0, 1.0) * levels(splits[7], (N_SECTION, 2, D // 2), ((0, 4), (2, 2)), -0.4, 0.0), -1.0, 1.0).astype(jnp.bfloat16),
        "image_sides": draw_image_sides(jax.random.fold_in(splits[10], 71), 0),
        "cotangent": gaussian(splits[9], (TOKENS, D), 1.0, 6.0, ((0, 8),)),
    }


EPSILON = 1e-06
PRECISE = lax.Precision.HIGHEST

@jax.custom_vjp
def low(v):
    return lax.optimization_barrier(v.astype(jnp.bfloat16)).astype(jnp.float32)

@jax.custom_vjp
def low_back(v):
    return v

def low_keep(v):
    return (low(v), None)

def low_pass(kept, grad):
    return (grad,)

def back_keep(v):
    return (v, None)

def back_low(kept, grad):
    return (low(grad),)
low.defvjp(low_keep, low_pass)
low_back.defvjp(back_keep, back_low)

def layout(image_sides, capacity):
    counts = (image_sides * image_sides).astype(jnp.int32)
    end_pos = jnp.cumsum(counts).astype(jnp.int32)
    start_pos = (end_pos - counts).astype(jnp.int32)
    positions = jnp.arange(capacity, dtype=jnp.int32)
    segment = lax.optimization_barrier(jnp.sum((positions[:, None] >= end_pos[None, :]).astype(jnp.int32), axis=1)).astype(jnp.int32)
    slot_ids = jnp.arange(image_sides.shape[-1], dtype=jnp.int32)
    one_hot = (segment[:, None] == slot_ids[None, :]).astype(jnp.int32)
    start_tok = lax.optimization_barrier(jnp.sum(one_hot * start_pos[None, :], axis=1)).astype(jnp.int32)
    side_len = jnp.maximum(lax.optimization_barrier(jnp.sum(one_hot * image_sides[None, :], axis=1)), 1).astype(jnp.int32)
    local_idx = (positions - start_tok).astype(jnp.int32)
    is_valid = segment < image_sides.shape[-1]
    patch_row = jnp.where(is_valid, local_idx // side_len, 0).astype(jnp.int32)
    patch_col = jnp.where(is_valid, local_idx % side_len, 0).astype(jnp.int32)
    return (segment, patch_row, patch_col, is_valid)

def layer_norm(stream, norm_gain, norm_shift):
    average = lax.optimization_barrier(jnp.mean(stream, axis=-1, keepdims=True))
    centered = stream - average
    variance = lax.optimization_barrier(jnp.mean(centered * centered, axis=-1, keepdims=True))
    return centered * lax.rsqrt(variance + EPSILON) * norm_gain + norm_shift

def rotate(vectors, cosines, sine_vals):
    half_dim = vectors.shape[-1] // 2
    lower_half = vectors[..., :half_dim]
    upper_half = vectors[..., half_dim:]
    return jnp.concatenate([lower_half * cosines - upper_half * sine_vals, lower_half * sine_vals + upper_half * cosines], axis=-1)

def rope_angles(rope_freq, patch_row, patch_col):
    angles = patch_col.astype(jnp.float32)[:, None] * rope_freq[0][None, :] + patch_row.astype(jnp.float32)[:, None] * rope_freq[1][None, :]
    return angles.reshape(patch_row.shape[0], HEADS, HD // 2)

def attention_section(stream, params, segment, patch_row, patch_col):
    weight_in, weight_out, bias_in, bias_out, norm_gain, norm_shift, rope_freq = params
    normed = low(layer_norm(stream, norm_gain, norm_shift))
    projected = low_back(jnp.dot(normed, weight_in[:, :3 * D], precision=PRECISE) + bias_in[:3 * D])
    angles = rope_angles(rope_freq, patch_row, patch_col)
    cosines = jnp.cos(angles)
    sine_vals = jnp.sin(angles)
    queries = low(rotate(projected[:, :D].reshape(CAP, HEADS, HD), cosines, sine_vals))
    key_rows = low(rotate(projected[:, D:2 * D].reshape(CAP, HEADS, HD), cosines, sine_vals))
    value_rows = low(projected[:, 2 * D:].reshape(CAP, HEADS, HD))
    scores = low_back(jnp.einsum('qhd,khd->hqk', queries, key_rows, precision=PRECISE) * HD ** (-0.5))
    same_image = segment[:, None] == segment[None, :]
    attn_probs = jax.nn.softmax(jnp.where(same_image[None], scores, -1000000000.0), axis=-1)
    mixture = jnp.einsum('hqk,khd->qhd', low(attn_probs), value_rows, precision=PRECISE).reshape(CAP, D)
    mixture = low_back(low(mixture))
    return stream + jnp.dot(mixture, weight_out[:D], precision=PRECISE) + bias_out

def feed_forward_section(stream, params):
    weight_in, weight_out, bias_in, bias_out, norm_gain, norm_shift, rope_freq = params
    normed = low(layer_norm(stream, norm_gain, norm_shift))
    up_proj = low_back(jnp.dot(normed, weight_in, precision=PRECISE) + bias_in)
    activated = low(jax.nn.gelu(up_proj, approximate=False))
    return stream + jnp.dot(activated, weight_out, precision=PRECISE) + bias_out

def run_all(values, image_sides):
    activations = values[0]
    weights = values[1:8]
    nudge = values[8]
    batches = image_sides.shape[0]
    start = activations.reshape(batches, CAP, D)
    extra = jnp.moveaxis(nudge.reshape(N_SECTION - 1, batches, CAP, D), 0, 1)

    def one_batch(item):
        stream, sides_row, bumps = item
        segment, patch_row, patch_col, is_valid = layout(sides_row, CAP)
        kept = []
        for section_index in range(N_SECTION):
            params = tuple((source[section_index] for source in weights))
            if section_index % 2 == 0:
                stream = attention_section(stream, params, segment, patch_row, patch_col)
            else:
                stream = feed_forward_section(stream, params)
            stream = low(stream)
            kept.append(stream)
            if section_index < N_SECTION - 1:
                stream = low_back(stream + bumps[section_index])
        return jnp.stack(kept)
    return lax.map(jax.checkpoint(one_batch), (start, image_sides, extra))

def reference(activations, weight_in, weight_out, bias_in, bias_out, norm_gain, norm_shift, rope_freq, image_sides, cotangent):
    batches = image_sides.shape[0]
    floats = tuple((source.astype(jnp.float32) for source in (activations, weight_in, weight_out, bias_in, bias_out, norm_gain, norm_shift, rope_freq)))
    nudge = jnp.zeros((N_SECTION - 1, batches * CAP, D), jnp.float32)

    def forward(*values):
        return run_all(values, image_sides)
    outputs, back = jax.vjp(forward, *floats, nudge)
    is_valid = jax.vmap(lambda sides_row: layout(sides_row, CAP)[3])(image_sides)
    seed_last = cotangent.astype(jnp.float32).reshape(batches, CAP, D) * is_valid[:, :, None].astype(jnp.float32)
    seeds = jnp.zeros_like(outputs).at[:, N_SECTION - 1].set(seed_last)
    grads = back(seeds)
    section_out = jnp.moveaxis(outputs, 1, 0).reshape(N_SECTION, batches * CAP, D).astype(jnp.bfloat16)
    section_grad = jnp.concatenate([grads[0][None], grads[8]], axis=0).astype(jnp.bfloat16)
    return (section_out, section_grad, grads[1], grads[2], grads[3], grads[4], grads[5], grads[6], grads[7])
```

```python
from functools import partial

import jax
import jax.numpy as jnp
from jax import lax
from jax.experimental import pallas as pl
from jax.experimental.pallas import tpu as pltpu
from jax.sharding import PartitionSpec as P

D = 768
HEADS = 12
HD = 64
FF = 3072
HALF = D // 2
PAIRS = HEADS // 2
QKV = 3 * D
EPSILON = 1e-06
BF = jnp.bfloat16
F32 = jnp.float32
NT = (((1,), (1,)), ((), ()))
TN = (((0,), (0,)), ((), ()))
VMEM_BYTES = 52 * 1024 * 1024


def dot(a, b):
    return jnp.dot(a, b, preferred_element_type=F32)


def dot_nt(a, b):
    return lax.dot_general(a, b, NT, preferred_element_type=F32)


def dot_tn(a, b):
    return lax.dot_general(a, b, TN, preferred_element_type=F32)


def normalize(h):
    average = jnp.mean(h, axis=-1, keepdims=True)
    centered = h - average
    variance = jnp.mean(centered * centered, axis=-1, keepdims=True)
    scale = lax.rsqrt(variance + EPSILON)
    return centered * scale, scale


def turn_halves(x, rot):
    return jnp.where(rot == 0, x, jnp.concatenate([x[:, HALF:], x[:, :HALF]], axis=1))


def swap_pairs(x):
    lanes = lax.broadcasted_iota(jnp.int32, x.shape, 1)
    low = (lanes % HD) < HD // 2
    return jnp.where(
        low, pltpu.roll(x, x.shape[1] - HD // 2, 1), pltpu.roll(x, HD // 2, 1)
    )


def norm_backward(h, gain, grad, d_normed):
    xhat, scale = normalize(h)
    e = d_normed * gain
    mean_e = jnp.mean(e, axis=-1, keepdims=True)
    mean_ex = jnp.mean(e * xhat, axis=-1, keepdims=True)
    g = grad + scale * (e - mean_e - xhat * mean_ex)
    d_gain = jnp.sum(d_normed * xhat, axis=0, keepdims=True)
    d_shift = jnp.sum(d_normed, axis=0, keepdims=True)
    return g, d_gain, d_shift


def qkv_kernel(rot_ref, h_ref, par_ref, wa_ref, wb_ref, bias_ref, cos_ref, sin_ref, out_ref, nrm_ref):
    j = pl.program_id(0)

    @pl.when(j == 0)
    def _():
        xhat, _ = normalize(h_ref[...].astype(F32))
        normed = xhat * par_ref[0:1, :] + par_ref[1:2, :]
        nrm_ref[...] = turn_halves(normed, rot_ref[0]).astype(BF)

    x = dot(nrm_ref[:, :HALF], wa_ref[...]) + dot(nrm_ref[:, HALF:], wb_ref[...]) + bias_ref[...]

    @pl.when(j < 2)
    def _():
        y = x * cos_ref[...] + swap_pairs(x) * sin_ref[...]
        out_ref[...] = (y * jnp.where(j == 0, HD ** (-0.5), 1.0)).astype(BF)

    @pl.when(j == 2)
    def _():
        out_ref[...] = x.astype(BF)


def attend_kernel(
    rot_ref, q_ref, km_ref, vm_ref, kt_ref, vt_ref, segq_ref, segm_ref, segt_ref, h_ref,
    woa_ref, wob_ref, bias_ref, o_ref, lse_ref, out_ref, lse_scr,
):
    j = pl.program_id(0)
    rows = q_ref.shape[0]
    lanes = lax.broadcasted_iota(jnp.int32, (rows, 2 * HD), 1)
    q = q_ref[...]
    same_m = segq_ref[...] == segm_ref[...]
    same_t = segq_ref[...] == segt_ref[...]
    outs = []
    for side in range(2):
        mine = (lanes >= HD) if side else (lanes < HD)
        q_head = jnp.where(mine, q, jnp.zeros_like(q))
        s_m = jnp.where(same_m, dot_nt(q_head, km_ref[...]), -1e9)
        s_t = jnp.where(same_t, dot_nt(q_head, kt_ref[...]), -1e9)
        top = jnp.maximum(
            jnp.max(s_m, axis=-1, keepdims=True), jnp.max(s_t, axis=-1, keepdims=True)
        )
        p_m = jnp.exp(s_m - top)
        p_t = jnp.exp(s_t - top)
        total = jnp.sum(p_m, axis=-1, keepdims=True) + jnp.sum(p_t, axis=-1, keepdims=True)
        o = dot(p_m.astype(BF), vm_ref[...]) + dot(p_t.astype(BF), vt_ref[...])
        outs.append(o / total)
        lse_scr[...] = jnp.where(lanes == 2 * j + side, top + jnp.log(total), lse_scr[...])
    o_ref[:, pl.ds(pl.multiple_of(j * 2 * HD, 2 * HD), 2 * HD)] = jnp.where(
        lanes < HD, outs[0], outs[1]
    ).astype(BF)

    @pl.when(j == PAIRS - 1)
    def _():
        lse_ref[...] = jnp.transpose(lse_scr[...])[:16, :]
        o_all = turn_halves(o_ref[...].astype(F32), rot_ref[0]).astype(BF)
        y = dot(o_all[:, :HALF], woa_ref[...]) + dot(o_all[:, HALF:], wob_ref[...])
        out_ref[...] = (h_ref[...].astype(F32) + y + bias_ref[...]).astype(BF)


def ff_kernel(
    rot_ref, h_ref, par_ref, wia_ref, wib_ref, bias_ref, woa_ref, wob_ref, bout_ref,
    act_ref, slope_ref, nrm_ref, out_ref, acc_ref,
):
    j = pl.program_id(0)
    n = pl.num_programs(0)

    @pl.when(j == 0)
    def _():
        xhat, _ = normalize(h_ref[...].astype(F32))
        normed = xhat * par_ref[0:1, :] + par_ref[1:2, :]
        nrm_ref[...] = turn_halves(normed, rot_ref[0]).astype(BF)
        acc_ref[...] = h_ref[...].astype(F32) + bout_ref[...]

    u = dot(nrm_ref[:, :HALF], wia_ref[...]) + dot(nrm_ref[:, HALF:], wib_ref[...]) + bias_ref[...]
    cdf = 0.5 + 0.5 * lax.erf(u * (0.5**0.5))
    act = (u * cdf).astype(BF)
    act_ref[...] = act
    pdf = jnp.exp(u * u * -0.5) * 0.3989422804014327
    slope_ref[...] = (cdf + u * pdf).astype(BF)

    @pl.when(j < n // 2)
    def _():
        acc_ref[...] += dot(act, woa_ref[...])

    @pl.when(j >= n // 2)
    def _():
        acc_ref[...] += dot(act, wob_ref[...])

    @pl.when(j == n - 1)
    def _():
        out_ref[...] = acc_ref[...].astype(BF)


def ff_back_kernel(
    rot_ref, g_ref, act_ref, slope_ref, nrm_ref, wia_ref, wib_ref, woa_ref, wob_ref, h_ref, par_ref,
    dia_ref, dib_ref, doa_ref, dob_ref, dbin_ref, small_ref, out_ref, acc_ref,
):
    j = pl.program_id(0)
    n = pl.num_programs(0)

    @pl.when(j == 0)
    def _():
        acc_ref[...] = jnp.zeros_like(acc_ref)

    def step(wo_ref, do_ref):
        g = g_ref[...]
        d_up_f = dot_nt(g, wo_ref[...]) * slope_ref[...].astype(F32)
        d_up = d_up_f.astype(BF)
        do_ref[...] = dot_tn(act_ref[...], g).astype(BF)
        dbin_ref[...] = jnp.sum(d_up_f, axis=0, keepdims=True)
        dia_ref[...] = dot_tn(nrm_ref[:, :HALF], d_up).astype(BF)
        dib_ref[...] = dot_tn(nrm_ref[:, HALF:], d_up).astype(BF)
        acc_ref[:, :HALF] += dot_nt(d_up, wia_ref[...])
        acc_ref[:, HALF:] += dot_nt(d_up, wib_ref[...])

    @pl.when(j < n // 2)
    def _():
        step(woa_ref, doa_ref)

    @pl.when(j >= n // 2)
    def _():
        step(wob_ref, dob_ref)

    @pl.when(j == n - 1)
    def _():
        g = g_ref[...].astype(F32)
        d_normed = turn_halves(acc_ref[...], rot_ref[0])
        out, d_gain, d_shift = norm_backward(h_ref[...].astype(F32), par_ref[0:1, :], g, d_normed)
        out_ref[...] = out.astype(BF)
        small_ref[0:1, :] = jnp.sum(g, axis=0, keepdims=True)
        small_ref[1:2, :] = d_gain
        small_ref[2:3, :] = d_shift
        small_ref[3:8, :] = jnp.zeros((5, D), F32)


def mix_back_kernel(rot_ref, g_ref, o_ref, woa_ref, wob_ref, dmix_ref, delta_ref, doa_ref, dob_ref):
    g = g_ref[...]
    rot = rot_ref[0]
    d_mix = jnp.concatenate([dot_nt(g, woa_ref[...]), dot_nt(g, wob_ref[...])], axis=1)
    d_mix = turn_halves(d_mix, rot).astype(BF)
    dmix_ref[...] = d_mix
    o = o_ref[...].astype(F32)
    product = d_mix.astype(F32) * o
    head = lax.broadcasted_iota(jnp.int32, (16, D), 0)
    lanes = lax.broadcasted_iota(jnp.int32, (16, D), 1)
    chosen = jnp.where(lanes // HD == head, 1.0, 0.0)
    delta_ref[...] = lax.dot_general(
        chosen, product, NT, preferred_element_type=F32, precision=lax.Precision.HIGHEST
    )
    turned = turn_halves(o, rot).astype(BF)
    doa_ref[...] = dot_tn(turned[:, :HALF], g).astype(BF)
    dob_ref[...] = dot_tn(turned[:, HALF:], g).astype(BF)


def attend_back_kernel(
    q_ref, km_ref, vm_ref, kt_ref, vt_ref, do_ref, lse_ref, delta_ref, segq_ref, segm_ref, segt_ref,
    dq_ref, dkm_ref, dvm_ref, dkt_ref, dvt_ref,
):
    j = pl.program_id(0)
    rows = q_ref.shape[0]
    lanes = lax.broadcasted_iota(jnp.int32, (rows, 2 * HD), 1)
    q = q_ref[...]
    do = do_ref[...]
    zero = jnp.zeros_like(q)
    d_q = jnp.zeros((rows, 2 * HD), F32)
    sets = ((km_ref, vm_ref, segm_ref), (kt_ref, vt_ref, segt_ref))
    d_k = [0.0, 0.0]
    d_v = [0.0, 0.0]
    for side in range(2):
        mine = (lanes >= HD) if side else (lanes < HD)
        q_head = jnp.where(mine, q, zero)
        do_head = jnp.where(mine, do, zero)
        lse = lse_ref[pl.ds(2 * j + side, 1), :]
        delta = delta_ref[pl.ds(2 * j + side, 1), :]
        for i, (k_ref, v_ref, seg_ref) in enumerate(sets):
            k = k_ref[...]
            s_t = dot_nt(k, q_head)
            p_t = jnp.where(seg_ref[...] == segq_ref[...], jnp.exp(s_t - lse), 0.0)
            d_p = dot_nt(v_ref[...], do_head)
            d_s = (p_t * (d_p - delta)).astype(BF)
            d_v[i] += dot(p_t.astype(BF), do_head)
            d_k[i] += dot(d_s, q_head)
            d_q += dot_tn(d_s, jnp.where(mine, k, zero))
    dq_ref[...] = d_q
    dkm_ref[...] = d_k[0]
    dvm_ref[...] = d_v[0]
    dkt_ref[...] = d_k[1].astype(BF)
    dvt_ref[...] = d_v[1].astype(BF)


def qkv_back_kernel(
    rot_ref, dq_ref, dkm_ref, dvm_ref, dkr_ref, dvr_ref, qkv_ref, cos_ref, sin_ref, pos_ref,
    nrm_ref, wa_ref, wb_ref, h_ref, par_ref, g_ref,
    dia_ref, dib_ref, dbin_ref, small_ref, out_ref, acc_ref, dp_ref,
):
    j = pl.program_id(0)
    n = pl.num_programs(0)

    @pl.when(j == 0)
    def _():
        acc_ref[...] = jnp.zeros_like(acc_ref)
        small_ref[...] = jnp.zeros_like(small_ref)

    def turned_back(dy, y):
        swapped = swap_pairs(dy)
        d_angle = y * swapped - swap_pairs(y) * dy
        small_ref[3:4, :] += jnp.sum(d_angle * pos_ref[:, 0:1], axis=0, keepdims=True)
        small_ref[4:5, :] += jnp.sum(d_angle * pos_ref[:, 1:2], axis=0, keepdims=True)
        return dy * cos_ref[...] - swapped * sin_ref[...]

    @pl.when(j == 0)
    def _():
        d_y = dq_ref[...] * HD ** (-0.5)
        y = qkv_ref[...].astype(F32) * HD**0.5
        dp_ref[...] = turned_back(d_y, y)

    @pl.when(j == 1)
    def _():
        d_y = dkm_ref[...] + dkr_ref[...].astype(F32)
        dp_ref[...] = turned_back(d_y, qkv_ref[...].astype(F32))

    @pl.when(j == 2)
    def _():
        dp_ref[...] = dvm_ref[...] + dvr_ref[...].astype(F32)

    d_f = dp_ref[...]
    d_p = d_f.astype(BF)
    dbin_ref[...] = jnp.sum(d_f, axis=0, keepdims=True)
    dia_ref[...] = dot_tn(nrm_ref[:, :HALF], d_p).astype(BF)
    dib_ref[...] = dot_tn(nrm_ref[:, HALF:], d_p).astype(BF)
    acc_ref[:, :HALF] += dot_nt(d_p, wa_ref[...])
    acc_ref[:, HALF:] += dot_nt(d_p, wb_ref[...])

    @pl.when(j == n - 1)
    def _():
        g = g_ref[...].astype(F32)
        d_normed = turn_halves(acc_ref[...], rot_ref[0])
        out, d_gain, d_shift = norm_backward(h_ref[...].astype(F32), par_ref[0:1, :], g, d_normed)
        out_ref[...] = out.astype(BF)
        small_ref[0:1, :] = jnp.sum(g, axis=0, keepdims=True)
        small_ref[1:2, :] = d_gain
        small_ref[2:3, :] = d_shift


def params_of(n=1):
    return pltpu.CompilerParams(
        dimension_semantics=("arbitrary",) * n, vmem_limit_bytes=VMEM_BYTES
    )


def whole(shape):
    return pl.BlockSpec(shape, lambda *_: (0,) * len(shape))


def sds(shape, dtype):
    return jax.ShapeDtypeStruct(shape, dtype)


def cost(flops, nbytes, trans=0):
    return pl.CostEstimate(flops=flops, bytes_accessed=nbytes, transcendentals=trans)


def qkv_call(rot, h, par, wa, wb, bias, cosines, sines):
    t = h.shape[0]
    return pl.pallas_call(
        qkv_kernel,
        out_shape=(sds((t, QKV), BF), sds((t, D), BF)),
        grid_spec=pltpu.PrefetchScalarGridSpec(
            num_scalar_prefetch=1,
            grid=(3,),
            in_specs=[
                whole((t, D)), whole((8, D)),
                pl.BlockSpec((HALF, D), lambda j, r: (0, j)),
                pl.BlockSpec((HALF, D), lambda j, r: (0, j)),
                pl.BlockSpec((1, D), lambda j, r: (0, j)),
                whole((t, D)), whole((t, D)),
            ],
            out_specs=[pl.BlockSpec((t, D), lambda j, r: (0, j)), whole((t, D))],
        ),
        compiler_params=params_of(),
        cost_estimate=cost(2 * t * D * QKV, 2 * D * QKV + 8 * t * D + 2 * t * QKV),
        name="qkv",
    )(rot, h, par, wa, wb, bias, cosines, sines)


def attend_call(rot, qkv, kv_t, seg_col, seg_m, seg_t, h, woa, wob, bias):
    t = h.shape[0]
    w = 2 * HD
    return pl.pallas_call(
        attend_kernel,
        out_shape=(sds((t, D), BF), sds((16, t), F32), sds((t, D), BF)),
        grid_spec=pltpu.PrefetchScalarGridSpec(
            num_scalar_prefetch=1,
            grid=(PAIRS,),
            in_specs=[
                pl.BlockSpec((t, w), lambda j, r: (0, j)),
                pl.BlockSpec((t, w), lambda j, r: (0, j + PAIRS)),
                pl.BlockSpec((t, w), lambda j, r: (0, j + 2 * PAIRS)),
                pl.BlockSpec((t, w), lambda j, r: (0, j)),
                pl.BlockSpec((t, w), lambda j, r: (0, j + PAIRS)),
                whole((t, 1)), whole((1, t)), whole((1, t)), whole((t, D)),
                whole((HALF, D)), whole((HALF, D)), whole((1, D)),
            ],
            out_specs=[whole((t, D)), whole((16, t)), whole((t, D))],
            scratch_shapes=[pltpu.VMEM((t, w), F32)],
        ),
        compiler_params=params_of(),
        cost_estimate=cost(8 * t * t * D * 4, 16 * t * D, 2 * t * t * HEADS),
        name="attend",
    )(rot, qkv, qkv, qkv, kv_t, kv_t, seg_col, seg_m, seg_t, h, woa, wob, bias)


def ff_specs(t, blocks):
    width = FF // blocks
    half = blocks // 2
    w_in = pl.BlockSpec((HALF, width), lambda j, r: (0, (j + half * r[0]) % blocks))
    b_in = pl.BlockSpec((1, width), lambda j, r: (0, (j + half * r[0]) % blocks))
    w_a = pl.BlockSpec((width, D), lambda j, r: (jnp.minimum(j, half - 1), 0))
    w_b = pl.BlockSpec((width, D), lambda j, r: (jnp.maximum(j - half, 0), 0))
    hid = pl.BlockSpec((t, width), lambda j, r: (0, j))
    return w_in, b_in, w_a, w_b, hid


def ff_call(rot, h, par, wia, wib, bias, woa, wob, bout):
    t = h.shape[0]
    blocks = 6
    w_in, b_in, w_a, w_b, hid = ff_specs(t, blocks)
    return pl.pallas_call(
        ff_kernel,
        out_shape=(sds((t, FF), BF), sds((t, FF), BF), sds((t, D), BF), sds((t, D), BF)),
        grid_spec=pltpu.PrefetchScalarGridSpec(
            num_scalar_prefetch=1,
            grid=(blocks,),
            in_specs=[whole((t, D)), whole((8, D)), w_in, w_in, b_in, w_a, w_b, whole((1, D))],
            out_specs=[hid, hid, whole((t, D)), whole((t, D))],
            scratch_shapes=[pltpu.VMEM((t, D), F32)],
        ),
        compiler_params=params_of(),
        cost_estimate=cost(4 * t * D * FF, 4 * D * FF + 4 * t * FF, 2 * t * FF),
        name="feed",
    )(rot, h, par, wia, wib, bias, woa, wob, bout)


def ff_back_call(rot, g, act, slope, nrm, wia, wib, woa, wob, h, par):
    t = h.shape[0]
    blocks = 6
    w_in, b_in, w_a, w_b, hid = ff_specs(t, blocks)
    return pl.pallas_call(
        ff_back_kernel,
        out_shape=(
            sds((HALF, FF), BF), sds((HALF, FF), BF), sds((FF // 2, D), BF), sds((FF // 2, D), BF),
            sds((1, FF), F32), sds((8, D), F32), sds((t, D), BF),
        ),
        grid_spec=pltpu.PrefetchScalarGridSpec(
            num_scalar_prefetch=1,
            grid=(blocks,),
            in_specs=[
                whole((t, D)), hid, hid, whole((t, D)), w_in, w_in, w_a, w_b, whole((t, D)),
                whole((8, D)),
            ],
            out_specs=[w_in, w_in, w_a, w_b, b_in, whole((8, D)), whole((t, D))],
            scratch_shapes=[pltpu.VMEM((t, D), F32)],
        ),
        compiler_params=params_of(),
        cost_estimate=cost(8 * t * D * FF, 8 * D * FF + 4 * t * FF),
        name="feed_back",
    )(rot, g, act, slope, nrm, wia, wib, woa, wob, h, par)


def mix_back_call(rot, g, o, woa, wob):
    t = g.shape[0]
    return pl.pallas_call(
        mix_back_kernel,
        out_shape=(sds((t, D), BF), sds((16, t), F32), sds((HALF, D), BF), sds((HALF, D), BF)),
        grid_spec=pltpu.PrefetchScalarGridSpec(
            num_scalar_prefetch=1,
            grid=(1,),
            in_specs=[whole((t, D)), whole((t, D)), whole((HALF, D)), whole((HALF, D))],
            out_specs=[whole((t, D)), whole((16, t)), whole((HALF, D)), whole((HALF, D))],
        ),
        compiler_params=params_of(),
        cost_estimate=cost(4 * t * D * D, 4 * D * D + 6 * t * D),
        name="mix_back",
    )(rot, g, o, woa, wob)


def attend_back_call(qkv, kv_t, dmix, lse, delta, seg_row, seg_m, seg_t):
    t = dmix.shape[0]
    w = 2 * HD
    col = pl.BlockSpec((t, w), lambda j: (0, j))
    return pl.pallas_call(
        attend_back_kernel,
        out_shape=(sds((t, D), F32), sds((t, D), F32), sds((t, D), F32), sds((t, D), BF), sds((t, D), BF)),
        grid=(PAIRS,),
        in_specs=[
            col,
            pl.BlockSpec((t, w), lambda j: (0, j + PAIRS)),
            pl.BlockSpec((t, w), lambda j: (0, j + 2 * PAIRS)),
            col,
            pl.BlockSpec((t, w), lambda j: (0, j + PAIRS)),
            col, whole((16, t)), whole((16, t)), whole((1, t)), whole((t, 1)), whole((t, 1)),
        ],
        out_specs=[col] * 5,
        compiler_params=params_of(),
        cost_estimate=cost(20 * t * t * D * 4, 30 * t * D, 2 * t * t * HEADS),
        name="attend_back",
    )(qkv, qkv, qkv, kv_t, kv_t, dmix, lse, delta, seg_row, seg_m, seg_t)


def qkv_back_call(rot, dq, dkm, dvm, dkr, dvr, qkv, cosines, sines, pos, nrm, wa, wb, h, par, g):
    t = h.shape[0]
    w_in = pl.BlockSpec((HALF, D), lambda j, r: (0, j))
    rows = whole((t, D))
    return pl.pallas_call(
        qkv_back_kernel,
        out_shape=(
            sds((HALF, QKV), BF), sds((HALF, QKV), BF), sds((1, QKV), F32), sds((8, D), F32),
            sds((t, D), BF),
        ),
        grid_spec=pltpu.PrefetchScalarGridSpec(
            num_scalar_prefetch=1,
            grid=(3,),
            in_specs=[
                rows, rows, rows, rows, rows, pl.BlockSpec((t, D), lambda j, r: (0, j)), rows, rows,
                whole((t, 2)), rows, w_in, w_in, rows, whole((8, D)), rows,
            ],
            out_specs=[w_in, w_in, pl.BlockSpec((1, D), lambda j, r: (0, j)), whole((8, D)), rows],
            scratch_shapes=[pltpu.VMEM((t, D), F32), pltpu.VMEM((t, D), F32)],
        ),
        compiler_params=params_of(),
        cost_estimate=cost(4 * t * D * QKV, 4 * D * QKV + 30 * t * D),
        name="qkv_back",
    )(rot, dq, dkm, dvm, dkr, dvr, qkv, cosines, sines, pos, nrm, wa, wb, h, par, g)


def layout(image_sides, capacity):
    counts = image_sides * image_sides
    end_pos = jnp.cumsum(counts)
    start_pos = end_pos - counts
    positions = jnp.arange(capacity, dtype=jnp.int32)
    segment = jnp.sum((positions[:, None] >= end_pos[None, :]).astype(jnp.int32), axis=1)
    slot_ids = jnp.arange(image_sides.shape[-1], dtype=jnp.int32)
    one_hot = (segment[:, None] == slot_ids[None, :]).astype(jnp.int32)
    start_tok = jnp.sum(one_hot * start_pos[None, :], axis=1)
    side_len = jnp.maximum(jnp.sum(one_hot * image_sides[None, :], axis=1), 1)
    local_idx = positions - start_tok
    is_valid = segment < image_sides.shape[-1]
    patch_row = jnp.where(is_valid, local_idx // side_len, 0)
    patch_col = jnp.where(is_valid, local_idx % side_len, 0)
    return segment, patch_row, patch_col, is_valid


def turning(freq, pos):
    wide = jnp.concatenate([freq.reshape(2, HEADS, HD // 2)] * 2, axis=2).reshape(2, D)
    angles = pos[:, 0:1] * wide[0][None, :] + pos[:, 1:2] * wide[1][None, :]
    low = (jnp.arange(D) % HD) < HD // 2
    sines = jnp.sin(angles)
    return jnp.cos(angles), jnp.where(low[None, :], -sines, sines)


def flipped(x, axis, bit):
    return lax.ppermute(x, axis, [(i, i ^ bit) for i in range(lax.axis_size(axis))])


def sent(x, source, target):
    return lax.ppermute(x, "section", [(source, target)])


def added(a, b):
    return (a.astype(F32) + b.astype(F32)).astype(a.dtype)


def spread(blocks, owner, section):
    near = [sent(b, owner, owner ^ 1) for b in blocks]
    far = [sent(b, owner, owner ^ 2) for b in blocks]
    last = [sent(near[0], owner ^ 1, owner ^ 3), sent(far[1], owner ^ 2, owner ^ 3)]
    return [
        jnp.where(section == owner, b, n + f + l) for b, n, f, l in zip(blocks, near, far, last)
    ]


def plane_sum(x, section, order):
    x = x.reshape(2, 2, *x.shape[1:])
    low, high = section % 2, section // 2
    if order == 0:
        keep, give = x[:, low], x[:, 1 - low]
        keep = added(keep, flipped(give, "section", 1))
        return added(keep[high], flipped(keep[1 - high], "section", 2))
    keep, give = x[high], x[1 - high]
    keep = added(keep, flipped(give, "section", 2))
    return added(keep[low], flipped(keep[1 - low], "section", 1))


def line_sum(x, axis):
    n = lax.axis_size(axis)
    me = lax.axis_index(axis)
    if n == 1:
        return x[0]
    up = [(i, i + 1) for i in range(n - 1)]
    down = [(i + 1, i) for i in range(n - 1)]
    right = left = None
    for t in range(n - 1):
        a = x[jnp.minimum(n - 1 - t + me, n - 1)]
        b = x[jnp.maximum(me - (n - 1) + t, 0)]
        right = lax.ppermute(a if right is None else added(a, right), axis, up)
        left = lax.ppermute(b if left is None else added(b, left), axis, down)
    return (x[me].astype(F32) + right.astype(F32) + left.astype(F32)).astype(x.dtype)


def line_gather(x, axis, owner=None):
    n = lax.axis_size(axis)
    me = lax.axis_index(axis)
    if owner is None:
        names, base = axis, 0
    else:
        names, base = ("section", axis), owner * n
    up = [(base + i, base + i + 1) for i in range(n - 1)]
    down = [(base + i + 1, base + i) for i in range(n - 1)]
    out = jnp.zeros((n,) + x.shape, x.dtype)
    out = lax.dynamic_update_index_in_dim(out, x, me, 0)
    right = left = x
    ids = jnp.arange(n).reshape((n,) + (1,) * x.ndim)
    for t in range(n - 1):
        right = lax.ppermute(right, names, up)
        left = lax.ppermute(left, names, down)
        out = jnp.where(ids == me - 1 - t, right[None], out)
        out = jnp.where(ids == me + 1 + t, left[None], out)
    return out


def plane_gather(x, owner):
    parts = [None] * 4
    parts[owner] = x
    for d in range(1, 4):
        parts[owner ^ d] = sent(x, owner ^ d, owner)
    return jnp.stack(parts)


def reduce_block(x, owner, section, order, early):
    rows, cols = x.shape
    n = lax.axis_size("dp")
    part = plane_sum(x.reshape(4, rows // 4, cols), section, order)
    piece = line_sum(part.reshape(n, rows // 4 // n, cols), "dp")
    if early:
        held = line_gather(plane_gather(piece, owner), "dp", owner)
        return held.transpose(1, 0, 2, 3).reshape(rows, cols)
    held = line_gather(piece, "dp").reshape(rows // 4, cols)
    return plane_gather(held, owner).reshape(rows, cols)


def to_owners(blocks, section, core):
    stacked = jnp.stack(blocks)
    got = [stacked[section]] + [flipped(stacked[section ^ d], "section", d) for d in (1, 2, 3)]
    here = (section // 2) == core
    near = jnp.stack(got[:2])
    away = jnp.stack(got[2:])
    mine = jnp.where(here, near, away)
    other = flipped(jnp.where(here, away, near), "group", 1)

    def in_order(pair):
        return jnp.where(section % 2 == 0, pair, pair[::-1])

    mine, other = in_order(mine), in_order(other)
    first = jnp.where(core == 0, mine, other)
    second = jnp.where(core == 0, other, mine)
    return jnp.concatenate([first, second], axis=1).reshape(-1, D)


MESH = pl.DeviceIdType.MESH
SMALL = 6144 // 128
UNITS = ((3, 0), (3, 1), (1, 0), (1, 1), (2, 0), (2, 1), (0, 0), (0, 1))
SEMS = 21


def unit_shape(s, part):
    if s % 2:
        return (FF // 2, D) if part else (HALF, FF)
    return (HALF, D) if part else (HALF, QKV)


def reduce_kernel(*refs):
    ins, small_in = refs[:16], refs[16]
    outs, small_out = refs[17:21], refs[21]
    own, core_in, plane1, plane2, up_in, down_in = (refs[22 + 8 * i : 30 + 8 * i] for i in range(6))
    sm, sm_core, sm_x, sm_y, sm_z, send, recv, sm_send, sm_recv = refs[70:]
    c = lax.axis_index("section")
    g = lax.axis_index("group")
    z = lax.axis_index("dp")
    x, y = c % 2, c // 2
    n = 4

    def flip(v, bit):
        if bit == 1:
            return v + 1 - 2 * (v % 2)
        if bit == 2:
            return (v + 2) % 4
        return 3 - v

    barrier = pltpu.get_barrier_semaphore()
    pl.semaphore_signal(barrier, inc=1, device_id={"group": 1 - g}, device_id_type=MESH)
    for bit in (1, 2, 3):
        pl.semaphore_signal(barrier, inc=1, device_id={"section": flip(c, bit)}, device_id_type=MESH)
        pl.semaphore_signal(barrier, inc=1, device_id={"dp": flip(z, bit)}, device_id_type=MESH)
    pl.semaphore_wait(barrier, 7)

    pending = []

    def push(cond, src, dst, u, k, device, start=True):
        copy = pltpu.make_async_remote_copy(
            src_ref=src, dst_ref=dst, send_sem=send.at[u, k], recv_sem=recv.at[u, k],
            device_id=device, device_id_type=MESH,
        )
        if cond is None:
            copy.start()
        else:
            pl.when(cond)(copy.start)
        pending.append((cond, copy))

    def landed(cond, dst, u, k):
        copy = pltpu.make_async_remote_copy(
            src_ref=dst, dst_ref=dst, send_sem=send.at[u, k], recv_sem=recv.at[u, k],
            device_id={"group": 1 - g}, device_id_type=MESH,
        )
        if cond is None:
            copy.wait_recv()
        else:
            pl.when(cond)(copy.wait_recv)

    def accumulate(into, terms, rows):
        strip = 32 if rows % 32 == 0 else 16

        def one(i, _):
            at = pl.ds(pl.multiple_of(i * strip, strip), strip)
            total = into[at, :].astype(F32)
            for term in terms:
                total = total + term[at, :].astype(F32)
            into[at, :] = total.astype(BF)
            return 0

        lax.fori_loop(0, rows // strip, one, 0)

    def quarter(u, q):
        rows = own[u].shape[0] // 4
        return own[u].at[pl.ds(pl.multiple_of(q * rows, rows), rows), :]

    def core_quarter(u, q):
        rows = own[u].shape[0] // 4
        return core_in[u].at[pl.ds(pl.multiple_of(q * rows, rows), rows), :]

    def piece(u, k):
        rows, cols = own[u].shape[0] // 8, own[u].shape[1] // 2
        first = c * 2 * rows + (k // 2) * rows
        return own[u].at[
            pl.ds(pl.multiple_of(first, rows), rows), pl.ds(pl.multiple_of((k % 2) * cols, cols), cols)
        ]

    def load(u):
        s, part = UNITS[u]
        copy = pltpu.make_async_copy(ins[4 * s + 2 * part], own[u], send.at[u, 0])
        copy.start()
        push(None, ins[4 * s + 2 * part + 1], core_in[u], u, 1, {"group": 1 - g})

    def split(u, b):
        if UNITS[u][1] == 0:
            return 2 * b + x, 2 * b + 1 - x
        return 2 * y + b, 2 * (1 - y) + b

    def first_step(u):
        part = UNITS[u][1]
        pltpu.make_async_copy(ins[4 * UNITS[u][0] + 2 * part], own[u], send.at[u, 0]).wait()
        landed(None, core_in[u], u, 1)
        rows = own[u].shape[0] // 4
        other = {"section": flip(c, 2 if part else 1)}
        for b in range(2):
            q = split(u, b)[1]
            accumulate(quarter(u, q), [core_quarter(u, q)], rows)
            push(None, quarter(u, q), plane1[u].at[b], u, 2 + b, other)
        for b in range(2):
            q = split(u, b)[0]
            accumulate(quarter(u, q), [core_quarter(u, q)], rows)

    def second_step(u):
        part = UNITS[u][1]
        rows = own[u].shape[0] // 4
        other = {"section": flip(c, 1 if part else 2)}
        for b in range(2):
            landed(None, plane1[u].at[b], u, 2 + b)
        b = (1 - x) if part else (1 - y)
        q = (2 * y + 1 - x) if part else (2 * (1 - y) + x)
        accumulate(quarter(u, q), [plane1[u].at[b]], rows)
        push(None, quarter(u, q), plane2[u], u, 4, other)
        accumulate(quarter(u, c), [plane1[u].at[1 - b]], rows)

    def line_step(u, t):
        rows = own[u].shape[0] // 8
        if t == 0:
            landed(None, plane2[u], u, 4)
            accumulate(quarter(u, c), [plane2[u]], 2 * rows)
        up = (z < n - 1) & (z <= t)
        down = (z > 0) & (z >= n - 1 - t)
        k_up = jnp.minimum(n - 1 - t + z, n - 1)
        k_down = jnp.maximum(z - (n - 1) + t, 0)
        if t > 0:

            @pl.when(up & (z > 0))
            def _():
                landed(None, up_in[u].at[t - 1], u, 5 + t - 1)
                accumulate(piece(u, k_up), [up_in[u].at[t - 1]], rows)

            @pl.when(down & (z < n - 1))
            def _():
                landed(None, down_in[u].at[t - 1], u, 8 + t - 1)
                accumulate(piece(u, k_down), [down_in[u].at[t - 1]], rows)

        push(up, piece(u, k_up), up_in[u].at[t], u, 5 + t, {"dp": jnp.minimum(z + 1, n - 1)})
        push(down, piece(u, k_down), down_in[u].at[t], u, 8 + t, {"dp": jnp.maximum(z - 1, 0)})

    def out_of(u):
        s, part = UNITS[u]
        return outs[2 * (s % 2) + part]

    def gather(u):
        s = UNITS[u][0]
        rows = own[u].shape[0] // 8

        @pl.when(z > 0)
        def _():
            landed(None, up_in[u].at[n - 2], u, 5 + n - 2)
            accumulate(piece(u, z), [up_in[u].at[n - 2]], rows)

        @pl.when(z < n - 1)
        def _():
            landed(None, down_in[u].at[n - 2], u, 8 + n - 2)
            accumulate(piece(u, z), [down_in[u].at[n - 2]], rows)

        held = out_of(u)
        for q in range(4):
            if q == s:
                copy = pltpu.make_async_copy(piece(u, z), held.at[z, q], send.at[u, 11 + q])
                pl.when(c == s)(copy.start)
            else:
                push(c == q, piece(u, z), held.at[z, q], u, 11 + q, {"section": s})

    def out_step(u, t):
        s = UNITS[u][0]
        held = out_of(u)
        mine = c == s
        if t == 0:
            for q in range(4):
                if q == s:
                    copy = pltpu.make_async_copy(piece(u, z), held.at[z, q], send.at[u, 11 + q])
                    pl.when(mine)(copy.wait)
                else:
                    landed(mine, held.at[z, q], u, 11 + q)
        else:
            landed(mine & (z >= t), held.at[jnp.maximum(z - t, 0)], u, 15 + t - 1)
            landed(mine & (z + t < n), held.at[jnp.minimum(z + t, n - 1)], u, 18 + t - 1)
        if t < n - 1:
            low, high = jnp.maximum(z - t, 0), jnp.minimum(z + t, n - 1)
            push(
                mine & (z >= t) & (z < n - 1), held.at[low], held.at[low], u, 15 + t,
                {"dp": jnp.minimum(z + 1, n - 1)},
            )
            push(
                mine & (z + t < n) & (z > 0), held.at[high], held.at[high], u, 18 + t,
                {"dp": jnp.maximum(z - 1, 0)},
            )

    def small_push(src, dst, k, device):
        copy = pltpu.make_async_remote_copy(
            src_ref=src, dst_ref=dst, send_sem=sm_send.at[k], recv_sem=sm_recv.at[k],
            device_id=device, device_id_type=MESH,
        )
        copy.start()
        pending.append((None, copy))
        return copy

    def small_step(k):
        if k == 0:
            sm[...] = small_in[...]
            small_push(sm, sm_core, 0, {"group": 1 - g}).wait_recv()
            both = jnp.where(g == 0, sm[...] + sm_core[...], sm_core[...] + sm[...])
            sm_x[0] = both
        elif k == 1:
            for b in range(2):
                small_push(sm_x.at[0, 2 * b + 1 - x], sm_x.at[1, b], 1 + b, {"section": flip(c, 1)})
        elif k == 2:
            for b in range(2):
                landed_small(sm_x.at[1, b], 1 + b)
                sm_y[b] = sm_x[0, 2 * b + x] + sm_x[1, b]
            small_push(sm_y.at[1 - y], sm_y.at[2], 3, {"section": flip(c, 2)})
        elif k == 3:
            landed_small(sm_y.at[2], 3)
            sm_z[z] = sm_y[y] + sm_y[2]
            for bit in (1, 2, 3):
                small_push(sm_z.at[z], sm_z.at[z], 3 + bit, {"dp": flip(z, bit)})
        else:
            for bit in (1, 2, 3):
                landed_small(sm_z.at[flip(z, bit)], 3 + bit)
            small_out[...] = sm_z[0] + sm_z[1] + sm_z[2] + sm_z[3]

    def landed_small(dst, k):
        pltpu.make_async_remote_copy(
            src_ref=dst, dst_ref=dst, send_sem=sm_send.at[k], recv_sem=sm_recv.at[k],
            device_id={"group": 1 - g}, device_id_type=MESH,
        ).wait_recv()

    stages = (
        [first_step, second_step]
        + [partial(line_step, t=t) for t in range(n - 1)]
        + [gather]
        + [partial(out_step, t=t) for t in range(n)]
    )
    for u in range(4):
        load(u)
    small_step(0)
    jobs = len(UNITS) // 2
    for slot in range(jobs + len(stages) - 1):
        if slot < 2:
            load(2 * slot + 4)
            load(2 * slot + 5)
        if 1 <= slot <= 4:
            small_step(slot)
        for job in reversed(range(jobs)):
            stage = slot - job
            if 0 <= stage < len(stages):
                for u in (2 * job, 2 * job + 1):
                    stages[stage](u)
    for cond, copy in pending:
        if cond is None:
            copy.wait_send()
        else:
            pl.when(cond)(copy.wait_send)


def reduce_call(grads, small):
    ins = [x for s in range(4) for x in grads[s]]
    hbm = pl.BlockSpec(memory_space=pl.ANY)
    shapes = [unit_shape(*u) for u in UNITS]
    held = [unit_shape(s, part) for s in (0, 1) for part in (0, 1)]
    pieces = [(r // 8, w // 2) for r, w in shapes]
    scratch = (
        [pltpu.VMEM(s, BF) for s in shapes]
        + [pltpu.VMEM(s, BF) for s in shapes]
        + [pltpu.VMEM((2, r // 4, w), BF) for r, w in shapes]
        + [pltpu.VMEM((r // 4, w), BF) for r, w in shapes]
        + [pltpu.VMEM((3,) + p, BF) for p in pieces]
        + [pltpu.VMEM((3,) + p, BF) for p in pieces]
        + [
            pltpu.VMEM((4, SMALL, 128), F32),
            pltpu.VMEM((4, SMALL, 128), F32),
            pltpu.VMEM((2, 4, SMALL, 128), F32),
            pltpu.VMEM((3, SMALL, 128), F32),
            pltpu.VMEM((4, SMALL, 128), F32),
            pltpu.SemaphoreType.DMA((len(UNITS), SEMS)),
            pltpu.SemaphoreType.DMA((len(UNITS), SEMS)),
            pltpu.SemaphoreType.DMA((7,)),
            pltpu.SemaphoreType.DMA((7,)),
        ]
    )
    *out, small = pl.pallas_call(
        reduce_kernel,
        out_shape=[sds((4, 4, r // 8, w // 2), BF) for r, w in held] + [sds((SMALL, 128), F32)],
        in_specs=[hbm] * 16 + [pl.BlockSpec(memory_space=pltpu.VMEM)],
        out_specs=[hbm] * 4 + [pl.BlockSpec(memory_space=pltpu.VMEM)],
        scratch_shapes=scratch,
        compiler_params=pltpu.CompilerParams(
            collective_id=1, has_side_effects=True, vmem_limit_bytes=62 * 1024 * 1024
        ),
        name="reduce",
    )(*ins, small)

    def in_place(x):
        _, _, r, w = x.shape
        x = x.reshape(2, 2, 4, r, w).transpose(2, 0, 3, 1, 4)
        return x.reshape(8 * r, 2 * w)

    return [in_place(x) for x in out], small


def body(
    activations, weight_in, weight_out, bias_in, bias_out, norm_gain, norm_shift, rope_freq,
    image_sides, cotangent,
):
    sections = lax.axis_size("section")
    groups = lax.axis_size("group")
    section = lax.axis_index("section")
    group = lax.axis_index("group")
    core = group % 2
    micro = image_sides.shape[0]
    capacity = activations.shape[0] // micro
    tokens = capacity // 2
    assert sections == 4 and groups % 2 == 0 and 2 * micro == sections
    fast = groups == 2 and lax.axis_size("dp") == 4

    here = (section // 2) == core
    local = section % 2

    def take(x):
        own = lax.dynamic_index_in_dim(x.reshape(micro, capacity, D), local, 0, keepdims=False)
        give = lax.dynamic_slice_in_dim(own, (1 - core) * tokens, tokens, 0)
        keep = lax.dynamic_slice_in_dim(own, core * tokens, tokens, 0)
        return jnp.where(here, keep, flipped(give, "group", 1))

    h = take(activations)
    own_sides = lax.dynamic_index_in_dim(image_sides, local, 0, keepdims=False)
    sides = jnp.where(here, own_sides, flipped(own_sides, "group", 1))
    segment, patch_row, patch_col, is_valid = layout(sides, capacity)
    pos_all = jnp.stack([patch_col, patch_row], axis=1).astype(F32)

    def half_of(x, which):
        return lax.dynamic_slice_in_dim(x, which * tokens, tokens, 0)

    pos = half_of(pos_all, core)
    seg_m, seg_t = half_of(segment, core), half_of(segment, 1 - core)
    valid = half_of(is_valid, core)
    g = take(cotangent) * valid[:, None].astype(BF)

    small = jnp.concatenate(
        [bias_in[0], bias_out[0], norm_gain[0], norm_shift[0], rope_freq[0].reshape(-1)]
    )
    small = lax.all_gather(small, ("section", "group")).reshape(4, groups, -1).astype(F32)
    widths = [FF // groups, D // groups, D // groups, D // groups, D // groups]
    starts = [sum(widths[:i]) for i in range(5)]
    b_in, b_out, gain, shift, freq = (
        small[:, :, a : a + w] for a, w in zip(starts, widths)
    )
    b_in, b_out, gain, shift = (x.reshape(4, 1, -1) for x in (b_in, b_out, gain, shift))
    freq = freq.reshape(4, groups, 2, -1).transpose(0, 2, 1, 3).reshape(4, 2, D // 2)
    pars = [
        jnp.concatenate([gain[s], shift[s], jnp.zeros((6, D), F32)], axis=0) for s in range(4)
    ]
    turns = [turning(freq[s], pos) for s in (0, 2)]

    weights = []
    if fast:
        rot = core.reshape(1).astype(jnp.int32)
        shared = lax.ppermute(weight_out[0, HALF:D], "group", [(0, 1)])
        low_out = jnp.where(core == 0, weight_out[0, :HALF], shared)
        for s in range(4):
            if s % 2 == 0:
                blocks = [weight_in[0, :, :QKV], low_out]
            else:
                blocks = [weight_in[0], weight_out[0]]
            blocks = spread(blocks, s, section)
            others = [flipped(b, "group", 1) for b in blocks]
            weights.append((blocks[0], others[0], blocks[1], others[1]))
    else:
        rot = jnp.zeros((1,), jnp.int32)
        all_in = lax.all_gather(weight_in, "group", axis=1, tiled=True)
        all_out = lax.all_gather(weight_out, "group", axis=1, tiled=True)
        all_in = lax.all_gather(all_in, "section", axis=0, tiled=True)
        all_out = lax.all_gather(all_out, "section", axis=0, tiled=True)
        for s in range(4):
            cols, rows = (QKV, D) if s % 2 == 0 else (FF, FF)
            w_in, w_out = all_in[s, :, :cols], all_out[s, :rows]
            weights.append((w_in[:HALF], w_in[HALF:], w_out[: rows // 2], w_out[rows // 2 :]))

    saved = []
    streams = [h]
    for s in range(4):
        wia, wib, woa, wob = weights[s]
        if s % 2 == 0:
            cosines, sines = turns[s // 2]
            qkv, nrm = qkv_call(rot, h, pars[s], wia, wib, b_in[s, :, :QKV], cosines, sines)
            kv_t = flipped(qkv[:, D:], "group", 1)
            o, lse, h = attend_call(
                rot, qkv, kv_t, seg_m[:, None], seg_m[None], seg_t[None], h, woa, wob, b_out[s]
            )
            saved.append((qkv, nrm, kv_t, o, lse))
        else:
            act, slope, nrm, h = ff_call(rot, h, pars[s], wia, wib, b_in[s], woa, wob, b_out[s])
            saved.append((act, slope, nrm))
        streams.append(h)

    outputs = to_owners(streams[1:], section, core)

    grads = [None] * 4
    in_grads = [None] * 4
    smalls = [None] * 4
    for s in (3, 2, 1, 0):
        wia, wib, woa, wob = weights[s]
        if s % 2 == 0:
            qkv, nrm, kv_t, o, lse = saved[s]
            cosines, sines = turns[s // 2]
            dmix, delta, doa, dob = mix_back_call(rot, g, o, woa, wob)
            dq, dkm, dvm, dkt, dvt = attend_back_call(
                qkv, kv_t, dmix, lse, delta, seg_m[None], seg_m[:, None], seg_t[:, None]
            )
            dkr, dvr = flipped(dkt, "group", 1), flipped(dvt, "group", 1)
            dia, dib, dbin, rest, g = qkv_back_call(
                rot, dq, dkm, dvm, dkr, dvr, qkv, cosines, sines, pos, nrm, wia, wib,
                streams[s], pars[s], g,
            )
            dbin = jnp.concatenate([dbin, jnp.zeros((1, FF - QKV), F32)], axis=1)
            dfreq = rest[3:5].reshape(2, HEADS, HD)[:, :, : HD // 2].reshape(-1)
        else:
            act, slope, nrm = saved[s]
            dia, dib, doa, dob, dbin, rest, g = ff_back_call(
                rot, g, act, slope, nrm, wia, wib, woa, wob, streams[s], pars[s]
            )
            dfreq = jnp.zeros((D,), F32)
        in_grads[s] = g
        grads[s] = (dia, dib, doa, dob)
        smalls[s] = jnp.concatenate([dbin.reshape(-1), rest[:3].reshape(-1), dfreq])
    input_grads = to_owners(in_grads, section, core)

    small_sum = jnp.stack(smalls)
    if fast:
        sums, small_sum = reduce_call(grads, small_sum.reshape(4, SMALL, 128))
        small_sum = small_sum.reshape(-1)
        in_a, out_a, in_f, out_f = sums
        both = jnp.concatenate([out_a, flipped(out_a, "group", 1)], axis=0)
        both = jnp.where(core == 0, jnp.pad(both, ((0, FF // 2 - D), (0, 0))), jnp.zeros((), BF))
        attends = section % 2 == 0
        out_in = jnp.where(attends, jnp.pad(in_a, ((0, 0), (0, FF - QKV))), in_f).astype(F32)
        out_out = jnp.where(attends, both, out_f).astype(F32)
    else:
        small_sum = lax.psum(small_sum, ("section", "group", "dp"))[section]
        rows_in, rows_out = D // groups, FF // groups
        d_in = jnp.stack(
            [
                jnp.pad(jnp.concatenate(x[:2]), ((0, 0), (0, FF - x[0].shape[1])))
                for x in grads
            ]
        )
        d_out = jnp.stack(
            [
                jnp.pad(jnp.concatenate(x[2:]), ((0, FF - 2 * x[2].shape[0]), (0, 0)))
                for x in grads
            ]
        )

        def owned(x, rows):
            x = lax.psum_scatter(x, "section", scatter_dimension=0, tiled=True)[0]
            x = lax.psum_scatter(x, "group", scatter_dimension=0, tiled=True)
            return lax.psum(x, "dp").astype(F32)

        out_in, out_out = owned(d_in, rows_in), owned(d_out, rows_out)

    def piece(start, width):
        w = width // groups
        return lax.dynamic_slice_in_dim(small_sum, start + group * w, w, 0)[None]

    d_freq = small_sum[FF + 3 * D :].reshape(2, D // 2)
    d_freq = lax.dynamic_slice_in_dim(d_freq, group * (D // 2 // groups), D // 2 // groups, 1)
    return (
        outputs[None],
        input_grads[None],
        out_in[None],
        out_out[None],
        piece(0, FF),
        piece(FF, D),
        piece(FF + D, D),
        piece(FF + 2 * D, D),
        d_freq[None],
    )


def solution(mesh):
    placed = (
        P(("group", "dp"), None),
        P("section", "group", None),
        P("section", "group", None),
        P("section", "group"),
        P("section", "group"),
        P("section", "group"),
        P("section", "group"),
        P("section", None, "group"),
        P(("group", "dp"), None),
        P(("group", "dp"), None),
    )
    return jax.shard_map(
        body,
        mesh=mesh,
        in_specs=placed,
        out_specs=(
            P("section", ("group", "dp"), None),
            P("section", ("group", "dp"), None),
            P("section", "group", None),
            P("section", "group", None),
            P("section", "group"),
            P("section", "group"),
            P("section", "group"),
            P("section", "group"),
            P("section", None, "group"),
        ),
        check_vma=False,
    )
```

```python
from functools import partial

import jax
import jax.numpy as jnp
from jax import lax
from jax.experimental import pallas as pl
from jax.experimental.pallas import tpu as pltpu
from jax.sharding import PartitionSpec as P

D = 768
HEADS = 12
HD = 64
FF = 3072
HALF = D // 2
PAIRS = HEADS // 2
QKV = 3 * D
EPSILON = 1e-06
BF = jnp.bfloat16
F32 = jnp.float32
NT = (((1,), (1,)), ((), ()))
TN = (((0,), (0,)), ((), ()))
VMEM_BYTES = 52 * 1024 * 1024


def dot(a, b):
    return jnp.dot(a, b, preferred_element_type=F32)


def dot_nt(a, b):
    return lax.dot_general(a, b, NT, preferred_element_type=F32)


def dot_tn(a, b):
    return lax.dot_general(a, b, TN, preferred_element_type=F32)


def normalize(h):
    average = jnp.mean(h, axis=-1, keepdims=True)
    centered = h - average
    variance = jnp.mean(centered * centered, axis=-1, keepdims=True)
    scale = lax.rsqrt(variance + EPSILON)
    return centered * scale, scale


def turn_halves(x, rot):
    return jnp.where(rot == 0, x, jnp.concatenate([x[:, HALF:], x[:, :HALF]], axis=1))


def swap_pairs(x):
    lanes = lax.broadcasted_iota(jnp.int32, x.shape, 1)
    low = (lanes % HD) < HD // 2
    return jnp.where(
        low, pltpu.roll(x, x.shape[1] - HD // 2, 1), pltpu.roll(x, HD // 2, 1)
    )


def norm_backward(h, gain, grad, d_normed):
    xhat, scale = normalize(h)
    e = d_normed * gain
    mean_e = jnp.mean(e, axis=-1, keepdims=True)
    mean_ex = jnp.mean(e * xhat, axis=-1, keepdims=True)
    g = grad + scale * (e - mean_e - xhat * mean_ex)
    d_gain = jnp.sum(d_normed * xhat, axis=0, keepdims=True)
    d_shift = jnp.sum(d_normed, axis=0, keepdims=True)
    return g, d_gain, d_shift


def qkv_kernel(rot_ref, h_ref, par_ref, wa_ref, wb_ref, bias_ref, cos_ref, sin_ref, out_ref, nrm_ref):
    j = pl.program_id(0)

    @pl.when(j == 0)
    def _():
        xhat, _ = normalize(h_ref[...].astype(F32))
        normed = xhat * par_ref[0:1, :] + par_ref[1:2, :]
        nrm_ref[...] = turn_halves(normed, rot_ref[0]).astype(BF)

    x = dot(nrm_ref[:, :HALF], wa_ref[...]) + dot(nrm_ref[:, HALF:], wb_ref[...]) + bias_ref[...]

    @pl.when(j < 2)
    def _():
        y = x * cos_ref[...] + swap_pairs(x) * sin_ref[...]
        out_ref[...] = (y * jnp.where(j == 0, HD ** (-0.5), 1.0)).astype(BF)

    @pl.when(j == 2)
    def _():
        out_ref[...] = x.astype(BF)


def attend_kernel(
    rot_ref, q_ref, km_ref, vm_ref, kt_ref, vt_ref, segq_ref, segm_ref, segt_ref, h_ref,
    woa_ref, wob_ref, bias_ref, o_ref, lse_ref, out_ref, lse_scr,
):
    j = pl.program_id(0)
    rows = q_ref.shape[0]
    lanes = lax.broadcasted_iota(jnp.int32, (rows, 2 * HD), 1)
    q = q_ref[...]
    same_m = segq_ref[...] == segm_ref[...]
    same_t = segq_ref[...] == segt_ref[...]
    outs = []
    for side in range(2):
        mine = (lanes >= HD) if side else (lanes < HD)
        q_head = jnp.where(mine, q, jnp.zeros_like(q))
        s_m = jnp.where(same_m, dot_nt(q_head, km_ref[...]), -1e9)
        s_t = jnp.where(same_t, dot_nt(q_head, kt_ref[...]), -1e9)
        top = jnp.maximum(
            jnp.max(s_m, axis=-1, keepdims=True), jnp.max(s_t, axis=-1, keepdims=True)
        )
        p_m = jnp.exp(s_m - top)
        p_t = jnp.exp(s_t - top)
        total = jnp.sum(p_m, axis=-1, keepdims=True) + jnp.sum(p_t, axis=-1, keepdims=True)
        o = dot(p_m.astype(BF), vm_ref[...]) + dot(p_t.astype(BF), vt_ref[...])
        outs.append(o / total)
        lse_scr[...] = jnp.where(lanes == 2 * j + side, top + jnp.log(total), lse_scr[...])
    o_ref[:, pl.ds(pl.multiple_of(j * 2 * HD, 2 * HD), 2 * HD)] = jnp.where(
        lanes < HD, outs[0], outs[1]
    ).astype(BF)

    @pl.when(j == PAIRS - 1)
    def _():
        lse_ref[...] = jnp.transpose(lse_scr[...])[:16, :]
        o_all = turn_halves(o_ref[...].astype(F32), rot_ref[0]).astype(BF)
        y = dot(o_all[:, :HALF], woa_ref[...]) + dot(o_all[:, HALF:], wob_ref[...])
        out_ref[...] = (h_ref[...].astype(F32) + y + bias_ref[...]).astype(BF)


def ff_kernel(
    rot_ref, h_ref, par_ref, wia_ref, wib_ref, bias_ref, woa_ref, wob_ref, bout_ref,
    act_ref, slope_ref, nrm_ref, out_ref, acc_ref,
):
    j = pl.program_id(0)
    n = pl.num_programs(0)

    @pl.when(j == 0)
    def _():
        xhat, _ = normalize(h_ref[...].astype(F32))
        normed = xhat * par_ref[0:1, :] + par_ref[1:2, :]
        nrm_ref[...] = turn_halves(normed, rot_ref[0]).astype(BF)
        acc_ref[...] = h_ref[...].astype(F32) + bout_ref[...]

    u = dot(nrm_ref[:, :HALF], wia_ref[...]) + dot(nrm_ref[:, HALF:], wib_ref[...]) + bias_ref[...]
    cdf = 0.5 + 0.5 * lax.erf(u * (0.5**0.5))
    act = (u * cdf).astype(BF)
    act_ref[...] = act
    pdf = jnp.exp(u * u * -0.5) * 0.3989422804014327
    slope_ref[...] = (cdf + u * pdf).astype(BF)

    @pl.when(j < n // 2)
    def _():
        acc_ref[...] += dot(act, woa_ref[...])

    @pl.when(j >= n // 2)
    def _():
        acc_ref[...] += dot(act, wob_ref[...])

    @pl.when(j == n - 1)
    def _():
        out_ref[...] = acc_ref[...].astype(BF)


def ff_back_kernel(
    rot_ref, g_ref, act_ref, slope_ref, nrm_ref, wia_ref, wib_ref, woa_ref, wob_ref, h_ref, par_ref,
    dia_ref, dib_ref, doa_ref, dob_ref, dbin_ref, small_ref, out_ref, acc_ref,
):
    j = pl.program_id(0)
    n = pl.num_programs(0)

    @pl.when(j == 0)
    def _():
        acc_ref[...] = jnp.zeros_like(acc_ref)

    def step(wo_ref, do_ref):
        g = g_ref[...]
        d_up_f = dot_nt(g, wo_ref[...]) * slope_ref[...].astype(F32)
        d_up = d_up_f.astype(BF)
        do_ref[...] = dot_tn(act_ref[...], g).astype(BF)
        dbin_ref[...] = jnp.sum(d_up_f, axis=0, keepdims=True)
        dia_ref[...] = dot_tn(nrm_ref[:, :HALF], d_up).astype(BF)
        dib_ref[...] = dot_tn(nrm_ref[:, HALF:], d_up).astype(BF)
        acc_ref[:, :HALF] += dot_nt(d_up, wia_ref[...])
        acc_ref[:, HALF:] += dot_nt(d_up, wib_ref[...])

    @pl.when(j < n // 2)
    def _():
        step(woa_ref, doa_ref)

    @pl.when(j >= n // 2)
    def _():
        step(wob_ref, dob_ref)

    @pl.when(j == n - 1)
    def _():
        g = g_ref[...].astype(F32)
        d_normed = turn_halves(acc_ref[...], rot_ref[0])
        out, d_gain, d_shift = norm_backward(h_ref[...].astype(F32), par_ref[0:1, :], g, d_normed)
        out_ref[...] = out.astype(BF)
        small_ref[0:1, :] = jnp.sum(g, axis=0, keepdims=True)
        small_ref[1:2, :] = d_gain
        small_ref[2:3, :] = d_shift
        small_ref[3:8, :] = jnp.zeros((5, D), F32)


def mix_back_kernel(rot_ref, g_ref, o_ref, woa_ref, wob_ref, dmix_ref, delta_ref, doa_ref, dob_ref):
    g = g_ref[...]
    rot = rot_ref[0]
    d_mix = jnp.concatenate([dot_nt(g, woa_ref[...]), dot_nt(g, wob_ref[...])], axis=1)
    d_mix = turn_halves(d_mix, rot).astype(BF)
    dmix_ref[...] = d_mix
    o = o_ref[...].astype(F32)
    product = d_mix.astype(F32) * o
    head = lax.broadcasted_iota(jnp.int32, (16, D), 0)
    lanes = lax.broadcasted_iota(jnp.int32, (16, D), 1)
    chosen = jnp.where(lanes // HD == head, 1.0, 0.0)
    delta_ref[...] = lax.dot_general(
        chosen, product, NT, preferred_element_type=F32, precision=lax.Precision.HIGHEST
    )
    turned = turn_halves(o, rot).astype(BF)
    doa_ref[...] = dot_tn(turned[:, :HALF], g).astype(BF)
    dob_ref[...] = dot_tn(turned[:, HALF:], g).astype(BF)


def attend_back_kernel(
    q_ref, km_ref, vm_ref, kt_ref, vt_ref, do_ref, lse_ref, delta_ref, segq_ref, segm_ref, segt_ref,
    dq_ref, dkm_ref, dvm_ref, dkt_ref, dvt_ref,
):
    j = pl.program_id(0)
    rows = q_ref.shape[0]
    lanes = lax.broadcasted_iota(jnp.int32, (rows, 2 * HD), 1)
    q = q_ref[...]
    do = do_ref[...]
    zero = jnp.zeros_like(q)
    d_q = jnp.zeros((rows, 2 * HD), F32)
    sets = ((km_ref, vm_ref, segm_ref), (kt_ref, vt_ref, segt_ref))
    d_k = [0.0, 0.0]
    d_v = [0.0, 0.0]
    for side in range(2):
        mine = (lanes >= HD) if side else (lanes < HD)
        q_head = jnp.where(mine, q, zero)
        do_head = jnp.where(mine, do, zero)
        lse = lse_ref[pl.ds(2 * j + side, 1), :]
        delta = delta_ref[pl.ds(2 * j + side, 1), :]
        for i, (k_ref, v_ref, seg_ref) in enumerate(sets):
            k = k_ref[...]
            s_t = dot_nt(k, q_head)
            p_t = jnp.where(seg_ref[...] == segq_ref[...], jnp.exp(s_t - lse), 0.0)
            d_p = dot_nt(v_ref[...], do_head)
            d_s = (p_t * (d_p - delta)).astype(BF)
            d_v[i] += dot(p_t.astype(BF), do_head)
            d_k[i] += dot(d_s, q_head)
            d_q += dot_tn(d_s, jnp.where(mine, k, zero))
    dq_ref[...] = d_q
    dkm_ref[...] = d_k[0]
    dvm_ref[...] = d_v[0]
    dkt_ref[...] = d_k[1].astype(BF)
    dvt_ref[...] = d_v[1].astype(BF)


def qkv_back_kernel(
    rot_ref, dq_ref, dkm_ref, dvm_ref, dkr_ref, dvr_ref, qkv_ref, cos_ref, sin_ref, pos_ref,
    nrm_ref, wa_ref, wb_ref, h_ref, par_ref, g_ref,
    dia_ref, dib_ref, dbin_ref, small_ref, out_ref, acc_ref, dp_ref,
):
    j = pl.program_id(0)
    n = pl.num_programs(0)

    @pl.when(j == 0)
    def _():
        acc_ref[...] = jnp.zeros_like(acc_ref)
        small_ref[...] = jnp.zeros_like(small_ref)

    def turned_back(dy, y):
        swapped = swap_pairs(dy)
        d_angle = y * swapped - swap_pairs(y) * dy
        small_ref[3:4, :] += jnp.sum(d_angle * pos_ref[:, 0:1], axis=0, keepdims=True)
        small_ref[4:5, :] += jnp.sum(d_angle * pos_ref[:, 1:2], axis=0, keepdims=True)
        return dy * cos_ref[...] - swapped * sin_ref[...]

    @pl.when(j == 0)
    def _():
        d_y = dq_ref[...] * HD ** (-0.5)
        y = qkv_ref[...].astype(F32) * HD**0.5
        dp_ref[...] = turned_back(d_y, y)

    @pl.when(j == 1)
    def _():
        d_y = dkm_ref[...] + dkr_ref[...].astype(F32)
        dp_ref[...] = turned_back(d_y, qkv_ref[...].astype(F32))

    @pl.when(j == 2)
    def _():
        dp_ref[...] = dvm_ref[...] + dvr_ref[...].astype(F32)

    d_f = dp_ref[...]
    d_p = d_f.astype(BF)
    dbin_ref[...] = jnp.sum(d_f, axis=0, keepdims=True)
    dia_ref[...] = dot_tn(nrm_ref[:, :HALF], d_p).astype(BF)
    dib_ref[...] = dot_tn(nrm_ref[:, HALF:], d_p).astype(BF)
    acc_ref[:, :HALF] += dot_nt(d_p, wa_ref[...])
    acc_ref[:, HALF:] += dot_nt(d_p, wb_ref[...])

    @pl.when(j == n - 1)
    def _():
        g = g_ref[...].astype(F32)
        d_normed = turn_halves(acc_ref[...], rot_ref[0])
        out, d_gain, d_shift = norm_backward(h_ref[...].astype(F32), par_ref[0:1, :], g, d_normed)
        out_ref[...] = out.astype(BF)
        small_ref[0:1, :] = jnp.sum(g, axis=0, keepdims=True)
        small_ref[1:2, :] = d_gain
        small_ref[2:3, :] = d_shift


def params_of(n=1):
    return pltpu.CompilerParams(
        dimension_semantics=("arbitrary",) * n, vmem_limit_bytes=VMEM_BYTES
    )


def whole(shape):
    return pl.BlockSpec(shape, lambda *_: (0,) * len(shape))


def sds(shape, dtype):
    return jax.ShapeDtypeStruct(shape, dtype)


def cost(flops, nbytes, trans=0):
    return pl.CostEstimate(flops=flops, bytes_accessed=nbytes, transcendentals=trans)


def qkv_call(rot, h, par, wa, wb, bias, cosines, sines):
    t = h.shape[0]
    return pl.pallas_call(
        qkv_kernel,
        out_shape=(sds((t, QKV), BF), sds((t, D), BF)),
        grid_spec=pltpu.PrefetchScalarGridSpec(
            num_scalar_prefetch=1,
            grid=(3,),
            in_specs=[
                whole((t, D)), whole((8, D)),
                pl.BlockSpec((HALF, D), lambda j, r: (0, j)),
                pl.BlockSpec((HALF, D), lambda j, r: (0, j)),
                pl.BlockSpec((1, D), lambda j, r: (0, j)),
                whole((t, D)), whole((t, D)),
            ],
            out_specs=[pl.BlockSpec((t, D), lambda j, r: (0, j)), whole((t, D))],
        ),
        compiler_params=params_of(),
        cost_estimate=cost(2 * t * D * QKV, 2 * D * QKV + 8 * t * D + 2 * t * QKV),
        name="qkv",
    )(rot, h, par, wa, wb, bias, cosines, sines)


def attend_call(rot, qkv, kv_t, seg_col, seg_m, seg_t, h, woa, wob, bias):
    t = h.shape[0]
    w = 2 * HD
    return pl.pallas_call(
        attend_kernel,
        out_shape=(sds((t, D), BF), sds((16, t), F32), sds((t, D), BF)),
        grid_spec=pltpu.PrefetchScalarGridSpec(
            num_scalar_prefetch=1,
            grid=(PAIRS,),
            in_specs=[
                pl.BlockSpec((t, w), lambda j, r: (0, j)),
                pl.BlockSpec((t, w), lambda j, r: (0, j + PAIRS)),
                pl.BlockSpec((t, w), lambda j, r: (0, j + 2 * PAIRS)),
                pl.BlockSpec((t, w), lambda j, r: (0, j)),
                pl.BlockSpec((t, w), lambda j, r: (0, j + PAIRS)),
                whole((t, 1)), whole((1, t)), whole((1, t)), whole((t, D)),
                whole((HALF, D)), whole((HALF, D)), whole((1, D)),
            ],
            out_specs=[whole((t, D)), whole((16, t)), whole((t, D))],
            scratch_shapes=[pltpu.VMEM((t, w), F32)],
        ),
        compiler_params=params_of(),
        cost_estimate=cost(8 * t * t * D * 4, 16 * t * D, 2 * t * t * HEADS),
        name="attend",
    )(rot, qkv, qkv, qkv, kv_t, kv_t, seg_col, seg_m, seg_t, h, woa, wob, bias)


def ff_specs(t, blocks):
    width = FF // blocks
    half = blocks // 2
    w_in = pl.BlockSpec((HALF, width), lambda j, r: (0, (j + half * r[0]) % blocks))
    b_in = pl.BlockSpec((1, width), lambda j, r: (0, (j + half * r[0]) % blocks))
    w_a = pl.BlockSpec((width, D), lambda j, r: (jnp.minimum(j, half - 1), 0))
    w_b = pl.BlockSpec((width, D), lambda j, r: (jnp.maximum(j - half, 0), 0))
    hid = pl.BlockSpec((t, width), lambda j, r: (0, j))
    return w_in, b_in, w_a, w_b, hid


def ff_call(rot, h, par, wia, wib, bias, woa, wob, bout):
    t = h.shape[0]
    blocks = 6
    w_in, b_in, w_a, w_b, hid = ff_specs(t, blocks)
    return pl.pallas_call(
        ff_kernel,
        out_shape=(sds((t, FF), BF), sds((t, FF), BF), sds((t, D), BF), sds((t, D), BF)),
        grid_spec=pltpu.PrefetchScalarGridSpec(
            num_scalar_prefetch=1,
            grid=(blocks,),
            in_specs=[whole((t, D)), whole((8, D)), w_in, w_in, b_in, w_a, w_b, whole((1, D))],
            out_specs=[hid, hid, whole((t, D)), whole((t, D))],
            scratch_shapes=[pltpu.VMEM((t, D), F32)],
        ),
        compiler_params=params_of(),
        cost_estimate=cost(4 * t * D * FF, 4 * D * FF + 4 * t * FF, 2 * t * FF),
        name="feed",
    )(rot, h, par, wia, wib, bias, woa, wob, bout)


def ff_back_call(rot, g, act, slope, nrm, wia, wib, woa, wob, h, par):
    t = h.shape[0]
    blocks = 6
    w_in, b_in, w_a, w_b, hid = ff_specs(t, blocks)
    return pl.pallas_call(
        ff_back_kernel,
        out_shape=(
            sds((HALF, FF), BF), sds((HALF, FF), BF), sds((FF // 2, D), BF), sds((FF // 2, D), BF),
            sds((1, FF), F32), sds((8, D), F32), sds((t, D), BF),
        ),
        grid_spec=pltpu.PrefetchScalarGridSpec(
            num_scalar_prefetch=1,
            grid=(blocks,),
            in_specs=[
                whole((t, D)), hid, hid, whole((t, D)), w_in, w_in, w_a, w_b, whole((t, D)),
                whole((8, D)),
            ],
            out_specs=[w_in, w_in, w_a, w_b, b_in, whole((8, D)), whole((t, D))],
            scratch_shapes=[pltpu.VMEM((t, D), F32)],
        ),
        compiler_params=params_of(),
        cost_estimate=cost(8 * t * D * FF, 8 * D * FF + 4 * t * FF),
        name="feed_back",
    )(rot, g, act, slope, nrm, wia, wib, woa, wob, h, par)


def mix_back_call(rot, g, o, woa, wob):
    t = g.shape[0]
    return pl.pallas_call(
        mix_back_kernel,
        out_shape=(sds((t, D), BF), sds((16, t), F32), sds((HALF, D), BF), sds((HALF, D), BF)),
        grid_spec=pltpu.PrefetchScalarGridSpec(
            num_scalar_prefetch=1,
            grid=(1,),
            in_specs=[whole((t, D)), whole((t, D)), whole((HALF, D)), whole((HALF, D))],
            out_specs=[whole((t, D)), whole((16, t)), whole((HALF, D)), whole((HALF, D))],
        ),
        compiler_params=params_of(),
        cost_estimate=cost(4 * t * D * D, 4 * D * D + 6 * t * D),
        name="mix_back",
    )(rot, g, o, woa, wob)


def attend_back_call(qkv, kv_t, dmix, lse, delta, seg_row, seg_m, seg_t):
    t = dmix.shape[0]
    w = 2 * HD
    col = pl.BlockSpec((t, w), lambda j: (0, j))
    return pl.pallas_call(
        attend_back_kernel,
        out_shape=(sds((t, D), F32), sds((t, D), F32), sds((t, D), F32), sds((t, D), BF), sds((t, D), BF)),
        grid=(PAIRS,),
        in_specs=[
            col,
            pl.BlockSpec((t, w), lambda j: (0, j + PAIRS)),
            pl.BlockSpec((t, w), lambda j: (0, j + 2 * PAIRS)),
            col,
            pl.BlockSpec((t, w), lambda j: (0, j + PAIRS)),
            col, whole((16, t)), whole((16, t)), whole((1, t)), whole((t, 1)), whole((t, 1)),
        ],
        out_specs=[col] * 5,
        compiler_params=params_of(),
        cost_estimate=cost(20 * t * t * D * 4, 30 * t * D, 2 * t * t * HEADS),
        name="attend_back",
    )(qkv, qkv, qkv, kv_t, kv_t, dmix, lse, delta, seg_row, seg_m, seg_t)


def qkv_back_call(rot, dq, dkm, dvm, dkr, dvr, qkv, cosines, sines, pos, nrm, wa, wb, h, par, g):
    t = h.shape[0]
    w_in = pl.BlockSpec((HALF, D), lambda j, r: (0, j))
    rows = whole((t, D))
    return pl.pallas_call(
        qkv_back_kernel,
        out_shape=(
            sds((HALF, QKV), BF), sds((HALF, QKV), BF), sds((1, QKV), F32), sds((8, D), F32),
            sds((t, D), BF),
        ),
        grid_spec=pltpu.PrefetchScalarGridSpec(
            num_scalar_prefetch=1,
            grid=(3,),
            in_specs=[
                rows, rows, rows, rows, rows, pl.BlockSpec((t, D), lambda j, r: (0, j)), rows, rows,
                whole((t, 2)), rows, w_in, w_in, rows, whole((8, D)), rows,
            ],
            out_specs=[w_in, w_in, pl.BlockSpec((1, D), lambda j, r: (0, j)), whole((8, D)), rows],
            scratch_shapes=[pltpu.VMEM((t, D), F32), pltpu.VMEM((t, D), F32)],
        ),
        compiler_params=params_of(),
        cost_estimate=cost(4 * t * D * QKV, 4 * D * QKV + 30 * t * D),
        name="qkv_back",
    )(rot, dq, dkm, dvm, dkr, dvr, qkv, cosines, sines, pos, nrm, wa, wb, h, par, g)


def layout(image_sides, capacity):
    counts = image_sides * image_sides
    end_pos = jnp.cumsum(counts)
    start_pos = end_pos - counts
    positions = jnp.arange(capacity, dtype=jnp.int32)
    segment = jnp.sum((positions[:, None] >= end_pos[None, :]).astype(jnp.int32), axis=1)
    slot_ids = jnp.arange(image_sides.shape[-1], dtype=jnp.int32)
    one_hot = (segment[:, None] == slot_ids[None, :]).astype(jnp.int32)
    start_tok = jnp.sum(one_hot * start_pos[None, :], axis=1)
    side_len = jnp.maximum(jnp.sum(one_hot * image_sides[None, :], axis=1), 1)
    local_idx = positions - start_tok
    is_valid = segment < image_sides.shape[-1]
    patch_row = jnp.where(is_valid, local_idx // side_len, 0)
    patch_col = jnp.where(is_valid, local_idx % side_len, 0)
    return segment, patch_row, patch_col, is_valid


def turning(freq, pos):
    wide = jnp.concatenate([freq.reshape(2, HEADS, HD // 2)] * 2, axis=2).reshape(2, D)
    angles = pos[:, 0:1] * wide[0][None, :] + pos[:, 1:2] * wide[1][None, :]
    low = (jnp.arange(D) % HD) < HD // 2
    sines = jnp.sin(angles)
    return jnp.cos(angles), jnp.where(low[None, :], -sines, sines)


def flipped(x, axis, bit):
    return lax.ppermute(x, axis, [(i, i ^ bit) for i in range(lax.axis_size(axis))])


def to_owners(blocks, section, core):
    stacked = jnp.stack(blocks)
    got = [stacked[section]] + [flipped(stacked[section ^ d], "section", d) for d in (1, 2, 3)]
    here = (section // 2) == core
    near = jnp.stack(got[:2])
    away = jnp.stack(got[2:])
    mine = jnp.where(here, near, away)
    other = flipped(jnp.where(here, away, near), "group", 1)

    def in_order(pair):
        return jnp.where(section % 2 == 0, pair, pair[::-1])

    mine, other = in_order(mine), in_order(other)
    first = jnp.where(core == 0, mine, other)
    second = jnp.where(core == 0, other, mine)
    return jnp.concatenate([first, second], axis=1).reshape(-1, D)


MESH = pl.DeviceIdType.MESH
SMALL = 6144 // 128
UNITS = ((3, 0), (3, 1), (1, 0), (1, 1), (2, 0), (2, 1), (0, 0), (0, 1))
SEMS = 21


def unit_shape(s, part):
    if s % 2:
        return (FF // 2, D) if part else (HALF, FF)
    return (HALF, D) if part else (HALF, QKV)


def reduce_kernel(*refs):
    ins, small_in = refs[:16], refs[16]
    outs, small_out = refs[17:21], refs[21]
    own, core_in, plane1, plane2, up_in, down_in = (refs[22 + 8 * i : 30 + 8 * i] for i in range(6))
    sm, sm_core, sm_x, sm_y, sm_z, send, recv, sm_send, sm_recv = refs[70:]
    c = lax.axis_index("section")
    g = lax.axis_index("group")
    z = lax.axis_index("dp")
    x, y = c % 2, c // 2
    n = 4

    def flip(v, bit):
        if bit == 1:
            return v + 1 - 2 * (v % 2)
        if bit == 2:
            return (v + 2) % 4
        return 3 - v

    barrier = pltpu.get_barrier_semaphore()
    pl.semaphore_signal(barrier, inc=1, device_id={"group": 1 - g}, device_id_type=MESH)
    for bit in (1, 2, 3):
        pl.semaphore_signal(barrier, inc=1, device_id={"section": flip(c, bit)}, device_id_type=MESH)
        pl.semaphore_signal(barrier, inc=1, device_id={"dp": flip(z, bit)}, device_id_type=MESH)
    pl.semaphore_wait(barrier, 7)

    pending = []

    def push(cond, src, dst, u, k, device, start=True):
        copy = pltpu.make_async_remote_copy(
            src_ref=src, dst_ref=dst, send_sem=send.at[u, k], recv_sem=recv.at[u, k],
            device_id=device, device_id_type=MESH,
        )
        if cond is None:
            copy.start()
        else:
            pl.when(cond)(copy.start)
        pending.append((cond, copy))

    def landed(cond, dst, u, k):
        copy = pltpu.make_async_remote_copy(
            src_ref=dst, dst_ref=dst, send_sem=send.at[u, k], recv_sem=recv.at[u, k],
            device_id={"group": 1 - g}, device_id_type=MESH,
        )
        if cond is None:
            copy.wait_recv()
        else:
            pl.when(cond)(copy.wait_recv)

    def accumulate(into, terms, rows):
        strip = 32 if rows % 32 == 0 else 16

        def one(i, _):
            at = pl.ds(pl.multiple_of(i * strip, strip), strip)
            total = into[at, :].astype(F32)
            for term in terms:
                total = total + term[at, :].astype(F32)
            into[at, :] = total.astype(BF)
            return 0

        lax.fori_loop(0, rows // strip, one, 0)

    def quarter(u, q):
        rows = own[u].shape[0] // 4
        return own[u].at[pl.ds(pl.multiple_of(q * rows, rows), rows), :]

    def core_quarter(u, q):
        rows = own[u].shape[0] // 4
        return core_in[u].at[pl.ds(pl.multiple_of(q * rows, rows), rows), :]

    def piece(u, k):
        rows, cols = own[u].shape[0] // 8, own[u].shape[1] // 2
        first = c * 2 * rows + (k // 2) * rows
        return own[u].at[
            pl.ds(pl.multiple_of(first, rows), rows), pl.ds(pl.multiple_of((k % 2) * cols, cols), cols)
        ]

    def load(u):
        s, part = UNITS[u]
        copy = pltpu.make_async_copy(ins[4 * s + 2 * part], own[u], send.at[u, 0])
        copy.start()
        push(None, ins[4 * s + 2 * part + 1], core_in[u], u, 1, {"group": 1 - g})

    def split(u, b):
        if UNITS[u][1] == 0:
            return 2 * b + x, 2 * b + 1 - x
        return 2 * y + b, 2 * (1 - y) + b

    def first_step(u):
        part = UNITS[u][1]
        pltpu.make_async_copy(ins[4 * UNITS[u][0] + 2 * part], own[u], send.at[u, 0]).wait()
        landed(None, core_in[u], u, 1)
        rows = own[u].shape[0] // 4
        other = {"section": flip(c, 2 if part else 1)}
        for b in range(2):
            q = split(u, b)[1]
            accumulate(quarter(u, q), [core_quarter(u, q)], rows)
            push(None, quarter(u, q), plane1[u].at[b], u, 2 + b, other)
        for b in range(2):
            q = split(u, b)[0]
            accumulate(quarter(u, q), [core_quarter(u, q)], rows)

    def second_step(u):
        part = UNITS[u][1]
        rows = own[u].shape[0] // 4
        other = {"section": flip(c, 1 if part else 2)}
        for b in range(2):
            landed(None, plane1[u].at[b], u, 2 + b)
        b = (1 - x) if part else (1 - y)
        q = (2 * y + 1 - x) if part else (2 * (1 - y) + x)
        accumulate(quarter(u, q), [plane1[u].at[b]], rows)
        push(None, quarter(u, q), plane2[u], u, 4, other)
        accumulate(quarter(u, c), [plane1[u].at[1 - b]], rows)

    def line_step(u, t):
        rows = own[u].shape[0] // 8
        if t == 0:
            landed(None, plane2[u], u, 4)
            accumulate(quarter(u, c), [plane2[u]], 2 * rows)
        up = (z < n - 1) & (z <= t)
        down = (z > 0) & (z >= n - 1 - t)
        k_up = jnp.minimum(n - 1 - t + z, n - 1)
        k_down = jnp.maximum(z - (n - 1) + t, 0)
        if t > 0:

            @pl.when(up & (z > 0))
            def _():
                landed(None, up_in[u].at[t - 1], u, 5 + t - 1)
                accumulate(piece(u, k_up), [up_in[u].at[t - 1]], rows)

            @pl.when(down & (z < n - 1))
            def _():
                landed(None, down_in[u].at[t - 1], u, 8 + t - 1)
                accumulate(piece(u, k_down), [down_in[u].at[t - 1]], rows)

        push(up, piece(u, k_up), up_in[u].at[t], u, 5 + t, {"dp": jnp.minimum(z + 1, n - 1)})
        push(down, piece(u, k_down), down_in[u].at[t], u, 8 + t, {"dp": jnp.maximum(z - 1, 0)})

    def out_of(u):
        s, part = UNITS[u]
        return outs[2 * (s % 2) + part]

    def gather(u):
        s = UNITS[u][0]
        rows = own[u].shape[0] // 8

        @pl.when(z > 0)
        def _():
            landed(None, up_in[u].at[n - 2], u, 5 + n - 2)
            accumulate(piece(u, z), [up_in[u].at[n - 2]], rows)

        @pl.when(z < n - 1)
        def _():
            landed(None, down_in[u].at[n - 2], u, 8 + n - 2)
            accumulate(piece(u, z), [down_in[u].at[n - 2]], rows)

        held = out_of(u)
        for q in range(4):
            if q == s:
                copy = pltpu.make_async_copy(piece(u, z), held.at[z, q], send.at[u, 11 + q])
                pl.when(c == s)(copy.start)
            else:
                push(c == q, piece(u, z), held.at[z, q], u, 11 + q, {"section": s})

    def out_step(u, t):
        s = UNITS[u][0]
        held = out_of(u)
        mine = c == s
        if t == 0:
            for q in range(4):
                if q == s:
                    copy = pltpu.make_async_copy(piece(u, z), held.at[z, q], send.at[u, 11 + q])
                    pl.when(mine)(copy.wait)
                else:
                    landed(mine, held.at[z, q], u, 11 + q)
        else:
            landed(mine & (z >= t), held.at[jnp.maximum(z - t, 0)], u, 15 + t - 1)
            landed(mine & (z + t < n), held.at[jnp.minimum(z + t, n - 1)], u, 18 + t - 1)
        if t < n - 1:
            low, high = jnp.maximum(z - t, 0), jnp.minimum(z + t, n - 1)
            push(
                mine & (z >= t) & (z < n - 1), held.at[low], held.at[low], u, 15 + t,
                {"dp": jnp.minimum(z + 1, n - 1)},
            )
            push(
                mine & (z + t < n) & (z > 0), held.at[high], held.at[high], u, 18 + t,
                {"dp": jnp.maximum(z - 1, 0)},
            )

    def small_push(src, dst, k, device):
        copy = pltpu.make_async_remote_copy(
            src_ref=src, dst_ref=dst, send_sem=sm_send.at[k], recv_sem=sm_recv.at[k],
            device_id=device, device_id_type=MESH,
        )
        copy.start()
        pending.append((None, copy))
        return copy

    def small_step(k):
        if k == 0:
            sm[...] = small_in[...]
            small_push(sm, sm_core, 0, {"group": 1 - g}).wait_recv()
            both = jnp.where(g == 0, sm[...] + sm_core[...], sm_core[...] + sm[...])
            sm_x[0] = both
        elif k == 1:
            for b in range(2):
                small_push(sm_x.at[0, 2 * b + 1 - x], sm_x.at[1, b], 1 + b, {"section": flip(c, 1)})
        elif k == 2:
            for b in range(2):
                landed_small(sm_x.at[1, b], 1 + b)
                sm_y[b] = sm_x[0, 2 * b + x] + sm_x[1, b]
            small_push(sm_y.at[1 - y], sm_y.at[2], 3, {"section": flip(c, 2)})
        elif k == 3:
            landed_small(sm_y.at[2], 3)
            sm_z[z] = sm_y[y] + sm_y[2]
            for bit in (1, 2, 3):
                small_push(sm_z.at[z], sm_z.at[z], 3 + bit, {"dp": flip(z, bit)})
        else:
            for bit in (1, 2, 3):
                landed_small(sm_z.at[flip(z, bit)], 3 + bit)
            small_out[...] = sm_z[0] + sm_z[1] + sm_z[2] + sm_z[3]

    def landed_small(dst, k):
        pltpu.make_async_remote_copy(
            src_ref=dst, dst_ref=dst, send_sem=sm_send.at[k], recv_sem=sm_recv.at[k],
            device_id={"group": 1 - g}, device_id_type=MESH,
        ).wait_recv()

    stages = (
        [first_step, second_step]
        + [partial(line_step, t=t) for t in range(n - 1)]
        + [gather]
        + [partial(out_step, t=t) for t in range(n)]
    )
    for u in range(4):
        load(u)
    small_step(0)
    jobs = len(UNITS) // 2
    for slot in range(jobs + len(stages) - 1):
        if slot < 2:
            load(2 * slot + 4)
            load(2 * slot + 5)
        if 1 <= slot <= 4:
            small_step(slot)
        for job in reversed(range(jobs)):
            stage = slot - job
            if 0 <= stage < len(stages):
                for u in (2 * job, 2 * job + 1):
                    stages[stage](u)
    for cond, copy in pending:
        if cond is None:
            copy.wait_send()
        else:
            pl.when(cond)(copy.wait_send)


def reduce_call(grads, small):
    ins = [x for s in range(4) for x in grads[s]]
    hbm = pl.BlockSpec(memory_space=pl.ANY)
    shapes = [unit_shape(*u) for u in UNITS]
    held = [unit_shape(s, part) for s in (0, 1) for part in (0, 1)]
    pieces = [(r // 8, w // 2) for r, w in shapes]
    scratch = (
        [pltpu.VMEM(s, BF) for s in shapes]
        + [pltpu.VMEM(s, BF) for s in shapes]
        + [pltpu.VMEM((2, r // 4, w), BF) for r, w in shapes]
        + [pltpu.VMEM((r // 4, w), BF) for r, w in shapes]
        + [pltpu.VMEM((3,) + p, BF) for p in pieces]
        + [pltpu.VMEM((3,) + p, BF) for p in pieces]
        + [
            pltpu.VMEM((4, SMALL, 128), F32),
            pltpu.VMEM((4, SMALL, 128), F32),
            pltpu.VMEM((2, 4, SMALL, 128), F32),
            pltpu.VMEM((3, SMALL, 128), F32),
            pltpu.VMEM((4, SMALL, 128), F32),
            pltpu.SemaphoreType.DMA((len(UNITS), SEMS)),
            pltpu.SemaphoreType.DMA((len(UNITS), SEMS)),
            pltpu.SemaphoreType.DMA((7,)),
            pltpu.SemaphoreType.DMA((7,)),
        ]
    )
    *out, small = pl.pallas_call(
        reduce_kernel,
        out_shape=[sds((4, 4, r // 8, w // 2), BF) for r, w in held] + [sds((SMALL, 128), F32)],
        in_specs=[hbm] * 16 + [pl.BlockSpec(memory_space=pltpu.VMEM)],
        out_specs=[hbm] * 4 + [pl.BlockSpec(memory_space=pltpu.VMEM)],
        scratch_shapes=scratch,
        compiler_params=pltpu.CompilerParams(
            collective_id=1, has_side_effects=True, vmem_limit_bytes=62 * 1024 * 1024
        ),
        name="reduce",
    )(*ins, small)

    def in_place(x):
        _, _, r, w = x.shape
        x = x.reshape(2, 2, 4, r, w).transpose(2, 0, 3, 1, 4)
        return x.reshape(8 * r, 2 * w)

    return [in_place(x) for x in out], small


CHUNKS = 6


START = (0, 0, 0, 0)
RING = 4
SPAN = RING - 1 + 3
BESIDE = (None, None, None)


def chunk_of(ref, part, k):
    size = ref.shape[0 if part else 1] // CHUNKS
    at = pl.ds(pl.multiple_of(k * size, size), size)
    return ref.at[at, :] if part else ref.at[:, at]


def ring_place(chip):
    return 2 * (chip // 2) + (chip % 2 + chip // 2) % 2


def ring_chip(place):
    return 2 * (place // 2) + (place % 2 + place // 2) % 2


CLOCKWISE = ((True, False), (True, False), (False, True), (True, False))


def forward_kernel(*refs):
    (w_in, w_out, h0, pars, b_in, b_out, cos0, sin0, cos2, sin2, seg_col, seg_m, seg_t) = refs[:13]
    keep = [refs[13 + 4 * s : 17 + 4 * s] for s in range(4)]
    acts, slopes = refs[29:31], refs[31:33]
    qkvs, kv_ts, os, lses = refs[33:35], refs[35:37], refs[37:39], refs[39:41]
    nrms, hs = refs[41:45], refs[45:49]
    held = [refs[49 + 4 * s : 53 + 4 * s] for s in range(4)]
    acc, stage_a, stage_s, lse_scr = refs[65:69]
    own_sem, ring_s, ring_r, z_s, z_r, core_s, core_r, kv_sem, save_sem, stage_sem = refs[69:]
    c = lax.axis_index("section")
    g = lax.axis_index("group")
    z = lax.axis_index("dp")
    parity = z % 2
    place = ring_place(c)
    ahead, behind = ring_chip((place + 1) % 4), ring_chip((place + 3) % 4)
    partner = {"group": 1 - g}
    tokens = h0.shape[0]

    def remote(src, dst, ssem, rsem, device):
        return pltpu.make_async_remote_copy(
            src_ref=src, dst_ref=dst, send_sem=ssem, recv_sem=rsem, device_id=device,
            device_id_type=MESH,
        )

    barrier = pltpu.get_barrier_semaphore()
    pl.semaphore_signal(barrier, inc=1, device_id=partner, device_id_type=MESH)
    pl.semaphore_signal(barrier, inc=1, device_id={"section": ahead}, device_id_type=MESH)
    pl.semaphore_signal(barrier, inc=1, device_id={"section": behind}, device_id_type=MESH)
    pl.semaphore_signal(barrier, inc=1, device_id={"dp": z + 1 - 2 * parity}, device_id_type=MESH)
    pl.semaphore_wait(barrier, 4)

    def mine(s, part):
        return held[s][2 * part]

    def theirs(s, part):
        return held[s][2 * part + 1]

    def distance(s, part):
        d = place - ring_place(s)
        return (d + 4) % 4 if CLOCKWISE[s][part] else (4 - d) % 4

    def own_copies(s):
        first = pltpu.make_async_copy(
            w_in.at[:, : QKV] if s % 2 == 0 else w_in, mine(s, 0), own_sem.at[0]
        )
        source = w_out.at[:HALF, :] if s % 2 == 0 else w_out
        second = pltpu.make_async_copy(source, mine(s, 1), own_sem.at[1])
        over = remote(w_out.at[HALF:D, :], mine(s, 1), own_sem.at[2], own_sem.at[3], partner)
        return first, second, over

    for s in range(4):

        @pl.when(c == s)
        def _(s=s):
            first, second, over = own_copies(s)
            first.start()
            if s % 2:
                second.start()
            else:

                @pl.when(g == 0)
                def _():
                    second.start()
                    over.start()

    for s in range(4):

        @pl.when(c == s)
        def _(s=s):
            first, second, over = own_copies(s)
            first.wait()
            if s % 2:
                second.wait()
            else:

                @pl.when(g == 0)
                def _():
                    second.wait()
                    over.wait_send()

                @pl.when(g == 1)
                def _():
                    over.wait_recv()

    def ring_copy(s, part, k):
        ref = chunk_of(mine(s, part), part, jnp.where(k < 2, 2 * parity + k, k + 2))
        target = ahead if CLOCKWISE[s][part] else behind
        u = 2 * s + part
        return remote(ref, ref, ring_s.at[u, k], ring_r.at[u, k], {"section": target})

    def z_copy(s, part, j, sending):
        ref = chunk_of(mine(s, part), part, 2 * (parity if sending else 1 - parity) + j)
        u = 2 * s + part
        return remote(ref, ref, z_s.at[u, j], z_r.at[u, j], {"dp": z + 1 - 2 * parity})

    def core_copy(s, part, k):
        u = 2 * s + part
        return remote(
            chunk_of(mine(s, part), part, k), chunk_of(theirs(s, part), part, k),
            core_s.at[u, k], core_r.at[u, k], partner,
        )

    def event(s, part, k):
        p = distance(s, part)
        copy = ring_copy(s, part, k)
        pl.when(p > 0)(copy.wait_recv)
        pl.when(p < 3)(copy.start)

        @pl.when((k < 2) & (p > 0))
        def _():
            z_copy(s, part, jnp.minimum(k, 1), True).start()

        core_copy(s, part, jnp.where(k < 2, 2 * parity + k, k + 2)).start()

        @pl.when(k >= 2)
        def _():
            j = jnp.maximum(k - 2, 0)
            pl.when(p > 0)(z_copy(s, part, j, False).wait_recv)
            core_copy(s, part, 2 * (1 - parity) + j).start()

    def slot(t, first, last):
        for s in range(4):
            if START[s] <= last and first <= START[s] + SPAN:
                for part in range(2):
                    k = t - START[s] - distance(s, part)

                    @pl.when((k >= 0) & (k < RING))
                    def _(s=s, part=part, k=k):
                        event(s, part, jnp.clip(k, 0, RING - 1))

    def slots(first, last):
        loop(last - first + 1, lambda i: slot(first + i, first, last))

    def loop(n, body):
        def one(i, carried):
            body(i)
            return carried

        lax.fori_loop(0, n, one, 0)

    def arrived(s):
        def one(k):
            core_copy(s, 0, k).wait_recv()
            core_copy(s, 1, k).wait_recv()

        loop(CHUNKS, one)
        for i in range(4):
            pltpu.make_async_copy(held[s][i], keep[s][i], save_sem.at[4 * s + i]).start()

    def normed(s, h):
        xhat, _ = normalize(h[...].astype(F32))
        nrms[s][...] = turn_halves(
            xhat * pars[s, 0:1, :] + pars[s, 1:2, :], g
        ).astype(BF)

    def project(s, first, width):
        cols = pl.ds(first, width)
        return (
            dot(nrms[s][:, :HALF], mine(s, 0)[:, cols])
            + dot(nrms[s][:, HALF:], theirs(s, 0)[:, cols])
            + b_in[s, 0:1, cols]
        )

    def attention(s, h, out, beside):
        layer = s // 2
        qkv, kv_t, o_ref = qkvs[layer], kv_ts[layer], os[layer]
        cosines, sines = ((cos0, sin0), (cos2, sin2))[layer]
        normed(s, h)
        exchange = []
        for j in (1, 2, 0):
            x = project(s, j * D, D)
            if j < 2:
                x = x * cosines[...] + swap_pairs(x) * sines[...]
            if j == 0:
                x = x * HD ** (-0.5)
            qkv[:, j * D : (j + 1) * D] = x.astype(BF)
            if j:
                copy = remote(
                    qkv.at[:, j * D : (j + 1) * D], kv_t.at[:, (j - 1) * D : j * D],
                    kv_sem.at[0, 2 * layer + j - 1], kv_sem.at[1, 2 * layer + j - 1], partner,
                )
                copy.start()
                exchange.append(copy)
        for copy in exchange:
            copy.wait()
        lanes = lax.broadcasted_iota(jnp.int32, (tokens, 2 * HD), 1)

        def pair(j):
            if beside is not None:
                pl.when(beside[0] + j <= beside[1])(lambda: slot(beside[0] + j, *beside))

            def columns(ref, first):
                return ref[:, pl.ds(pl.multiple_of(first + j * 2 * HD, 2 * HD), 2 * HD)]

            q = columns(qkv, 0)
            km, vm = columns(qkv, D), columns(qkv, 2 * D)
            kt, vt = columns(kv_t, 0), columns(kv_t, D)
            same_m = seg_col[...] == seg_m[...]
            same_t = seg_col[...] == seg_t[...]
            found = []
            for side in range(2):
                head = (lanes >= HD) if side else (lanes < HD)
                q_head = jnp.where(head, q, jnp.zeros_like(q))
                s_m = jnp.where(same_m, dot_nt(q_head, km), -1e9)
                s_t = jnp.where(same_t, dot_nt(q_head, kt), -1e9)
                top = jnp.maximum(
                    jnp.max(s_m, axis=-1, keepdims=True), jnp.max(s_t, axis=-1, keepdims=True)
                )
                p_m = jnp.exp(s_m - top)
                p_t = jnp.exp(s_t - top)
                total = jnp.sum(p_m, axis=-1, keepdims=True) + jnp.sum(
                    p_t, axis=-1, keepdims=True
                )
                o = dot(p_m.astype(BF), vm) + dot(p_t.astype(BF), vt)
                found.append(o / total)
                lse_scr[...] = jnp.where(
                    lanes == 2 * j + side, top + jnp.log(total), lse_scr[...]
                )
            o_ref[:, pl.ds(pl.multiple_of(j * 2 * HD, 2 * HD), 2 * HD)] = jnp.where(
                lanes < HD, found[0], found[1]
            ).astype(BF)

        loop(PAIRS, pair)
        lses[layer][...] = jnp.transpose(lse_scr[...])[:16, :]
        turned = turn_halves(o_ref[...].astype(F32), g).astype(BF)
        y = dot(turned[:, :HALF], mine(s, 1)[...]) + dot(turned[:, HALF:], theirs(s, 1)[...])
        out[...] = (h[...].astype(F32) + y + b_out[s, 0:1, :]).astype(BF)

    def feed(s, h, out, beside):
        layer = s // 2
        width = FF // CHUNKS
        normed(s, h)
        acc[...] = h[...].astype(F32) + b_out[s, 0:1, :]

        def staged(j, i):
            turn = j % 2
            cols = pl.ds(pl.multiple_of(j * width, width), width)
            source, target = ((stage_a, acts[layer]), (stage_s, slopes[layer]))[i]
            return pltpu.make_async_copy(source.at[turn], target.at[:, cols], stage_sem.at[i, turn])

        def block(j):
            if beside is not None:
                pl.when(beside[0] + j <= beside[1])(lambda: slot(beside[0] + j, *beside))
            turn = j % 2

            @pl.when(j >= 2)
            def _():
                staged(j - 2, 0).wait()
                staged(j - 2, 1).wait()

            b = (j + g * (CHUNKS // 2)) % CHUNKS
            u = project(s, pl.multiple_of(b * width, width), width)
            cdf = 0.5 + 0.5 * lax.erf(u * (0.5**0.5))
            act = (u * cdf).astype(BF)
            stage_a[turn] = act
            pdf = jnp.exp(u * u * -0.5) * 0.3989422804014327
            stage_s[turn] = (cdf + u * pdf).astype(BF)
            staged(j, 0).start()
            staged(j, 1).start()
            for half in range(2):

                @pl.when(j // (CHUNKS // 2) == half)
                def _(half=half):
                    rows = pl.ds(pl.multiple_of((j % (CHUNKS // 2)) * width, width), width)
                    acc[...] += dot(act, held[s][2 + half][rows, :])

        loop(CHUNKS, block)
        for j in (CHUNKS - 2, CHUNKS - 1):
            staged(j, 0).wait()
            staged(j, 1).wait()
        out[...] = acc[...].astype(BF)

    slots(0, START[0] + SPAN)
    arrived(0)
    attention(0, h0, hs[0], BESIDE[0])
    arrived(1)
    feed(1, hs[0], hs[1], BESIDE[1])
    arrived(2)
    attention(2, hs[1], hs[2], BESIDE[2])
    arrived(3)
    feed(3, hs[2], hs[3], None)

    for s in range(4):
        for part in range(2):
            p = distance(s, part)

            def sent_out(k, s=s, part=part, p=p):
                core_copy(s, part, k).wait_send()
                pl.when((k < 4) & (p < 3))(ring_copy(s, part, jnp.minimum(k, 3)).wait_send)
                pl.when((k < 2) & (p > 0))(z_copy(s, part, jnp.minimum(k, 1), True).wait_send)

            loop(CHUNKS, sent_out)
        for i in range(4):
            pltpu.make_async_copy(held[s][i], keep[s][i], save_sem.at[4 * s + i]).wait()


def forward_call(w_in, w_out, h, pars, b_in, b_out, turns, seg_col, seg_m, seg_t):
    t = h.shape[0]
    hbm = pl.BlockSpec(memory_space=pl.ANY)
    vmem = pl.BlockSpec(memory_space=pltpu.VMEM)
    weights = []
    for s in range(4):
        (a, b), (d, e) = unit_shape(s, 0), unit_shape(s, 1)
        weights += [(a, b), (a, b), (d, e), (d, e)]
    rows = sds((t, D), BF)
    out_shape = (
        [sds(w, BF) for w in weights]
        + [sds((t, FF), BF)] * 4
        + [sds((t, QKV), BF)] * 2
        + [sds((t, 2 * D), BF)] * 2
        + [rows] * 2
        + [sds((16, t), F32)] * 2
        + [rows] * 8
    )
    dma = pltpu.SemaphoreType.DMA
    scratch = [pltpu.VMEM(w, BF) for w in weights] + [
        pltpu.VMEM((t, D), F32),
        pltpu.VMEM((2, t, FF // CHUNKS), BF),
        pltpu.VMEM((2, t, FF // CHUNKS), BF),
        pltpu.VMEM((t, 2 * HD), F32),
        dma((4,)), dma((8, 4)), dma((8, 4)), dma((8, 2)), dma((8, 2)), dma((8, 6)), dma((8, 6)),
        dma((2, 4)), dma((16,)), dma((2, 2)),
    ]
    out = pl.pallas_call(
        forward_kernel,
        out_shape=out_shape,
        in_specs=[hbm, hbm] + [vmem] * 11,
        out_specs=[hbm] * 20 + [vmem] * 16,
        scratch_shapes=scratch,
        compiler_params=pltpu.CompilerParams(
            collective_id=2, has_side_effects=True, vmem_limit_bytes=63 * 1024 * 1024
        ),
        name="forward",
    )(w_in, w_out, h, pars, b_in, b_out, *turns[0], *turns[1], seg_col, seg_m, seg_t)
    weights = [out[4 * s : 4 * s + 4] for s in range(4)]
    acts, slopes, qkvs, kv_ts, os, lses = (out[16 + 2 * i : 18 + 2 * i] for i in range(6))
    nrms, hs = out[28:32], out[32:36]
    saved = []
    for s in range(4):
        i = s // 2
        if s % 2 == 0:
            saved.append((qkvs[i], nrms[s], kv_ts[i], os[i], lses[i]))
        else:
            saved.append((acts[i], slopes[i], nrms[s]))
    return weights, saved, hs


def plain_weights(weight_in, weight_out):
    all_in = lax.all_gather(weight_in, "group", axis=1, tiled=True)
    all_out = lax.all_gather(weight_out, "group", axis=1, tiled=True)
    all_in = lax.all_gather(all_in, "section", axis=0, tiled=True)
    all_out = lax.all_gather(all_out, "section", axis=0, tiled=True)
    weights = []
    for s in range(4):
        cols, rows = (QKV, D) if s % 2 == 0 else (FF, FF)
        w_in, w_out = all_in[s, :, :cols], all_out[s, :rows]
        weights.append((w_in[:HALF], w_in[HALF:], w_out[: rows // 2], w_out[rows // 2 :]))
    return weights


def plain_forward(rot, h, weights, pars, b_in, b_out, turns, seg_m, seg_t):
    saved = []
    streams = [h]
    for s in range(4):
        wia, wib, woa, wob = weights[s]
        if s % 2 == 0:
            cosines, sines = turns[s // 2]
            qkv, nrm = qkv_call(rot, h, pars[s], wia, wib, b_in[s, :, :QKV], cosines, sines)
            kv_t = flipped(qkv[:, D:], "group", 1)
            o, lse, h = attend_call(
                rot, qkv, kv_t, seg_m[:, None], seg_m[None], seg_t[None], h, woa, wob, b_out[s]
            )
            saved.append((qkv, nrm, kv_t, o, lse))
        else:
            act, slope, nrm, h = ff_call(rot, h, pars[s], wia, wib, b_in[s], woa, wob, b_out[s])
            saved.append((act, slope, nrm))
        streams.append(h)
    return saved, streams


def body(
    activations, weight_in, weight_out, bias_in, bias_out, norm_gain, norm_shift, rope_freq,
    image_sides, cotangent,
):
    sections = lax.axis_size("section")
    groups = lax.axis_size("group")
    section = lax.axis_index("section")
    group = lax.axis_index("group")
    core = group % 2
    micro = image_sides.shape[0]
    capacity = activations.shape[0] // micro
    tokens = capacity // 2
    assert sections == 4 and groups % 2 == 0 and 2 * micro == sections
    fast = groups == 2 and lax.axis_size("dp") == 4

    here = (section // 2) == core
    local = section % 2

    def take(x):
        own = lax.dynamic_index_in_dim(x.reshape(micro, capacity, D), local, 0, keepdims=False)
        give = lax.dynamic_slice_in_dim(own, (1 - core) * tokens, tokens, 0)
        keep = lax.dynamic_slice_in_dim(own, core * tokens, tokens, 0)
        return jnp.where(here, keep, flipped(give, "group", 1))

    h = take(activations)
    own_sides = lax.dynamic_index_in_dim(image_sides, local, 0, keepdims=False)
    sides = jnp.where(here, own_sides, flipped(own_sides, "group", 1))
    segment, patch_row, patch_col, is_valid = layout(sides, capacity)
    pos_all = jnp.stack([patch_col, patch_row], axis=1).astype(F32)

    def half_of(x, which):
        return lax.dynamic_slice_in_dim(x, which * tokens, tokens, 0)

    pos = half_of(pos_all, core)
    seg_m, seg_t = half_of(segment, core), half_of(segment, 1 - core)
    valid = half_of(is_valid, core)
    g = take(cotangent) * valid[:, None].astype(BF)

    small = jnp.concatenate(
        [bias_in[0], bias_out[0], norm_gain[0], norm_shift[0], rope_freq[0].reshape(-1)]
    )
    small = lax.all_gather(small, ("section", "group")).reshape(4, groups, -1).astype(F32)
    widths = [FF // groups, D // groups, D // groups, D // groups, D // groups]
    starts = [sum(widths[:i]) for i in range(5)]
    b_in, b_out, gain, shift, freq = (
        small[:, :, a : a + w] for a, w in zip(starts, widths)
    )
    b_in, b_out, gain, shift = (x.reshape(4, 1, -1) for x in (b_in, b_out, gain, shift))
    freq = freq.reshape(4, groups, 2, -1).transpose(0, 2, 1, 3).reshape(4, 2, D // 2)
    pars = [
        jnp.concatenate([gain[s], shift[s], jnp.zeros((6, D), F32)], axis=0) for s in range(4)
    ]
    turns = [turning(freq[s], pos) for s in (0, 2)]

    if fast:
        rot = core.reshape(1).astype(jnp.int32)
        weights, saved, later = forward_call(
            weight_in[0], weight_out[0], h, jnp.stack(pars), b_in, b_out, turns,
            seg_m[:, None], seg_m[None], seg_t[None],
        )
        streams = [h] + list(later)
    else:
        rot = jnp.zeros((1,), jnp.int32)
        weights = plain_weights(weight_in, weight_out)
        saved, streams = plain_forward(
            rot, h, weights, pars, b_in, b_out, turns, seg_m, seg_t
        )

    outputs = to_owners(streams[1:], section, core)

    grads = [None] * 4
    in_grads = [None] * 4
    smalls = [None] * 4
    for s in (3, 2, 1, 0):
        wia, wib, woa, wob = weights[s]
        if s % 2 == 0:
            qkv, nrm, kv_t, o, lse = saved[s]
            cosines, sines = turns[s // 2]
            dmix, delta, doa, dob = mix_back_call(rot, g, o, woa, wob)
            dq, dkm, dvm, dkt, dvt = attend_back_call(
                qkv, kv_t, dmix, lse, delta, seg_m[None], seg_m[:, None], seg_t[:, None]
            )
            dkr, dvr = flipped(dkt, "group", 1), flipped(dvt, "group", 1)
            dia, dib, dbin, rest, g = qkv_back_call(
                rot, dq, dkm, dvm, dkr, dvr, qkv, cosines, sines, pos, nrm, wia, wib,
                streams[s], pars[s], g,
            )
            dbin = jnp.concatenate([dbin, jnp.zeros((1, FF - QKV), F32)], axis=1)
            dfreq = rest[3:5].reshape(2, HEADS, HD)[:, :, : HD // 2].reshape(-1)
        else:
            act, slope, nrm = saved[s]
            dia, dib, doa, dob, dbin, rest, g = ff_back_call(
                rot, g, act, slope, nrm, wia, wib, woa, wob, streams[s], pars[s]
            )
            dfreq = jnp.zeros((D,), F32)
        in_grads[s] = g
        grads[s] = (dia, dib, doa, dob)
        smalls[s] = jnp.concatenate([dbin.reshape(-1), rest[:3].reshape(-1), dfreq])
    input_grads = to_owners(in_grads, section, core)

    small_sum = jnp.stack(smalls)
    if fast:
        sums, small_sum = reduce_call(grads, small_sum.reshape(4, SMALL, 128))
        small_sum = small_sum.reshape(-1)
        in_a, out_a, in_f, out_f = sums
        both = jnp.concatenate([out_a, flipped(out_a, "group", 1)], axis=0)
        both = jnp.where(core == 0, jnp.pad(both, ((0, FF // 2 - D), (0, 0))), jnp.zeros((), BF))
        attends = section % 2 == 0
        out_in = jnp.where(attends, jnp.pad(in_a, ((0, 0), (0, FF - QKV))), in_f).astype(F32)
        out_out = jnp.where(attends, both, out_f).astype(F32)
    else:
        small_sum = lax.psum(small_sum, ("section", "group", "dp"))[section]
        rows_in, rows_out = D // groups, FF // groups
        d_in = jnp.stack(
            [
                jnp.pad(jnp.concatenate(x[:2]), ((0, 0), (0, FF - x[0].shape[1])))
                for x in grads
            ]
        )
        d_out = jnp.stack(
            [
                jnp.pad(jnp.concatenate(x[2:]), ((0, FF - 2 * x[2].shape[0]), (0, 0)))
                for x in grads
            ]
        )

        def owned(x, rows):
            x = lax.psum_scatter(x, "section", scatter_dimension=0, tiled=True)[0]
            x = lax.psum_scatter(x, "group", scatter_dimension=0, tiled=True)
            return lax.psum(x, "dp").astype(F32)

        out_in, out_out = owned(d_in, rows_in), owned(d_out, rows_out)

    def piece(start, width):
        w = width // groups
        return lax.dynamic_slice_in_dim(small_sum, start + group * w, w, 0)[None]

    d_freq = small_sum[FF + 3 * D :].reshape(2, D // 2)
    d_freq = lax.dynamic_slice_in_dim(d_freq, group * (D // 2 // groups), D // 2 // groups, 1)
    return (
        outputs[None],
        input_grads[None],
        out_in[None],
        out_out[None],
        piece(0, FF),
        piece(FF, D),
        piece(FF + D, D),
        piece(FF + 2 * D, D),
        d_freq[None],
    )


def solution(mesh):
    placed = (
        P(("group", "dp"), None),
        P("section", "group", None),
        P("section", "group", None),
        P("section", "group"),
        P("section", "group"),
        P("section", "group"),
        P("section", "group"),
        P("section", None, "group"),
        P(("group", "dp"), None),
        P(("group", "dp"), None),
    )
    return jax.shard_map(
        body,
        mesh=mesh,
        in_specs=placed,
        out_specs=(
            P("section", ("group", "dp"), None),
            P("section", ("group", "dp"), None),
            P("section", "group", None),
            P("section", "group", None),
            P("section", "group"),
            P("section", "group"),
            P("section", "group"),
            P("section", "group"),
            P("section", None, "group"),
        ),
        check_vma=False,
    )
```

```python
from functools import partial

import jax
import jax.numpy as jnp
from jax import lax
from jax.experimental import pallas as pl
from jax.experimental.pallas import tpu as pltpu
from jax.sharding import PartitionSpec as P

D = 768
HEADS = 12
HD = 64
FF = 3072
HALF = D // 2
PAIRS = HEADS // 2
QKV = 3 * D
EPSILON = 1e-06
BF = jnp.bfloat16
F32 = jnp.float32
NT = (((1,), (1,)), ((), ()))
TN = (((0,), (0,)), ((), ()))
VMEM_BYTES = 52 * 1024 * 1024


def dot(a, b):
    return jnp.dot(a, b, preferred_element_type=F32)


def dot_nt(a, b):
    return lax.dot_general(a, b, NT, preferred_element_type=F32)


def dot_tn(a, b):
    return lax.dot_general(a, b, TN, preferred_element_type=F32)


def normalize(h):
    average = jnp.mean(h, axis=-1, keepdims=True)
    centered = h - average
    variance = jnp.mean(centered * centered, axis=-1, keepdims=True)
    scale = lax.rsqrt(variance + EPSILON)
    return centered * scale, scale


def turn_halves(x, rot):
    return jnp.where(rot == 0, x, jnp.concatenate([x[:, HALF:], x[:, :HALF]], axis=1))


def swap_pairs(x):
    lanes = lax.broadcasted_iota(jnp.int32, x.shape, 1)
    low = (lanes % HD) < HD // 2
    return jnp.where(
        low, pltpu.roll(x, x.shape[1] - HD // 2, 1), pltpu.roll(x, HD // 2, 1)
    )


def norm_backward(h, gain, grad, d_normed):
    xhat, scale = normalize(h)
    e = d_normed * gain
    mean_e = jnp.mean(e, axis=-1, keepdims=True)
    mean_ex = jnp.mean(e * xhat, axis=-1, keepdims=True)
    g = grad + scale * (e - mean_e - xhat * mean_ex)
    d_gain = jnp.sum(d_normed * xhat, axis=0, keepdims=True)
    d_shift = jnp.sum(d_normed, axis=0, keepdims=True)
    return g, d_gain, d_shift


def qkv_kernel(rot_ref, h_ref, par_ref, wa_ref, wb_ref, bias_ref, cos_ref, sin_ref, out_ref, nrm_ref):
    j = pl.program_id(0)

    @pl.when(j == 0)
    def _():
        xhat, _ = normalize(h_ref[...].astype(F32))
        normed = xhat * par_ref[0:1, :] + par_ref[1:2, :]
        nrm_ref[...] = turn_halves(normed, rot_ref[0]).astype(BF)

    x = dot(nrm_ref[:, :HALF], wa_ref[...]) + dot(nrm_ref[:, HALF:], wb_ref[...]) + bias_ref[...]

    @pl.when(j < 2)
    def _():
        y = x * cos_ref[...] + swap_pairs(x) * sin_ref[...]
        out_ref[...] = (y * jnp.where(j == 0, HD ** (-0.5), 1.0)).astype(BF)

    @pl.when(j == 2)
    def _():
        out_ref[...] = x.astype(BF)


def attend_kernel(
    rot_ref, q_ref, km_ref, vm_ref, kt_ref, vt_ref, segq_ref, segm_ref, segt_ref, h_ref,
    woa_ref, wob_ref, bias_ref, o_ref, lse_ref, out_ref, lse_scr,
):
    j = pl.program_id(0)
    rows = q_ref.shape[0]
    lanes = lax.broadcasted_iota(jnp.int32, (rows, 2 * HD), 1)
    q = q_ref[...]
    same_m = segq_ref[...] == segm_ref[...]
    same_t = segq_ref[...] == segt_ref[...]
    outs = []
    for side in range(2):
        mine = (lanes >= HD) if side else (lanes < HD)
        q_head = jnp.where(mine, q, jnp.zeros_like(q))
        s_m = jnp.where(same_m, dot_nt(q_head, km_ref[...]), -1e9)
        s_t = jnp.where(same_t, dot_nt(q_head, kt_ref[...]), -1e9)
        top = jnp.maximum(
            jnp.max(s_m, axis=-1, keepdims=True), jnp.max(s_t, axis=-1, keepdims=True)
        )
        p_m = jnp.exp(s_m - top)
        p_t = jnp.exp(s_t - top)
        total = jnp.sum(p_m, axis=-1, keepdims=True) + jnp.sum(p_t, axis=-1, keepdims=True)
        o = dot(p_m.astype(BF), vm_ref[...]) + dot(p_t.astype(BF), vt_ref[...])
        outs.append(o / total)
        lse_scr[...] = jnp.where(lanes == 2 * j + side, top + jnp.log(total), lse_scr[...])
    o_ref[:, pl.ds(pl.multiple_of(j * 2 * HD, 2 * HD), 2 * HD)] = jnp.where(
        lanes < HD, outs[0], outs[1]
    ).astype(BF)

    @pl.when(j == PAIRS - 1)
    def _():
        lse_ref[...] = jnp.transpose(lse_scr[...])[:16, :]
        o_all = turn_halves(o_ref[...].astype(F32), rot_ref[0]).astype(BF)
        y = dot(o_all[:, :HALF], woa_ref[...]) + dot(o_all[:, HALF:], wob_ref[...])
        out_ref[...] = (h_ref[...].astype(F32) + y + bias_ref[...]).astype(BF)


def ff_kernel(
    rot_ref, h_ref, par_ref, wia_ref, wib_ref, bias_ref, woa_ref, wob_ref, bout_ref,
    act_ref, slope_ref, nrm_ref, out_ref, acc_ref,
):
    j = pl.program_id(0)
    n = pl.num_programs(0)

    @pl.when(j == 0)
    def _():
        xhat, _ = normalize(h_ref[...].astype(F32))
        normed = xhat * par_ref[0:1, :] + par_ref[1:2, :]
        nrm_ref[...] = turn_halves(normed, rot_ref[0]).astype(BF)
        acc_ref[...] = h_ref[...].astype(F32) + bout_ref[...]

    u = dot(nrm_ref[:, :HALF], wia_ref[...]) + dot(nrm_ref[:, HALF:], wib_ref[...]) + bias_ref[...]
    cdf = 0.5 + 0.5 * lax.erf(u * (0.5**0.5))
    act = (u * cdf).astype(BF)
    act_ref[...] = act
    pdf = jnp.exp(u * u * -0.5) * 0.3989422804014327
    slope_ref[...] = (cdf + u * pdf).astype(BF)

    @pl.when(j < n // 2)
    def _():
        acc_ref[...] += dot(act, woa_ref[...])

    @pl.when(j >= n // 2)
    def _():
        acc_ref[...] += dot(act, wob_ref[...])

    @pl.when(j == n - 1)
    def _():
        out_ref[...] = acc_ref[...].astype(BF)


def ff_back_kernel(
    rot_ref, g_ref, act_ref, slope_ref, nrm_ref, wia_ref, wib_ref, woa_ref, wob_ref, h_ref, par_ref,
    dia_ref, dib_ref, doa_ref, dob_ref, dbin_ref, small_ref, out_ref, acc_ref,
):
    j = pl.program_id(0)
    n = pl.num_programs(0)

    @pl.when(j == 0)
    def _():
        acc_ref[...] = jnp.zeros_like(acc_ref)

    def step(wo_ref, do_ref):
        g = g_ref[...]
        d_up_f = dot_nt(g, wo_ref[...]) * slope_ref[...].astype(F32)
        d_up = d_up_f.astype(BF)
        do_ref[...] = dot_tn(act_ref[...], g).astype(BF)
        dbin_ref[...] = jnp.sum(d_up_f, axis=0, keepdims=True)
        dia_ref[...] = dot_tn(nrm_ref[:, :HALF], d_up).astype(BF)
        dib_ref[...] = dot_tn(nrm_ref[:, HALF:], d_up).astype(BF)
        acc_ref[:, :HALF] += dot_nt(d_up, wia_ref[...])
        acc_ref[:, HALF:] += dot_nt(d_up, wib_ref[...])

    @pl.when(j < n // 2)
    def _():
        step(woa_ref, doa_ref)

    @pl.when(j >= n // 2)
    def _():
        step(wob_ref, dob_ref)

    @pl.when(j == n - 1)
    def _():
        g = g_ref[...].astype(F32)
        d_normed = turn_halves(acc_ref[...], rot_ref[0])
        out, d_gain, d_shift = norm_backward(h_ref[...].astype(F32), par_ref[0:1, :], g, d_normed)
        out_ref[...] = out.astype(BF)
        small_ref[0:1, :] = jnp.sum(g, axis=0, keepdims=True)
        small_ref[1:2, :] = d_gain
        small_ref[2:3, :] = d_shift
        small_ref[3:8, :] = jnp.zeros((5, D), F32)


def mix_back_kernel(rot_ref, g_ref, o_ref, woa_ref, wob_ref, dmix_ref, delta_ref, doa_ref, dob_ref):
    g = g_ref[...]
    rot = rot_ref[0]
    d_mix = jnp.concatenate([dot_nt(g, woa_ref[...]), dot_nt(g, wob_ref[...])], axis=1)
    d_mix = turn_halves(d_mix, rot).astype(BF)
    dmix_ref[...] = d_mix
    o = o_ref[...].astype(F32)
    product = d_mix.astype(F32) * o
    head = lax.broadcasted_iota(jnp.int32, (16, D), 0)
    lanes = lax.broadcasted_iota(jnp.int32, (16, D), 1)
    chosen = jnp.where(lanes // HD == head, 1.0, 0.0)
    delta_ref[...] = lax.dot_general(
        chosen, product, NT, preferred_element_type=F32, precision=lax.Precision.HIGHEST
    )
    turned = turn_halves(o, rot).astype(BF)
    doa_ref[...] = dot_tn(turned[:, :HALF], g).astype(BF)
    dob_ref[...] = dot_tn(turned[:, HALF:], g).astype(BF)


def attend_back_kernel(
    q_ref, km_ref, vm_ref, kt_ref, vt_ref, do_ref, lse_ref, delta_ref, segq_ref, segm_ref, segt_ref,
    dq_ref, dkm_ref, dvm_ref, dkt_ref, dvt_ref,
):
    j = pl.program_id(0)
    rows = q_ref.shape[0]
    lanes = lax.broadcasted_iota(jnp.int32, (rows, 2 * HD), 1)
    q = q_ref[...]
    do = do_ref[...]
    zero = jnp.zeros_like(q)
    d_q = jnp.zeros((rows, 2 * HD), F32)
    sets = ((km_ref, vm_ref, segm_ref), (kt_ref, vt_ref, segt_ref))
    d_k = [0.0, 0.0]
    d_v = [0.0, 0.0]
    for side in range(2):
        mine = (lanes >= HD) if side else (lanes < HD)
        q_head = jnp.where(mine, q, zero)
        do_head = jnp.where(mine, do, zero)
        lse = lse_ref[pl.ds(2 * j + side, 1), :]
        delta = delta_ref[pl.ds(2 * j + side, 1), :]
        for i, (k_ref, v_ref, seg_ref) in enumerate(sets):
            k = k_ref[...]
            s_t = dot_nt(k, q_head)
            p_t = jnp.where(seg_ref[...] == segq_ref[...], jnp.exp(s_t - lse), 0.0)
            d_p = dot_nt(v_ref[...], do_head)
            d_s = (p_t * (d_p - delta)).astype(BF)
            d_v[i] += dot(p_t.astype(BF), do_head)
            d_k[i] += dot(d_s, q_head)
            d_q += dot_tn(d_s, jnp.where(mine, k, zero))
    dq_ref[...] = d_q
    dkm_ref[...] = d_k[0]
    dvm_ref[...] = d_v[0]
    dkt_ref[...] = d_k[1].astype(BF)
    dvt_ref[...] = d_v[1].astype(BF)


def qkv_back_kernel(
    rot_ref, dq_ref, dkm_ref, dvm_ref, dkr_ref, dvr_ref, qkv_ref, cos_ref, sin_ref, pos_ref,
    nrm_ref, wa_ref, wb_ref, h_ref, par_ref, g_ref,
    dia_ref, dib_ref, dbin_ref, small_ref, out_ref, acc_ref, dp_ref,
):
    j = pl.program_id(0)
    n = pl.num_programs(0)

    @pl.when(j == 0)
    def _():
        acc_ref[...] = jnp.zeros_like(acc_ref)
        small_ref[...] = jnp.zeros_like(small_ref)

    def turned_back(dy, y):
        swapped = swap_pairs(dy)
        d_angle = y * swapped - swap_pairs(y) * dy
        small_ref[3:4, :] += jnp.sum(d_angle * pos_ref[:, 0:1], axis=0, keepdims=True)
        small_ref[4:5, :] += jnp.sum(d_angle * pos_ref[:, 1:2], axis=0, keepdims=True)
        return dy * cos_ref[...] - swapped * sin_ref[...]

    @pl.when(j == 0)
    def _():
        d_y = dq_ref[...] * HD ** (-0.5)
        y = qkv_ref[...].astype(F32) * HD**0.5
        dp_ref[...] = turned_back(d_y, y)

    @pl.when(j == 1)
    def _():
        d_y = dkm_ref[...] + dkr_ref[...].astype(F32)
        dp_ref[...] = turned_back(d_y, qkv_ref[...].astype(F32))

    @pl.when(j == 2)
    def _():
        dp_ref[...] = dvm_ref[...] + dvr_ref[...].astype(F32)

    d_f = dp_ref[...]
    d_p = d_f.astype(BF)
    dbin_ref[...] = jnp.sum(d_f, axis=0, keepdims=True)
    dia_ref[...] = dot_tn(nrm_ref[:, :HALF], d_p).astype(BF)
    dib_ref[...] = dot_tn(nrm_ref[:, HALF:], d_p).astype(BF)
    acc_ref[:, :HALF] += dot_nt(d_p, wa_ref[...])
    acc_ref[:, HALF:] += dot_nt(d_p, wb_ref[...])

    @pl.when(j == n - 1)
    def _():
        g = g_ref[...].astype(F32)
        d_normed = turn_halves(acc_ref[...], rot_ref[0])
        out, d_gain, d_shift = norm_backward(h_ref[...].astype(F32), par_ref[0:1, :], g, d_normed)
        out_ref[...] = out.astype(BF)
        small_ref[0:1, :] = jnp.sum(g, axis=0, keepdims=True)
        small_ref[1:2, :] = d_gain
        small_ref[2:3, :] = d_shift


def params_of(n=1):
    return pltpu.CompilerParams(
        dimension_semantics=("arbitrary",) * n, vmem_limit_bytes=VMEM_BYTES
    )


def whole(shape):
    return pl.BlockSpec(shape, lambda *_: (0,) * len(shape))


def sds(shape, dtype):
    return jax.ShapeDtypeStruct(shape, dtype)


def cost(flops, nbytes, trans=0):
    return pl.CostEstimate(flops=flops, bytes_accessed=nbytes, transcendentals=trans)


def qkv_call(rot, h, par, wa, wb, bias, cosines, sines):
    t = h.shape[0]
    return pl.pallas_call(
        qkv_kernel,
        out_shape=(sds((t, QKV), BF), sds((t, D), BF)),
        grid_spec=pltpu.PrefetchScalarGridSpec(
            num_scalar_prefetch=1,
            grid=(3,),
            in_specs=[
                whole((t, D)), whole((8, D)),
                pl.BlockSpec((HALF, D), lambda j, r: (0, j)),
                pl.BlockSpec((HALF, D), lambda j, r: (0, j)),
                pl.BlockSpec((1, D), lambda j, r: (0, j)),
                whole((t, D)), whole((t, D)),
            ],
            out_specs=[pl.BlockSpec((t, D), lambda j, r: (0, j)), whole((t, D))],
        ),
        compiler_params=params_of(),
        cost_estimate=cost(2 * t * D * QKV, 2 * D * QKV + 8 * t * D + 2 * t * QKV),
        name="qkv",
    )(rot, h, par, wa, wb, bias, cosines, sines)


def attend_call(rot, qkv, kv_t, seg_col, seg_m, seg_t, h, woa, wob, bias):
    t = h.shape[0]
    w = 2 * HD
    return pl.pallas_call(
        attend_kernel,
        out_shape=(sds((t, D), BF), sds((16, t), F32), sds((t, D), BF)),
        grid_spec=pltpu.PrefetchScalarGridSpec(
            num_scalar_prefetch=1,
            grid=(PAIRS,),
            in_specs=[
                pl.BlockSpec((t, w), lambda j, r: (0, j)),
                pl.BlockSpec((t, w), lambda j, r: (0, j + PAIRS)),
                pl.BlockSpec((t, w), lambda j, r: (0, j + 2 * PAIRS)),
                pl.BlockSpec((t, w), lambda j, r: (0, j)),
                pl.BlockSpec((t, w), lambda j, r: (0, j + PAIRS)),
                whole((t, 1)), whole((1, t)), whole((1, t)), whole((t, D)),
                whole((HALF, D)), whole((HALF, D)), whole((1, D)),
            ],
            out_specs=[whole((t, D)), whole((16, t)), whole((t, D))],
            scratch_shapes=[pltpu.VMEM((t, w), F32)],
        ),
        compiler_params=params_of(),
        cost_estimate=cost(8 * t * t * D * 4, 16 * t * D, 2 * t * t * HEADS),
        name="attend",
    )(rot, qkv, qkv, qkv, kv_t, kv_t, seg_col, seg_m, seg_t, h, woa, wob, bias)


def ff_specs(t, blocks):
    width = FF // blocks
    half = blocks // 2
    w_in = pl.BlockSpec((HALF, width), lambda j, r: (0, (j + half * r[0]) % blocks))
    b_in = pl.BlockSpec((1, width), lambda j, r: (0, (j + half * r[0]) % blocks))
    w_a = pl.BlockSpec((width, D), lambda j, r: (jnp.minimum(j, half - 1), 0))
    w_b = pl.BlockSpec((width, D), lambda j, r: (jnp.maximum(j - half, 0), 0))
    hid = pl.BlockSpec((t, width), lambda j, r: (0, j))
    return w_in, b_in, w_a, w_b, hid


def ff_call(rot, h, par, wia, wib, bias, woa, wob, bout):
    t = h.shape[0]
    blocks = 6
    w_in, b_in, w_a, w_b, hid = ff_specs(t, blocks)
    return pl.pallas_call(
        ff_kernel,
        out_shape=(sds((t, FF), BF), sds((t, FF), BF), sds((t, D), BF), sds((t, D), BF)),
        grid_spec=pltpu.PrefetchScalarGridSpec(
            num_scalar_prefetch=1,
            grid=(blocks,),
            in_specs=[whole((t, D)), whole((8, D)), w_in, w_in, b_in, w_a, w_b, whole((1, D))],
            out_specs=[hid, hid, whole((t, D)), whole((t, D))],
            scratch_shapes=[pltpu.VMEM((t, D), F32)],
        ),
        compiler_params=params_of(),
        cost_estimate=cost(4 * t * D * FF, 4 * D * FF + 4 * t * FF, 2 * t * FF),
        name="feed",
    )(rot, h, par, wia, wib, bias, woa, wob, bout)


def ff_back_call(rot, g, act, slope, nrm, wia, wib, woa, wob, h, par):
    t = h.shape[0]
    blocks = 6
    w_in, b_in, w_a, w_b, hid = ff_specs(t, blocks)
    return pl.pallas_call(
        ff_back_kernel,
        out_shape=(
            sds((HALF, FF), BF), sds((HALF, FF), BF), sds((FF // 2, D), BF), sds((FF // 2, D), BF),
            sds((1, FF), F32), sds((8, D), F32), sds((t, D), BF),
        ),
        grid_spec=pltpu.PrefetchScalarGridSpec(
            num_scalar_prefetch=1,
            grid=(blocks,),
            in_specs=[
                whole((t, D)), hid, hid, whole((t, D)), w_in, w_in, w_a, w_b, whole((t, D)),
                whole((8, D)),
            ],
            out_specs=[w_in, w_in, w_a, w_b, b_in, whole((8, D)), whole((t, D))],
            scratch_shapes=[pltpu.VMEM((t, D), F32)],
        ),
        compiler_params=params_of(),
        cost_estimate=cost(8 * t * D * FF, 8 * D * FF + 4 * t * FF),
        name="feed_back",
    )(rot, g, act, slope, nrm, wia, wib, woa, wob, h, par)


def mix_back_call(rot, g, o, woa, wob):
    t = g.shape[0]
    return pl.pallas_call(
        mix_back_kernel,
        out_shape=(sds((t, D), BF), sds((16, t), F32), sds((HALF, D), BF), sds((HALF, D), BF)),
        grid_spec=pltpu.PrefetchScalarGridSpec(
            num_scalar_prefetch=1,
            grid=(1,),
            in_specs=[whole((t, D)), whole((t, D)), whole((HALF, D)), whole((HALF, D))],
            out_specs=[whole((t, D)), whole((16, t)), whole((HALF, D)), whole((HALF, D))],
        ),
        compiler_params=params_of(),
        cost_estimate=cost(4 * t * D * D, 4 * D * D + 6 * t * D),
        name="mix_back",
    )(rot, g, o, woa, wob)


def attend_back_call(qkv, kv_t, dmix, lse, delta, seg_row, seg_m, seg_t):
    t = dmix.shape[0]
    w = 2 * HD
    col = pl.BlockSpec((t, w), lambda j: (0, j))
    return pl.pallas_call(
        attend_back_kernel,
        out_shape=(sds((t, D), F32), sds((t, D), F32), sds((t, D), F32), sds((t, D), BF), sds((t, D), BF)),
        grid=(PAIRS,),
        in_specs=[
            col,
            pl.BlockSpec((t, w), lambda j: (0, j + PAIRS)),
            pl.BlockSpec((t, w), lambda j: (0, j + 2 * PAIRS)),
            col,
            pl.BlockSpec((t, w), lambda j: (0, j + PAIRS)),
            col, whole((16, t)), whole((16, t)), whole((1, t)), whole((t, 1)), whole((t, 1)),
        ],
        out_specs=[col] * 5,
        compiler_params=params_of(),
        cost_estimate=cost(20 * t * t * D * 4, 30 * t * D, 2 * t * t * HEADS),
        name="attend_back",
    )(qkv, qkv, qkv, kv_t, kv_t, dmix, lse, delta, seg_row, seg_m, seg_t)


def qkv_back_call(rot, dq, dkm, dvm, dkr, dvr, qkv, cosines, sines, pos, nrm, wa, wb, h, par, g):
    t = h.shape[0]
    w_in = pl.BlockSpec((HALF, D), lambda j, r: (0, j))
    rows = whole((t, D))
    return pl.pallas_call(
        qkv_back_kernel,
        out_shape=(
            sds((HALF, QKV), BF), sds((HALF, QKV), BF), sds((1, QKV), F32), sds((8, D), F32),
            sds((t, D), BF),
        ),
        grid_spec=pltpu.PrefetchScalarGridSpec(
            num_scalar_prefetch=1,
            grid=(3,),
            in_specs=[
                rows, rows, rows, rows, rows, pl.BlockSpec((t, D), lambda j, r: (0, j)), rows, rows,
                whole((t, 2)), rows, w_in, w_in, rows, whole((8, D)), rows,
            ],
            out_specs=[w_in, w_in, pl.BlockSpec((1, D), lambda j, r: (0, j)), whole((8, D)), rows],
            scratch_shapes=[pltpu.VMEM((t, D), F32), pltpu.VMEM((t, D), F32)],
        ),
        compiler_params=params_of(),
        cost_estimate=cost(4 * t * D * QKV, 4 * D * QKV + 30 * t * D),
        name="qkv_back",
    )(rot, dq, dkm, dvm, dkr, dvr, qkv, cosines, sines, pos, nrm, wa, wb, h, par, g)


def layout(image_sides, capacity):
    counts = image_sides * image_sides
    end_pos = jnp.cumsum(counts)
    start_pos = end_pos - counts
    positions = jnp.arange(capacity, dtype=jnp.int32)
    segment = jnp.sum((positions[:, None] >= end_pos[None, :]).astype(jnp.int32), axis=1)
    slot_ids = jnp.arange(image_sides.shape[-1], dtype=jnp.int32)
    one_hot = (segment[:, None] == slot_ids[None, :]).astype(jnp.int32)
    start_tok = jnp.sum(one_hot * start_pos[None, :], axis=1)
    side_len = jnp.maximum(jnp.sum(one_hot * image_sides[None, :], axis=1), 1)
    local_idx = positions - start_tok
    is_valid = segment < image_sides.shape[-1]
    patch_row = jnp.where(is_valid, local_idx // side_len, 0)
    patch_col = jnp.where(is_valid, local_idx % side_len, 0)
    return segment, patch_row, patch_col, is_valid


def turning(freq, pos):
    wide = jnp.concatenate([freq.reshape(2, HEADS, HD // 2)] * 2, axis=2).reshape(2, D)
    angles = pos[:, 0:1] * wide[0][None, :] + pos[:, 1:2] * wide[1][None, :]
    low = (jnp.arange(D) % HD) < HD // 2
    sines = jnp.sin(angles)
    return jnp.cos(angles), jnp.where(low[None, :], -sines, sines)


def flipped(x, axis, bit):
    return lax.ppermute(x, axis, [(i, i ^ bit) for i in range(lax.axis_size(axis))])


def to_owners(blocks, section, core):
    stacked = jnp.stack(blocks)
    got = [stacked[section]] + [flipped(stacked[section ^ d], "section", d) for d in (1, 2, 3)]
    here = (section // 2) == core
    near = jnp.stack(got[:2])
    away = jnp.stack(got[2:])
    mine = jnp.where(here, near, away)
    other = flipped(jnp.where(here, away, near), "group", 1)

    def in_order(pair):
        return jnp.where(section % 2 == 0, pair, pair[::-1])

    mine, other = in_order(mine), in_order(other)
    first = jnp.where(core == 0, mine, other)
    second = jnp.where(core == 0, other, mine)
    return jnp.concatenate([first, second], axis=1).reshape(-1, D)


MESH = pl.DeviceIdType.MESH
SMALL = 6144 // 128
SEMS = 20
LINE = 4


def unit_shape(s, part):
    if s % 2:
        return (FF // 2, D) if part else (HALF, FF)
    return (HALF, D) if part else (HALF, QKV)


def grad_shape(s, part):
    if s % 2:
        return (FF // 2, D) if part else (HALF, FF)
    return (D, D) if part else (HALF, 2 * D)


def piece_shape(s, part):
    r, w = grad_shape(s, part)
    return (r // 8, w // 2)


def flip(v, bit):
    if bit == 1:
        return v + 1 - 2 * (v % 2)
    if bit == 2:
        return (v + 2) % 4
    return 3 - v


def here():
    return lax.axis_index("section"), lax.axis_index("group"), lax.axis_index("dp")


def loop(n, body):
    def one(i, carried):
        body(i)
        return carried

    lax.fori_loop(0, n, one, 0)


def greet(plane, line):
    c, g, z = here()
    barrier = pltpu.get_barrier_semaphore()
    pl.semaphore_signal(barrier, inc=1, device_id={"group": 1 - g}, device_id_type=MESH)
    count = 1
    for bit in (1, 2, 3):
        if plane:
            for core in (g, 1 - g):
                pl.semaphore_signal(
                    barrier, inc=1, device_id={"section": flip(c, bit), "group": core},
                    device_id_type=MESH,
                )
                count += 1
        if line:
            pl.semaphore_signal(barrier, inc=1, device_id={"dp": flip(z, bit)}, device_id_type=MESH)
            count += 1
    pl.semaphore_wait(barrier, count)


def guarded(cond, act):
    if cond is None:
        act()
    else:
        pl.when(cond)(act)


def accumulate(into, term, rows):
    strip = 32 if rows % 32 == 0 else 16

    def one(i):
        at = pl.ds(pl.multiple_of(i * strip, strip), strip)
        into[at, :] = (into[at, :].astype(F32) + term[at, :].astype(F32)).astype(BF)

    loop(rows // strip, one)


class Unit:
    def __init__(
        self, s, part, send, recv, own=None, quarter=None, final=None, plane=None, line=None,
        held=None, whole=None,
    ):
        self.s, self.part, self.own, self.quarter_ref, self.final = s, part, own, quarter, final
        self.send, self.recv = send, recv
        self.whole = whole
        self.rows, self.cols = grad_shape(s, part)
        self.plane1, self.plane2 = plane or (None, None)
        self.up_in, self.down_in = line or (None, None)
        self.held = held
        self.pending = []

    def push(self, cond, src, dst, k, device):
        copy = pltpu.make_async_remote_copy(
            src_ref=src, dst_ref=dst, send_sem=self.send.at[k], recv_sem=self.recv.at[k],
            device_id=device, device_id_type=MESH,
        )
        guarded(cond, copy.start)
        self.pending.append((cond, copy))

    def landed(self, cond, dst, k):
        copy = pltpu.make_async_remote_copy(
            src_ref=dst, dst_ref=dst, send_sem=self.send.at[k], recv_sem=self.recv.at[k],
            device_id={"group": 1 - lax.axis_index("group")}, device_id_type=MESH,
        )
        guarded(cond, copy.wait_recv)

    def finish(self):
        for cond, copy in self.pending:
            guarded(cond, copy.wait_send)

    def quarter(self, q):
        rows = self.rows // 4
        return self.own.at[pl.ds(pl.multiple_of(q * rows, rows), rows), :]

    def mine(self):
        if self.quarter_ref is not None:
            return self.quarter_ref
        return self.quarter(lax.axis_index("section"))

    def piece(self, k):
        rows, cols = self.rows // 8, self.cols // 2
        return self.mine().at[
            pl.ds(pl.multiple_of((k // 2) * rows, rows), rows),
            pl.ds(pl.multiple_of((k % 2) * cols, cols), cols),
        ]

    def first_step(self):
        c, _, _ = here()
        x, y = c % 2, c // 2
        other = {"section": flip(c, 2 if self.part else 1)}
        for b in range(2):
            q = 2 * (1 - y) + b if self.part else 2 * b + 1 - x
            self.push(None, self.quarter(q), self.plane1.at[b], 1 + b, other)

    def second_step(self):
        c, _, _ = here()
        x, y = c % 2, c // 2
        rows = self.rows // 4
        other = {"section": flip(c, 1 if self.part else 2)}
        for b in range(2):
            self.landed(None, self.plane1.at[b], 1 + b)
        b = (1 - x) if self.part else (1 - y)
        q = (2 * y + 1 - x) if self.part else (2 * (1 - y) + x)
        accumulate(self.quarter(q), self.plane1.at[b], rows)
        self.push(None, self.quarter(q), self.plane2, 3, other)
        accumulate(self.mine(), self.plane1.at[1 - b], rows)

    def third_step(self):
        self.landed(None, self.plane2, 3)
        accumulate(self.mine(), self.plane2, self.rows // 4)

    def line_step(self, t):
        _, _, z = here()
        n = LINE
        rows = self.rows // 8
        up = (z < n - 1) & (z <= t)
        down = (z > 0) & (z >= n - 1 - t)
        k_up = jnp.minimum(n - 1 - t + z, n - 1)
        k_down = jnp.maximum(z - (n - 1) + t, 0)
        if t > 0:

            @pl.when(up & (z > 0))
            def _():
                self.landed(None, self.up_in.at[t - 1], 4 + t - 1)
                accumulate(self.piece(k_up), self.up_in.at[t - 1], rows)

            @pl.when(down & (z < n - 1))
            def _():
                self.landed(None, self.down_in.at[t - 1], 7 + t - 1)
                accumulate(self.piece(k_down), self.down_in.at[t - 1], rows)

        self.push(up, self.piece(k_up), self.up_in.at[t], 4 + t, {"dp": jnp.minimum(z + 1, n - 1)})
        self.push(down, self.piece(k_down), self.down_in.at[t], 7 + t, {"dp": jnp.maximum(z - 1, 0)})

    def line_end(self):
        _, _, z = here()
        n = LINE
        rows = self.rows // 8

        @pl.when(z > 0)
        def _():
            self.landed(None, self.up_in.at[n - 2], 4 + n - 2)
            accumulate(self.piece(z), self.up_in.at[n - 2], rows)

        @pl.when(z < n - 1)
        def _():
            self.landed(None, self.down_in.at[n - 2], 7 + n - 2)
            accumulate(self.piece(z), self.down_in.at[n - 2], rows)

    def last_piece(self):
        return self.final if self.final is not None else self.piece(here()[2])

    def own_piece(self):
        _, _, z = here()
        return pltpu.make_async_copy(
            self.last_piece(), self.held.at[z, self.s], self.send.at[10 + self.s]
        )

    def gather(self):
        c, _, z = here()
        for q in range(4):
            if q == self.s:
                pl.when(c == q)(self.own_piece().start)
            else:
                self.push(
                    c == q, self.last_piece(), self.held.at[z, q], 10 + q, {"section": self.s}
                )

    def share_step(self, t):
        _, _, z = here()
        n = LINE
        whole = self.whole
        if t == 0:
            copy = pltpu.make_async_copy(self.last_piece(), whole.at[z], self.send.at[0])
            copy.start()
            copy.wait()
        else:
            self.landed(z >= t, whole.at[jnp.maximum(z - t, 0)], 14 + t - 1)
            self.landed(z + t < n, whole.at[jnp.minimum(z + t, n - 1)], 17 + t - 1)
        if t < n - 1:
            low, high = jnp.maximum(z - t, 0), jnp.minimum(z + t, n - 1)
            self.push(
                (z >= t) & (z < n - 1), whole.at[low], whole.at[low], 14 + t,
                {"dp": jnp.minimum(z + 1, n - 1)},
            )
            self.push(
                (z + t < n) & (z > 0), whole.at[high], whole.at[high], 17 + t,
                {"dp": jnp.maximum(z - 1, 0)},
            )

    def whole_copy(self):
        return pltpu.make_async_copy(self.whole, self.held.at[:, self.s], self.send.at[10 + self.s])

    def whole_gather(self):
        c, _, _ = here()
        for q in range(4):
            if q == self.s:
                pl.when(c == q)(self.whole_copy().start)
            else:
                self.push(c == q, self.whole, self.held.at[:, q], 10 + q, {"section": self.s})

    def whole_end(self):
        c, _, _ = here()
        for q in range(4):
            if q == self.s:
                pl.when(c == q)(self.whole_copy().wait)
            else:
                self.landed(c == self.s, self.held.at[:, q], 10 + q)

    def out_step(self, t):
        c, _, z = here()
        n = LINE
        mine = c == self.s
        held = self.held
        if t == 0:
            for q in range(4):
                if q == self.s:
                    pl.when(mine)(self.own_piece().wait)
                else:
                    self.landed(mine, held.at[z, q], 10 + q)
        else:
            self.landed(mine & (z >= t), held.at[jnp.maximum(z - t, 0)], 14 + t - 1)
            self.landed(mine & (z + t < n), held.at[jnp.minimum(z + t, n - 1)], 17 + t - 1)
        if t < n - 1:
            low, high = jnp.maximum(z - t, 0), jnp.minimum(z + t, n - 1)
            self.push(
                mine & (z >= t) & (z < n - 1), held.at[low], held.at[low], 14 + t,
                {"dp": jnp.minimum(z + 1, n - 1)},
            )
            self.push(
                mine & (z + t < n) & (z > 0), held.at[high], held.at[high], 17 + t,
                {"dp": jnp.maximum(z - 1, 0)},
            )


class Delivery:
    def __init__(self, sources, out, send, recv):
        self.sources, self.out, self.send, self.recv = sources, out, send, recv

    def copies(self, s):
        c, g, _ = here()
        slot = self.out.at[c % 2, g]
        near = pltpu.make_async_copy(self.sources[s], slot, self.send.at[s])
        far = pltpu.make_async_remote_copy(
            src_ref=self.sources[s], dst_ref=slot, send_sem=self.send.at[s],
            recv_sem=self.recv.at[(c % 2) * 2 + g], device_id={"section": s, "group": c // 2},
            device_id_type=MESH,
        )
        return near, far, (c == s) & (g == c // 2)

    def start(self, s):
        near, far, stays = self.copies(s)
        pl.when(stays)(near.start)
        pl.when(jnp.logical_not(stays))(far.start)

    def finish(self):
        c, g, _ = here()
        for s in range(4):
            near, far, stays = self.copies(s)
            pl.when(stays)(near.wait)
            pl.when(jnp.logical_not(stays))(far.wait_send)
        for m in range(2):
            for half in range(2):
                slot = self.out.at[m, half]
                copy = pltpu.make_async_remote_copy(
                    src_ref=slot, dst_ref=slot, send_sem=self.send.at[0],
                    recv_sem=self.recv.at[2 * m + half], device_id={"group": 1 - g},
                    device_id_type=MESH,
                )
                pl.when(jnp.logical_not((2 * g + m == c) & (g == half)))(copy.wait_recv)


def feed_back_kernel(s, carry, *refs):
    delivers = carry is None
    wim, wit, wom, wot, act_in, slope_in, streams = refs[:7]
    refs = refs[7:]
    count = 0 if delivers else len(carry.all)
    carried, refs = refs[:count], refs[count:]
    g_ref, nrm, par = refs[:3]
    d_in, d_out = refs[3:5]
    count = max(count, 1)
    results, refs = refs[5 : 5 + count], refs[5 + count :]
    dbin_ref, small_ref, out_ref = refs[:3]
    w_in, w_out, act, slope, h, own_i, own_o, their_i, their_o, core_i, core_o, acc, nrm_t = refs[3:16]
    load_sem, core_s, core_r, out_sem = refs[16:20]
    refs = refs[20:]
    _, g, _ = here()
    partner = {"group": 1 - g}
    width = FF // CHUNKS
    third = CHUNKS // 2

    def column(j):
        b = (j + g * third) % CHUNKS
        return pl.ds(pl.multiple_of(b * width, width), width)

    def line_of(j):
        return pl.ds(pl.multiple_of(j * width, width), width)

    def loads(j):
        cols, rows = column(j), line_of(j % third)
        first = j < third
        return (
            (None, pltpu.make_async_copy(wim.at[:, cols], w_in.at[0, :, cols], load_sem.at[j, 0])),
            (None, pltpu.make_async_copy(wit.at[:, cols], w_in.at[1, :, cols], load_sem.at[j, 1])),
            (first, pltpu.make_async_copy(wom.at[rows, :], w_out.at[line_of(j), :], load_sem.at[j, 2])),
            (
                jnp.logical_not(first),
                pltpu.make_async_copy(wot.at[rows, :], w_out.at[line_of(j), :], load_sem.at[j, 2]),
            ),
            (None, pltpu.make_async_copy(act_in.at[:, line_of(j)], act.at[:, line_of(j)], load_sem.at[j, 3])),
            (None, pltpu.make_async_copy(slope_in.at[:, line_of(j)], slope.at[:, line_of(j)], load_sem.at[j, 4])),
        )

    def load(j):
        for cond, copy in loads(j):
            guarded(cond, copy.start)

    def core_copies(j):
        cols, rows = column(j), line_of(j % third)
        return (
            pltpu.make_async_remote_copy(
                src_ref=their_i.at[:, cols], dst_ref=core_i.at[:, cols], send_sem=core_s.at[j, 0],
                recv_sem=core_r.at[j, 0], device_id=partner, device_id_type=MESH,
            ),
            pltpu.make_async_remote_copy(
                src_ref=their_o.at[rows, :], dst_ref=core_o.at[rows, :], send_sem=core_s.at[j, 1],
                recv_sem=core_r.at[j, 1], device_id=partner, device_id_type=MESH,
            ),
        )

    loop(CHUNKS, load)
    stream_copy = pltpu.make_async_copy(streams.at[s - 1], h, out_sem.at[2])
    stream_copy.start()
    if not delivers:
        carry.load(carried, results, refs)
    greet(True, not delivers)
    if delivers:
        delivery = Delivery([streams.at[i] for i in range(4)], results[0], refs[0], refs[1])
        for i in range(4):
            delivery.start(i)
    else:
        carry.begin()
    acc[...] = jnp.zeros_like(acc)
    nrm_t[...] = jnp.transpose(nrm[...])

    def block(j):
        for cond, copy in loads(j):
            guarded(cond, copy.wait)
        cols, rows = column(j), line_of(j)
        grad = g_ref[...]
        d_up_f = dot_nt(grad, w_out[rows, :]) * slope[:, rows].astype(F32)
        d_up = d_up_f.astype(BF)
        d_o = dot_tn(act[:, rows], grad).astype(BF)
        dbin_ref[:, cols] = jnp.sum(d_up_f, axis=0, keepdims=True)
        their_i[:, cols] = dot(nrm_t[HALF:, :], d_up).astype(BF)
        inward, outward = core_copies(j)
        inward.start()

        @pl.when(j >= third)
        def _():
            their_o[line_of(j % third), :] = d_o
            outward.start()

        @pl.when(j < third)
        def _():
            own_o[line_of(j % third), :] = d_o

        own_i[:, cols] = dot(nrm_t[:HALF, :], d_up).astype(BF)
        acc[:, :HALF] += dot_nt(d_up, w_in[0, :, cols])
        acc[:, HALF:] += dot_nt(d_up, w_in[1, :, cols])

    if delivers:
        loop(CHUNKS, block)
    else:
        for i in range(3):
            loop(CHUNKS // 3, lambda j, i=i: block(j + CHUNKS // 3 * i))
            carry.step(i + 1)
    stream_copy.wait()
    grad = g_ref[...].astype(F32)
    d_normed = turn_halves(acc[...], g)
    out, d_gain, d_shift = norm_backward(h[...].astype(F32), par[0:1, :], grad, d_normed)
    out_ref[...] = out.astype(BF)
    small_ref[0:1, :] = jnp.sum(grad, axis=0, keepdims=True)
    small_ref[1:2, :] = d_gain
    small_ref[2:3, :] = d_shift
    small_ref[3:8, :] = jnp.zeros((5, D), F32)

    def ended(j):
        inward, outward = core_copies(j)
        inward.wait()
        pl.when(j >= third)(outward.wait)

    loop(CHUNKS, ended)
    accumulate(own_i, core_i, HALF)
    saves = [pltpu.make_async_copy(own_i, d_in, out_sem.at[0])]
    saves[0].start()
    accumulate(own_o, core_o, FF // 2)
    saves.append(pltpu.make_async_copy(own_o, d_out, out_sem.at[1]))
    saves[1].start()
    if delivers:
        delivery.finish()
    else:
        carry.end()
    for copy in saves:
        copy.wait()


class Carry:
    def __init__(self, plane, line, hold):
        self.planes = [(plane, 0), (plane, 1)]
        self.line, self.hold = line, hold
        self.all = self.planes + list(line) + list(hold)

    def results(self):
        out = []
        for u in self.planes:
            r, w = grad_shape(*u)
            out.append(sds((r // 4, w), BF))
        out += [sds(piece_shape(*u), BF) for u in self.line]
        return out + [sds((4, 4) + piece_shape(*u), BF) for u in self.hold]

    def scratch(self):
        out = []
        for u in self.planes:
            r, w = grad_shape(*u)
            out += [pltpu.VMEM((r, w), BF), pltpu.VMEM((2, r // 4, w), BF), pltpu.VMEM((r // 4, w), BF)]
        for u in self.line:
            r, w = grad_shape(*u)
            out += [pltpu.VMEM((r // 4, w), BF)] + [pltpu.VMEM((3,) + piece_shape(*u), BF)] * 2
        out += [pltpu.VMEM(piece_shape(*u), BF) for u in self.hold]
        dma = pltpu.SemaphoreType.DMA
        return out + [dma((len(self.all), SEMS)), dma((len(self.all), SEMS))]

    def load(self, sources, results, refs):
        send, recv = refs[-2:]
        refs = list(refs[:-2])
        self.units, self.loads, self.targets = [], [], results
        for i, u in enumerate(self.all):
            sems = (send.at[i], recv.at[i])
            if i < 2:
                own, first, second = refs.pop(0), refs.pop(0), refs.pop(0)
                unit = Unit(*u, *sems, own=own, plane=(first, second))
            elif i < 2 + len(self.line):
                own, up, down = refs.pop(0), refs.pop(0), refs.pop(0)
                unit = Unit(*u, *sems, quarter=own, line=(up, down))
            else:
                own = refs.pop(0)
                unit = Unit(*u, *sems, final=own, held=results[i])
            copy = pltpu.make_async_copy(sources[i], own, sems[0].at[0])
            copy.start()
            self.units.append(unit)
            self.loads.append(copy)
        n = 2 + len(self.line)
        self.plane_units, self.line_units, self.hold_units = (
            self.units[:2], self.units[2:n], self.units[n:],
        )

    def begin(self):
        for copy in self.loads:
            copy.wait()
        for unit in self.plane_units:
            unit.first_step()
        for unit in self.line_units:
            unit.line_step(0)
        for unit in self.hold_units:
            unit.gather()

    def step(self, i):
        for unit in self.line_units:
            if i < LINE - 1:
                unit.line_step(i)
            else:
                unit.line_end()
        if i == 3:
            for unit in self.plane_units:
                unit.second_step()
        for unit in self.hold_units:
            unit.out_step(i - 1)

    def end(self):
        for unit in self.hold_units:
            unit.out_step(LINE - 1)
        saves = [
            pltpu.make_async_copy(unit.last_piece(), target, unit.send.at[0])
            for unit, target in zip(self.line_units, self.targets[2:])
        ]
        for copy in saves:
            copy.start()
        for unit, target in zip(self.plane_units, self.targets):
            unit.third_step()
            copy = pltpu.make_async_copy(unit.mine(), target, unit.send.at[0])
            copy.start()
            saves.append(copy)
        for copy in saves:
            copy.wait()
        for unit in self.units:
            unit.finish()


def feed_back_call(s, weights, act, slope, streams, g, nrm, par, carry, carried, collective):
    t = g.shape[0]
    hbm = pl.BlockSpec(memory_space=pl.ANY)
    vmem = pl.BlockSpec(memory_space=pltpu.VMEM)
    delivers = carry is None
    dma = pltpu.SemaphoreType.DMA
    half_i, half_o = grad_shape(s, 0), grad_shape(s, 1)
    results = [sds((2, 2, t, D), BF)] if delivers else carry.results()
    scratch = [
        pltpu.VMEM((2, HALF, FF), BF), pltpu.VMEM((FF, D), BF), pltpu.VMEM((t, FF), BF),
        pltpu.VMEM((t, FF), BF), pltpu.VMEM((t, D), BF),
        pltpu.VMEM(half_i, BF), pltpu.VMEM(half_o, BF), pltpu.VMEM(half_i, BF),
        pltpu.VMEM(half_o, BF), pltpu.VMEM(half_i, BF), pltpu.VMEM(half_o, BF),
        pltpu.VMEM((t, D), F32), pltpu.VMEM((D, t), BF),
        dma((CHUNKS, 5)), dma((CHUNKS, 2)), dma((CHUNKS, 2)), dma((3,)),
    ] + ([dma((4,)), dma((4,))] if delivers else carry.scratch())
    out = pl.pallas_call(
        partial(feed_back_kernel, s, carry),
        out_shape=[sds(half_i, BF), sds(half_o, BF)] + results
        + [sds((1, FF), F32), sds((8, D), F32), sds((t, D), BF)],
        in_specs=[hbm] * (7 + len(carried)) + [vmem] * 3,
        out_specs=[hbm] * (2 + len(results)) + [vmem] * 3,
        scratch_shapes=scratch,
        compiler_params=pltpu.CompilerParams(
            collective_id=collective, has_side_effects=True, vmem_limit_bytes=62 * 1024 * 1024
        ),
        name="feed_back_carry",
    )(*weights, act, slope, streams, *carried, g, nrm, par)
    return out[:2], out[2 : 2 + len(results)], out[2 + len(results) :]


def attention_back_kernel(s, carry, *refs):
    wim, wit, wom, wot = refs[:4]
    count = len(carry.all)
    carried = refs[4 : 4 + count]
    refs = refs[4 + count :]
    g_ref, o_ref, qkv, kv_t, lse_ref, seg_row, seg_m, seg_t, cosines, sines, pos, nrm, h, par = refs[:14]
    d_first, d_second = refs[14:16]
    results, refs = refs[16 : 16 + count], refs[16 + count :]
    dbin_ref, small_ref, out_ref = refs[:3]
    w_in, w_out, dmix, d_q, d_k, d_v, give_k, give_v, got_k, got_v = refs[3:13]
    own, their, core = refs[13:15], refs[15:17], refs[17:19]
    acc, dp, delta_ref, nrm_t = refs[19:23]
    load_sem, kv_s, kv_r, core_s, core_r, out_sem = refs[23:29]
    carry.load(carried, results, refs[29:])
    _, g, _ = here()
    partner = {"group": 1 - g}
    tokens = g_ref.shape[0]

    def remote(src, dst, ssem, rsem):
        return pltpu.make_async_remote_copy(
            src_ref=src, dst_ref=dst, send_sem=ssem, recv_sem=rsem, device_id=partner,
            device_id_type=MESH,
        )

    loads = [
        pltpu.make_async_copy(src, dst, load_sem.at[i])
        for i, (src, dst) in enumerate(
            (
                (wom, w_out.at[0]), (wot, w_out.at[1]), (wim, w_in.at[0]), (wit, w_in.at[1]),
            )
        )
    ]
    for copy in loads:
        copy.start()
    greet(True, True)
    carry.begin()

    loads[0].wait()
    loads[1].wait()
    grad = g_ref[...]
    d_mix = jnp.concatenate([dot_nt(grad, w_out[0]), dot_nt(grad, w_out[1])], axis=1)
    dmix[...] = turn_halves(d_mix, g).astype(BF)
    o = o_ref[...].astype(F32)
    head = lax.broadcasted_iota(jnp.int32, (16, D), 0)
    lane = lax.broadcasted_iota(jnp.int32, (16, D), 1)
    delta_ref[...] = lax.dot_general(
        jnp.where(lane // HD == head, 1.0, 0.0), dmix[...].astype(F32) * o, NT,
        preferred_element_type=F32, precision=lax.Precision.HIGHEST,
    )
    turned = turn_halves(o, g).astype(BF)
    turned_t = jnp.transpose(turned)
    nrm_t[...] = jnp.transpose(nrm[...])
    their[1][HALF:, :] = dot(turned_t[HALF:, :], grad).astype(BF)
    core_copies = [remote(their[1].at[HALF:, :], core[1].at[HALF:, :], core_s.at[3], core_r.at[3])]
    core_copies[0].start()
    own[1][HALF:, :] = dot(turned_t[:HALF, :], grad).astype(BF)

    lanes = lax.broadcasted_iota(jnp.int32, (tokens, 2 * HD), 1)

    def pair(j):
        def columns(first):
            return pl.ds(pl.multiple_of(first + j * 2 * HD, 2 * HD), 2 * HD)

        q = qkv[:, columns(0)]
        do = dmix[:, columns(0)]
        zero = jnp.zeros_like(q)
        sets = (
            (qkv[:, columns(D)], qkv[:, columns(2 * D)], seg_m),
            (kv_t[:, columns(0)], kv_t[:, columns(D)], seg_t),
        )
        total_q = [0.0, 0.0]
        keys_t = [jnp.transpose(sets[i][0]) for i in range(2)]
        total_k = [jnp.zeros((tokens, 2 * HD), F32)] * 2
        total_v = [jnp.zeros((tokens, 2 * HD), F32)] * 2
        for side in range(2):
            mine = (lanes >= HD) if side else (lanes < HD)
            q_head = jnp.where(mine, q, zero)
            do_head = jnp.where(mine, do, zero)
            lse = lse_ref[pl.ds(2 * j + side, 1), :]
            delta = delta_ref[pl.ds(2 * j + side, 1), :]
            for i, (k, v, seg) in enumerate(sets):
                p_t = jnp.where(
                    seg[...] == seg_row[...], jnp.exp(dot_nt(k, q_head) - lse), 0.0
                )
                d_s = (p_t * (dot_nt(v, do_head) - delta)).astype(BF)
                total_v[i] = total_v[i] + dot(p_t.astype(BF), do_head)
                total_k[i] = total_k[i] + dot(d_s, q_head)
                total_q[side] = total_q[side] + dot(keys_t[i][side * HD : (side + 1) * HD, :], d_s)
        d_q[:, columns(0)] = jnp.transpose(jnp.concatenate(total_q, axis=0))
        d_k[:, columns(0)] = total_k[0]
        d_v[:, columns(0)] = total_v[0]
        give_k[:, columns(0)] = total_k[1].astype(BF)
        give_v[:, columns(0)] = total_v[1].astype(BF)

    def exchanges(i):
        cols = pl.ds(i * 4 * HD, 4 * HD)
        return (
            remote(give_k.at[:, cols], got_k.at[:, cols], kv_s.at[0, i], kv_r.at[0, i]),
            remote(give_v.at[:, cols], got_v.at[:, cols], kv_s.at[1, i], kv_r.at[1, i]),
        )

    for i in range(PAIRS // 2):
        loop(2, lambda j, i=i: pair(2 * i + j))
        for copy in exchanges(i):
            copy.start()
        carry.step(i + 1)

    loads[2].wait()
    loads[3].wait()
    acc[...] = jnp.zeros_like(acc)
    small_ref[...] = jnp.zeros_like(small_ref)

    def turned_back(dy, y):
        swapped = swap_pairs(dy)
        d_angle = y * swapped - swap_pairs(y) * dy
        small_ref[3:4, :] += jnp.sum(d_angle * pos[:, 0:1], axis=0, keepdims=True)
        small_ref[4:5, :] += jnp.sum(d_angle * pos[:, 1:2], axis=0, keepdims=True)
        return dy * cosines[...] - swapped * sines[...]

    for j in range(3):
        cols = slice(j * D, (j + 1) * D)
        if j == 0:
            dp[...] = turned_back(
                d_q[...] * HD ** (-0.5), qkv[:, :D].astype(F32) * HD**0.5
            )
        elif j == 1:
            for i in range(PAIRS // 2):
                for copy in exchanges(i):
                    copy.wait()
            dp[...] = turned_back(d_k[...] + got_k[...].astype(F32), qkv[:, D : 2 * D].astype(F32))
        else:
            dp[...] = d_v[...] + got_v[...].astype(F32)
        d_p = dp[...].astype(BF)
        dbin_ref[:, cols] = jnp.sum(dp[...], axis=0, keepdims=True)
        if j < 2:
            place = (0, (slice(None), cols))
        else:
            place = (1, (slice(0, HALF), slice(None)))
        part, at = place
        their[part][at] = dot(nrm_t[HALF:, :], d_p).astype(BF)
        copy = remote(their[part].at[at], core[part].at[at], core_s.at[j], core_r.at[j])
        copy.start()
        core_copies.append(copy)
        own[part][at] = dot(nrm_t[:HALF, :], d_p).astype(BF)
        acc[:, :HALF] += dot_nt(d_p, w_in[0, :, cols])
        acc[:, HALF:] += dot_nt(d_p, w_in[1, :, cols])
    grad = g_ref[...].astype(F32)
    d_normed = turn_halves(acc[...], g)
    out, d_gain, d_shift = norm_backward(h[...].astype(F32), par[0:1, :], grad, d_normed)
    out_ref[...] = out.astype(BF)
    small_ref[0:1, :] = jnp.sum(grad, axis=0, keepdims=True)
    small_ref[1:2, :] = d_gain
    small_ref[2:3, :] = d_shift

    for copy in core_copies:
        copy.wait()
    saves = []
    for part, target in enumerate((d_first, d_second)):
        accumulate(own[part], core[part], own[part].shape[0])
        copy = pltpu.make_async_copy(own[part], target, out_sem.at[part])
        copy.start()
        saves.append(copy)
    carry.end()
    for copy in saves:
        copy.wait()


def attention_back_call(
    s, weights, carry, carried, g, saved, seg_row, seg_m, seg_t, turns, pos, h, par, collective
):
    t = g.shape[0]
    qkv, nrm, kv_t, o, lse = saved
    hbm = pl.BlockSpec(memory_space=pl.ANY)
    vmem = pl.BlockSpec(memory_space=pltpu.VMEM)
    dma = pltpu.SemaphoreType.DMA
    halves = [grad_shape(s, 0), grad_shape(s, 1)]
    rows, wide = pltpu.VMEM((t, D), BF), pltpu.VMEM((t, D), F32)
    results = carry.results()
    scratch = [
        pltpu.VMEM((2, HALF, QKV), BF), pltpu.VMEM((2, HALF, D), BF), rows, wide, wide, wide,
        rows, rows, rows, rows,
        *[pltpu.VMEM(x, BF) for x in halves * 3],
        wide, wide, pltpu.VMEM((16, t), F32), pltpu.VMEM((D, t), BF),
        dma((4,)), dma((2, 3)), dma((2, 3)), dma((4,)), dma((4,)), dma((2,)),
    ] + carry.scratch()
    out = pl.pallas_call(
        partial(attention_back_kernel, s, carry),
        out_shape=[sds(x, BF) for x in halves] + results
        + [sds((1, QKV), F32), sds((8, D), F32), sds((t, D), BF)],
        in_specs=[hbm] * (4 + len(carried)) + [vmem] * 14,
        out_specs=[hbm] * (2 + len(results)) + [vmem] * 3,
        scratch_shapes=scratch,
        compiler_params=pltpu.CompilerParams(
            collective_id=collective, has_side_effects=True, vmem_limit_bytes=62 * 1024 * 1024
        ),
        name="attention_back_carry",
    )(*weights, *carried, g, o, qkv, kv_t, lse, seg_row, seg_m, seg_t, *turns, pos, nrm, h, par)
    return out[:2], out[2:-3], out[-3:]


LAST = (
    (0, 0, "own"), (0, 1, "own"), (1, 0, "quarter"), (1, 1, "quarter"),
    (3, 1, "final"), (2, 0, "final"), (2, 1, "final"),
)


def last_kernel(*refs):
    n = len(LAST)
    sources, streams, small_in = refs[:n], refs[n : n + 4], refs[n + 4]
    refs = refs[n + 5 :]
    outs, delivered, small_out = refs[:4], refs[4], refs[5]
    refs = refs[6:]
    owns = refs[:n]
    planes = ((refs[n], refs[n + 1]), (refs[n + 2], refs[n + 3]))
    refs = refs[n + 4 :]
    ups, downs, whole = refs[:4], refs[4:8], refs[8]
    sm, sm_core, sm_x, sm_y, sm_z = refs[9:14]
    send, recv, sm_send, sm_recv, del_send, del_recv = refs[14:]
    c, g, z = here()
    x, y = c % 2, c // 2
    units, copies = [], []
    for u, (s, part, kind) in enumerate(LAST):
        copy = pltpu.make_async_copy(sources[u], owns[u], send.at[u, 0])
        copy.start()
        copies.append(copy)
        units.append(
            Unit(
                s, part, send.at[u], recv.at[u], plane=planes[u] if u < 2 else None,
                line=(ups[u], downs[u]) if u < 4 else None, held=outs[2 * (s % 2) + part],
                whole=whole if u == 3 else None, **{kind: owns[u]},
            )
        )
    greet(True, True)

    pending = []

    def small_push(src, dst, k, device):
        copy = pltpu.make_async_remote_copy(
            src_ref=src, dst_ref=dst, send_sem=sm_send.at[k], recv_sem=sm_recv.at[k],
            device_id=device, device_id_type=MESH,
        )
        copy.start()
        pending.append(copy)
        return copy

    def small_landed(dst, k):
        pltpu.make_async_remote_copy(
            src_ref=dst, dst_ref=dst, send_sem=sm_send.at[k], recv_sem=sm_recv.at[k],
            device_id={"group": 1 - g}, device_id_type=MESH,
        ).wait_recv()

    def small_step(k):
        if k == 0:
            sm[...] = small_in[...]
            small_push(sm, sm_core, 0, {"group": 1 - g})
        elif k == 1:
            small_landed(sm_core, 0)
            sm_x[0] = sm[...] + sm_core[...]
            for b in range(2):
                small_push(sm_x.at[0, 2 * b + 1 - x], sm_x.at[1, b], 1 + b, {"section": flip(c, 1)})
        elif k == 2:
            for b in range(2):
                small_landed(sm_x.at[1, b], 1 + b)
                sm_y[b] = sm_x[0, 2 * b + x] + sm_x[1, b]
            small_push(sm_y.at[1 - y], sm_y.at[2], 3, {"section": flip(c, 2)})
        elif k == 3:
            small_landed(sm_y.at[2], 3)
            sm_z[z] = sm_y[y] + sm_y[2]
            for bit in (1, 2, 3):
                small_push(sm_z.at[z], sm_z.at[z], 3 + bit, {"dp": flip(z, bit)})
        else:
            for bit in (1, 2, 3):
                small_landed(sm_z.at[flip(z, bit)], 3 + bit)
            small_out[...] = sm_z[0] + sm_z[1] + sm_z[2] + sm_z[3]

    delivery = Delivery(streams, delivered, del_send, del_recv)

    def every(which, act, *args):
        for unit in which:
            getattr(unit, act)(*args)

    for copy in copies:
        copy.wait()
    whole_a, halves_f, ready = units[:2], units[2:4], units[4:]
    held_f, shared_f = units[2], units[3]
    every(whole_a, "first_step")
    every(halves_f, "line_step", 0)
    every(ready, "gather")
    small_step(0)
    every(halves_f, "line_step", 1)
    small_step(1)
    every(whole_a, "second_step")
    every(halves_f, "line_step", 2)
    every(ready, "out_step", 0)
    small_step(2)
    every(halves_f, "line_end")
    held_f.gather()
    shared_f.share_step(0)
    every(whole_a, "third_step")
    every(whole_a, "line_step", 0)
    small_step(3)
    for s in range(4):
        delivery.start(s)
    shared_f.share_step(1)
    every(whole_a, "line_step", 1)
    held_f.out_step(0)
    shared_f.share_step(2)
    every(whole_a, "line_step", 2)
    small_step(4)
    every(ready, "out_step", 1)
    shared_f.share_step(3)
    shared_f.whole_gather()
    every(whole_a, "line_end")
    every(whole_a, "gather")
    held_f.out_step(1)
    every(ready, "out_step", 2)
    every(whole_a, "out_step", 0)
    held_f.out_step(2)
    every(ready, "out_step", 3)
    every(whole_a, "out_step", 1)
    held_f.out_step(3)
    every(whole_a, "out_step", 2)
    every(whole_a, "out_step", 3)
    shared_f.whole_end()
    delivery.finish()
    for unit in units:
        unit.finish()
    for copy in pending:
        copy.wait_send()


def last_call(sources, streams, small):
    t = streams[0].shape[0]
    hbm = pl.BlockSpec(memory_space=pl.ANY)
    vmem = pl.BlockSpec(memory_space=pltpu.VMEM)
    dma = pltpu.SemaphoreType.DMA
    planes = []
    for r, w in (grad_shape(0, 0), grad_shape(0, 1)):
        planes += [pltpu.VMEM((2, r // 4, w), BF), pltpu.VMEM((r // 4, w), BF)]
    lines = [pltpu.VMEM((3,) + piece_shape(s, part), BF) for s, part, _ in LAST[:4]]
    scratch = (
        [pltpu.VMEM(x.shape, BF) for x in sources]
        + planes
        + lines
        + lines
        + [pltpu.VMEM((4,) + piece_shape(*LAST[3][:2]), BF)]
        + [
            pltpu.VMEM((4, SMALL, 128), F32),
            pltpu.VMEM((4, SMALL, 128), F32),
            pltpu.VMEM((2, 4, SMALL, 128), F32),
            pltpu.VMEM((3, SMALL, 128), F32),
            pltpu.VMEM((4, SMALL, 128), F32),
            dma((len(LAST), SEMS)), dma((len(LAST), SEMS)), dma((7,)), dma((7,)), dma((4,)), dma((4,)),
        ]
    )
    *out, delivered, small = pl.pallas_call(
        last_kernel,
        out_shape=[sds((4, 4) + piece_shape(s, part), BF) for s in (0, 1) for part in (0, 1)]
        + [sds((2, 2, t, D), BF), sds((SMALL, 128), F32)],
        in_specs=[hbm] * (len(LAST) + 4) + [vmem],
        out_specs=[hbm] * 5 + [vmem],
        scratch_shapes=scratch,
        compiler_params=pltpu.CompilerParams(
            collective_id=1, has_side_effects=True, vmem_limit_bytes=56 * 1024 * 1024
        ),
        name="last",
    )(*sources, *streams, small)

    return out, delivered.reshape(-1, D), small


def in_place(x):
    _, _, r, w = x.shape
    x = x.reshape(2, 2, 4, r, w).transpose(2, 0, 3, 1, 4)
    return x.reshape(8 * r, 2 * w)


CHUNKS = 6


START = (0, 0, 0, 0)
RING = 4
SPAN = RING - 1 + 3
BESIDE = (None, None, None)


def chunk_of(ref, part, k):
    size = ref.shape[0 if part else 1] // CHUNKS
    at = pl.ds(pl.multiple_of(k * size, size), size)
    return ref.at[at, :] if part else ref.at[:, at]


def ring_place(chip):
    return 2 * (chip // 2) + (chip % 2 + chip // 2) % 2


def ring_chip(place):
    return 2 * (place // 2) + (place % 2 + place // 2) % 2


CLOCKWISE = ((True, False), (True, False), (False, True), (True, False))


def forward_kernel(*refs):
    (w_in, w_out, h0, pars, b_in, b_out, cos0, sin0, cos2, sin2, seg_col, seg_m, seg_t) = refs[:13]
    keep = [refs[13 + 4 * s : 17 + 4 * s] for s in range(4)]
    acts, slopes = refs[29:31], refs[31:33]
    qkvs, kv_ts, os, lses = refs[33:35], refs[35:37], refs[37:39], refs[39:41]
    nrms, hs = refs[41:45], [refs[45].at[s] for s in range(4)]
    held = [refs[46 + 4 * s : 50 + 4 * s] for s in range(4)]
    acc, stage_a, stage_s, lse_scr = refs[62:66]
    own_sem, ring_s, ring_r, z_s, z_r, core_s, core_r, kv_sem, save_sem, stage_sem = refs[66:]
    c = lax.axis_index("section")
    g = lax.axis_index("group")
    z = lax.axis_index("dp")
    parity = z % 2
    place = ring_place(c)
    ahead, behind = ring_chip((place + 1) % 4), ring_chip((place + 3) % 4)
    partner = {"group": 1 - g}
    tokens = h0.shape[0]

    def remote(src, dst, ssem, rsem, device):
        return pltpu.make_async_remote_copy(
            src_ref=src, dst_ref=dst, send_sem=ssem, recv_sem=rsem, device_id=device,
            device_id_type=MESH,
        )

    barrier = pltpu.get_barrier_semaphore()
    pl.semaphore_signal(barrier, inc=1, device_id=partner, device_id_type=MESH)
    pl.semaphore_signal(barrier, inc=1, device_id={"section": ahead}, device_id_type=MESH)
    pl.semaphore_signal(barrier, inc=1, device_id={"section": behind}, device_id_type=MESH)
    pl.semaphore_signal(barrier, inc=1, device_id={"dp": z + 1 - 2 * parity}, device_id_type=MESH)
    pl.semaphore_wait(barrier, 4)

    def mine(s, part):
        return held[s][2 * part]

    def theirs(s, part):
        return held[s][2 * part + 1]

    def distance(s, part):
        d = place - ring_place(s)
        return (d + 4) % 4 if CLOCKWISE[s][part] else (4 - d) % 4

    def own_copies(s):
        first = pltpu.make_async_copy(
            w_in.at[:, : QKV] if s % 2 == 0 else w_in, mine(s, 0), own_sem.at[0]
        )
        source = w_out.at[:HALF, :] if s % 2 == 0 else w_out
        second = pltpu.make_async_copy(source, mine(s, 1), own_sem.at[1])
        over = remote(w_out.at[HALF:D, :], mine(s, 1), own_sem.at[2], own_sem.at[3], partner)
        return first, second, over

    for s in range(4):

        @pl.when(c == s)
        def _(s=s):
            first, second, over = own_copies(s)
            first.start()
            if s % 2:
                second.start()
            else:

                @pl.when(g == 0)
                def _():
                    second.start()
                    over.start()

    for s in range(4):

        @pl.when(c == s)
        def _(s=s):
            first, second, over = own_copies(s)
            first.wait()
            if s % 2:
                second.wait()
            else:

                @pl.when(g == 0)
                def _():
                    second.wait()
                    over.wait_send()

                @pl.when(g == 1)
                def _():
                    over.wait_recv()

    def ring_copy(s, part, k):
        ref = chunk_of(mine(s, part), part, jnp.where(k < 2, 2 * parity + k, k + 2))
        target = ahead if CLOCKWISE[s][part] else behind
        u = 2 * s + part
        return remote(ref, ref, ring_s.at[u, k], ring_r.at[u, k], {"section": target})

    def z_copy(s, part, j, sending):
        ref = chunk_of(mine(s, part), part, 2 * (parity if sending else 1 - parity) + j)
        u = 2 * s + part
        return remote(ref, ref, z_s.at[u, j], z_r.at[u, j], {"dp": z + 1 - 2 * parity})

    def core_copy(s, part, k):
        u = 2 * s + part
        return remote(
            chunk_of(mine(s, part), part, k), chunk_of(theirs(s, part), part, k),
            core_s.at[u, k], core_r.at[u, k], partner,
        )

    def event(s, part, k):
        p = distance(s, part)
        copy = ring_copy(s, part, k)
        pl.when(p > 0)(copy.wait_recv)
        pl.when(p < 3)(copy.start)

        @pl.when((k < 2) & (p > 0))
        def _():
            z_copy(s, part, jnp.minimum(k, 1), True).start()

        core_copy(s, part, jnp.where(k < 2, 2 * parity + k, k + 2)).start()

        @pl.when(k >= 2)
        def _():
            j = jnp.maximum(k - 2, 0)
            pl.when(p > 0)(z_copy(s, part, j, False).wait_recv)
            core_copy(s, part, 2 * (1 - parity) + j).start()

    def slot(t, first, last):
        for s in range(4):
            if START[s] <= last and first <= START[s] + SPAN:
                for part in range(2):
                    k = t - START[s] - distance(s, part)

                    @pl.when((k >= 0) & (k < RING))
                    def _(s=s, part=part, k=k):
                        event(s, part, jnp.clip(k, 0, RING - 1))

    def slots(first, last):
        loop(last - first + 1, lambda i: slot(first + i, first, last))

    def arrived(s):
        def one(k):
            core_copy(s, 0, k).wait_recv()
            core_copy(s, 1, k).wait_recv()

        loop(CHUNKS, one)
        for i in range(4):
            pltpu.make_async_copy(held[s][i], keep[s][i], save_sem.at[4 * s + i]).start()

    def normed(s, h):
        xhat, _ = normalize(h[...].astype(F32))
        nrms[s][...] = turn_halves(
            xhat * pars[s, 0:1, :] + pars[s, 1:2, :], g
        ).astype(BF)

    def project(s, first, width):
        cols = pl.ds(first, width)
        return (
            dot(nrms[s][:, :HALF], mine(s, 0)[:, cols])
            + dot(nrms[s][:, HALF:], theirs(s, 0)[:, cols])
            + b_in[s, 0:1, cols]
        )

    def attention(s, h, out, beside):
        layer = s // 2
        qkv, kv_t, o_ref = qkvs[layer], kv_ts[layer], os[layer]
        cosines, sines = ((cos0, sin0), (cos2, sin2))[layer]
        normed(s, h)
        exchange = []
        for j in (1, 2, 0):
            x = project(s, j * D, D)
            if j < 2:
                x = x * cosines[...] + swap_pairs(x) * sines[...]
            if j == 0:
                x = x * HD ** (-0.5)
            qkv[:, j * D : (j + 1) * D] = x.astype(BF)
            if j:
                copy = remote(
                    qkv.at[:, j * D : (j + 1) * D], kv_t.at[:, (j - 1) * D : j * D],
                    kv_sem.at[0, 2 * layer + j - 1], kv_sem.at[1, 2 * layer + j - 1], partner,
                )
                copy.start()
                exchange.append(copy)
        for copy in exchange:
            copy.wait()
        lanes = lax.broadcasted_iota(jnp.int32, (tokens, 2 * HD), 1)

        def pair(j):
            if beside is not None:
                pl.when(beside[0] + j <= beside[1])(lambda: slot(beside[0] + j, *beside))

            def columns(ref, first):
                return ref[:, pl.ds(pl.multiple_of(first + j * 2 * HD, 2 * HD), 2 * HD)]

            q = columns(qkv, 0)
            km, vm = columns(qkv, D), columns(qkv, 2 * D)
            kt, vt = columns(kv_t, 0), columns(kv_t, D)
            same_m = seg_col[...] == seg_m[...]
            same_t = seg_col[...] == seg_t[...]
            found = []
            for side in range(2):
                head = (lanes >= HD) if side else (lanes < HD)
                q_head = jnp.where(head, q, jnp.zeros_like(q))
                s_m = jnp.where(same_m, dot_nt(q_head, km), -1e9)
                s_t = jnp.where(same_t, dot_nt(q_head, kt), -1e9)
                top = jnp.maximum(
                    jnp.max(s_m, axis=-1, keepdims=True), jnp.max(s_t, axis=-1, keepdims=True)
                )
                p_m = jnp.exp(s_m - top)
                p_t = jnp.exp(s_t - top)
                total = jnp.sum(p_m, axis=-1, keepdims=True) + jnp.sum(
                    p_t, axis=-1, keepdims=True
                )
                o = dot(p_m.astype(BF), vm) + dot(p_t.astype(BF), vt)
                found.append(o / total)
                lse_scr[...] = jnp.where(
                    lanes == 2 * j + side, top + jnp.log(total), lse_scr[...]
                )
            o_ref[:, pl.ds(pl.multiple_of(j * 2 * HD, 2 * HD), 2 * HD)] = jnp.where(
                lanes < HD, found[0], found[1]
            ).astype(BF)

        loop(PAIRS, pair)
        lses[layer][...] = jnp.transpose(lse_scr[...])[:16, :]
        turned = turn_halves(o_ref[...].astype(F32), g).astype(BF)
        y = dot(turned[:, :HALF], mine(s, 1)[...]) + dot(turned[:, HALF:], theirs(s, 1)[...])
        out[...] = (h[...].astype(F32) + y + b_out[s, 0:1, :]).astype(BF)

    def feed(s, h, out, beside):
        layer = s // 2
        width = FF // CHUNKS
        normed(s, h)
        acc[...] = h[...].astype(F32) + b_out[s, 0:1, :]

        def staged(j, i):
            turn = j % 2
            cols = pl.ds(pl.multiple_of(j * width, width), width)
            source, target = ((stage_a, acts[layer]), (stage_s, slopes[layer]))[i]
            return pltpu.make_async_copy(source.at[turn], target.at[:, cols], stage_sem.at[i, turn])

        def block(j):
            if beside is not None:
                pl.when(beside[0] + j <= beside[1])(lambda: slot(beside[0] + j, *beside))
            turn = j % 2

            @pl.when(j >= 2)
            def _():
                staged(j - 2, 0).wait()
                staged(j - 2, 1).wait()

            b = (j + g * (CHUNKS // 2)) % CHUNKS
            u = project(s, pl.multiple_of(b * width, width), width)
            cdf = 0.5 + 0.5 * lax.erf(u * (0.5**0.5))
            act = (u * cdf).astype(BF)
            stage_a[turn] = act
            pdf = jnp.exp(u * u * -0.5) * 0.3989422804014327
            stage_s[turn] = (cdf + u * pdf).astype(BF)
            staged(j, 0).start()
            staged(j, 1).start()
            for half in range(2):

                @pl.when(j // (CHUNKS // 2) == half)
                def _(half=half):
                    rows = pl.ds(pl.multiple_of((j % (CHUNKS // 2)) * width, width), width)
                    acc[...] += dot(act, held[s][2 + half][rows, :])

        loop(CHUNKS, block)
        for j in (CHUNKS - 2, CHUNKS - 1):
            staged(j, 0).wait()
            staged(j, 1).wait()
        out[...] = acc[...].astype(BF)

    slots(0, START[0] + SPAN)
    arrived(0)
    attention(0, h0, hs[0], BESIDE[0])
    arrived(1)
    feed(1, hs[0], hs[1], BESIDE[1])
    arrived(2)
    attention(2, hs[1], hs[2], BESIDE[2])
    arrived(3)
    feed(3, hs[2], hs[3], None)

    for s in range(4):
        for part in range(2):
            p = distance(s, part)

            def sent_out(k, s=s, part=part, p=p):
                core_copy(s, part, k).wait_send()
                pl.when((k < 4) & (p < 3))(ring_copy(s, part, jnp.minimum(k, 3)).wait_send)
                pl.when((k < 2) & (p > 0))(z_copy(s, part, jnp.minimum(k, 1), True).wait_send)

            loop(CHUNKS, sent_out)
        for i in range(4):
            pltpu.make_async_copy(held[s][i], keep[s][i], save_sem.at[4 * s + i]).wait()


def forward_call(w_in, w_out, h, pars, b_in, b_out, turns, seg_col, seg_m, seg_t):
    t = h.shape[0]
    hbm = pl.BlockSpec(memory_space=pl.ANY)
    vmem = pl.BlockSpec(memory_space=pltpu.VMEM)
    weights = []
    for s in range(4):
        (a, b), (d, e) = unit_shape(s, 0), unit_shape(s, 1)
        weights += [(a, b), (a, b), (d, e), (d, e)]
    rows = sds((t, D), BF)
    out_shape = (
        [sds(w, BF) for w in weights]
        + [sds((t, FF), BF)] * 4
        + [sds((t, QKV), BF)] * 2
        + [sds((t, 2 * D), BF)] * 2
        + [rows] * 2
        + [sds((16, t), F32)] * 2
        + [rows] * 4
        + [sds((4, t, D), BF)]
    )
    dma = pltpu.SemaphoreType.DMA
    scratch = [pltpu.VMEM(w, BF) for w in weights] + [
        pltpu.VMEM((t, D), F32),
        pltpu.VMEM((2, t, FF // CHUNKS), BF),
        pltpu.VMEM((2, t, FF // CHUNKS), BF),
        pltpu.VMEM((t, 2 * HD), F32),
        dma((4,)), dma((8, 4)), dma((8, 4)), dma((8, 2)), dma((8, 2)), dma((8, 6)), dma((8, 6)),
        dma((2, 4)), dma((16,)), dma((2, 2)),
    ]
    out = pl.pallas_call(
        forward_kernel,
        out_shape=out_shape,
        in_specs=[hbm, hbm] + [vmem] * 11,
        out_specs=[hbm] * 20 + [vmem] * 13,
        scratch_shapes=scratch,
        compiler_params=pltpu.CompilerParams(
            collective_id=2, has_side_effects=True, vmem_limit_bytes=63 * 1024 * 1024
        ),
        name="forward",
    )(w_in, w_out, h, pars, b_in, b_out, *turns[0], *turns[1], seg_col, seg_m, seg_t)
    weights = [out[4 * s : 4 * s + 4] for s in range(4)]
    acts, slopes, qkvs, kv_ts, os, lses = (out[16 + 2 * i : 18 + 2 * i] for i in range(6))
    nrms, hs = out[28:32], out[32]
    saved = []
    for s in range(4):
        i = s // 2
        if s % 2 == 0:
            saved.append((qkvs[i], nrms[s], kv_ts[i], os[i], lses[i]))
        else:
            saved.append((acts[i], slopes[i], nrms[s]))
    return weights, saved, hs


def small_row(dbin, rest, attends):
    dbin = jnp.pad(dbin.reshape(-1), (0, FF - dbin.size))
    dfreq = rest[3:5].reshape(2, HEADS, HD)[:, :, : HD // 2].reshape(-1)
    if not attends:
        dfreq = jnp.zeros_like(dfreq)
    return jnp.concatenate([dbin, rest[:3].reshape(-1), dfreq])


def carried_passes(weight_in, weight_out, h, g, pars, b_in, b_out, turns, pos, seg_m, seg_t):
    section, core = lax.axis_index("section"), lax.axis_index("group")
    weights, saved, streams = forward_call(
        weight_in[0], weight_out[0], h, jnp.stack(pars), b_in, b_out, turns,
        seg_m[:, None], seg_m[None], seg_t[None],
    )
    smalls, grads, in_grads = [None] * 4, [None] * 4, [None] * 4
    rows = (seg_m[None], seg_m[:, None], seg_t[:, None])

    def feed_back(s, g, carry, carried):
        act, slope, nrm = saved[s]
        grads[s], results, (dbin, rest, in_grads[s]) = feed_back_call(
            s, weights[s], act, slope, streams, g, nrm, pars[s], carry, carried, 3 + s
        )
        smalls[s] = small_row(dbin, rest, False)
        return results

    def attention_back(s, g, carry, carried):
        grads[s], results, (dbin, rest, in_grads[s]) = attention_back_call(
            s, weights[s], carry, carried, g, saved[s], *rows, turns[s // 2], pos,
            streams[s - 1] if s else h, pars[s], 3 + s,
        )
        smalls[s] = small_row(dbin, rest, True)
        return results

    (outputs,) = feed_back(3, g, None, ())
    quarters3 = attention_back(2, in_grads[3], Carry(3, (), ()), grads[3])
    *quarters2, first3, second3 = feed_back(
        1, in_grads[2], Carry(2, ((3, 0), (3, 1)), ()), (*grads[2], *quarters3)
    )
    *quarters1, first2, second2, held3 = attention_back(
        0, in_grads[1], Carry(1, ((2, 0), (2, 1)), ((3, 0),)), (*grads[1], *quarters2, first3)
    )
    sums, input_grads, small_sum = last_call(
        (*grads[0], *quarters1, second3, first2, second2), in_grads,
        jnp.stack(smalls).reshape(4, SMALL, 128),
    )
    first_a, second_a, first_f, second_f = sums
    second_a = in_place(second_a)
    in_a = jnp.concatenate([in_place(first_a), second_a[:HALF]], axis=1)
    both = jnp.concatenate([second_a[HALF:], flipped(second_a[HALF:], "group", 1)], axis=0)
    both = jnp.where(core == 0, jnp.pad(both, ((0, FF // 2 - D), (0, 0))), jnp.zeros((), BF))
    attends = section % 2 == 0
    in_f = in_place(jnp.where(section == 3, held3, first_f))
    out_in = jnp.where(attends, jnp.pad(in_a, ((0, 0), (0, FF - QKV))), in_f).astype(F32)
    out_out = jnp.where(attends, both, in_place(second_f)).astype(F32)
    return outputs.reshape(-1, D), input_grads, out_in, out_out, small_sum.reshape(-1)


def plain_passes(weight_in, weight_out, h, g, pars, b_in, b_out, turns, pos, seg_m, seg_t):
    section, group = lax.axis_index("section"), lax.axis_index("group")
    groups = lax.axis_size("group")
    core = group % 2
    rot = jnp.zeros((1,), jnp.int32)
    all_in = lax.all_gather(weight_in, "group", axis=1, tiled=True)
    all_out = lax.all_gather(weight_out, "group", axis=1, tiled=True)
    all_in = lax.all_gather(all_in, "section", axis=0, tiled=True)
    all_out = lax.all_gather(all_out, "section", axis=0, tiled=True)
    weights, saved, streams = [], [], [h]
    for s in range(4):
        cols, rows = (QKV, D) if s % 2 == 0 else (FF, FF)
        w_in, w_out = all_in[s, :, :cols], all_out[s, :rows]
        weights.append((w_in[:HALF], w_in[HALF:], w_out[: rows // 2], w_out[rows // 2 :]))
        wia, wib, woa, wob = weights[s]
        if s % 2 == 0:
            cosines, sines = turns[s // 2]
            qkv, nrm = qkv_call(rot, h, pars[s], wia, wib, b_in[s, :, :QKV], cosines, sines)
            kv_t = flipped(qkv[:, D:], "group", 1)
            o, lse, h = attend_call(
                rot, qkv, kv_t, seg_m[:, None], seg_m[None], seg_t[None], h, woa, wob, b_out[s]
            )
            saved.append((qkv, nrm, kv_t, o, lse))
        else:
            act, slope, nrm, h = ff_call(rot, h, pars[s], wia, wib, b_in[s], woa, wob, b_out[s])
            saved.append((act, slope, nrm))
        streams.append(h)
    outputs = to_owners(streams[1:], section, core)
    smalls, grads, in_grads = [None] * 4, [None] * 4, [None] * 4
    for s in (3, 2, 1, 0):
        wia, wib, woa, wob = weights[s]
        if s % 2 == 0:
            qkv, nrm, kv_t, o, lse = saved[s]
            cosines, sines = turns[s // 2]
            dmix, delta, doa, dob = mix_back_call(rot, g, o, woa, wob)
            dq, dkm, dvm, dkt, dvt = attend_back_call(
                qkv, kv_t, dmix, lse, delta, seg_m[None], seg_m[:, None], seg_t[:, None]
            )
            dkr, dvr = flipped(dkt, "group", 1), flipped(dvt, "group", 1)
            dia, dib, dbin, rest, g = qkv_back_call(
                rot, dq, dkm, dvm, dkr, dvr, qkv, cosines, sines, pos, nrm, wia, wib,
                streams[s], pars[s], g,
            )
        else:
            act, slope, nrm = saved[s]
            dia, dib, doa, dob, dbin, rest, g = ff_back_call(
                rot, g, act, slope, nrm, wia, wib, woa, wob, streams[s], pars[s]
            )
        in_grads[s] = g
        grads[s] = (
            jnp.pad(jnp.concatenate([dia, dib]), ((0, 0), (0, FF - dia.shape[1]))),
            jnp.pad(jnp.concatenate([doa, dob]), ((0, FF - 2 * doa.shape[0]), (0, 0))),
        )
        smalls[s] = small_row(dbin, rest, s % 2 == 0)
    input_grads = to_owners(in_grads, section, core)
    small_sum = lax.psum(jnp.stack(smalls), ("section", "group", "dp"))[section]

    def owned(x):
        x = lax.psum_scatter(x, "section", scatter_dimension=0, tiled=True)[0]
        x = lax.psum_scatter(x, "group", scatter_dimension=0, tiled=True)
        return lax.psum(x, "dp").astype(F32)

    out_in = owned(jnp.stack([x[0] for x in grads]))
    out_out = owned(jnp.stack([x[1] for x in grads]))
    return outputs, input_grads, out_in, out_out, small_sum


def body(
    activations, weight_in, weight_out, bias_in, bias_out, norm_gain, norm_shift, rope_freq,
    image_sides, cotangent,
):
    sections = lax.axis_size("section")
    groups = lax.axis_size("group")
    section = lax.axis_index("section")
    group = lax.axis_index("group")
    core = group % 2
    micro = image_sides.shape[0]
    capacity = activations.shape[0] // micro
    tokens = capacity // 2
    assert sections == 4 and groups % 2 == 0 and 2 * micro == sections
    fast = groups == 2 and lax.axis_size("dp") == 4

    here = (section // 2) == core
    local = section % 2

    def take(x):
        own = lax.dynamic_index_in_dim(x.reshape(micro, capacity, D), local, 0, keepdims=False)
        give = lax.dynamic_slice_in_dim(own, (1 - core) * tokens, tokens, 0)
        keep = lax.dynamic_slice_in_dim(own, core * tokens, tokens, 0)
        return jnp.where(here, keep, flipped(give, "group", 1))

    h = take(activations)
    own_sides = lax.dynamic_index_in_dim(image_sides, local, 0, keepdims=False)
    sides = jnp.where(here, own_sides, flipped(own_sides, "group", 1))
    segment, patch_row, patch_col, is_valid = layout(sides, capacity)
    pos_all = jnp.stack([patch_col, patch_row], axis=1).astype(F32)

    def half_of(x, which):
        return lax.dynamic_slice_in_dim(x, which * tokens, tokens, 0)

    pos = half_of(pos_all, core)
    seg_m, seg_t = half_of(segment, core), half_of(segment, 1 - core)
    valid = half_of(is_valid, core)
    g = take(cotangent) * valid[:, None].astype(BF)

    small = jnp.concatenate(
        [bias_in[0], bias_out[0], norm_gain[0], norm_shift[0], rope_freq[0].reshape(-1)]
    )
    small = lax.all_gather(small, ("section", "group")).reshape(4, groups, -1).astype(F32)
    widths = [FF // groups, D // groups, D // groups, D // groups, D // groups]
    starts = [sum(widths[:i]) for i in range(5)]
    b_in, b_out, gain, shift, freq = (
        small[:, :, a : a + w] for a, w in zip(starts, widths)
    )
    b_in, b_out, gain, shift = (x.reshape(4, 1, -1) for x in (b_in, b_out, gain, shift))
    freq = freq.reshape(4, groups, 2, -1).transpose(0, 2, 1, 3).reshape(4, 2, D // 2)
    pars = [
        jnp.concatenate([gain[s], shift[s], jnp.zeros((6, D), F32)], axis=0) for s in range(4)
    ]
    turns = [turning(freq[s], pos) for s in (0, 2)]

    if fast:
        outputs, input_grads, out_in, out_out, small_sum = carried_passes(
            weight_in, weight_out, h, g, pars, b_in, b_out, turns, pos, seg_m, seg_t
        )
    else:
        outputs, input_grads, out_in, out_out, small_sum = plain_passes(
            weight_in, weight_out, h, g, pars, b_in, b_out, turns, pos, seg_m, seg_t
        )

    def piece(start, width):
        w = width // groups
        return lax.dynamic_slice_in_dim(small_sum, start + group * w, w, 0)[None]

    d_freq = small_sum[FF + 3 * D :].reshape(2, D // 2)
    d_freq = lax.dynamic_slice_in_dim(d_freq, group * (D // 2 // groups), D // 2 // groups, 1)
    return (
        outputs[None],
        input_grads[None],
        out_in[None],
        out_out[None],
        piece(0, FF),
        piece(FF, D),
        piece(FF + D, D),
        piece(FF + 2 * D, D),
        d_freq[None],
    )


def solution(mesh):
    placed = (
        P(("group", "dp"), None),
        P("section", "group", None),
        P("section", "group", None),
        P("section", "group"),
        P("section", "group"),
        P("section", "group"),
        P("section", "group"),
        P("section", None, "group"),
        P(("group", "dp"), None),
        P(("group", "dp"), None),
    )
    return jax.shard_map(
        body,
        mesh=mesh,
        in_specs=placed,
        out_specs=(
            P("section", ("group", "dp"), None),
            P("section", ("group", "dp"), None),
            P("section", "group", None),
            P("section", "group", None),
            P("section", "group"),
            P("section", "group"),
            P("section", "group"),
            P("section", "group"),
            P("section", None, "group"),
        ),
        check_vma=False,
    )
```

```python
from functools import partial

import jax
import jax.numpy as jnp
from jax import lax
from jax.experimental import pallas as pl
from jax.experimental.pallas import tpu as pltpu
from jax.sharding import PartitionSpec as P

D = 768
HEADS = 12
HD = 64
FF = 3072
HALF = D // 2
PAIRS = HEADS // 2
QKV = 3 * D
EPSILON = 1e-06
BF = jnp.bfloat16
F32 = jnp.float32
NT = (((1,), (1,)), ((), ()))
TN = (((0,), (0,)), ((), ()))
VMEM_BYTES = 52 * 1024 * 1024


def dot(a, b):
    return jnp.dot(a, b, preferred_element_type=F32)


def dot_nt(a, b):
    return lax.dot_general(a, b, NT, preferred_element_type=F32)


def dot_tn(a, b):
    return lax.dot_general(a, b, TN, preferred_element_type=F32)


def normalize(h):
    average = jnp.mean(h, axis=-1, keepdims=True)
    centered = h - average
    variance = jnp.mean(centered * centered, axis=-1, keepdims=True)
    scale = lax.rsqrt(variance + EPSILON)
    return centered * scale, scale


def turn_halves(x, rot):
    return jnp.where(rot == 0, x, jnp.concatenate([x[:, HALF:], x[:, :HALF]], axis=1))


def swap_pairs(x):
    lanes = lax.broadcasted_iota(jnp.int32, x.shape, 1)
    low = (lanes % HD) < HD // 2
    return jnp.where(
        low, pltpu.roll(x, x.shape[1] - HD // 2, 1), pltpu.roll(x, HD // 2, 1)
    )


def norm_backward(h, gain, grad, d_normed):
    xhat, scale = normalize(h)
    e = d_normed * gain
    mean_e = jnp.mean(e, axis=-1, keepdims=True)
    mean_ex = jnp.mean(e * xhat, axis=-1, keepdims=True)
    g = grad + scale * (e - mean_e - xhat * mean_ex)
    d_gain = jnp.sum(d_normed * xhat, axis=0, keepdims=True)
    d_shift = jnp.sum(d_normed, axis=0, keepdims=True)
    return g, d_gain, d_shift


def qkv_kernel(rot_ref, h_ref, par_ref, wa_ref, wb_ref, bias_ref, cos_ref, sin_ref, out_ref, nrm_ref):
    j = pl.program_id(0)

    @pl.when(j == 0)
    def _():
        xhat, _ = normalize(h_ref[...].astype(F32))
        normed = xhat * par_ref[0:1, :] + par_ref[1:2, :]
        nrm_ref[...] = turn_halves(normed, rot_ref[0]).astype(BF)

    x = dot(nrm_ref[:, :HALF], wa_ref[...]) + dot(nrm_ref[:, HALF:], wb_ref[...]) + bias_ref[...]

    @pl.when(j < 2)
    def _():
        y = x * cos_ref[...] + swap_pairs(x) * sin_ref[...]
        out_ref[...] = (y * jnp.where(j == 0, HD ** (-0.5), 1.0)).astype(BF)

    @pl.when(j == 2)
    def _():
        out_ref[...] = x.astype(BF)


def attend_kernel(
    rot_ref, q_ref, km_ref, vm_ref, kt_ref, vt_ref, segq_ref, segm_ref, segt_ref, h_ref,
    woa_ref, wob_ref, bias_ref, o_ref, lse_ref, out_ref, lse_scr,
):
    j = pl.program_id(0)
    rows = q_ref.shape[0]
    lanes = lax.broadcasted_iota(jnp.int32, (rows, 2 * HD), 1)
    q = q_ref[...]
    same_m = segq_ref[...] == segm_ref[...]
    same_t = segq_ref[...] == segt_ref[...]
    outs = []
    for side in range(2):
        mine = (lanes >= HD) if side else (lanes < HD)
        q_head = jnp.where(mine, q, jnp.zeros_like(q))
        s_m = jnp.where(same_m, dot_nt(q_head, km_ref[...]), -1e9)
        s_t = jnp.where(same_t, dot_nt(q_head, kt_ref[...]), -1e9)
        top = jnp.maximum(
            jnp.max(s_m, axis=-1, keepdims=True), jnp.max(s_t, axis=-1, keepdims=True)
        )
        p_m = jnp.exp(s_m - top)
        p_t = jnp.exp(s_t - top)
        total = jnp.sum(p_m, axis=-1, keepdims=True) + jnp.sum(p_t, axis=-1, keepdims=True)
        o = dot(p_m.astype(BF), vm_ref[...]) + dot(p_t.astype(BF), vt_ref[...])
        outs.append(o / total)
        lse_scr[...] = jnp.where(lanes == 2 * j + side, top + jnp.log(total), lse_scr[...])
    o_ref[:, pl.ds(pl.multiple_of(j * 2 * HD, 2 * HD), 2 * HD)] = jnp.where(
        lanes < HD, outs[0], outs[1]
    ).astype(BF)

    @pl.when(j == PAIRS - 1)
    def _():
        lse_ref[...] = jnp.transpose(lse_scr[...])[:16, :]
        o_all = turn_halves(o_ref[...].astype(F32), rot_ref[0]).astype(BF)
        y = dot(o_all[:, :HALF], woa_ref[...]) + dot(o_all[:, HALF:], wob_ref[...])
        out_ref[...] = (h_ref[...].astype(F32) + y + bias_ref[...]).astype(BF)


def ff_kernel(
    rot_ref, h_ref, par_ref, wia_ref, wib_ref, bias_ref, woa_ref, wob_ref, bout_ref,
    act_ref, slope_ref, nrm_ref, out_ref, acc_ref,
):
    j = pl.program_id(0)
    n = pl.num_programs(0)

    @pl.when(j == 0)
    def _():
        xhat, _ = normalize(h_ref[...].astype(F32))
        normed = xhat * par_ref[0:1, :] + par_ref[1:2, :]
        nrm_ref[...] = turn_halves(normed, rot_ref[0]).astype(BF)
        acc_ref[...] = h_ref[...].astype(F32) + bout_ref[...]

    u = dot(nrm_ref[:, :HALF], wia_ref[...]) + dot(nrm_ref[:, HALF:], wib_ref[...]) + bias_ref[...]
    cdf = 0.5 + 0.5 * lax.erf(u * (0.5**0.5))
    act = (u * cdf).astype(BF)
    act_ref[...] = act
    pdf = jnp.exp(u * u * -0.5) * 0.3989422804014327
    slope_ref[...] = (cdf + u * pdf).astype(BF)

    @pl.when(j < n // 2)
    def _():
        acc_ref[...] += dot(act, woa_ref[...])

    @pl.when(j >= n // 2)
    def _():
        acc_ref[...] += dot(act, wob_ref[...])

    @pl.when(j == n - 1)
    def _():
        out_ref[...] = acc_ref[...].astype(BF)


def ff_back_kernel(
    rot_ref, g_ref, act_ref, slope_ref, nrm_ref, wia_ref, wib_ref, woa_ref, wob_ref, h_ref, par_ref,
    dia_ref, dib_ref, doa_ref, dob_ref, dbin_ref, small_ref, out_ref, acc_ref,
):
    j = pl.program_id(0)
    n = pl.num_programs(0)

    @pl.when(j == 0)
    def _():
        acc_ref[...] = jnp.zeros_like(acc_ref)

    def step(wo_ref, do_ref):
        g = g_ref[...]
        d_up_f = dot_nt(g, wo_ref[...]) * slope_ref[...].astype(F32)
        d_up = d_up_f.astype(BF)
        do_ref[...] = dot_tn(act_ref[...], g).astype(BF)
        dbin_ref[...] = jnp.sum(d_up_f, axis=0, keepdims=True)
        dia_ref[...] = dot_tn(nrm_ref[:, :HALF], d_up).astype(BF)
        dib_ref[...] = dot_tn(nrm_ref[:, HALF:], d_up).astype(BF)
        acc_ref[:, :HALF] += dot_nt(d_up, wia_ref[...])
        acc_ref[:, HALF:] += dot_nt(d_up, wib_ref[...])

    @pl.when(j < n // 2)
    def _():
        step(woa_ref, doa_ref)

    @pl.when(j >= n // 2)
    def _():
        step(wob_ref, dob_ref)

    @pl.when(j == n - 1)
    def _():
        g = g_ref[...].astype(F32)
        d_normed = turn_halves(acc_ref[...], rot_ref[0])
        out, d_gain, d_shift = norm_backward(h_ref[...].astype(F32), par_ref[0:1, :], g, d_normed)
        out_ref[...] = out.astype(BF)
        small_ref[0:1, :] = jnp.sum(g, axis=0, keepdims=True)
        small_ref[1:2, :] = d_gain
        small_ref[2:3, :] = d_shift
        small_ref[3:8, :] = jnp.zeros((5, D), F32)


def mix_back_kernel(rot_ref, g_ref, o_ref, woa_ref, wob_ref, dmix_ref, delta_ref, doa_ref, dob_ref):
    g = g_ref[...]
    rot = rot_ref[0]
    d_mix = jnp.concatenate([dot_nt(g, woa_ref[...]), dot_nt(g, wob_ref[...])], axis=1)
    d_mix = turn_halves(d_mix, rot).astype(BF)
    dmix_ref[...] = d_mix
    o = o_ref[...].astype(F32)
    product = d_mix.astype(F32) * o
    head = lax.broadcasted_iota(jnp.int32, (16, D), 0)
    lanes = lax.broadcasted_iota(jnp.int32, (16, D), 1)
    chosen = jnp.where(lanes // HD == head, 1.0, 0.0)
    delta_ref[...] = lax.dot_general(
        chosen, product, NT, preferred_element_type=F32, precision=lax.Precision.HIGHEST
    )
    turned = turn_halves(o, rot).astype(BF)
    doa_ref[...] = dot_tn(turned[:, :HALF], g).astype(BF)
    dob_ref[...] = dot_tn(turned[:, HALF:], g).astype(BF)


def attend_back_kernel(
    q_ref, km_ref, vm_ref, kt_ref, vt_ref, do_ref, lse_ref, delta_ref, segq_ref, segm_ref, segt_ref,
    dq_ref, dkm_ref, dvm_ref, dkt_ref, dvt_ref,
):
    j = pl.program_id(0)
    rows = q_ref.shape[0]
    lanes = lax.broadcasted_iota(jnp.int32, (rows, 2 * HD), 1)
    q = q_ref[...]
    do = do_ref[...]
    zero = jnp.zeros_like(q)
    d_q = jnp.zeros((rows, 2 * HD), F32)
    sets = ((km_ref, vm_ref, segm_ref), (kt_ref, vt_ref, segt_ref))
    d_k = [0.0, 0.0]
    d_v = [0.0, 0.0]
    for side in range(2):
        mine = (lanes >= HD) if side else (lanes < HD)
        q_head = jnp.where(mine, q, zero)
        do_head = jnp.where(mine, do, zero)
        lse = lse_ref[pl.ds(2 * j + side, 1), :]
        delta = delta_ref[pl.ds(2 * j + side, 1), :]
        for i, (k_ref, v_ref, seg_ref) in enumerate(sets):
            k = k_ref[...]
            s_t = dot_nt(k, q_head)
            p_t = jnp.where(seg_ref[...] == segq_ref[...], jnp.exp(s_t - lse), 0.0)
            d_p = dot_nt(v_ref[...], do_head)
            d_s = (p_t * (d_p - delta)).astype(BF)
            d_v[i] += dot(p_t.astype(BF), do_head)
            d_k[i] += dot(d_s, q_head)
            d_q += dot_tn(d_s, jnp.where(mine, k, zero))
    dq_ref[...] = d_q
    dkm_ref[...] = d_k[0]
    dvm_ref[...] = d_v[0]
    dkt_ref[...] = d_k[1].astype(BF)
    dvt_ref[...] = d_v[1].astype(BF)


def qkv_back_kernel(
    rot_ref, dq_ref, dkm_ref, dvm_ref, dkr_ref, dvr_ref, qkv_ref, cos_ref, sin_ref, pos_ref,
    nrm_ref, wa_ref, wb_ref, h_ref, par_ref, g_ref,
    dia_ref, dib_ref, dbin_ref, small_ref, out_ref, acc_ref, dp_ref,
):
    j = pl.program_id(0)
    n = pl.num_programs(0)

    @pl.when(j == 0)
    def _():
        acc_ref[...] = jnp.zeros_like(acc_ref)
        small_ref[...] = jnp.zeros_like(small_ref)

    def turned_back(dy, y):
        swapped = swap_pairs(dy)
        d_angle = y * swapped - swap_pairs(y) * dy
        small_ref[3:4, :] += jnp.sum(d_angle * pos_ref[:, 0:1], axis=0, keepdims=True)
        small_ref[4:5, :] += jnp.sum(d_angle * pos_ref[:, 1:2], axis=0, keepdims=True)
        return dy * cos_ref[...] - swapped * sin_ref[...]

    @pl.when(j == 0)
    def _():
        d_y = dq_ref[...] * HD ** (-0.5)
        y = qkv_ref[...].astype(F32) * HD**0.5
        dp_ref[...] = turned_back(d_y, y)

    @pl.when(j == 1)
    def _():
        d_y = dkm_ref[...] + dkr_ref[...].astype(F32)
        dp_ref[...] = turned_back(d_y, qkv_ref[...].astype(F32))

    @pl.when(j == 2)
    def _():
        dp_ref[...] = dvm_ref[...] + dvr_ref[...].astype(F32)

    d_f = dp_ref[...]
    d_p = d_f.astype(BF)
    dbin_ref[...] = jnp.sum(d_f, axis=0, keepdims=True)
    dia_ref[...] = dot_tn(nrm_ref[:, :HALF], d_p).astype(BF)
    dib_ref[...] = dot_tn(nrm_ref[:, HALF:], d_p).astype(BF)
    acc_ref[:, :HALF] += dot_nt(d_p, wa_ref[...])
    acc_ref[:, HALF:] += dot_nt(d_p, wb_ref[...])

    @pl.when(j == n - 1)
    def _():
        g = g_ref[...].astype(F32)
        d_normed = turn_halves(acc_ref[...], rot_ref[0])
        out, d_gain, d_shift = norm_backward(h_ref[...].astype(F32), par_ref[0:1, :], g, d_normed)
        out_ref[...] = out.astype(BF)
        small_ref[0:1, :] = jnp.sum(g, axis=0, keepdims=True)
        small_ref[1:2, :] = d_gain
        small_ref[2:3, :] = d_shift


def params_of(n=1):
    return pltpu.CompilerParams(
        dimension_semantics=("arbitrary",) * n, vmem_limit_bytes=VMEM_BYTES
    )


def whole(shape):
    return pl.BlockSpec(shape, lambda *_: (0,) * len(shape))


def sds(shape, dtype):
    return jax.ShapeDtypeStruct(shape, dtype)


def cost(flops, nbytes, trans=0):
    return pl.CostEstimate(flops=flops, bytes_accessed=nbytes, transcendentals=trans)


def qkv_call(rot, h, par, wa, wb, bias, cosines, sines):
    t = h.shape[0]
    return pl.pallas_call(
        qkv_kernel,
        out_shape=(sds((t, QKV), BF), sds((t, D), BF)),
        grid_spec=pltpu.PrefetchScalarGridSpec(
            num_scalar_prefetch=1,
            grid=(3,),
            in_specs=[
                whole((t, D)), whole((8, D)),
                pl.BlockSpec((HALF, D), lambda j, r: (0, j)),
                pl.BlockSpec((HALF, D), lambda j, r: (0, j)),
                pl.BlockSpec((1, D), lambda j, r: (0, j)),
                whole((t, D)), whole((t, D)),
            ],
            out_specs=[pl.BlockSpec((t, D), lambda j, r: (0, j)), whole((t, D))],
        ),
        compiler_params=params_of(),
        cost_estimate=cost(2 * t * D * QKV, 2 * D * QKV + 8 * t * D + 2 * t * QKV),
        name="qkv",
    )(rot, h, par, wa, wb, bias, cosines, sines)


def attend_call(rot, qkv, kv_t, seg_col, seg_m, seg_t, h, woa, wob, bias):
    t = h.shape[0]
    w = 2 * HD
    return pl.pallas_call(
        attend_kernel,
        out_shape=(sds((t, D), BF), sds((16, t), F32), sds((t, D), BF)),
        grid_spec=pltpu.PrefetchScalarGridSpec(
            num_scalar_prefetch=1,
            grid=(PAIRS,),
            in_specs=[
                pl.BlockSpec((t, w), lambda j, r: (0, j)),
                pl.BlockSpec((t, w), lambda j, r: (0, j + PAIRS)),
                pl.BlockSpec((t, w), lambda j, r: (0, j + 2 * PAIRS)),
                pl.BlockSpec((t, w), lambda j, r: (0, j)),
                pl.BlockSpec((t, w), lambda j, r: (0, j + PAIRS)),
                whole((t, 1)), whole((1, t)), whole((1, t)), whole((t, D)),
                whole((HALF, D)), whole((HALF, D)), whole((1, D)),
            ],
            out_specs=[whole((t, D)), whole((16, t)), whole((t, D))],
            scratch_shapes=[pltpu.VMEM((t, w), F32)],
        ),
        compiler_params=params_of(),
        cost_estimate=cost(8 * t * t * D * 4, 16 * t * D, 2 * t * t * HEADS),
        name="attend",
    )(rot, qkv, qkv, qkv, kv_t, kv_t, seg_col, seg_m, seg_t, h, woa, wob, bias)


def ff_specs(t, blocks):
    width = FF // blocks
    half = blocks // 2
    w_in = pl.BlockSpec((HALF, width), lambda j, r: (0, (j + half * r[0]) % blocks))
    b_in = pl.BlockSpec((1, width), lambda j, r: (0, (j + half * r[0]) % blocks))
    w_a = pl.BlockSpec((width, D), lambda j, r: (jnp.minimum(j, half - 1), 0))
    w_b = pl.BlockSpec((width, D), lambda j, r: (jnp.maximum(j - half, 0), 0))
    hid = pl.BlockSpec((t, width), lambda j, r: (0, j))
    return w_in, b_in, w_a, w_b, hid


def ff_call(rot, h, par, wia, wib, bias, woa, wob, bout):
    t = h.shape[0]
    blocks = 6
    w_in, b_in, w_a, w_b, hid = ff_specs(t, blocks)
    return pl.pallas_call(
        ff_kernel,
        out_shape=(sds((t, FF), BF), sds((t, FF), BF), sds((t, D), BF), sds((t, D), BF)),
        grid_spec=pltpu.PrefetchScalarGridSpec(
            num_scalar_prefetch=1,
            grid=(blocks,),
            in_specs=[whole((t, D)), whole((8, D)), w_in, w_in, b_in, w_a, w_b, whole((1, D))],
            out_specs=[hid, hid, whole((t, D)), whole((t, D))],
            scratch_shapes=[pltpu.VMEM((t, D), F32)],
        ),
        compiler_params=params_of(),
        cost_estimate=cost(4 * t * D * FF, 4 * D * FF + 4 * t * FF, 2 * t * FF),
        name="feed",
    )(rot, h, par, wia, wib, bias, woa, wob, bout)


def ff_back_call(rot, g, act, slope, nrm, wia, wib, woa, wob, h, par):
    t = h.shape[0]
    blocks = 6
    w_in, b_in, w_a, w_b, hid = ff_specs(t, blocks)
    return pl.pallas_call(
        ff_back_kernel,
        out_shape=(
            sds((HALF, FF), BF), sds((HALF, FF), BF), sds((FF // 2, D), BF), sds((FF // 2, D), BF),
            sds((1, FF), F32), sds((8, D), F32), sds((t, D), BF),
        ),
        grid_spec=pltpu.PrefetchScalarGridSpec(
            num_scalar_prefetch=1,
            grid=(blocks,),
            in_specs=[
                whole((t, D)), hid, hid, whole((t, D)), w_in, w_in, w_a, w_b, whole((t, D)),
                whole((8, D)),
            ],
            out_specs=[w_in, w_in, w_a, w_b, b_in, whole((8, D)), whole((t, D))],
            scratch_shapes=[pltpu.VMEM((t, D), F32)],
        ),
        compiler_params=params_of(),
        cost_estimate=cost(8 * t * D * FF, 8 * D * FF + 4 * t * FF),
        name="feed_back",
    )(rot, g, act, slope, nrm, wia, wib, woa, wob, h, par)


def mix_back_call(rot, g, o, woa, wob):
    t = g.shape[0]
    return pl.pallas_call(
        mix_back_kernel,
        out_shape=(sds((t, D), BF), sds((16, t), F32), sds((HALF, D), BF), sds((HALF, D), BF)),
        grid_spec=pltpu.PrefetchScalarGridSpec(
            num_scalar_prefetch=1,
            grid=(1,),
            in_specs=[whole((t, D)), whole((t, D)), whole((HALF, D)), whole((HALF, D))],
            out_specs=[whole((t, D)), whole((16, t)), whole((HALF, D)), whole((HALF, D))],
        ),
        compiler_params=params_of(),
        cost_estimate=cost(4 * t * D * D, 4 * D * D + 6 * t * D),
        name="mix_back",
    )(rot, g, o, woa, wob)


def attend_back_call(qkv, kv_t, dmix, lse, delta, seg_row, seg_m, seg_t):
    t = dmix.shape[0]
    w = 2 * HD
    col = pl.BlockSpec((t, w), lambda j: (0, j))
    return pl.pallas_call(
        attend_back_kernel,
        out_shape=(sds((t, D), F32), sds((t, D), F32), sds((t, D), F32), sds((t, D), BF), sds((t, D), BF)),
        grid=(PAIRS,),
        in_specs=[
            col,
            pl.BlockSpec((t, w), lambda j: (0, j + PAIRS)),
            pl.BlockSpec((t, w), lambda j: (0, j + 2 * PAIRS)),
            col,
            pl.BlockSpec((t, w), lambda j: (0, j + PAIRS)),
            col, whole((16, t)), whole((16, t)), whole((1, t)), whole((t, 1)), whole((t, 1)),
        ],
        out_specs=[col] * 5,
        compiler_params=params_of(),
        cost_estimate=cost(20 * t * t * D * 4, 30 * t * D, 2 * t * t * HEADS),
        name="attend_back",
    )(qkv, qkv, qkv, kv_t, kv_t, dmix, lse, delta, seg_row, seg_m, seg_t)


def qkv_back_call(rot, dq, dkm, dvm, dkr, dvr, qkv, cosines, sines, pos, nrm, wa, wb, h, par, g):
    t = h.shape[0]
    w_in = pl.BlockSpec((HALF, D), lambda j, r: (0, j))
    rows = whole((t, D))
    return pl.pallas_call(
        qkv_back_kernel,
        out_shape=(
            sds((HALF, QKV), BF), sds((HALF, QKV), BF), sds((1, QKV), F32), sds((8, D), F32),
            sds((t, D), BF),
        ),
        grid_spec=pltpu.PrefetchScalarGridSpec(
            num_scalar_prefetch=1,
            grid=(3,),
            in_specs=[
                rows, rows, rows, rows, rows, pl.BlockSpec((t, D), lambda j, r: (0, j)), rows, rows,
                whole((t, 2)), rows, w_in, w_in, rows, whole((8, D)), rows,
            ],
            out_specs=[w_in, w_in, pl.BlockSpec((1, D), lambda j, r: (0, j)), whole((8, D)), rows],
            scratch_shapes=[pltpu.VMEM((t, D), F32), pltpu.VMEM((t, D), F32)],
        ),
        compiler_params=params_of(),
        cost_estimate=cost(4 * t * D * QKV, 4 * D * QKV + 30 * t * D),
        name="qkv_back",
    )(rot, dq, dkm, dvm, dkr, dvr, qkv, cosines, sines, pos, nrm, wa, wb, h, par, g)


def layout(image_sides, capacity):
    counts = image_sides * image_sides
    end_pos = jnp.cumsum(counts)
    start_pos = end_pos - counts
    positions = jnp.arange(capacity, dtype=jnp.int32)
    segment = jnp.sum((positions[:, None] >= end_pos[None, :]).astype(jnp.int32), axis=1)
    slot_ids = jnp.arange(image_sides.shape[-1], dtype=jnp.int32)
    one_hot = (segment[:, None] == slot_ids[None, :]).astype(jnp.int32)
    start_tok = jnp.sum(one_hot * start_pos[None, :], axis=1)
    side_len = jnp.maximum(jnp.sum(one_hot * image_sides[None, :], axis=1), 1)
    local_idx = positions - start_tok
    is_valid = segment < image_sides.shape[-1]
    patch_row = jnp.where(is_valid, local_idx // side_len, 0)
    patch_col = jnp.where(is_valid, local_idx % side_len, 0)
    return segment, patch_row, patch_col, is_valid


def turning(freq, pos):
    wide = jnp.concatenate([freq.reshape(2, HEADS, HD // 2)] * 2, axis=2).reshape(2, D)
    angles = pos[:, 0:1] * wide[0][None, :] + pos[:, 1:2] * wide[1][None, :]
    low = (jnp.arange(D) % HD) < HD // 2
    sines = jnp.sin(angles)
    return jnp.cos(angles), jnp.where(low[None, :], -sines, sines)


def flipped(x, axis, bit):
    return lax.ppermute(x, axis, [(i, i ^ bit) for i in range(lax.axis_size(axis))])


def to_owners(blocks, section, core):
    stacked = jnp.stack(blocks)
    got = [stacked[section]] + [flipped(stacked[section ^ d], "section", d) for d in (1, 2, 3)]
    here = (section // 2) == core
    near = jnp.stack(got[:2])
    away = jnp.stack(got[2:])
    mine = jnp.where(here, near, away)
    other = flipped(jnp.where(here, away, near), "group", 1)

    def in_order(pair):
        return jnp.where(section % 2 == 0, pair, pair[::-1])

    mine, other = in_order(mine), in_order(other)
    first = jnp.where(core == 0, mine, other)
    second = jnp.where(core == 0, other, mine)
    return jnp.concatenate([first, second], axis=1).reshape(-1, D)


MESH = pl.DeviceIdType.MESH
SMALL = 6144 // 128
SEMS = 20
LINE = 4


def unit_shape(s, part):
    if s % 2:
        return (FF // 2, D) if part else (HALF, FF)
    return (HALF, D) if part else (HALF, QKV)


def grad_shape(s, part):
    if s % 2:
        return (FF // 2, D) if part else (HALF, FF)
    return (D, D) if part else (HALF, 2 * D)


def piece_shape(s, part):
    r, w = grad_shape(s, part)
    return (r // 8, w // 2)


def held_shape(s, part):
    r, w = grad_shape(s, part)
    return (4, 2, r // 8, w)


def columns_of(k, width):
    return pl.ds(pl.multiple_of((k % 2) * width, width), width)


def flip(v, bit):
    if bit == 1:
        return v + 1 - 2 * (v % 2)
    if bit == 2:
        return (v + 2) % 4
    return 3 - v


def here():
    return lax.axis_index("section"), lax.axis_index("group"), lax.axis_index("dp")


def loop(n, body):
    def one(i, carried):
        body(i)
        return carried

    lax.fori_loop(0, n, one, 0)


def greet(plane, line):
    c, g, z = here()
    barrier = pltpu.get_barrier_semaphore()
    pl.semaphore_signal(barrier, inc=1, device_id={"group": 1 - g}, device_id_type=MESH)
    count = 1
    for bit in (1, 2, 3):
        if plane:
            for core in (g, 1 - g):
                pl.semaphore_signal(
                    barrier, inc=1, device_id={"section": flip(c, bit), "group": core},
                    device_id_type=MESH,
                )
                count += 1
        if line:
            pl.semaphore_signal(barrier, inc=1, device_id={"dp": flip(z, bit)}, device_id_type=MESH)
            count += 1
    pl.semaphore_wait(barrier, count)


def guarded(cond, act):
    if cond is None:
        act()
    else:
        pl.when(cond)(act)


def accumulate(into, term, rows):
    strip = 32 if rows % 32 == 0 else 16

    def one(i):
        at = pl.ds(pl.multiple_of(i * strip, strip), strip)
        into[at, :] = (into[at, :].astype(F32) + term[at, :].astype(F32)).astype(BF)

    loop(rows // strip, one)


class Unit:
    def __init__(
        self, s, part, send, recv, own=None, quarter=None, final=None, plane=None, line=None,
        held=None, whole=None,
    ):
        self.s, self.part, self.own, self.quarter_ref, self.final = s, part, own, quarter, final
        self.send, self.recv = send, recv
        self.whole = whole
        self.rows, self.cols = grad_shape(s, part)
        self.plane1, self.plane2 = plane or (None, None)
        self.up_in, self.down_in = line or (None, None)
        self.held = held
        self.pending = []

    def push(self, cond, src, dst, k, device):
        copy = pltpu.make_async_remote_copy(
            src_ref=src, dst_ref=dst, send_sem=self.send.at[k], recv_sem=self.recv.at[k],
            device_id=device, device_id_type=MESH,
        )
        guarded(cond, copy.start)
        self.pending.append((cond, copy))

    def landed(self, cond, dst, k):
        copy = pltpu.make_async_remote_copy(
            src_ref=dst, dst_ref=dst, send_sem=self.send.at[k], recv_sem=self.recv.at[k],
            device_id={"group": 1 - lax.axis_index("group")}, device_id_type=MESH,
        )
        guarded(cond, copy.wait_recv)

    def finish(self):
        for cond, copy in self.pending:
            guarded(cond, copy.wait_send)

    def quarter(self, q):
        rows = self.rows // 4
        return self.own.at[pl.ds(pl.multiple_of(q * rows, rows), rows), :]

    def mine(self):
        if self.quarter_ref is not None:
            return self.quarter_ref
        return self.quarter(lax.axis_index("section"))

    def piece(self, k):
        rows, cols = self.rows // 8, self.cols // 2
        return self.mine().at[
            pl.ds(pl.multiple_of((k // 2) * rows, rows), rows),
            pl.ds(pl.multiple_of((k % 2) * cols, cols), cols),
        ]

    def first_step(self):
        c, _, _ = here()
        x, y = c % 2, c // 2
        other = {"section": flip(c, 2 if self.part else 1)}
        for b in range(2):
            q = 2 * (1 - y) + b if self.part else 2 * b + 1 - x
            self.push(None, self.quarter(q), self.plane1.at[b], 1 + b, other)

    def second_step(self):
        c, _, _ = here()
        x, y = c % 2, c // 2
        rows = self.rows // 4
        other = {"section": flip(c, 1 if self.part else 2)}
        for b in range(2):
            self.landed(None, self.plane1.at[b], 1 + b)
        b = (1 - x) if self.part else (1 - y)
        q = (2 * y + 1 - x) if self.part else (2 * (1 - y) + x)
        accumulate(self.quarter(q), self.plane1.at[b], rows)
        self.push(None, self.quarter(q), self.plane2, 3, other)
        accumulate(self.mine(), self.plane1.at[1 - b], rows)

    def third_step(self):
        self.landed(None, self.plane2, 3)
        accumulate(self.mine(), self.plane2, self.rows // 4)

    def line_step(self, t):
        _, _, z = here()
        n = LINE
        rows = self.rows // 8
        up = (z < n - 1) & (z <= t)
        down = (z > 0) & (z >= n - 1 - t)
        k_up = jnp.minimum(n - 1 - t + z, n - 1)
        k_down = jnp.maximum(z - (n - 1) + t, 0)
        if t > 0:

            @pl.when(up & (z > 0))
            def _():
                self.landed(None, self.up_in.at[t - 1], 4 + t - 1)
                accumulate(self.piece(k_up), self.up_in.at[t - 1], rows)

            @pl.when(down & (z < n - 1))
            def _():
                self.landed(None, self.down_in.at[t - 1], 7 + t - 1)
                accumulate(self.piece(k_down), self.down_in.at[t - 1], rows)

        self.push(up, self.piece(k_up), self.up_in.at[t], 4 + t, {"dp": jnp.minimum(z + 1, n - 1)})
        self.push(down, self.piece(k_down), self.down_in.at[t], 7 + t, {"dp": jnp.maximum(z - 1, 0)})

    def line_end(self):
        _, _, z = here()
        n = LINE
        rows = self.rows // 8

        @pl.when(z > 0)
        def _():
            self.landed(None, self.up_in.at[n - 2], 4 + n - 2)
            accumulate(self.piece(z), self.up_in.at[n - 2], rows)

        @pl.when(z < n - 1)
        def _():
            self.landed(None, self.down_in.at[n - 2], 7 + n - 2)
            accumulate(self.piece(z), self.down_in.at[n - 2], rows)

    def held_at(self, k, q=None):
        cols = columns_of(k, self.cols // 2)
        return self.held.at[:, k // 2, :, cols] if q is None else self.held.at[q, k // 2, :, cols]

    def whole_at(self, k):
        return self.whole.at[k // 2, :, columns_of(k, self.cols // 2)]

    def last_piece(self):
        return self.final if self.final is not None else self.piece(here()[2])

    def own_piece(self):
        _, _, z = here()
        return pltpu.make_async_copy(
            self.last_piece(), self.held_at(z, self.s), self.send.at[10 + self.s]
        )

    def gather(self):
        c, _, z = here()
        for q in range(4):
            if q == self.s:
                pl.when(c == q)(self.own_piece().start)
            else:
                self.push(
                    c == q, self.last_piece(), self.held_at(z, q), 10 + q, {"section": self.s}
                )

    def share_step(self, t):
        _, _, z = here()
        n = LINE
        whole = self.whole_at
        if t == 0:
            copy = pltpu.make_async_copy(self.last_piece(), whole(z), self.send.at[0])
            copy.start()
            copy.wait()
        else:
            self.landed(z >= t, whole(jnp.maximum(z - t, 0)), 14 + t - 1)
            self.landed(z + t < n, whole(jnp.minimum(z + t, n - 1)), 17 + t - 1)
        if t < n - 1:
            low, high = jnp.maximum(z - t, 0), jnp.minimum(z + t, n - 1)
            self.push(
                (z >= t) & (z < n - 1), whole(low), whole(low), 14 + t,
                {"dp": jnp.minimum(z + 1, n - 1)},
            )
            self.push(
                (z + t < n) & (z > 0), whole(high), whole(high), 17 + t,
                {"dp": jnp.maximum(z - 1, 0)},
            )

    def whole_copy(self):
        return pltpu.make_async_copy(self.whole, self.held.at[self.s], self.send.at[10 + self.s])

    def whole_gather(self):
        c, _, _ = here()
        for q in range(4):
            if q == self.s:
                pl.when(c == q)(self.whole_copy().start)
            else:
                self.push(c == q, self.whole, self.held.at[q], 10 + q, {"section": self.s})

    def whole_end(self):
        c, _, _ = here()
        for q in range(4):
            if q == self.s:
                pl.when(c == q)(self.whole_copy().wait)
            else:
                self.landed(c == self.s, self.held.at[q], 10 + q)

    def out_step(self, t):
        c, _, z = here()
        n = LINE
        mine = c == self.s
        held = self.held_at
        if t == 0:
            for q in range(4):
                if q == self.s:
                    pl.when(mine)(self.own_piece().wait)
                else:
                    self.landed(mine, held(z, q), 10 + q)
        else:
            self.landed(mine & (z >= t), held(jnp.maximum(z - t, 0)), 14 + t - 1)
            self.landed(mine & (z + t < n), held(jnp.minimum(z + t, n - 1)), 17 + t - 1)
        if t < n - 1:
            low, high = jnp.maximum(z - t, 0), jnp.minimum(z + t, n - 1)
            self.push(
                mine & (z >= t) & (z < n - 1), held(low), held(low), 14 + t,
                {"dp": jnp.minimum(z + 1, n - 1)},
            )
            self.push(
                mine & (z + t < n) & (z > 0), held(high), held(high), 17 + t,
                {"dp": jnp.maximum(z - 1, 0)},
            )


class Delivery:
    def __init__(self, sources, parts, out, send, recv):
        self.sources, self.parts, self.out, self.send, self.recv = sources, parts, out, send, recv

    def rows(self, block):
        size = self.sources[self.parts[0][0]].shape[0] // 2
        return pl.ds(block * size, size)

    def copies(self, s, block):
        c, g, _ = here()
        slot = self.out.at[c % 2, g, self.rows(block), :]
        source = self.sources[s].at[self.rows(block), :]
        near = pltpu.make_async_copy(source, slot, self.send.at[s, block])
        far = pltpu.make_async_remote_copy(
            src_ref=source, dst_ref=slot, send_sem=self.send.at[s, block],
            recv_sem=self.recv.at[(c % 2) * 2 + g, block],
            device_id={"section": s, "group": c // 2}, device_id_type=MESH,
        )
        return near, far, (c == s) & (g == c // 2)

    def start(self, parts):
        for part in parts:
            near, far, stays = self.copies(*part)
            pl.when(stays)(near.start)
            pl.when(jnp.logical_not(stays))(far.start)

    def finish(self):
        c, g, _ = here()
        for s, block in self.parts:
            near, far, stays = self.copies(s, block)
            pl.when(stays)(near.wait)
            pl.when(jnp.logical_not(stays))(far.wait_send)
            for m in range(2):
                for half in range(2):
                    slot = self.out.at[m, half, self.rows(block), :]
                    copy = pltpu.make_async_remote_copy(
                        src_ref=slot, dst_ref=slot, send_sem=self.send.at[0, 0],
                        recv_sem=self.recv.at[2 * m + half, block], device_id={"group": 1 - g},
                        device_id_type=MESH,
                    )
                    arrives = (c == s) & jnp.logical_not((2 * g + m == c) & (g == half))
                    pl.when(arrives)(copy.wait_recv)


EARLY = ((2, 0), (3, 0))
LATE = ((0, 0), (1, 0), (0, 1), (1, 1), (2, 1), (3, 1))
ALL = tuple((s, block) for block in range(2) for s in range(4))


def feed_back_kernel(s, carry, *refs):
    delivers = carry is None
    wim, wit, wom, wot, act_in, slope_in, streams = refs[:7]
    refs = refs[7:]
    count = 0 if delivers else len(carry.all)
    carried, refs = refs[:count], refs[count:]
    if delivers:
        sources, parts = {i: streams.at[i] for i in range(4)}, ALL
    else:
        sources, parts = {3: refs[0], 2: refs[1]}, EARLY
        refs = refs[2:]
    g_ref, nrm, par = refs[:3]
    d_in, d_out = refs[3:5]
    delivered, results, refs = refs[5], refs[6 : 6 + count], refs[6 + count :]
    dbin_ref, small_ref, out_ref = refs[:3]
    w_in, w_out, act, slope, h, own_i, own_o, their_i, their_o, core_i, core_o, acc, nrm_t = refs[3:16]
    load_sem, core_s, core_r, out_sem = refs[16:20]
    del_sems, refs = refs[20:22], refs[22:]
    _, g, _ = here()
    partner = {"group": 1 - g}
    width = FF // CHUNKS
    third = CHUNKS // 2

    def column(j):
        b = (j + g * third) % CHUNKS
        return pl.ds(pl.multiple_of(b * width, width), width)

    def line_of(j):
        return pl.ds(pl.multiple_of(j * width, width), width)

    def loads(j):
        cols, rows = column(j), line_of(j % third)
        first = j < third
        return (
            (None, pltpu.make_async_copy(wim.at[:, cols], w_in.at[0, :, cols], load_sem.at[j, 0])),
            (None, pltpu.make_async_copy(wit.at[:, cols], w_in.at[1, :, cols], load_sem.at[j, 1])),
            (first, pltpu.make_async_copy(wom.at[rows, :], w_out.at[line_of(j), :], load_sem.at[j, 2])),
            (
                jnp.logical_not(first),
                pltpu.make_async_copy(wot.at[rows, :], w_out.at[line_of(j), :], load_sem.at[j, 2]),
            ),
            (None, pltpu.make_async_copy(act_in.at[:, line_of(j)], act.at[:, line_of(j)], load_sem.at[j, 3])),
            (None, pltpu.make_async_copy(slope_in.at[:, line_of(j)], slope.at[:, line_of(j)], load_sem.at[j, 4])),
        )

    def load(j):
        for cond, copy in loads(j):
            guarded(cond, copy.start)

    def core_copies(j):
        cols, rows = column(j), line_of(j % third)
        return (
            pltpu.make_async_remote_copy(
                src_ref=their_i.at[:, cols], dst_ref=core_i.at[:, cols], send_sem=core_s.at[j, 0],
                recv_sem=core_r.at[j, 0], device_id=partner, device_id_type=MESH,
            ),
            pltpu.make_async_remote_copy(
                src_ref=their_o.at[rows, :], dst_ref=core_o.at[rows, :], send_sem=core_s.at[j, 1],
                recv_sem=core_r.at[j, 1], device_id=partner, device_id_type=MESH,
            ),
        )

    loop(CHUNKS, load)
    stream_copy = pltpu.make_async_copy(streams.at[s - 1], h, out_sem.at[2])
    stream_copy.start()
    if not delivers:
        carry.load(carried, results, refs)
    greet(True, not delivers)
    delivery = Delivery(sources, parts, delivered, *del_sems)
    if not delivers:
        carry.begin()
    delivery.start(parts)
    acc[...] = jnp.zeros_like(acc)
    nrm_t[...] = jnp.transpose(nrm[...])

    def block(j):
        for cond, copy in loads(j):
            guarded(cond, copy.wait)
        cols, rows = column(j), line_of(j)
        grad = g_ref[...]
        d_up_f = dot_nt(grad, w_out[rows, :]) * slope[:, rows].astype(F32)
        d_up = d_up_f.astype(BF)
        d_o = dot_tn(act[:, rows], grad).astype(BF)
        dbin_ref[:, cols] = jnp.sum(d_up_f, axis=0, keepdims=True)
        their_i[:, cols] = dot(nrm_t[HALF:, :], d_up).astype(BF)
        inward, outward = core_copies(j)
        inward.start()

        @pl.when(j >= third)
        def _():
            their_o[line_of(j % third), :] = d_o
            outward.start()

        @pl.when(j < third)
        def _():
            own_o[line_of(j % third), :] = d_o

        own_i[:, cols] = dot(nrm_t[:HALF, :], d_up).astype(BF)
        acc[:, :HALF] += dot_nt(d_up, w_in[0, :, cols])
        acc[:, HALF:] += dot_nt(d_up, w_in[1, :, cols])

    if delivers:
        loop(CHUNKS, block)
    else:
        for i in range(3):
            loop(CHUNKS // 3, lambda j, i=i: block(j + CHUNKS // 3 * i))
            carry.step(i + 1)
    stream_copy.wait()
    grad = g_ref[...].astype(F32)
    d_normed = turn_halves(acc[...], g)
    out, d_gain, d_shift = norm_backward(h[...].astype(F32), par[0:1, :], grad, d_normed)
    out_ref[...] = out.astype(BF)
    small_ref[0:1, :] = jnp.sum(grad, axis=0, keepdims=True)
    small_ref[1:2, :] = d_gain
    small_ref[2:3, :] = d_shift
    small_ref[3:8, :] = jnp.zeros((5, D), F32)

    def ended(j):
        inward, outward = core_copies(j)
        inward.wait()
        pl.when(j >= third)(outward.wait)

    loop(CHUNKS, ended)
    accumulate(own_i, core_i, HALF)
    saves = [pltpu.make_async_copy(own_i, d_in, out_sem.at[0])]
    saves[0].start()
    accumulate(own_o, core_o, FF // 2)
    saves.append(pltpu.make_async_copy(own_o, d_out, out_sem.at[1]))
    saves[1].start()
    if not delivers:
        carry.end()
    delivery.finish()
    for copy in saves:
        copy.wait()


class Carry:
    def __init__(self, plane, line, hold):
        self.planes = [(plane, 0), (plane, 1)]
        self.line, self.hold = line, hold
        self.all = self.planes + list(line) + list(hold)

    def results(self):
        out = []
        for u in self.planes:
            r, w = grad_shape(*u)
            out.append(sds((r // 4, w), BF))
        out += [sds(piece_shape(*u), BF) for u in self.line]
        return out + [sds(held_shape(*u), BF) for u in self.hold]

    def scratch(self):
        out = []
        for u in self.planes:
            r, w = grad_shape(*u)
            out += [pltpu.VMEM((r, w), BF), pltpu.VMEM((2, r // 4, w), BF), pltpu.VMEM((r // 4, w), BF)]
        for u in self.line:
            r, w = grad_shape(*u)
            out += [pltpu.VMEM((r // 4, w), BF)] + [pltpu.VMEM((3,) + piece_shape(*u), BF)] * 2
        out += [pltpu.VMEM(piece_shape(*u), BF) for u in self.hold]
        dma = pltpu.SemaphoreType.DMA
        return out + [dma((len(self.all), SEMS)), dma((len(self.all), SEMS))]

    def load(self, sources, results, refs):
        send, recv = refs[-2:]
        refs = list(refs[:-2])
        self.units, self.loads, self.targets = [], [], results
        for i, u in enumerate(self.all):
            sems = (send.at[i], recv.at[i])
            if i < 2:
                own, first, second = refs.pop(0), refs.pop(0), refs.pop(0)
                unit = Unit(*u, *sems, own=own, plane=(first, second))
            elif i < 2 + len(self.line):
                own, up, down = refs.pop(0), refs.pop(0), refs.pop(0)
                unit = Unit(*u, *sems, quarter=own, line=(up, down))
            else:
                own = refs.pop(0)
                unit = Unit(*u, *sems, final=own, held=results[i])
            copy = pltpu.make_async_copy(sources[i], own, sems[0].at[0])
            copy.start()
            self.units.append(unit)
            self.loads.append(copy)
        n = 2 + len(self.line)
        self.plane_units, self.line_units, self.hold_units = (
            self.units[:2], self.units[2:n], self.units[n:],
        )

    def begin(self):
        for copy in self.loads:
            copy.wait()
        for unit in self.hold_units:
            unit.gather()
        for unit in self.line_units:
            unit.line_step(0)
        for unit in self.plane_units:
            unit.first_step()

    def step(self, i):
        for unit in self.line_units:
            if i < LINE - 1:
                unit.line_step(i)
            else:
                unit.line_end()
        if i == 3:
            for unit in self.plane_units:
                unit.second_step()
        for unit in self.hold_units:
            if i < 3:
                unit.out_step(i - 1)

    def late_step(self):
        for unit in self.hold_units:
            unit.out_step(LINE - 2)

    def end(self):
        saves = [
            pltpu.make_async_copy(unit.last_piece(), target, unit.send.at[0])
            for unit, target in zip(self.line_units, self.targets[2:])
        ]
        for copy in saves:
            copy.start()
        for unit, target in zip(self.plane_units, self.targets):
            unit.third_step()
            copy = pltpu.make_async_copy(unit.mine(), target, unit.send.at[0])
            copy.start()
            saves.append(copy)
        for unit in self.hold_units:
            unit.out_step(LINE - 1)
        for copy in saves:
            copy.wait()
        for unit in self.units:
            unit.finish()


def feed_back_call(s, weights, act, slope, streams, g, nrm, par, carry, carried, leaving, collective):
    t = g.shape[0]
    hbm = pl.BlockSpec(memory_space=pl.ANY)
    vmem = pl.BlockSpec(memory_space=pltpu.VMEM)
    delivers = carry is None
    dma = pltpu.SemaphoreType.DMA
    half_i, half_o = grad_shape(s, 0), grad_shape(s, 1)
    results = [sds((2, 2, t if delivers else t // 2, D), BF)]
    results += [] if delivers else carry.results()
    scratch = [
        pltpu.VMEM((2, HALF, FF), BF), pltpu.VMEM((FF, D), BF), pltpu.VMEM((t, FF), BF),
        pltpu.VMEM((t, FF), BF), pltpu.VMEM((t, D), BF),
        pltpu.VMEM(half_i, BF), pltpu.VMEM(half_o, BF), pltpu.VMEM(half_i, BF),
        pltpu.VMEM(half_o, BF), pltpu.VMEM(half_i, BF), pltpu.VMEM(half_o, BF),
        pltpu.VMEM((t, D), F32), pltpu.VMEM((D, t), BF),
        dma((CHUNKS, 5)), dma((CHUNKS, 2)), dma((CHUNKS, 2)), dma((3,)),
        dma((4, 2)), dma((4, 2)),
    ] + ([] if delivers else carry.scratch())
    out = pl.pallas_call(
        partial(feed_back_kernel, s, carry),
        out_shape=[sds(half_i, BF), sds(half_o, BF)] + results
        + [sds((1, FF), F32), sds((8, D), F32), sds((t, D), BF)],
        in_specs=[hbm] * (7 + len(carried) + len(leaving)) + [vmem] * 3,
        out_specs=[hbm] * (2 + len(results)) + [vmem] * 3,
        scratch_shapes=scratch,
        compiler_params=pltpu.CompilerParams(
            collective_id=collective, has_side_effects=True, vmem_limit_bytes=62 * 1024 * 1024
        ),
        name="feed_back_carry",
    )(*weights, act, slope, streams, *carried, *leaving, g, nrm, par)
    return out[:2], out[2 : 2 + len(results)], out[2 + len(results) :]


def attention_back_kernel(s, carry, *refs):
    wim, wit, wom, wot = refs[:4]
    count = len(carry.all)
    carried = refs[4 : 4 + count]
    refs = refs[4 + count :]
    large, (g_ref, lse_ref, seg_row, seg_m, seg_t, pos, par) = refs[:7], refs[7:14]
    d_first, d_second = refs[14:16]
    results, refs = refs[16 : 16 + count], refs[16 + count :]
    dbin_ref, small_ref, out_ref = refs[:3]
    w_in, w_out, dmix, d_q, d_k, d_v, give_k, give_v, got_k, got_v = refs[3:13]
    own, their, core = refs[13:15], refs[15:17], refs[17:19]
    acc, dp, delta_ref, nrm_t = refs[19:23]
    load_sem, kv_s, kv_r, core_s, core_r, out_sem = refs[23:29]
    o_ref, qkv, kv_t, nrm, cosines, sines, h = refs[29:36]
    carry.load(carried, results, refs[36:])
    if s:
        large = large[:6] + (large[6].at[s - 1],)
    _, g, _ = here()
    partner = {"group": 1 - g}
    tokens = g_ref.shape[0]

    def remote(src, dst, ssem, rsem):
        return pltpu.make_async_remote_copy(
            src_ref=src, dst_ref=dst, send_sem=ssem, recv_sem=rsem, device_id=partner,
            device_id_type=MESH,
        )

    pairs = [(wom, w_out.at[0]), (wot, w_out.at[1])]
    pairs += list(zip(large[:4], (o_ref, qkv, kv_t, nrm)))
    pairs += [(wim, w_in.at[0]), (wit, w_in.at[1])]
    pairs += list(zip(large[4:], (cosines, sines, h)))
    loads = [
        pltpu.make_async_copy(src, dst, load_sem.at[i]) for i, (src, dst) in enumerate(pairs)
    ]
    for copy in loads:
        copy.start()
    greet(True, True)
    carry.begin()

    for copy in loads[:3]:
        copy.wait()
    grad = g_ref[...]
    d_mix = jnp.concatenate([dot_nt(grad, w_out[0]), dot_nt(grad, w_out[1])], axis=1)
    dmix[...] = turn_halves(d_mix, g).astype(BF)
    o = o_ref[...].astype(F32)
    head = lax.broadcasted_iota(jnp.int32, (16, D), 0)
    lane = lax.broadcasted_iota(jnp.int32, (16, D), 1)
    delta_ref[...] = lax.dot_general(
        jnp.where(lane // HD == head, 1.0, 0.0), dmix[...].astype(F32) * o, NT,
        preferred_element_type=F32, precision=lax.Precision.HIGHEST,
    )
    turned = turn_halves(o, g).astype(BF)
    turned_t = jnp.transpose(turned)
    their[1][HALF:, :] = dot(turned_t[HALF:, :], grad).astype(BF)
    core_copies = [remote(their[1].at[HALF:, :], core[1].at[HALF:, :], core_s.at[3], core_r.at[3])]
    core_copies[0].start()
    own[1][HALF:, :] = dot(turned_t[:HALF, :], grad).astype(BF)

    lanes = lax.broadcasted_iota(jnp.int32, (tokens, 2 * HD), 1)

    def pair(j):
        def columns(first):
            return pl.ds(pl.multiple_of(first + j * 2 * HD, 2 * HD), 2 * HD)

        q = qkv[:, columns(0)]
        do = dmix[:, columns(0)]
        zero = jnp.zeros_like(q)
        sets = (
            (qkv[:, columns(D)], qkv[:, columns(2 * D)], seg_m),
            (kv_t[:, columns(0)], kv_t[:, columns(D)], seg_t),
        )
        total_q = [0.0, 0.0]
        keys_t = [jnp.transpose(sets[i][0]) for i in range(2)]
        total_k = [jnp.zeros((tokens, 2 * HD), F32)] * 2
        total_v = [jnp.zeros((tokens, 2 * HD), F32)] * 2
        for side in range(2):
            mine = (lanes >= HD) if side else (lanes < HD)
            q_head = jnp.where(mine, q, zero)
            do_head = jnp.where(mine, do, zero)
            lse = lse_ref[pl.ds(2 * j + side, 1), :]
            delta = delta_ref[pl.ds(2 * j + side, 1), :]
            for i, (k, v, seg) in enumerate(sets):
                p_t = jnp.where(
                    seg[...] == seg_row[...], jnp.exp(dot_nt(k, q_head) - lse), 0.0
                )
                d_s = (p_t * (dot_nt(v, do_head) - delta)).astype(BF)
                total_v[i] = total_v[i] + dot(p_t.astype(BF), do_head)
                total_k[i] = total_k[i] + dot(d_s, q_head)
                total_q[side] = total_q[side] + dot(keys_t[i][side * HD : (side + 1) * HD, :], d_s)
        d_q[:, columns(0)] = jnp.transpose(jnp.concatenate(total_q, axis=0))
        d_k[:, columns(0)] = total_k[0]
        d_v[:, columns(0)] = total_v[0]
        give_k[:, columns(0)] = total_k[1].astype(BF)
        give_v[:, columns(0)] = total_v[1].astype(BF)

    def exchanges(i):
        cols = pl.ds(i * 4 * HD, 4 * HD)
        return (
            remote(give_k.at[:, cols], got_k.at[:, cols], kv_s.at[0, i], kv_r.at[0, i]),
            remote(give_v.at[:, cols], got_v.at[:, cols], kv_s.at[1, i], kv_r.at[1, i]),
        )

    for copy in loads[3:6]:
        copy.wait()
    nrm_t[...] = jnp.transpose(nrm[...])
    for i in range(PAIRS // 2):
        loop(2, lambda j, i=i: pair(2 * i + j))
        for copy in exchanges(i):
            copy.start()
        carry.step(i + 1)

    for copy in loads[6:]:
        copy.wait()
    acc[...] = jnp.zeros_like(acc)
    small_ref[...] = jnp.zeros_like(small_ref)

    def turned_back(dy, y):
        swapped = swap_pairs(dy)
        d_angle = y * swapped - swap_pairs(y) * dy
        small_ref[3:4, :] += jnp.sum(d_angle * pos[:, 0:1], axis=0, keepdims=True)
        small_ref[4:5, :] += jnp.sum(d_angle * pos[:, 1:2], axis=0, keepdims=True)
        return dy * cosines[...] - swapped * sines[...]

    for j in range(3):
        cols = slice(j * D, (j + 1) * D)
        if j == 0:
            dp[...] = turned_back(
                d_q[...] * HD ** (-0.5), qkv[:, :D].astype(F32) * HD**0.5
            )
        elif j == 1:
            for i in range(PAIRS // 2):
                for copy in exchanges(i):
                    copy.wait()
            dp[...] = turned_back(d_k[...] + got_k[...].astype(F32), qkv[:, D : 2 * D].astype(F32))
        else:
            dp[...] = d_v[...] + got_v[...].astype(F32)
        d_p = dp[...].astype(BF)
        dbin_ref[:, cols] = jnp.sum(dp[...], axis=0, keepdims=True)
        if j < 2:
            place = (0, (slice(None), cols))
        else:
            place = (1, (slice(0, HALF), slice(None)))
        part, at = place
        their[part][at] = dot(nrm_t[HALF:, :], d_p).astype(BF)
        copy = remote(their[part].at[at], core[part].at[at], core_s.at[j], core_r.at[j])
        copy.start()
        core_copies.append(copy)
        own[part][at] = dot(nrm_t[:HALF, :], d_p).astype(BF)
        if j == 1:
            carry.late_step()
        acc[:, :HALF] += dot_nt(d_p, w_in[0, :, cols])
        acc[:, HALF:] += dot_nt(d_p, w_in[1, :, cols])
    grad = g_ref[...].astype(F32)
    d_normed = turn_halves(acc[...], g)
    out, d_gain, d_shift = norm_backward(h[...].astype(F32), par[0:1, :], grad, d_normed)
    out_ref[...] = out.astype(BF)
    small_ref[0:1, :] = jnp.sum(grad, axis=0, keepdims=True)
    small_ref[1:2, :] = d_gain
    small_ref[2:3, :] = d_shift

    for copy in core_copies:
        copy.wait()
    saves = []
    for part, target in enumerate((d_first, d_second)):
        accumulate(own[part], core[part], own[part].shape[0])
        copy = pltpu.make_async_copy(own[part], target, out_sem.at[part])
        copy.start()
        saves.append(copy)
    carry.end()
    for copy in saves:
        copy.wait()


def attention_back_call(
    s, weights, carry, carried, g, saved, seg_row, seg_m, seg_t, turns, pos, h, par, collective
):
    t = g.shape[0]
    qkv, nrm, kv_t, o, lse = saved
    hbm = pl.BlockSpec(memory_space=pl.ANY)
    vmem = pl.BlockSpec(memory_space=pltpu.VMEM)
    dma = pltpu.SemaphoreType.DMA
    halves = [grad_shape(s, 0), grad_shape(s, 1)]
    rows, wide = pltpu.VMEM((t, D), BF), pltpu.VMEM((t, D), F32)
    results = carry.results()
    scratch = [
        pltpu.VMEM((2, HALF, QKV), BF), pltpu.VMEM((2, HALF, D), BF), rows, wide, wide, wide,
        rows, rows, rows, rows,
        *[pltpu.VMEM(x, BF) for x in halves * 3],
        wide, wide, pltpu.VMEM((16, t), F32), pltpu.VMEM((D, t), BF),
        dma((11,)), dma((2, 3)), dma((2, 3)), dma((4,)), dma((4,)), dma((2,)),
        rows, pltpu.VMEM((t, QKV), BF), pltpu.VMEM((t, 2 * D), BF), rows, wide, wide, rows,
    ] + carry.scratch()
    out = pl.pallas_call(
        partial(attention_back_kernel, s, carry),
        out_shape=[sds(x, BF) for x in halves] + results
        + [sds((1, QKV), F32), sds((8, D), F32), sds((t, D), BF)],
        in_specs=[hbm] * (4 + len(carried) + 7) + [vmem] * 7,
        out_specs=[hbm] * (2 + len(results)) + [vmem] * 3,
        scratch_shapes=scratch,
        compiler_params=pltpu.CompilerParams(
            collective_id=collective, has_side_effects=True, vmem_limit_bytes=62 * 1024 * 1024
        ),
        name="attention_back_carry",
    )(*weights, *carried, o, qkv, kv_t, nrm, *turns, h, g, lse, seg_row, seg_m, seg_t, pos, par)
    return out[:2], out[2:-3], out[-3:]


LAST = (
    (0, 0, "own"), (0, 1, "own"), (1, 0, "quarter"), (1, 1, "quarter"),
    (3, 1, "final"), (2, 0, "final"), (2, 1, "final"),
)


def last_kernel(*refs):
    n = len(LAST)
    sources, streams, small_in = refs[:n], refs[n : n + 4], refs[n + 4]
    refs = refs[n + 5 :]
    outs, delivered, small_out = refs[:4], refs[4], refs[5]
    refs = refs[6:]
    owns = refs[:n]
    planes = ((refs[n], refs[n + 1]), (refs[n + 2], refs[n + 3]))
    refs = refs[n + 4 :]
    ups, downs, wholes = refs[:4], refs[4:8], {1: refs[8], 3: refs[9]}
    sm, sm_core, sm_x, sm_y, sm_z = refs[10:15]
    send, recv, sm_send, sm_recv, del_send, del_recv = refs[15:]
    c, g, z = here()
    x, y = c % 2, c // 2
    units, copies = [], []
    for u, (s, part, kind) in enumerate(LAST):
        copy = pltpu.make_async_copy(sources[u], owns[u], send.at[u, 0])
        copy.start()
        copies.append(copy)
        units.append(
            Unit(
                s, part, send.at[u], recv.at[u], plane=planes[u] if u < 2 else None,
                line=(ups[u], downs[u]) if u < 4 else None, held=outs[2 * (s % 2) + part],
                whole=wholes.get(u), **{kind: owns[u]},
            )
        )
    greet(True, True)

    pending = []

    def small_push(src, dst, k, device):
        copy = pltpu.make_async_remote_copy(
            src_ref=src, dst_ref=dst, send_sem=sm_send.at[k], recv_sem=sm_recv.at[k],
            device_id=device, device_id_type=MESH,
        )
        copy.start()
        pending.append(copy)
        return copy

    def small_landed(dst, k):
        pltpu.make_async_remote_copy(
            src_ref=dst, dst_ref=dst, send_sem=sm_send.at[k], recv_sem=sm_recv.at[k],
            device_id={"group": 1 - g}, device_id_type=MESH,
        ).wait_recv()

    def small_step(k):
        if k == 0:
            sm[...] = small_in[...]
            small_push(sm, sm_core, 0, {"group": 1 - g})
        elif k == 1:
            small_landed(sm_core, 0)
            sm_x[0] = sm[...] + sm_core[...]
            for b in range(2):
                small_push(sm_x.at[0, 2 * b + 1 - x], sm_x.at[1, b], 1 + b, {"section": flip(c, 1)})
        elif k == 2:
            for b in range(2):
                small_landed(sm_x.at[1, b], 1 + b)
                sm_y[b] = sm_x[0, 2 * b + x] + sm_x[1, b]
            small_push(sm_y.at[1 - y], sm_y.at[2], 3, {"section": flip(c, 2)})
        elif k == 3:
            small_landed(sm_y.at[2], 3)
            sm_z[z] = sm_y[y] + sm_y[2]
            for bit in (1, 2, 3):
                small_push(sm_z.at[z], sm_z.at[z], 3 + bit, {"dp": flip(z, bit)})
        else:
            for bit in (1, 2, 3):
                small_landed(sm_z.at[flip(z, bit)], 3 + bit)
            small_out[...] = sm_z[0] + sm_z[1] + sm_z[2] + sm_z[3]

    delivery = Delivery(streams, LATE, delivered, del_send, del_recv)

    def every(which, act, *args):
        for unit in which:
            getattr(unit, act)(*args)

    for copy in copies:
        copy.wait()
    whole_a, halves_f, ready = units[:2], units[2:4], units[4:]
    (held_a, shared_a), (held_f, shared_f) = whole_a, halves_f
    every(whole_a, "first_step")
    every(halves_f, "line_step", 0)
    every(ready, "gather")
    small_step(0)
    every(halves_f, "line_step", 1)
    small_step(1)
    every(halves_f, "line_step", 2)
    every(whole_a, "second_step")
    small_step(2)
    every(halves_f, "line_end")
    held_f.gather()
    shared_f.share_step(0)
    every(whole_a, "third_step")
    every(whole_a, "line_step", 0)
    small_step(3)
    delivery.start(LATE[:2])
    every(ready, "out_step", 0)
    shared_f.share_step(1)
    every(whole_a, "line_step", 1)
    held_f.out_step(0)
    shared_f.share_step(2)
    every(whole_a, "line_step", 2)
    small_step(4)
    shared_f.share_step(3)
    shared_f.whole_gather()
    every(whole_a, "line_end")
    held_a.gather()
    shared_a.share_step(0)
    every(ready, "out_step", 1)
    held_f.out_step(1)
    shared_a.share_step(1)
    held_a.out_step(0)
    shared_a.share_step(2)
    every(ready, "out_step", 2)
    held_a.out_step(1)
    shared_a.share_step(3)
    shared_a.whole_gather()
    delivery.start(LATE[2:])
    held_f.out_step(2)
    held_a.out_step(2)
    every(ready, "out_step", 3)
    held_f.out_step(3)
    held_a.out_step(3)
    shared_f.whole_end()
    shared_a.whole_end()
    delivery.finish()
    for unit in units:
        unit.finish()
    for copy in pending:
        copy.wait_send()


def last_call(sources, streams, small):
    t = streams[0].shape[0]
    hbm = pl.BlockSpec(memory_space=pl.ANY)
    vmem = pl.BlockSpec(memory_space=pltpu.VMEM)
    dma = pltpu.SemaphoreType.DMA
    planes = []
    for r, w in (grad_shape(0, 0), grad_shape(0, 1)):
        planes += [pltpu.VMEM((2, r // 4, w), BF), pltpu.VMEM((r // 4, w), BF)]
    lines = [pltpu.VMEM((3,) + piece_shape(s, part), BF) for s, part, _ in LAST[:4]]
    scratch = (
        [pltpu.VMEM(x.shape, BF) for x in sources]
        + planes
        + lines
        + lines
        + [pltpu.VMEM(held_shape(*LAST[u][:2])[1:], BF) for u in (1, 3)]
        + [
            pltpu.VMEM((4, SMALL, 128), F32),
            pltpu.VMEM((4, SMALL, 128), F32),
            pltpu.VMEM((2, 4, SMALL, 128), F32),
            pltpu.VMEM((3, SMALL, 128), F32),
            pltpu.VMEM((4, SMALL, 128), F32),
            dma((len(LAST), SEMS)), dma((len(LAST), SEMS)), dma((7,)), dma((7,)), dma((4, 2)), dma((4, 2)),
        ]
    )
    *out, delivered, small = pl.pallas_call(
        last_kernel,
        out_shape=[sds(held_shape(s, part), BF) for s in (0, 1) for part in (0, 1)]
        + [sds((2, 2, t, D), BF), sds((SMALL, 128), F32)],
        in_specs=[hbm] * (len(LAST) + 4) + [vmem],
        out_specs=[hbm] * 5 + [vmem],
        scratch_shapes=scratch,
        compiler_params=pltpu.CompilerParams(
            collective_id=1, has_side_effects=True, vmem_limit_bytes=56 * 1024 * 1024
        ),
        name="last",
    )(*sources, *streams, small)

    return out, delivered, small


def in_place(x):
    return x.reshape(-1, x.shape[-1])


CHUNKS = 6


START = (0, 0, 0, 0)
RING = 4
GROUP = (1, 1, 1, 1)
SPAN = 6
BESIDE = (None, None, None)


def chunk_of(ref, part, k):
    size = ref.shape[0 if part else 1] // CHUNKS
    at = pl.ds(pl.multiple_of(k * size, size), size)
    return ref.at[at, :] if part else ref.at[:, at]


def ring_place(chip):
    return 2 * (chip // 2) + (chip % 2 + chip // 2) % 2


def ring_chip(place):
    return 2 * (place // 2) + (place % 2 + place // 2) % 2


CLOCKWISE = ((True, False), (True, False), (False, True), (True, False))


def forward_kernel(*refs):
    w_in, w_out, h0, small, pos, seg_col, seg_m, seg_t = refs[:8]
    refs = refs[8:]
    keep = [refs[4 * s : 4 * s + 4] for s in range(4)]
    acts, slopes = refs[16:18], refs[18:20]
    results = refs[20:38]
    refs = refs[38:]
    work, refs = refs[:18], refs[18:]
    qkvs, kv_ts, os, lses = work[0:2], work[2:4], work[4:6], work[6:8]
    nrms, hs = work[8:12], [work[12].at[s] for s in range(4)]
    turns, pars = (work[13:15], work[15:17]), work[17]
    held = [refs[4 * s : 4 * s + 4] for s in range(4)]
    acc, stage_a, stage_s, lse_scr, smalls, b_in, b_out, freqs = refs[16:24]
    own_sem, ring_s, ring_r, z_s, z_r, core_s, core_r, kv_sem, save_sem, stage_sem = refs[24:34]
    small_s, small_r, result_sem = refs[34:]

    def kept(i):
        return pltpu.make_async_copy(work[i], results[i], result_sem.at[i])

    c = lax.axis_index("section")
    g = lax.axis_index("group")
    z = lax.axis_index("dp")
    parity = z % 2
    place = ring_place(c)
    ahead, behind = ring_chip((place + 1) % 4), ring_chip((place + 3) % 4)
    partner = {"group": 1 - g}
    tokens = h0.shape[0]

    def remote(src, dst, ssem, rsem, device):
        return pltpu.make_async_remote_copy(
            src_ref=src, dst_ref=dst, send_sem=ssem, recv_sem=rsem, device_id=device,
            device_id_type=MESH,
        )

    greet(True, True)

    def small_copies():
        slot = smalls.at[2 * c + g]
        out = []
        for bit in range(4):
            for core in range(2):
                if bit or core:
                    target = {"section": flip(c, bit) if bit else c, "group": (g + core) % 2}
                    out.append(remote(small, slot, small_s.at[2 * bit + core], small_r.at[2 * c + g], target))
        return out

    for copy in small_copies():
        copy.start()
    smalls[2 * c + g] = small[...]

    def mine(s, part):
        return held[s][2 * part]

    def theirs(s, part):
        return held[s][2 * part + 1]

    def distance(s, part):
        d = place - ring_place(s)
        return (d + 4) % 4 if CLOCKWISE[s][part] else (4 - d) % 4

    def own_copies(s):
        first = pltpu.make_async_copy(
            w_in.at[:, : QKV] if s % 2 == 0 else w_in, mine(s, 0), own_sem.at[0]
        )
        source = w_out.at[:HALF, :] if s % 2 == 0 else w_out
        second = pltpu.make_async_copy(source, mine(s, 1), own_sem.at[1])
        over = remote(w_out.at[HALF:D, :], mine(s, 1), own_sem.at[2], own_sem.at[3], partner)
        return first, second, over

    for s in range(4):

        @pl.when(c == s)
        def _(s=s):
            first, second, over = own_copies(s)
            first.start()
            if s % 2:
                second.start()
            else:

                @pl.when(g == 0)
                def _():
                    second.start()
                    over.start()

    for s in range(4):

        @pl.when(c == s)
        def _(s=s):
            first, second, over = own_copies(s)
            first.wait()
            if s % 2:
                second.wait()
            else:

                @pl.when(g == 0)
                def _():
                    second.wait()
                    over.wait_send()

                @pl.when(g == 1)
                def _():
                    over.wait_recv()

    def ring_copy(s, part, k):
        ref = chunk_of(mine(s, part), part, jnp.where(k < 2, 2 * parity + k, k + 2))
        target = ahead if CLOCKWISE[s][part] else behind
        u = 2 * s + part
        return remote(ref, ref, ring_s.at[u, k], ring_r.at[u, k], {"section": target})

    def z_copy(s, part, j, sending):
        ref = chunk_of(mine(s, part), part, 2 * (parity if sending else 1 - parity) + j)
        u = 2 * s + part
        return remote(ref, ref, z_s.at[u, j], z_r.at[u, j], {"dp": z + 1 - 2 * parity})

    def core_copy(s, part, k):
        u = 2 * s + part
        return remote(
            chunk_of(mine(s, part), part, k), chunk_of(theirs(s, part), part, k),
            core_s.at[u, k], core_r.at[u, k], partner,
        )

    def event(s, part, k):
        p = distance(s, part)
        copy = ring_copy(s, part, k)
        pl.when(p > 0)(copy.wait_recv)
        pl.when(p < 3)(copy.start)

        @pl.when((k < 2) & (p > 0))
        def _():
            z_copy(s, part, jnp.minimum(k, 1), True).start()

        core_copy(s, part, jnp.where(k < 2, 2 * parity + k, k + 2)).start()

        @pl.when(k >= 2)
        def _():
            j = jnp.maximum(k - 2, 0)
            pl.when(p > 0)(z_copy(s, part, j, False).wait_recv)
            core_copy(s, part, 2 * (1 - parity) + j).start()

    def slot(t, first, last):
        for s in range(4):
            if START[s] <= last and first <= START[s] + RING // GROUP[s] + 2:
                for part in range(2):
                    k = t - START[s] - distance(s, part)

                    @pl.when((k >= 0) & (k < RING // GROUP[s]))
                    def _(s=s, part=part, k=k):
                        k = jnp.clip(k, 0, RING // GROUP[s] - 1)
                        for i in range(GROUP[s]):
                            event(s, part, k * GROUP[s] + i)

    def slots(first, last):
        loop(last - first + 1, lambda i: slot(first + i, first, last))

    def arrived(s):
        def one(k):
            core_copy(s, 0, k).wait_recv()
            core_copy(s, 1, k).wait_recv()

        loop(CHUNKS, one)
        for i in range(4):
            pltpu.make_async_copy(held[s][i], keep[s][i], save_sem.at[4 * s + i]).start()

    def assemble():
        for i in range(8):
            slot = smalls.at[i]
            copy = remote(slot, slot, small_s.at[0], small_r.at[i], partner)
            pl.when(2 * c + g != i)(copy.wait_recv)
        for s in range(4):

            def both(first, width, s=s):
                at = slice(first, first + width)
                return jnp.concatenate([smalls[2 * s, :, at], smalls[2 * s + 1, :, at]], axis=1)

            half = FF // 2
            b_in[s] = both(0, half)
            b_out[s] = both(half, HALF)
            pars[s] = jnp.concatenate(
                [both(half + HALF, HALF), both(half + 2 * HALF, HALF), jnp.zeros((6, D), F32)], axis=0
            )
            if s % 2 == 0:
                freqs[s // 2] = jnp.concatenate(
                    [both(half + 3 * HALF, HALF), both(half + 4 * HALF, HALF)], axis=0
                )

    def turn_rows(i):
        rows = tokens // 2
        at = pl.ds(pl.multiple_of((i % 2) * rows, rows), rows)
        for layer in range(2):

            @pl.when(i // 2 == layer)
            def _(layer=layer):
                angles = (
                    pos[at, 0:1] * freqs[layer, 0:1, :] + pos[at, 1:2] * freqs[layer, 1:2, :]
                )
                lanes = lax.broadcasted_iota(jnp.int32, angles.shape, 1)
                sines = jnp.sin(angles)
                turns[layer][0][at, :] = jnp.cos(angles)
                turns[layer][1][at, :] = jnp.where((lanes % HD) < HD // 2, -sines, sines)

    def normed(s, h):
        xhat, _ = normalize(h[...].astype(F32))
        nrms[s][...] = turn_halves(
            xhat * pars[s, 0:1, :] + pars[s, 1:2, :], g
        ).astype(BF)

    def project(s, first, width):
        cols = pl.ds(first, width)
        return (
            dot(nrms[s][:, :HALF], mine(s, 0)[:, cols])
            + dot(nrms[s][:, HALF:], theirs(s, 0)[:, cols])
            + b_in[s, 0:1, cols]
        )

    def attention(s, h, out, beside):
        layer = s // 2
        qkv, kv_t, o_ref = qkvs[layer], kv_ts[layer], os[layer]
        cosines, sines = turns[layer]
        normed(s, h)
        exchange = []
        for j in (1, 2, 0):
            x = project(s, j * D, D)
            if j < 2:
                x = x * cosines[...] + swap_pairs(x) * sines[...]
            if j == 0:
                x = x * HD ** (-0.5)
            qkv[:, j * D : (j + 1) * D] = x.astype(BF)
            if j:
                copy = remote(
                    qkv.at[:, j * D : (j + 1) * D], kv_t.at[:, (j - 1) * D : j * D],
                    kv_sem.at[0, 2 * layer + j - 1], kv_sem.at[1, 2 * layer + j - 1], partner,
                )
                copy.start()
                exchange.append(copy)
        for copy in exchange:
            copy.wait()
        for i in (layer, 2 + layer, 8 + s):
            kept(i).start()
        lanes = lax.broadcasted_iota(jnp.int32, (tokens, 2 * HD), 1)

        def pair(j):
            if beside is not None:
                pl.when(beside[0] + j <= beside[1])(lambda: slot(beside[0] + j, *beside))

            def columns(ref, first):
                return ref[:, pl.ds(pl.multiple_of(first + j * 2 * HD, 2 * HD), 2 * HD)]

            q = columns(qkv, 0)
            km, vm = columns(qkv, D), columns(qkv, 2 * D)
            kt, vt = columns(kv_t, 0), columns(kv_t, D)
            same_m = seg_col[...] == seg_m[...]
            same_t = seg_col[...] == seg_t[...]
            found = []
            for side in range(2):
                head = (lanes >= HD) if side else (lanes < HD)
                q_head = jnp.where(head, q, jnp.zeros_like(q))
                s_m = jnp.where(same_m, dot_nt(q_head, km), -1e9)
                s_t = jnp.where(same_t, dot_nt(q_head, kt), -1e9)
                top = jnp.maximum(
                    jnp.max(s_m, axis=-1, keepdims=True), jnp.max(s_t, axis=-1, keepdims=True)
                )
                p_m = jnp.exp(s_m - top)
                p_t = jnp.exp(s_t - top)
                total = jnp.sum(p_m, axis=-1, keepdims=True) + jnp.sum(
                    p_t, axis=-1, keepdims=True
                )
                o = dot(p_m.astype(BF), vm) + dot(p_t.astype(BF), vt)
                found.append(o / total)
                lse_scr[...] = jnp.where(
                    lanes == 2 * j + side, top + jnp.log(total), lse_scr[...]
                )
            o_ref[:, pl.ds(pl.multiple_of(j * 2 * HD, 2 * HD), 2 * HD)] = jnp.where(
                lanes < HD, found[0], found[1]
            ).astype(BF)

        loop(PAIRS, pair)
        lses[layer][...] = jnp.transpose(lse_scr[...])[:16, :]
        turned = turn_halves(o_ref[...].astype(F32), g).astype(BF)
        y = dot(turned[:, :HALF], mine(s, 1)[...]) + dot(turned[:, HALF:], theirs(s, 1)[...])
        out[...] = (h[...].astype(F32) + y + b_out[s, 0:1, :]).astype(BF)
        for i in (4 + layer, 6 + layer):
            kept(i).start()

    def feed(s, h, out, beside):
        layer = s // 2
        width = FF // CHUNKS
        normed(s, h)
        kept(8 + s).start()
        acc[...] = h[...].astype(F32) + b_out[s, 0:1, :]

        def staged(j, i):
            turn = j % 2
            cols = pl.ds(pl.multiple_of(j * width, width), width)
            source, target = ((stage_a, acts[layer]), (stage_s, slopes[layer]))[i]
            return pltpu.make_async_copy(source.at[turn], target.at[:, cols], stage_sem.at[i, turn])

        def block(j):
            if beside is not None:
                pl.when(beside[0] + j <= beside[1])(lambda: slot(beside[0] + j, *beside))
            turn = j % 2

            @pl.when(j >= 2)
            def _():
                staged(j - 2, 0).wait()
                staged(j - 2, 1).wait()

            b = (j + g * (CHUNKS // 2)) % CHUNKS
            u = project(s, pl.multiple_of(b * width, width), width)
            cdf = 0.5 + 0.5 * lax.erf(u * (0.5**0.5))
            act = (u * cdf).astype(BF)
            stage_a[turn] = act
            pdf = jnp.exp(u * u * -0.5) * 0.3989422804014327
            stage_s[turn] = (cdf + u * pdf).astype(BF)
            staged(j, 0).start()
            staged(j, 1).start()
            for half in range(2):

                @pl.when(j // (CHUNKS // 2) == half)
                def _(half=half):
                    rows = pl.ds(pl.multiple_of((j % (CHUNKS // 2)) * width, width), width)
                    acc[...] += dot(act, held[s][2 + half][rows, :])

        loop(CHUNKS, block)
        for j in (CHUNKS - 2, CHUNKS - 1):
            staged(j, 0).wait()
            staged(j, 1).wait()
        out[...] = acc[...].astype(BF)

    slots(0, 0)
    assemble()

    def wait_and_turn(i):
        slot(1 + i, 1, SPAN)
        pl.when(i < 4)(lambda: turn_rows(i))

    loop(SPAN, wait_and_turn)
    for i in range(13, 18):
        kept(i).start()
    arrived(0)
    attention(0, h0, hs[0], BESIDE[0])
    arrived(1)
    feed(1, hs[0], hs[1], BESIDE[1])
    arrived(2)
    attention(2, hs[1], hs[2], BESIDE[2])
    arrived(3)
    feed(3, hs[2], hs[3], None)

    kept(12).start()

    for copy in small_copies():
        copy.wait_send()
    for i in range(18):
        kept(i).wait()
    for s in range(4):
        for part in range(2):
            p = distance(s, part)

            def sent_out(k, s=s, part=part, p=p):
                core_copy(s, part, k).wait_send()
                pl.when((k < 4) & (p < 3))(ring_copy(s, part, jnp.minimum(k, 3)).wait_send)
                pl.when((k < 2) & (p > 0))(z_copy(s, part, jnp.minimum(k, 1), True).wait_send)

            loop(CHUNKS, sent_out)
        for i in range(4):
            pltpu.make_async_copy(held[s][i], keep[s][i], save_sem.at[4 * s + i]).wait()


def forward_call(w_in, w_out, h, small, pos, seg_col, seg_m, seg_t):
    t = h.shape[0]
    hbm = pl.BlockSpec(memory_space=pl.ANY)
    vmem = pl.BlockSpec(memory_space=pltpu.VMEM)
    weights = []
    for s in range(4):
        (a, b), (d, e) = unit_shape(s, 0), unit_shape(s, 1)
        weights += [(a, b), (a, b), (d, e), (d, e)]
    rows = sds((t, D), BF)
    out_shape = (
        [sds(w, BF) for w in weights]
        + [sds((t, FF), BF)] * 4
        + [sds((t, QKV), BF)] * 2
        + [sds((t, 2 * D), BF)] * 2
        + [rows] * 2
        + [sds((16, t), F32)] * 2
        + [rows] * 4
        + [sds((4, t, D), BF)]
        + [sds((t, D), F32)] * 4
        + [sds((4, 8, D), F32)]
    )
    dma = pltpu.SemaphoreType.DMA
    scratch = [pltpu.VMEM(x.shape, x.dtype) for x in out_shape[20:]]
    scratch += [pltpu.VMEM(w, BF) for w in weights] + [
        pltpu.VMEM((t, D), F32),
        pltpu.VMEM((2, t, FF // CHUNKS), BF),
        pltpu.VMEM((2, t, FF // CHUNKS), BF),
        pltpu.VMEM((t, 2 * HD), F32),
        pltpu.VMEM((8,) + small.shape, F32),
        pltpu.VMEM((4, 1, FF), F32),
        pltpu.VMEM((4, 1, D), F32),
        pltpu.VMEM((2, 2, D), F32),
        dma((4,)), dma((8, 4)), dma((8, 4)), dma((8, 2)), dma((8, 2)), dma((8, 6)), dma((8, 6)),
        dma((2, 4)), dma((16,)), dma((2, 2)), dma((8,)), dma((8,)), dma((18,)),
    ]
    out = pl.pallas_call(
        forward_kernel,
        out_shape=out_shape,
        in_specs=[hbm, hbm] + [vmem] * 6,
        out_specs=[hbm] * 38,
        scratch_shapes=scratch,
        compiler_params=pltpu.CompilerParams(
            collective_id=2, has_side_effects=True, vmem_limit_bytes=63 * 1024 * 1024
        ),
        name="forward",
    )(w_in, w_out, h, small, pos, seg_col, seg_m, seg_t)
    weights = [out[4 * s : 4 * s + 4] for s in range(4)]
    acts, slopes, qkvs, kv_ts, os, lses = (out[16 + 2 * i : 18 + 2 * i] for i in range(6))
    nrms, hs = out[28:32], out[32]
    saved = []
    for s in range(4):
        i = s // 2
        if s % 2 == 0:
            saved.append((qkvs[i], nrms[s], kv_ts[i], os[i], lses[i]))
        else:
            saved.append((acts[i], slopes[i], nrms[s]))
    return weights, saved, hs, (out[33:35], out[35:37]), out[37]


def small_row(dbin, rest, attends):
    dbin = jnp.pad(dbin.reshape(-1), (0, FF - dbin.size))
    dfreq = rest[3:5].reshape(2, HEADS, HD)[:, :, : HD // 2].reshape(-1)
    if not attends:
        dfreq = jnp.zeros_like(dfreq)
    return jnp.concatenate([dbin, rest[:3].reshape(-1), dfreq])


def carried_passes(weight_in, weight_out, h, g, small, freq, pos, seg_m, seg_t):
    section, core = lax.axis_index("section"), lax.axis_index("group")
    wide = jnp.concatenate([freq.reshape(2, PAIRS, HD // 2)] * 2, axis=2).reshape(-1)
    small = jnp.concatenate([*small, wide]).astype(F32)[None]
    weights, saved, streams, turns, pars = forward_call(
        weight_in[0], weight_out[0], h, small, pos, seg_m[:, None], seg_m[None], seg_t[None]
    )
    smalls, grads, in_grads = [None] * 4, [None] * 4, [None] * 4
    rows = (seg_m[None], seg_m[:, None], seg_t[:, None])

    def feed_back(s, g, carry, carried, leaving):
        act, slope, nrm = saved[s]
        grads[s], results, (dbin, rest, in_grads[s]) = feed_back_call(
            s, weights[s], act, slope, streams, g, nrm, pars[s], carry, carried, leaving, 3 + s
        )
        smalls[s] = small_row(dbin, rest, False)
        return results

    def attention_back(s, g, carry, carried):
        grads[s], results, (dbin, rest, in_grads[s]) = attention_back_call(
            s, weights[s], carry, carried, g, saved[s], *rows, turns[s // 2], pos,
            streams if s else h, pars[s], 3 + s,
        )
        smalls[s] = small_row(dbin, rest, True)
        return results

    (outputs,) = feed_back(3, g, None, (), ())
    quarters3 = attention_back(2, in_grads[3], Carry(3, (), ()), grads[3])
    early, *quarters2, first3, second3 = feed_back(
        1, in_grads[2], Carry(2, ((3, 0), (3, 1)), ()), (*grads[2], *quarters3),
        (in_grads[3], in_grads[2]),
    )
    *quarters1, first2, second2, held3 = attention_back(
        0, in_grads[1], Carry(1, ((2, 0), (2, 1)), ((3, 0),)), (*grads[1], *quarters2, first3)
    )
    sums, input_grads, small_sum = last_call(
        (*grads[0], *quarters1, second3, first2, second2), in_grads,
        jnp.stack(smalls).reshape(4, SMALL, 128),
    )
    first_rows = jnp.where(section >= 2, early, input_grads[:, :, : early.shape[2]])
    input_grads = jnp.concatenate([first_rows, input_grads[:, :, early.shape[2] :]], axis=2)
    first_a, second_a, first_f, second_f = sums
    second_a = in_place(second_a)
    in_a = jnp.concatenate([in_place(first_a), second_a[:HALF]], axis=1)
    both = jnp.concatenate([second_a[HALF:], flipped(second_a[HALF:], "group", 1)], axis=0)
    both = jnp.where(core == 0, jnp.pad(both, ((0, FF // 2 - D), (0, 0))), jnp.zeros((), BF))
    attends = section % 2 == 0
    in_f = in_place(jnp.where(section == 3, held3, first_f))
    out_in = jnp.where(attends, jnp.pad(in_a, ((0, 0), (0, FF - QKV))), in_f).astype(F32)
    out_out = jnp.where(attends, both, in_place(second_f)).astype(F32)
    return outputs.reshape(-1, D), input_grads.reshape(-1, D), out_in, out_out, small_sum.reshape(-1)


def plain_passes(weight_in, weight_out, h, g, small, freq, pos, seg_m, seg_t):
    section, group = lax.axis_index("section"), lax.axis_index("group")
    groups = lax.axis_size("group")
    small = jnp.concatenate([*small, freq.reshape(-1)])
    small = lax.all_gather(small, ("section", "group")).reshape(4, groups, -1).astype(F32)
    widths = [FF // groups, D // groups, D // groups, D // groups, D // groups]
    starts = [sum(widths[:i]) for i in range(5)]
    b_in, b_out, gain, shift, freq = (
        small[:, :, a : a + w] for a, w in zip(starts, widths)
    )
    b_in, b_out, gain, shift = (x.reshape(4, 1, -1) for x in (b_in, b_out, gain, shift))
    freq = freq.reshape(4, groups, 2, -1).transpose(0, 2, 1, 3).reshape(4, 2, D // 2)
    pars = [
        jnp.concatenate([gain[s], shift[s], jnp.zeros((6, D), F32)], axis=0) for s in range(4)
    ]
    turns = [turning(freq[s], pos) for s in (0, 2)]

    core = group % 2
    rot = jnp.zeros((1,), jnp.int32)
    all_in = lax.all_gather(weight_in, "group", axis=1, tiled=True)
    all_out = lax.all_gather(weight_out, "group", axis=1, tiled=True)
    all_in = lax.all_gather(all_in, "section", axis=0, tiled=True)
    all_out = lax.all_gather(all_out, "section", axis=0, tiled=True)
    weights, saved, streams = [], [], [h]
    for s in range(4):
        cols, rows = (QKV, D) if s % 2 == 0 else (FF, FF)
        w_in, w_out = all_in[s, :, :cols], all_out[s, :rows]
        weights.append((w_in[:HALF], w_in[HALF:], w_out[: rows // 2], w_out[rows // 2 :]))
        wia, wib, woa, wob = weights[s]
        if s % 2 == 0:
            cosines, sines = turns[s // 2]
            qkv, nrm = qkv_call(rot, h, pars[s], wia, wib, b_in[s, :, :QKV], cosines, sines)
            kv_t = flipped(qkv[:, D:], "group", 1)
            o, lse, h = attend_call(
                rot, qkv, kv_t, seg_m[:, None], seg_m[None], seg_t[None], h, woa, wob, b_out[s]
            )
            saved.append((qkv, nrm, kv_t, o, lse))
        else:
            act, slope, nrm, h = ff_call(rot, h, pars[s], wia, wib, b_in[s], woa, wob, b_out[s])
            saved.append((act, slope, nrm))
        streams.append(h)
    outputs = to_owners(streams[1:], section, core)
    smalls, grads, in_grads = [None] * 4, [None] * 4, [None] * 4
    for s in (3, 2, 1, 0):
        wia, wib, woa, wob = weights[s]
        if s % 2 == 0:
            qkv, nrm, kv_t, o, lse = saved[s]
            cosines, sines = turns[s // 2]
            dmix, delta, doa, dob = mix_back_call(rot, g, o, woa, wob)
            dq, dkm, dvm, dkt, dvt = attend_back_call(
                qkv, kv_t, dmix, lse, delta, seg_m[None], seg_m[:, None], seg_t[:, None]
            )
            dkr, dvr = flipped(dkt, "group", 1), flipped(dvt, "group", 1)
            dia, dib, dbin, rest, g = qkv_back_call(
                rot, dq, dkm, dvm, dkr, dvr, qkv, cosines, sines, pos, nrm, wia, wib,
                streams[s], pars[s], g,
            )
        else:
            act, slope, nrm = saved[s]
            dia, dib, doa, dob, dbin, rest, g = ff_back_call(
                rot, g, act, slope, nrm, wia, wib, woa, wob, streams[s], pars[s]
            )
        in_grads[s] = g
        grads[s] = (
            jnp.pad(jnp.concatenate([dia, dib]), ((0, 0), (0, FF - dia.shape[1]))),
            jnp.pad(jnp.concatenate([doa, dob]), ((0, FF - 2 * doa.shape[0]), (0, 0))),
        )
        smalls[s] = small_row(dbin, rest, s % 2 == 0)
    input_grads = to_owners(in_grads, section, core)
    small_sum = lax.psum(jnp.stack(smalls), ("section", "group", "dp"))[section]

    def owned(x):
        x = lax.psum_scatter(x, "section", scatter_dimension=0, tiled=True)[0]
        x = lax.psum_scatter(x, "group", scatter_dimension=0, tiled=True)
        return lax.psum(x, "dp").astype(F32)

    out_in = owned(jnp.stack([x[0] for x in grads]))
    out_out = owned(jnp.stack([x[1] for x in grads]))
    return outputs, input_grads, out_in, out_out, small_sum


def body(
    activations, weight_in, weight_out, bias_in, bias_out, norm_gain, norm_shift, rope_freq,
    image_sides, cotangent,
):
    sections = lax.axis_size("section")
    groups = lax.axis_size("group")
    section = lax.axis_index("section")
    group = lax.axis_index("group")
    core = group % 2
    micro = image_sides.shape[0]
    capacity = activations.shape[0] // micro
    tokens = capacity // 2
    assert sections == 4 and groups % 2 == 0 and 2 * micro == sections
    fast = groups == 2 and lax.axis_size("dp") == 4

    here = (section // 2) == core
    local = section % 2

    def take(x):
        own = lax.dynamic_index_in_dim(x.reshape(micro, capacity, D), local, 0, keepdims=False)
        give = lax.dynamic_slice_in_dim(own, (1 - core) * tokens, tokens, 0)
        keep = lax.dynamic_slice_in_dim(own, core * tokens, tokens, 0)
        return jnp.where(here, keep, flipped(give, "group", 1))

    h = take(activations)
    own_sides = lax.dynamic_index_in_dim(image_sides, local, 0, keepdims=False)
    sides = jnp.where(here, own_sides, flipped(own_sides, "group", 1))
    segment, patch_row, patch_col, is_valid = layout(sides, capacity)
    pos_all = jnp.stack([patch_col, patch_row], axis=1).astype(F32)

    def half_of(x, which):
        return lax.dynamic_slice_in_dim(x, which * tokens, tokens, 0)

    pos = half_of(pos_all, core)
    seg_m, seg_t = half_of(segment, core), half_of(segment, 1 - core)
    valid = half_of(is_valid, core)
    g = take(cotangent) * valid[:, None].astype(BF)

    passes = carried_passes if fast else plain_passes
    outputs, input_grads, out_in, out_out, small_sum = passes(
        weight_in, weight_out, h, g, (bias_in[0], bias_out[0], norm_gain[0], norm_shift[0]),
        rope_freq[0], pos, seg_m, seg_t,
    )

    def piece(start, width):
        w = width // groups
        return lax.dynamic_slice_in_dim(small_sum, start + group * w, w, 0)[None]

    d_freq = small_sum[FF + 3 * D :].reshape(2, D // 2)
    d_freq = lax.dynamic_slice_in_dim(d_freq, group * (D // 2 // groups), D // 2 // groups, 1)
    return (
        outputs[None],
        input_grads[None],
        out_in[None],
        out_out[None],
        piece(0, FF),
        piece(FF, D),
        piece(FF + D, D),
        piece(FF + 2 * D, D),
        d_freq[None],
    )


def solution(mesh):
    placed = (
        P(("group", "dp"), None),
        P("section", "group", None),
        P("section", "group", None),
        P("section", "group"),
        P("section", "group"),
        P("section", "group"),
        P("section", "group"),
        P("section", None, "group"),
        P(("group", "dp"), None),
        P(("group", "dp"), None),
    )
    return jax.shard_map(
        body,
        mesh=mesh,
        in_specs=placed,
        out_specs=(
            P("section", ("group", "dp"), None),
            P("section", ("group", "dp"), None),
            P("section", "group", None),
            P("section", "group", None),
            P("section", "group"),
            P("section", "group"),
            P("section", "group"),
            P("section", "group"),
            P("section", None, "group"),
        ),
        check_vma=False,
    )
```

```python
from functools import partial

import jax
import jax.numpy as jnp
from jax import lax
from jax.experimental import pallas as pl
from jax.experimental.pallas import tpu as pltpu
from jax.sharding import PartitionSpec as P

D = 768
HEADS = 12
HD = 64
FF = 3072
HALF = D // 2
PAIRS = HEADS // 2
QKV = 3 * D
EPSILON = 1e-06
BF = jnp.bfloat16
F32 = jnp.float32
NT = (((1,), (1,)), ((), ()))
TN = (((0,), (0,)), ((), ()))
VMEM_BYTES = 52 * 1024 * 1024


def dot(a, b):
    return jnp.dot(a, b, preferred_element_type=F32)


def dot_nt(a, b):
    return lax.dot_general(a, b, NT, preferred_element_type=F32)


def dot_tn(a, b):
    return lax.dot_general(a, b, TN, preferred_element_type=F32)


def normalize(h):
    average = jnp.mean(h, axis=-1, keepdims=True)
    centered = h - average
    variance = jnp.mean(centered * centered, axis=-1, keepdims=True)
    scale = lax.rsqrt(variance + EPSILON)
    return centered * scale, scale


def turn_halves(x, rot):
    return jnp.where(rot == 0, x, jnp.concatenate([x[:, HALF:], x[:, :HALF]], axis=1))


def swap_pairs(x):
    lanes = lax.broadcasted_iota(jnp.int32, x.shape, 1)
    low = (lanes % HD) < HD // 2
    return jnp.where(
        low, pltpu.roll(x, x.shape[1] - HD // 2, 1), pltpu.roll(x, HD // 2, 1)
    )


def norm_backward(h, gain, grad, d_normed):
    xhat, scale = normalize(h)
    e = d_normed * gain
    mean_e = jnp.mean(e, axis=-1, keepdims=True)
    mean_ex = jnp.mean(e * xhat, axis=-1, keepdims=True)
    g = grad + scale * (e - mean_e - xhat * mean_ex)
    d_gain = jnp.sum(d_normed * xhat, axis=0, keepdims=True)
    d_shift = jnp.sum(d_normed, axis=0, keepdims=True)
    return g, d_gain, d_shift


def qkv_kernel(rot_ref, h_ref, par_ref, wa_ref, wb_ref, bias_ref, cos_ref, sin_ref, out_ref, nrm_ref):
    j = pl.program_id(0)

    @pl.when(j == 0)
    def _():
        xhat, _ = normalize(h_ref[...].astype(F32))
        normed = xhat * par_ref[0:1, :] + par_ref[1:2, :]
        nrm_ref[...] = turn_halves(normed, rot_ref[0]).astype(BF)

    x = dot(nrm_ref[:, :HALF], wa_ref[...]) + dot(nrm_ref[:, HALF:], wb_ref[...]) + bias_ref[...]

    @pl.when(j < 2)
    def _():
        y = x * cos_ref[...] + swap_pairs(x) * sin_ref[...]
        out_ref[...] = (y * jnp.where(j == 0, HD ** (-0.5), 1.0)).astype(BF)

    @pl.when(j == 2)
    def _():
        out_ref[...] = x.astype(BF)


def attend_kernel(
    rot_ref, q_ref, km_ref, vm_ref, kt_ref, vt_ref, segq_ref, segm_ref, segt_ref, h_ref,
    woa_ref, wob_ref, bias_ref, o_ref, lse_ref, out_ref, lse_scr,
):
    j = pl.program_id(0)
    rows = q_ref.shape[0]
    lanes = lax.broadcasted_iota(jnp.int32, (rows, 2 * HD), 1)
    q = q_ref[...]
    same_m = segq_ref[...] == segm_ref[...]
    same_t = segq_ref[...] == segt_ref[...]
    outs = []
    for side in range(2):
        mine = (lanes >= HD) if side else (lanes < HD)
        q_head = jnp.where(mine, q, jnp.zeros_like(q))
        s_m = jnp.where(same_m, dot_nt(q_head, km_ref[...]), -1e9)
        s_t = jnp.where(same_t, dot_nt(q_head, kt_ref[...]), -1e9)
        top = jnp.maximum(
            jnp.max(s_m, axis=-1, keepdims=True), jnp.max(s_t, axis=-1, keepdims=True)
        )
        p_m = jnp.exp(s_m - top)
        p_t = jnp.exp(s_t - top)
        total = jnp.sum(p_m, axis=-1, keepdims=True) + jnp.sum(p_t, axis=-1, keepdims=True)
        o = dot(p_m.astype(BF), vm_ref[...]) + dot(p_t.astype(BF), vt_ref[...])
        outs.append(o / total)
        lse_scr[...] = jnp.where(lanes == 2 * j + side, top + jnp.log(total), lse_scr[...])
    o_ref[:, pl.ds(pl.multiple_of(j * 2 * HD, 2 * HD), 2 * HD)] = jnp.where(
        lanes < HD, outs[0], outs[1]
    ).astype(BF)

    @pl.when(j == PAIRS - 1)
    def _():
        lse_ref[...] = jnp.transpose(lse_scr[...])[:16, :]
        o_all = turn_halves(o_ref[...].astype(F32), rot_ref[0]).astype(BF)
        y = dot(o_all[:, :HALF], woa_ref[...]) + dot(o_all[:, HALF:], wob_ref[...])
        out_ref[...] = (h_ref[...].astype(F32) + y + bias_ref[...]).astype(BF)


def ff_kernel(
    rot_ref, h_ref, par_ref, wia_ref, wib_ref, bias_ref, woa_ref, wob_ref, bout_ref,
    act_ref, slope_ref, nrm_ref, out_ref, acc_ref,
):
    j = pl.program_id(0)
    n = pl.num_programs(0)

    @pl.when(j == 0)
    def _():
        xhat, _ = normalize(h_ref[...].astype(F32))
        normed = xhat * par_ref[0:1, :] + par_ref[1:2, :]
        nrm_ref[...] = turn_halves(normed, rot_ref[0]).astype(BF)
        acc_ref[...] = h_ref[...].astype(F32) + bout_ref[...]

    u = dot(nrm_ref[:, :HALF], wia_ref[...]) + dot(nrm_ref[:, HALF:], wib_ref[...]) + bias_ref[...]
    cdf = 0.5 + 0.5 * lax.erf(u * (0.5**0.5))
    act = (u * cdf).astype(BF)
    act_ref[...] = act
    pdf = jnp.exp(u * u * -0.5) * 0.3989422804014327
    slope_ref[...] = (cdf + u * pdf).astype(BF)

    @pl.when(j < n // 2)
    def _():
        acc_ref[...] += dot(act, woa_ref[...])

    @pl.when(j >= n // 2)
    def _():
        acc_ref[...] += dot(act, wob_ref[...])

    @pl.when(j == n - 1)
    def _():
        out_ref[...] = acc_ref[...].astype(BF)


def ff_back_kernel(
    rot_ref, g_ref, act_ref, slope_ref, nrm_ref, wia_ref, wib_ref, woa_ref, wob_ref, h_ref, par_ref,
    dia_ref, dib_ref, doa_ref, dob_ref, dbin_ref, small_ref, out_ref, acc_ref,
):
    j = pl.program_id(0)
    n = pl.num_programs(0)

    @pl.when(j == 0)
    def _():
        acc_ref[...] = jnp.zeros_like(acc_ref)

    def step(wo_ref, do_ref):
        g = g_ref[...]
        d_up_f = dot_nt(g, wo_ref[...]) * slope_ref[...].astype(F32)
        d_up = d_up_f.astype(BF)
        do_ref[...] = dot_tn(act_ref[...], g).astype(BF)
        dbin_ref[...] = jnp.sum(d_up_f, axis=0, keepdims=True)
        dia_ref[...] = dot_tn(nrm_ref[:, :HALF], d_up).astype(BF)
        dib_ref[...] = dot_tn(nrm_ref[:, HALF:], d_up).astype(BF)
        acc_ref[:, :HALF] += dot_nt(d_up, wia_ref[...])
        acc_ref[:, HALF:] += dot_nt(d_up, wib_ref[...])

    @pl.when(j < n // 2)
    def _():
        step(woa_ref, doa_ref)

    @pl.when(j >= n // 2)
    def _():
        step(wob_ref, dob_ref)

    @pl.when(j == n - 1)
    def _():
        g = g_ref[...].astype(F32)
        d_normed = turn_halves(acc_ref[...], rot_ref[0])
        out, d_gain, d_shift = norm_backward(h_ref[...].astype(F32), par_ref[0:1, :], g, d_normed)
        out_ref[...] = out.astype(BF)
        small_ref[0:1, :] = jnp.sum(g, axis=0, keepdims=True)
        small_ref[1:2, :] = d_gain
        small_ref[2:3, :] = d_shift
        small_ref[3:8, :] = jnp.zeros((5, D), F32)


def mix_back_kernel(rot_ref, g_ref, o_ref, woa_ref, wob_ref, dmix_ref, delta_ref, doa_ref, dob_ref):
    g = g_ref[...]
    rot = rot_ref[0]
    d_mix = jnp.concatenate([dot_nt(g, woa_ref[...]), dot_nt(g, wob_ref[...])], axis=1)
    d_mix = turn_halves(d_mix, rot).astype(BF)
    dmix_ref[...] = d_mix
    o = o_ref[...].astype(F32)
    product = d_mix.astype(F32) * o
    head = lax.broadcasted_iota(jnp.int32, (16, D), 0)
    lanes = lax.broadcasted_iota(jnp.int32, (16, D), 1)
    chosen = jnp.where(lanes // HD == head, 1.0, 0.0)
    delta_ref[...] = lax.dot_general(
        chosen, product, NT, preferred_element_type=F32, precision=lax.Precision.HIGHEST
    )
    turned = turn_halves(o, rot).astype(BF)
    doa_ref[...] = dot_tn(turned[:, :HALF], g).astype(BF)
    dob_ref[...] = dot_tn(turned[:, HALF:], g).astype(BF)


def attend_back_kernel(
    q_ref, km_ref, vm_ref, kt_ref, vt_ref, do_ref, lse_ref, delta_ref, segq_ref, segm_ref, segt_ref,
    dq_ref, dkm_ref, dvm_ref, dkt_ref, dvt_ref,
):
    j = pl.program_id(0)
    rows = q_ref.shape[0]
    lanes = lax.broadcasted_iota(jnp.int32, (rows, 2 * HD), 1)
    q = q_ref[...]
    do = do_ref[...]
    zero = jnp.zeros_like(q)
    d_q = jnp.zeros((rows, 2 * HD), F32)
    sets = ((km_ref, vm_ref, segm_ref), (kt_ref, vt_ref, segt_ref))
    d_k = [0.0, 0.0]
    d_v = [0.0, 0.0]
    for side in range(2):
        mine = (lanes >= HD) if side else (lanes < HD)
        q_head = jnp.where(mine, q, zero)
        do_head = jnp.where(mine, do, zero)
        lse = lse_ref[pl.ds(2 * j + side, 1), :]
        delta = delta_ref[pl.ds(2 * j + side, 1), :]
        for i, (k_ref, v_ref, seg_ref) in enumerate(sets):
            k = k_ref[...]
            s_t = dot_nt(k, q_head)
            p_t = jnp.where(seg_ref[...] == segq_ref[...], jnp.exp(s_t - lse), 0.0)
            d_p = dot_nt(v_ref[...], do_head)
            d_s = (p_t * (d_p - delta)).astype(BF)
            d_v[i] += dot(p_t.astype(BF), do_head)
            d_k[i] += dot(d_s, q_head)
            d_q += dot_tn(d_s, jnp.where(mine, k, zero))
    dq_ref[...] = d_q
    dkm_ref[...] = d_k[0]
    dvm_ref[...] = d_v[0]
    dkt_ref[...] = d_k[1].astype(BF)
    dvt_ref[...] = d_v[1].astype(BF)


def qkv_back_kernel(
    rot_ref, dq_ref, dkm_ref, dvm_ref, dkr_ref, dvr_ref, qkv_ref, cos_ref, sin_ref, pos_ref,
    nrm_ref, wa_ref, wb_ref, h_ref, par_ref, g_ref,
    dia_ref, dib_ref, dbin_ref, small_ref, out_ref, acc_ref, dp_ref,
):
    j = pl.program_id(0)
    n = pl.num_programs(0)

    @pl.when(j == 0)
    def _():
        acc_ref[...] = jnp.zeros_like(acc_ref)
        small_ref[...] = jnp.zeros_like(small_ref)

    def turned_back(dy, y):
        swapped = swap_pairs(dy)
        d_angle = y * swapped - swap_pairs(y) * dy
        small_ref[3:4, :] += jnp.sum(d_angle * pos_ref[:, 0:1], axis=0, keepdims=True)
        small_ref[4:5, :] += jnp.sum(d_angle * pos_ref[:, 1:2], axis=0, keepdims=True)
        return dy * cos_ref[...] - swapped * sin_ref[...]

    @pl.when(j == 0)
    def _():
        d_y = dq_ref[...] * HD ** (-0.5)
        y = qkv_ref[...].astype(F32) * HD**0.5
        dp_ref[...] = turned_back(d_y, y)

    @pl.when(j == 1)
    def _():
        d_y = dkm_ref[...] + dkr_ref[...].astype(F32)
        dp_ref[...] = turned_back(d_y, qkv_ref[...].astype(F32))

    @pl.when(j == 2)
    def _():
        dp_ref[...] = dvm_ref[...] + dvr_ref[...].astype(F32)

    d_f = dp_ref[...]
    d_p = d_f.astype(BF)
    dbin_ref[...] = jnp.sum(d_f, axis=0, keepdims=True)
    dia_ref[...] = dot_tn(nrm_ref[:, :HALF], d_p).astype(BF)
    dib_ref[...] = dot_tn(nrm_ref[:, HALF:], d_p).astype(BF)
    acc_ref[:, :HALF] += dot_nt(d_p, wa_ref[...])
    acc_ref[:, HALF:] += dot_nt(d_p, wb_ref[...])

    @pl.when(j == n - 1)
    def _():
        g = g_ref[...].astype(F32)
        d_normed = turn_halves(acc_ref[...], rot_ref[0])
        out, d_gain, d_shift = norm_backward(h_ref[...].astype(F32), par_ref[0:1, :], g, d_normed)
        out_ref[...] = out.astype(BF)
        small_ref[0:1, :] = jnp.sum(g, axis=0, keepdims=True)
        small_ref[1:2, :] = d_gain
        small_ref[2:3, :] = d_shift


def params_of(n=1):
    return pltpu.CompilerParams(
        dimension_semantics=("arbitrary",) * n, vmem_limit_bytes=VMEM_BYTES
    )


def whole(shape):
    return pl.BlockSpec(shape, lambda *_: (0,) * len(shape))


def sds(shape, dtype):
    return jax.ShapeDtypeStruct(shape, dtype)


def cost(flops, nbytes, trans=0):
    return pl.CostEstimate(flops=flops, bytes_accessed=nbytes, transcendentals=trans)


def qkv_call(rot, h, par, wa, wb, bias, cosines, sines):
    t = h.shape[0]
    return pl.pallas_call(
        qkv_kernel,
        out_shape=(sds((t, QKV), BF), sds((t, D), BF)),
        grid_spec=pltpu.PrefetchScalarGridSpec(
            num_scalar_prefetch=1,
            grid=(3,),
            in_specs=[
                whole((t, D)), whole((8, D)),
                pl.BlockSpec((HALF, D), lambda j, r: (0, j)),
                pl.BlockSpec((HALF, D), lambda j, r: (0, j)),
                pl.BlockSpec((1, D), lambda j, r: (0, j)),
                whole((t, D)), whole((t, D)),
            ],
            out_specs=[pl.BlockSpec((t, D), lambda j, r: (0, j)), whole((t, D))],
        ),
        compiler_params=params_of(),
        cost_estimate=cost(2 * t * D * QKV, 2 * D * QKV + 8 * t * D + 2 * t * QKV),
        name="qkv",
    )(rot, h, par, wa, wb, bias, cosines, sines)


def attend_call(rot, qkv, kv_t, seg_col, seg_m, seg_t, h, woa, wob, bias):
    t = h.shape[0]
    w = 2 * HD
    return pl.pallas_call(
        attend_kernel,
        out_shape=(sds((t, D), BF), sds((16, t), F32), sds((t, D), BF)),
        grid_spec=pltpu.PrefetchScalarGridSpec(
            num_scalar_prefetch=1,
            grid=(PAIRS,),
            in_specs=[
                pl.BlockSpec((t, w), lambda j, r: (0, j)),
                pl.BlockSpec((t, w), lambda j, r: (0, j + PAIRS)),
                pl.BlockSpec((t, w), lambda j, r: (0, j + 2 * PAIRS)),
                pl.BlockSpec((t, w), lambda j, r: (0, j)),
                pl.BlockSpec((t, w), lambda j, r: (0, j + PAIRS)),
                whole((t, 1)), whole((1, t)), whole((1, t)), whole((t, D)),
                whole((HALF, D)), whole((HALF, D)), whole((1, D)),
            ],
            out_specs=[whole((t, D)), whole((16, t)), whole((t, D))],
            scratch_shapes=[pltpu.VMEM((t, w), F32)],
        ),
        compiler_params=params_of(),
        cost_estimate=cost(8 * t * t * D * 4, 16 * t * D, 2 * t * t * HEADS),
        name="attend",
    )(rot, qkv, qkv, qkv, kv_t, kv_t, seg_col, seg_m, seg_t, h, woa, wob, bias)


def ff_specs(t, blocks):
    width = FF // blocks
    half = blocks // 2
    w_in = pl.BlockSpec((HALF, width), lambda j, r: (0, (j + half * r[0]) % blocks))
    b_in = pl.BlockSpec((1, width), lambda j, r: (0, (j + half * r[0]) % blocks))
    w_a = pl.BlockSpec((width, D), lambda j, r: (jnp.minimum(j, half - 1), 0))
    w_b = pl.BlockSpec((width, D), lambda j, r: (jnp.maximum(j - half, 0), 0))
    hid = pl.BlockSpec((t, width), lambda j, r: (0, j))
    return w_in, b_in, w_a, w_b, hid


def ff_call(rot, h, par, wia, wib, bias, woa, wob, bout):
    t = h.shape[0]
    blocks = 6
    w_in, b_in, w_a, w_b, hid = ff_specs(t, blocks)
    return pl.pallas_call(
        ff_kernel,
        out_shape=(sds((t, FF), BF), sds((t, FF), BF), sds((t, D), BF), sds((t, D), BF)),
        grid_spec=pltpu.PrefetchScalarGridSpec(
            num_scalar_prefetch=1,
            grid=(blocks,),
            in_specs=[whole((t, D)), whole((8, D)), w_in, w_in, b_in, w_a, w_b, whole((1, D))],
            out_specs=[hid, hid, whole((t, D)), whole((t, D))],
            scratch_shapes=[pltpu.VMEM((t, D), F32)],
        ),
        compiler_params=params_of(),
        cost_estimate=cost(4 * t * D * FF, 4 * D * FF + 4 * t * FF, 2 * t * FF),
        name="feed",
    )(rot, h, par, wia, wib, bias, woa, wob, bout)


def ff_back_call(rot, g, act, slope, nrm, wia, wib, woa, wob, h, par):
    t = h.shape[0]
    blocks = 6
    w_in, b_in, w_a, w_b, hid = ff_specs(t, blocks)
    return pl.pallas_call(
        ff_back_kernel,
        out_shape=(
            sds((HALF, FF), BF), sds((HALF, FF), BF), sds((FF // 2, D), BF), sds((FF // 2, D), BF),
            sds((1, FF), F32), sds((8, D), F32), sds((t, D), BF),
        ),
        grid_spec=pltpu.PrefetchScalarGridSpec(
            num_scalar_prefetch=1,
            grid=(blocks,),
            in_specs=[
                whole((t, D)), hid, hid, whole((t, D)), w_in, w_in, w_a, w_b, whole((t, D)),
                whole((8, D)),
            ],
            out_specs=[w_in, w_in, w_a, w_b, b_in, whole((8, D)), whole((t, D))],
            scratch_shapes=[pltpu.VMEM((t, D), F32)],
        ),
        compiler_params=params_of(),
        cost_estimate=cost(8 * t * D * FF, 8 * D * FF + 4 * t * FF),
        name="feed_back",
    )(rot, g, act, slope, nrm, wia, wib, woa, wob, h, par)


def mix_back_call(rot, g, o, woa, wob):
    t = g.shape[0]
    return pl.pallas_call(
        mix_back_kernel,
        out_shape=(sds((t, D), BF), sds((16, t), F32), sds((HALF, D), BF), sds((HALF, D), BF)),
        grid_spec=pltpu.PrefetchScalarGridSpec(
            num_scalar_prefetch=1,
            grid=(1,),
            in_specs=[whole((t, D)), whole((t, D)), whole((HALF, D)), whole((HALF, D))],
            out_specs=[whole((t, D)), whole((16, t)), whole((HALF, D)), whole((HALF, D))],
        ),
        compiler_params=params_of(),
        cost_estimate=cost(4 * t * D * D, 4 * D * D + 6 * t * D),
        name="mix_back",
    )(rot, g, o, woa, wob)


def attend_back_call(qkv, kv_t, dmix, lse, delta, seg_row, seg_m, seg_t):
    t = dmix.shape[0]
    w = 2 * HD
    col = pl.BlockSpec((t, w), lambda j: (0, j))
    return pl.pallas_call(
        attend_back_kernel,
        out_shape=(sds((t, D), F32), sds((t, D), F32), sds((t, D), F32), sds((t, D), BF), sds((t, D), BF)),
        grid=(PAIRS,),
        in_specs=[
            col,
            pl.BlockSpec((t, w), lambda j: (0, j + PAIRS)),
            pl.BlockSpec((t, w), lambda j: (0, j + 2 * PAIRS)),
            col,
            pl.BlockSpec((t, w), lambda j: (0, j + PAIRS)),
            col, whole((16, t)), whole((16, t)), whole((1, t)), whole((t, 1)), whole((t, 1)),
        ],
        out_specs=[col] * 5,
        compiler_params=params_of(),
        cost_estimate=cost(20 * t * t * D * 4, 30 * t * D, 2 * t * t * HEADS),
        name="attend_back",
    )(qkv, qkv, qkv, kv_t, kv_t, dmix, lse, delta, seg_row, seg_m, seg_t)


def qkv_back_call(rot, dq, dkm, dvm, dkr, dvr, qkv, cosines, sines, pos, nrm, wa, wb, h, par, g):
    t = h.shape[0]
    w_in = pl.BlockSpec((HALF, D), lambda j, r: (0, j))
    rows = whole((t, D))
    return pl.pallas_call(
        qkv_back_kernel,
        out_shape=(
            sds((HALF, QKV), BF), sds((HALF, QKV), BF), sds((1, QKV), F32), sds((8, D), F32),
            sds((t, D), BF),
        ),
        grid_spec=pltpu.PrefetchScalarGridSpec(
            num_scalar_prefetch=1,
            grid=(3,),
            in_specs=[
                rows, rows, rows, rows, rows, pl.BlockSpec((t, D), lambda j, r: (0, j)), rows, rows,
                whole((t, 2)), rows, w_in, w_in, rows, whole((8, D)), rows,
            ],
            out_specs=[w_in, w_in, pl.BlockSpec((1, D), lambda j, r: (0, j)), whole((8, D)), rows],
            scratch_shapes=[pltpu.VMEM((t, D), F32), pltpu.VMEM((t, D), F32)],
        ),
        compiler_params=params_of(),
        cost_estimate=cost(4 * t * D * QKV, 4 * D * QKV + 30 * t * D),
        name="qkv_back",
    )(rot, dq, dkm, dvm, dkr, dvr, qkv, cosines, sines, pos, nrm, wa, wb, h, par, g)


def layout(image_sides, capacity):
    counts = image_sides * image_sides
    end_pos = jnp.cumsum(counts)
    start_pos = end_pos - counts
    positions = jnp.arange(capacity, dtype=jnp.int32)
    segment = jnp.sum((positions[:, None] >= end_pos[None, :]).astype(jnp.int32), axis=1)
    slot_ids = jnp.arange(image_sides.shape[-1], dtype=jnp.int32)
    one_hot = (segment[:, None] == slot_ids[None, :]).astype(jnp.int32)
    start_tok = jnp.sum(one_hot * start_pos[None, :], axis=1)
    side_len = jnp.maximum(jnp.sum(one_hot * image_sides[None, :], axis=1), 1)
    local_idx = positions - start_tok
    is_valid = segment < image_sides.shape[-1]
    patch_row = jnp.where(is_valid, local_idx // side_len, 0)
    patch_col = jnp.where(is_valid, local_idx % side_len, 0)
    return segment, patch_row, patch_col, is_valid


def turning(freq, pos):
    wide = jnp.concatenate([freq.reshape(2, HEADS, HD // 2)] * 2, axis=2).reshape(2, D)
    angles = pos[:, 0:1] * wide[0][None, :] + pos[:, 1:2] * wide[1][None, :]
    low = (jnp.arange(D) % HD) < HD // 2
    sines = jnp.sin(angles)
    return jnp.cos(angles), jnp.where(low[None, :], -sines, sines)


def flipped(x, axis, bit):
    return lax.ppermute(x, axis, [(i, i ^ bit) for i in range(lax.axis_size(axis))])


def to_owners(blocks, section, core):
    stacked = jnp.stack(blocks)
    got = [stacked[section]] + [flipped(stacked[section ^ d], "section", d) for d in (1, 2, 3)]
    here = (section // 2) == core
    near = jnp.stack(got[:2])
    away = jnp.stack(got[2:])
    mine = jnp.where(here, near, away)
    other = flipped(jnp.where(here, away, near), "group", 1)

    def in_order(pair):
        return jnp.where(section % 2 == 0, pair, pair[::-1])

    mine, other = in_order(mine), in_order(other)
    first = jnp.where(core == 0, mine, other)
    second = jnp.where(core == 0, other, mine)
    return jnp.concatenate([first, second], axis=1).reshape(-1, D)


MESH = pl.DeviceIdType.MESH
SMALL = (16, D)
SEMS = 20
LINE = 4


def unit_shape(s, part):
    if s % 2:
        return (FF // 2, D) if part else (HALF, FF)
    return (HALF, D) if part else (HALF, QKV)


def grad_shape(s, part):
    if s % 2:
        return (FF // 2, D) if part else (HALF, FF)
    return (D, D) if part else (HALF, 2 * D)


def piece_shape(s, part):
    r, w = grad_shape(s, part)
    return (r // 8, w // 2)


def held_shape(s, part):
    r, w = grad_shape(s, part)
    return (4, 2, r // 8, w)


def columns_of(k, width):
    return pl.ds(pl.multiple_of((k % 2) * width, width), width)


def flip(v, bit):
    if bit == 1:
        return v + 1 - 2 * (v % 2)
    if bit == 2:
        return (v + 2) % 4
    return 3 - v


def here():
    return lax.axis_index("section"), lax.axis_index("group"), lax.axis_index("dp")


def loop(n, body):
    def one(i, carried):
        body(i)
        return carried

    lax.fori_loop(0, n, one, 0)


def greet(plane, line):
    c, g, z = here()
    barrier = pltpu.get_barrier_semaphore()
    pl.semaphore_signal(barrier, inc=1, device_id={"group": 1 - g}, device_id_type=MESH)
    count = 1
    for bit in (1, 2, 3):
        if plane:
            for core in (g, 1 - g):
                pl.semaphore_signal(
                    barrier, inc=1, device_id={"section": flip(c, bit), "group": core},
                    device_id_type=MESH,
                )
                count += 1
        if line:
            pl.semaphore_signal(barrier, inc=1, device_id={"dp": flip(z, bit)}, device_id_type=MESH)
            count += 1
    pl.semaphore_wait(barrier, count)


def guarded(cond, act):
    if cond is None:
        act()
    else:
        pl.when(cond)(act)


def accumulate(into, term, rows):
    strip = 32 if rows % 32 == 0 else 16

    def one(i):
        at = pl.ds(pl.multiple_of(i * strip, strip), strip)
        into[at, :] = (into[at, :].astype(F32) + term[at, :].astype(F32)).astype(BF)

    loop(rows // strip, one)


class Unit:
    def __init__(
        self, s, part, send, recv, own=None, quarter=None, final=None, plane=None, line=None,
        held=None, whole=None,
    ):
        self.s, self.part, self.own, self.quarter_ref, self.final = s, part, own, quarter, final
        self.send, self.recv = send, recv
        self.whole = whole
        self.rows, self.cols = grad_shape(s, part)
        self.plane1, self.plane2 = plane or (None, None)
        self.up_in, self.down_in = line or (None, None)
        self.held = held
        self.pending = []

    def push(self, cond, src, dst, k, device):
        copy = pltpu.make_async_remote_copy(
            src_ref=src, dst_ref=dst, send_sem=self.send.at[k], recv_sem=self.recv.at[k],
            device_id=device, device_id_type=MESH,
        )
        guarded(cond, copy.start)
        self.pending.append((cond, copy))

    def landed(self, cond, dst, k):
        copy = pltpu.make_async_remote_copy(
            src_ref=dst, dst_ref=dst, send_sem=self.send.at[k], recv_sem=self.recv.at[k],
            device_id={"group": 1 - lax.axis_index("group")}, device_id_type=MESH,
        )
        guarded(cond, copy.wait_recv)

    def finish(self):
        for cond, copy in self.pending:
            guarded(cond, copy.wait_send)

    def quarter(self, q):
        rows = self.rows // 4
        return self.own.at[pl.ds(pl.multiple_of(q * rows, rows), rows), :]

    def mine(self):
        if self.quarter_ref is not None:
            return self.quarter_ref
        return self.quarter(lax.axis_index("section"))

    def piece(self, k):
        rows, cols = self.rows // 8, self.cols // 2
        return self.mine().at[
            pl.ds(pl.multiple_of((k // 2) * rows, rows), rows),
            pl.ds(pl.multiple_of((k % 2) * cols, cols), cols),
        ]

    def first_step(self):
        c, _, _ = here()
        x, y = c % 2, c // 2
        other = {"section": flip(c, 2 if self.part else 1)}
        for b in range(2):
            q = 2 * (1 - y) + b if self.part else 2 * b + 1 - x
            self.push(None, self.quarter(q), self.plane1.at[b], 1 + b, other)

    def second_step(self):
        c, _, _ = here()
        x, y = c % 2, c // 2
        rows = self.rows // 4
        other = {"section": flip(c, 1 if self.part else 2)}
        for b in range(2):
            self.landed(None, self.plane1.at[b], 1 + b)
        b = (1 - x) if self.part else (1 - y)
        q = (2 * y + 1 - x) if self.part else (2 * (1 - y) + x)
        accumulate(self.quarter(q), self.plane1.at[b], rows)
        self.push(None, self.quarter(q), self.plane2, 3, other)
        accumulate(self.mine(), self.plane1.at[1 - b], rows)

    def third_step(self):
        self.landed(None, self.plane2, 3)
        accumulate(self.mine(), self.plane2, self.rows // 4)

    def line_step(self, t):
        _, _, z = here()
        n = LINE
        rows = self.rows // 8
        up = (z < n - 1) & (z <= t)
        down = (z > 0) & (z >= n - 1 - t)
        k_up = jnp.minimum(n - 1 - t + z, n - 1)
        k_down = jnp.maximum(z - (n - 1) + t, 0)
        if t > 0:

            @pl.when(up & (z > 0))
            def _():
                self.landed(None, self.up_in.at[t - 1], 4 + t - 1)
                accumulate(self.piece(k_up), self.up_in.at[t - 1], rows)

            @pl.when(down & (z < n - 1))
            def _():
                self.landed(None, self.down_in.at[t - 1], 7 + t - 1)
                accumulate(self.piece(k_down), self.down_in.at[t - 1], rows)

        self.push(up, self.piece(k_up), self.up_in.at[t], 4 + t, {"dp": jnp.minimum(z + 1, n - 1)})
        self.push(down, self.piece(k_down), self.down_in.at[t], 7 + t, {"dp": jnp.maximum(z - 1, 0)})

    def line_end(self):
        _, _, z = here()
        n = LINE
        rows = self.rows // 8

        @pl.when(z > 0)
        def _():
            self.landed(None, self.up_in.at[n - 2], 4 + n - 2)
            accumulate(self.piece(z), self.up_in.at[n - 2], rows)

        @pl.when(z < n - 1)
        def _():
            self.landed(None, self.down_in.at[n - 2], 7 + n - 2)
            accumulate(self.piece(z), self.down_in.at[n - 2], rows)

    def held_at(self, k, q=None):
        cols = columns_of(k, self.cols // 2)
        return self.held.at[:, k // 2, :, cols] if q is None else self.held.at[q, k // 2, :, cols]

    def whole_at(self, k):
        return self.whole.at[k // 2, :, columns_of(k, self.cols // 2)]

    def last_piece(self):
        return self.final if self.final is not None else self.piece(here()[2])

    def own_piece(self):
        _, _, z = here()
        return pltpu.make_async_copy(
            self.last_piece(), self.held_at(z, self.s), self.send.at[10 + self.s]
        )

    def gather(self):
        c, _, z = here()
        for q in range(4):
            if q == self.s:
                pl.when(c == q)(self.own_piece().start)
            else:
                self.push(
                    c == q, self.last_piece(), self.held_at(z, q), 10 + q, {"section": self.s}
                )

    def share_step(self, t):
        _, _, z = here()
        n = LINE
        whole = self.whole_at
        if t == 0:
            copy = pltpu.make_async_copy(self.last_piece(), whole(z), self.send.at[0])
            copy.start()
            copy.wait()
        else:
            self.landed(z >= t, whole(jnp.maximum(z - t, 0)), 14 + t - 1)
            self.landed(z + t < n, whole(jnp.minimum(z + t, n - 1)), 17 + t - 1)
        if t < n - 1:
            low, high = jnp.maximum(z - t, 0), jnp.minimum(z + t, n - 1)
            self.push(
                (z >= t) & (z < n - 1), whole(low), whole(low), 14 + t,
                {"dp": jnp.minimum(z + 1, n - 1)},
            )
            self.push(
                (z + t < n) & (z > 0), whole(high), whole(high), 17 + t,
                {"dp": jnp.maximum(z - 1, 0)},
            )

    def whole_copy(self):
        return pltpu.make_async_copy(self.whole, self.held.at[self.s], self.send.at[10 + self.s])

    def whole_gather(self):
        c, _, _ = here()
        for q in range(4):
            if q == self.s:
                pl.when(c == q)(self.whole_copy().start)
            else:
                self.push(c == q, self.whole, self.held.at[q], 10 + q, {"section": self.s})

    def whole_end(self):
        c, _, _ = here()
        for q in range(4):
            if q == self.s:
                pl.when(c == q)(self.whole_copy().wait)
            else:
                self.landed(c == self.s, self.held.at[q], 10 + q)

    def out_step(self, t):
        c, _, z = here()
        n = LINE
        mine = c == self.s
        held = self.held_at
        if t == 0:
            for q in range(4):
                if q == self.s:
                    pl.when(mine)(self.own_piece().wait)
                else:
                    self.landed(mine, held(z, q), 10 + q)
        else:
            self.landed(mine & (z >= t), held(jnp.maximum(z - t, 0)), 14 + t - 1)
            self.landed(mine & (z + t < n), held(jnp.minimum(z + t, n - 1)), 17 + t - 1)
        if t < n - 1:
            low, high = jnp.maximum(z - t, 0), jnp.minimum(z + t, n - 1)
            self.push(
                mine & (z >= t) & (z < n - 1), held(low), held(low), 14 + t,
                {"dp": jnp.minimum(z + 1, n - 1)},
            )
            self.push(
                mine & (z + t < n) & (z > 0), held(high), held(high), 17 + t,
                {"dp": jnp.maximum(z - 1, 0)},
            )


class Delivery:
    def __init__(self, sources, parts, out, send, recv):
        self.sources, self.parts, self.out, self.send, self.recv = sources, parts, out, send, recv

    def rows(self, block):
        size = self.sources[self.parts[0][0]].shape[0] // 2
        return pl.ds(block * size, size)

    def copies(self, s, block):
        c, g, _ = here()
        slot = self.out.at[c % 2, g, self.rows(block), :]
        source = self.sources[s].at[self.rows(block), :]
        near = pltpu.make_async_copy(source, slot, self.send.at[s, block])
        far = pltpu.make_async_remote_copy(
            src_ref=source, dst_ref=slot, send_sem=self.send.at[s, block],
            recv_sem=self.recv.at[(c % 2) * 2 + g, block],
            device_id={"section": s, "group": c // 2}, device_id_type=MESH,
        )
        return near, far, (c == s) & (g == c // 2)

    def start(self, parts):
        for part in parts:
            near, far, stays = self.copies(*part)
            pl.when(stays)(near.start)
            pl.when(jnp.logical_not(stays))(far.start)

    def finish(self):
        c, g, _ = here()
        for s, block in self.parts:
            near, far, stays = self.copies(s, block)
            pl.when(stays)(near.wait)
            pl.when(jnp.logical_not(stays))(far.wait_send)
            for m in range(2):
                for half in range(2):
                    slot = self.out.at[m, half, self.rows(block), :]
                    copy = pltpu.make_async_remote_copy(
                        src_ref=slot, dst_ref=slot, send_sem=self.send.at[0, 0],
                        recv_sem=self.recv.at[2 * m + half, block], device_id={"group": 1 - g},
                        device_id_type=MESH,
                    )
                    arrives = (c == s) & jnp.logical_not((2 * g + m == c) & (g == half))
                    pl.when(arrives)(copy.wait_recv)


EARLY = ((2, 0), (3, 0))
LATE = ((0, 0), (1, 0), (0, 1), (1, 1), (2, 1), (3, 1))
ALL = tuple((s, block) for block in range(2) for s in range(4))


def feed_back_kernel(s, carry, *refs):
    delivers = carry is None
    wim, wit, wom, wot, act_in, slope_in, streams = refs[:7]
    refs = refs[7:]
    count = 0 if delivers else len(carry.all)
    carried, refs = refs[:count], refs[count:]
    if delivers:
        sources, parts = {i: streams.at[i] for i in range(4)}, ALL
    else:
        sources, parts = {3: refs[0], 2: refs[1]}, EARLY
        refs = refs[2:]
    g_ref, nrm, par = refs[:3]
    d_in, d_out = refs[3:5]
    delivered, results, refs = refs[5], refs[6 : 6 + count], refs[6 + count :]
    dbin_ref, small_ref, out_ref = refs[:3]
    w_in, w_out, act, slope, h, own_i, own_o, their_i, their_o, core_i, core_o, acc, nrm_t = refs[3:16]
    load_sem, core_s, core_r, out_sem = refs[16:20]
    del_sems, refs = refs[20:22], refs[22:]
    _, g, _ = here()
    partner = {"group": 1 - g}
    width = FF // CHUNKS
    third = CHUNKS // 2

    def column(j):
        b = (j + g * third) % CHUNKS
        return pl.ds(pl.multiple_of(b * width, width), width)

    def line_of(j):
        return pl.ds(pl.multiple_of(j * width, width), width)

    def loads(j):
        cols, rows = column(j), line_of(j % third)
        first = j < third
        return (
            (None, pltpu.make_async_copy(wim.at[:, cols], w_in.at[0, :, cols], load_sem.at[j, 0])),
            (None, pltpu.make_async_copy(wit.at[:, cols], w_in.at[1, :, cols], load_sem.at[j, 1])),
            (first, pltpu.make_async_copy(wom.at[rows, :], w_out.at[line_of(j), :], load_sem.at[j, 2])),
            (
                jnp.logical_not(first),
                pltpu.make_async_copy(wot.at[rows, :], w_out.at[line_of(j), :], load_sem.at[j, 2]),
            ),
            (None, pltpu.make_async_copy(act_in.at[:, line_of(j)], act.at[:, line_of(j)], load_sem.at[j, 3])),
            (None, pltpu.make_async_copy(slope_in.at[:, line_of(j)], slope.at[:, line_of(j)], load_sem.at[j, 4])),
        )

    def load(j):
        for cond, copy in loads(j):
            guarded(cond, copy.start)

    def core_copies(j):
        cols, rows = column(j), line_of(j % third)
        return (
            pltpu.make_async_remote_copy(
                src_ref=their_i.at[:, cols], dst_ref=core_i.at[:, cols], send_sem=core_s.at[j, 0],
                recv_sem=core_r.at[j, 0], device_id=partner, device_id_type=MESH,
            ),
            pltpu.make_async_remote_copy(
                src_ref=their_o.at[rows, :], dst_ref=core_o.at[rows, :], send_sem=core_s.at[j, 1],
                recv_sem=core_r.at[j, 1], device_id=partner, device_id_type=MESH,
            ),
        )

    loop(CHUNKS, load)
    stream_copy = pltpu.make_async_copy(streams.at[s - 1], h, out_sem.at[2])
    stream_copy.start()
    if not delivers:
        carry.load(carried, results, refs)
    greet(True, not delivers)
    delivery = Delivery(sources, parts, delivered, *del_sems)
    if not delivers:
        carry.begin()
    delivery.start(parts)
    acc[...] = jnp.zeros_like(acc)
    nrm_t[...] = jnp.transpose(nrm[...])

    def block(j):
        for cond, copy in loads(j):
            guarded(cond, copy.wait)
        cols, rows = column(j), line_of(j)
        grad = g_ref[...]
        d_up_f = dot_nt(grad, w_out[rows, :]) * slope[:, rows].astype(F32)
        d_up = d_up_f.astype(BF)
        d_o = dot_tn(act[:, rows], grad).astype(BF)
        dbin_ref[:, cols] = jnp.sum(d_up_f, axis=0, keepdims=True)
        their_i[:, cols] = dot(nrm_t[HALF:, :], d_up).astype(BF)
        inward, outward = core_copies(j)
        inward.start()

        @pl.when(j >= third)
        def _():
            their_o[line_of(j % third), :] = d_o
            outward.start()

        @pl.when(j < third)
        def _():
            own_o[line_of(j % third), :] = d_o

        own_i[:, cols] = dot(nrm_t[:HALF, :], d_up).astype(BF)
        acc[:, :HALF] += dot_nt(d_up, w_in[0, :, cols])
        acc[:, HALF:] += dot_nt(d_up, w_in[1, :, cols])

    if delivers:
        loop(CHUNKS, block)
    else:
        for i in range(3):
            loop(CHUNKS // 3, lambda j, i=i: block(j + CHUNKS // 3 * i))
            carry.step(i + 1)
    stream_copy.wait()
    grad = g_ref[...].astype(F32)
    d_normed = turn_halves(acc[...], g)
    out, d_gain, d_shift = norm_backward(h[...].astype(F32), par[0:1, :], grad, d_normed)
    out_ref[...] = out.astype(BF)
    small_ref[0:1, :] = jnp.sum(grad, axis=0, keepdims=True)
    small_ref[1:2, :] = d_gain
    small_ref[2:3, :] = d_shift
    small_ref[3:8, :] = jnp.zeros((5, D), F32)

    def ended(j):
        inward, outward = core_copies(j)
        inward.wait()
        pl.when(j >= third)(outward.wait)

    loop(CHUNKS, ended)
    accumulate(own_i, core_i, HALF)
    saves = [pltpu.make_async_copy(own_i, d_in, out_sem.at[0])]
    saves[0].start()
    accumulate(own_o, core_o, FF // 2)
    saves.append(pltpu.make_async_copy(own_o, d_out, out_sem.at[1]))
    saves[1].start()
    if not delivers:
        carry.end()
    delivery.finish()
    for copy in saves:
        copy.wait()


def every(units, act, *args):
    for unit in units:
        getattr(unit, act)(*args)


class Carry:
    last = False

    def __init__(self, plane, line, hold):
        self.planes = [(plane, 0), (plane, 1)]
        self.line, self.hold = line, hold
        self.all = self.planes + list(line) + list(hold)

    def results(self):
        out = []
        for u in self.planes:
            r, w = grad_shape(*u)
            out.append(sds((r // 4, w), BF))
        out += [sds(piece_shape(*u), BF) for u in self.line]
        return out + [sds(held_shape(*u), BF) for u in self.hold]

    def scratch(self):
        out = []
        for u in self.planes:
            r, w = grad_shape(*u)
            out += [pltpu.VMEM((r, w), BF), pltpu.VMEM((2, r // 4, w), BF), pltpu.VMEM((r // 4, w), BF)]
        for u in self.line:
            r, w = grad_shape(*u)
            out += [pltpu.VMEM((r // 4, w), BF)] + [pltpu.VMEM((3,) + piece_shape(*u), BF)] * 2
        out += [pltpu.VMEM(piece_shape(*u), BF) for u in self.hold]
        dma = pltpu.SemaphoreType.DMA
        return out + [dma((len(self.all), SEMS)), dma((len(self.all), SEMS))]

    def load(self, sources, results, refs):
        send, recv = refs[-2:]
        refs = list(refs[:-2])
        self.units, self.loads, self.targets = [], [], results
        for i, u in enumerate(self.all):
            sems = (send.at[i], recv.at[i])
            if i < 2:
                own, first, second = refs.pop(0), refs.pop(0), refs.pop(0)
                unit = Unit(*u, *sems, own=own, plane=(first, second))
            elif i < 2 + len(self.line):
                own, up, down = refs.pop(0), refs.pop(0), refs.pop(0)
                unit = Unit(*u, *sems, quarter=own, line=(up, down))
            else:
                own = refs.pop(0)
                unit = Unit(*u, *sems, final=own, held=results[i])
            copy = pltpu.make_async_copy(sources[i], own, sems[0].at[0])
            copy.start()
            self.units.append(unit)
            self.loads.append(copy)
        n = 2 + len(self.line)
        self.plane_units, self.line_units, self.hold_units = (
            self.units[:2], self.units[2:n], self.units[n:],
        )

    def begin(self):
        for copy in self.loads:
            copy.wait()
        for unit in self.hold_units:
            unit.gather()
        for unit in self.line_units:
            unit.line_step(0)
        for unit in self.plane_units:
            unit.first_step()

    def step(self, i):
        for unit in self.line_units:
            if i < LINE - 1:
                unit.line_step(i)
            else:
                unit.line_end()
        if i == 3:
            for unit in self.plane_units:
                unit.second_step()
        for unit in self.hold_units:
            if i < 3:
                unit.out_step(i - 1)

    def late_step(self):
        for unit in self.hold_units:
            unit.out_step(LINE - 2)

    def end(self):
        saves = [
            pltpu.make_async_copy(unit.last_piece(), target, unit.send.at[0])
            for unit, target in zip(self.line_units, self.targets[2:])
        ]
        for copy in saves:
            copy.start()
        for unit, target in zip(self.plane_units, self.targets):
            unit.third_step()
            copy = pltpu.make_async_copy(unit.mine(), target, unit.send.at[0])
            copy.start()
            saves.append(copy)
        for unit in self.hold_units:
            unit.out_step(LINE - 1)
        for copy in saves:
            copy.wait()
        for unit in self.units:
            unit.finish()


class Finish:
    all = ((1, 0), (1, 1), (2, 0), (2, 1), (3, 0), (3, 1))
    own_units = ((0, 0), (0, 1))
    last = True

    def results(self):
        held = [sds(held_shape(s, part), BF) for s in (0, 1) for part in (0, 1)]
        return held + [sds((2, 2, self.tokens, D), BF), sds(SMALL, F32)]

    def scratch(self):
        out = []
        for u in self.all[:2]:
            r, w = grad_shape(*u)
            out += [pltpu.VMEM((r, w), BF), pltpu.VMEM((2, r // 4, w), BF), pltpu.VMEM((r // 4, w), BF)]
        for u in self.all[2:4]:
            r, w = grad_shape(*u)
            out.append(pltpu.VMEM((r // 4, w), BF))
        out += [pltpu.VMEM(piece_shape(*u), BF) for u in self.all[4:]]
        for u in self.own_units:
            r, w = grad_shape(*u)
            out += [pltpu.VMEM((2, r // 4, w), BF), pltpu.VMEM((r // 4, w), BF)]
        for u in self.all[:4] + self.own_units:
            out += [pltpu.VMEM((3,) + piece_shape(*u), BF)] * 2
        out += [pltpu.VMEM(held_shape(*u)[1:], BF) for u in ((1, 1), (0, 1))]
        dma = pltpu.SemaphoreType.DMA
        small = [pltpu.VMEM((n,) + SMALL, F32) for n in (4, 4, 4, 2, 3, 4)]
        return out + small + [
            dma((8, SEMS)), dma((8, SEMS)), dma((7,)), dma((7,)), dma((4, 2)), dma((4, 2)),
        ]

    def load(self, sources, results, refs, own, streams, small_in):
        refs = list(refs)

        def take(n):
            out = refs[:n]
            del refs[:n]
            return out

        halves = [take(3), take(3)]
        quarters, finals = take(2), take(2)
        planes = [take(2), take(2)]
        lines = [take(2) for _ in range(6)]
        wholes = take(2)
        self.sm, self.sm_core, self.sm_x, self.sm_got, self.sm_y, self.sm_z = take(6)
        send, recv, self.sm_send, self.sm_recv, del_send, del_recv = refs
        held, delivered, self.small_out = results[:4], results[4], results[5]
        self.small_in = small_in

        def unit(i, u, **more):
            return Unit(*u, send.at[i], recv.at[i], held=held[2 * (u[0] % 2) + u[1]], **more)

        self.f1 = [
            unit(i, self.all[i], own=halves[i][0], plane=halves[i][1:], line=lines[i],
                 whole=wholes[0] if i else None)
            for i in range(2)
        ]
        self.a2 = [unit(2 + i, self.all[2 + i], quarter=quarters[i], line=lines[2 + i]) for i in range(2)]
        self.f3 = [unit(4 + i, self.all[4 + i], final=finals[i]) for i in range(2)]
        self.a0 = [
            unit(6 + i, self.own_units[i], own=own[i], plane=planes[i], line=lines[4 + i],
                 whole=wholes[1] if i else None)
            for i in range(2)
        ]
        self.units = self.f1 + self.a2 + self.f3 + self.a0
        self.delivery = Delivery(streams, LATE, delivered, del_send, del_recv)
        self.loads = [
            pltpu.make_async_copy(source, target, send.at[i, 0])
            for i, (source, target) in enumerate(
                zip(sources, [halves[0][0], halves[1][0], *quarters, *finals])
            )
        ]
        for copy in self.loads:
            copy.start()
        self.pending = []

    def begin(self):
        for copy in self.loads:
            copy.wait()
        every(self.f3, "gather")
        every(self.a2, "line_step", 0)
        every(self.f1, "first_step")

    def step(self, i):
        if i < 3:
            every(self.a2, "line_step", i)
            self.f3[0].out_step(i - 1)
        else:
            every(self.a2, "line_end")
            every(self.a2, "gather")
            every(self.f1, "second_step")

    def late_step(self):
        pass

    def small_push(self, src, dst, k, device):
        copy = pltpu.make_async_remote_copy(
            src_ref=src, dst_ref=dst, send_sem=self.sm_send.at[k], recv_sem=self.sm_recv.at[k],
            device_id=device, device_id_type=MESH,
        )
        copy.start()
        self.pending.append(copy)

    def small_landed(self, dst, k):
        pltpu.make_async_remote_copy(
            src_ref=dst, dst_ref=dst, send_sem=self.sm_send.at[k], recv_sem=self.sm_recv.at[k],
            device_id={"group": 1 - lax.axis_index("group")}, device_id_type=MESH,
        ).wait_recv()

    def small_step(self, k):
        c, g, z = here()
        x, y = c % 2, c // 2
        if k == 0:
            self.small_push(self.sm, self.sm_core, 0, {"group": 1 - g})
        elif k == 1:
            self.small_landed(self.sm_core, 0)
            self.sm_x[...] = self.sm[...] + self.sm_core[...]
            for b in range(2):
                self.small_push(
                    self.sm_x.at[2 * b + 1 - x], self.sm_got.at[b], 1 + b, {"section": flip(c, 1)}
                )
        elif k == 2:
            for b in range(2):
                self.small_landed(self.sm_got.at[b], 1 + b)
                self.sm_y[b] = self.sm_x[2 * b + x] + self.sm_got[b]
            self.small_push(self.sm_y.at[1 - y], self.sm_y.at[2], 3, {"section": flip(c, 2)})
        elif k == 3:
            self.small_landed(self.sm_y.at[2], 3)
            self.sm_z[z] = self.sm_y[y] + self.sm_y[2]
            for bit in (1, 2, 3):
                self.small_push(self.sm_z.at[z], self.sm_z.at[z], 3 + bit, {"dp": flip(z, bit)})
        else:
            for bit in (1, 2, 3):
                self.small_landed(self.sm_z.at[flip(z, bit)], 3 + bit)
            self.small_out[...] = self.sm_z[0] + self.sm_z[1] + self.sm_z[2] + self.sm_z[3]

    def conclude(self, dbin, rest):
        f1, a2, f3, a0 = self.f1, self.a2, self.f3, self.a0
        (held_a, shared_a), (held_f, shared_f) = a0, f1
        every(a0, "first_step")
        every(f1, "third_step")
        every(f1, "line_step", 0)
        f3[0].out_step(2)
        self.sm[1:4] = self.small_in[...]
        self.sm[0] = jnp.zeros(SMALL, F32)
        for i in range(3):
            self.sm[0, i : i + 1, :] = dbin[:, i * D : (i + 1) * D]
        self.sm[0, 4:9, :] = rest[0:5, :]
        self.small_step(0)
        every(f1, "line_step", 1)
        self.small_step(1)
        every(a0, "second_step")
        every(f1, "line_step", 2)
        self.small_step(2)
        every(f1, "line_end")
        held_f.gather()
        shared_f.share_step(0)
        f3[0].out_step(3)
        every(a0, "third_step")
        every(a0, "line_step", 0)
        self.small_step(3)
        self.delivery.start(LATE[:2])
        shared_f.share_step(1)
        every(a0, "line_step", 1)
        shared_f.share_step(2)
        every(a0, "line_step", 2)
        self.small_step(4)
        shared_f.share_step(3)
        shared_f.whole_gather()
        every(a0, "line_end")
        held_a.gather()
        shared_a.share_step(0)
        slabs = [*a2, held_f, f3[1]]
        shared_a.share_step(1)
        shared_a.share_step(2)
        held_a.out_step(0)
        shared_a.share_step(3)
        shared_a.whole_gather()
        every(slabs, "out_step", 0)
        self.delivery.start(LATE[2:])
        every(slabs, "out_step", 1)
        held_a.out_step(1)
        every(slabs, "out_step", 2)
        held_a.out_step(2)
        every(slabs, "out_step", 3)
        held_a.out_step(3)
        shared_f.whole_end()
        shared_a.whole_end()
        self.delivery.finish()
        for unit in self.units:
            unit.finish()
        for copy in self.pending:
            copy.wait_send()


def feed_back_call(s, weights, act, slope, streams, g, nrm, par, carry, carried, leaving, collective):
    t = g.shape[0]
    hbm = pl.BlockSpec(memory_space=pl.ANY)
    vmem = pl.BlockSpec(memory_space=pltpu.VMEM)
    delivers = carry is None
    dma = pltpu.SemaphoreType.DMA
    half_i, half_o = grad_shape(s, 0), grad_shape(s, 1)
    results = [sds((2, 2, t if delivers else t // 2, D), BF)]
    results += [] if delivers else carry.results()
    scratch = [
        pltpu.VMEM((2, HALF, FF), BF), pltpu.VMEM((FF, D), BF), pltpu.VMEM((t, FF), BF),
        pltpu.VMEM((t, FF), BF), pltpu.VMEM((t, D), BF),
        pltpu.VMEM(half_i, BF), pltpu.VMEM(half_o, BF), pltpu.VMEM(half_i, BF),
        pltpu.VMEM(half_o, BF), pltpu.VMEM(half_i, BF), pltpu.VMEM(half_o, BF),
        pltpu.VMEM((t, D), F32), pltpu.VMEM((D, t), BF),
        dma((CHUNKS, 5)), dma((CHUNKS, 2)), dma((CHUNKS, 2)), dma((3,)),
        dma((4, 2)), dma((4, 2)),
    ] + ([] if delivers else carry.scratch())
    out = pl.pallas_call(
        partial(feed_back_kernel, s, carry),
        out_shape=[sds(half_i, BF), sds(half_o, BF)] + results
        + [sds((1, FF), F32), sds((8, D), F32), sds((t, D), BF)],
        in_specs=[hbm] * (7 + len(carried) + len(leaving)) + [vmem] * 3,
        out_specs=[hbm] * (2 + len(results)) + [vmem] * 3,
        scratch_shapes=scratch,
        compiler_params=pltpu.CompilerParams(
            collective_id=collective, has_side_effects=True, vmem_limit_bytes=62 * 1024 * 1024
        ),
        name="feed_back_carry",
    )(*weights, act, slope, streams, *carried, *leaving, g, nrm, par)
    return out[:2], out[2 : 2 + len(results)], out[2 + len(results) :]


def attention_back_kernel(s, carry, *refs):
    wim, wit, wom, wot = refs[:4]
    count = len(carry.all)
    carried = refs[4 : 4 + count]
    refs = refs[4 + count :]
    large, (g_ref, lse_ref, seg_row, seg_m, seg_t, pos, par) = refs[:7], refs[7:14]
    refs = refs[14:]
    if carry.last:
        streams, small_in, results, refs = refs[:3], refs[3], refs[4:10], refs[10:]
    else:
        d_first, d_second = refs[:2]
        results, refs = refs[2 : 2 + count], refs[2 + count :]
    dbin_ref, small_ref, out_ref = refs[:3]
    w_in, w_out, dmix, d_q, d_k, d_v, give_k, give_v, got_k, got_v = refs[3:13]
    own, their, core = refs[13:15], refs[15:17], refs[17:19]
    acc, dp, delta_ref, nrm_t = refs[19:23]
    load_sem, kv_s, kv_r, core_s, core_r, out_sem = refs[23:29]
    o_ref, qkv, kv_t, nrm, cosines, sines, h = refs[29:36]
    if carry.last:
        streams = {0: out_ref, **{i + 1: streams[i] for i in range(3)}}
        carry.load(carried, results, refs[36:], own, streams, small_in)
    else:
        carry.load(carried, results, refs[36:])
    if s:
        large = large[:6] + (large[6].at[s - 1],)
    _, g, _ = here()
    partner = {"group": 1 - g}
    tokens = g_ref.shape[0]

    def remote(src, dst, ssem, rsem):
        return pltpu.make_async_remote_copy(
            src_ref=src, dst_ref=dst, send_sem=ssem, recv_sem=rsem, device_id=partner,
            device_id_type=MESH,
        )

    pairs = [(wom, w_out.at[0]), (wot, w_out.at[1])]
    pairs += list(zip(large[:4], (o_ref, qkv, kv_t, nrm)))
    pairs += [(wim, w_in.at[0]), (wit, w_in.at[1])]
    pairs += list(zip(large[4:], (cosines, sines, h)))
    loads = [
        pltpu.make_async_copy(src, dst, load_sem.at[i]) for i, (src, dst) in enumerate(pairs)
    ]
    for copy in loads:
        copy.start()
    greet(True, True)
    carry.begin()

    for copy in loads[:3]:
        copy.wait()
    grad = g_ref[...]
    d_mix = jnp.concatenate([dot_nt(grad, w_out[0]), dot_nt(grad, w_out[1])], axis=1)
    dmix[...] = turn_halves(d_mix, g).astype(BF)
    o = o_ref[...].astype(F32)
    head = lax.broadcasted_iota(jnp.int32, (16, D), 0)
    lane = lax.broadcasted_iota(jnp.int32, (16, D), 1)
    delta_ref[...] = lax.dot_general(
        jnp.where(lane // HD == head, 1.0, 0.0), dmix[...].astype(F32) * o, NT,
        preferred_element_type=F32, precision=lax.Precision.HIGHEST,
    )
    turned = turn_halves(o, g).astype(BF)
    turned_t = jnp.transpose(turned)
    their[1][HALF:, :] = dot(turned_t[HALF:, :], grad).astype(BF)
    core_copies = [remote(their[1].at[HALF:, :], core[1].at[HALF:, :], core_s.at[3], core_r.at[3])]
    core_copies[0].start()
    own[1][HALF:, :] = dot(turned_t[:HALF, :], grad).astype(BF)

    lanes = lax.broadcasted_iota(jnp.int32, (tokens, 2 * HD), 1)

    def pair(j):
        def columns(first):
            return pl.ds(pl.multiple_of(first + j * 2 * HD, 2 * HD), 2 * HD)

        q = qkv[:, columns(0)]
        do = dmix[:, columns(0)]
        zero = jnp.zeros_like(q)
        sets = (
            (qkv[:, columns(D)], qkv[:, columns(2 * D)], seg_m),
            (kv_t[:, columns(0)], kv_t[:, columns(D)], seg_t),
        )
        total_q = [0.0, 0.0]
        keys_t = [jnp.transpose(sets[i][0]) for i in range(2)]
        total_k = [jnp.zeros((tokens, 2 * HD), F32)] * 2
        total_v = [jnp.zeros((tokens, 2 * HD), F32)] * 2
        for side in range(2):
            mine = (lanes >= HD) if side else (lanes < HD)
            q_head = jnp.where(mine, q, zero)
            do_head = jnp.where(mine, do, zero)
            lse = lse_ref[pl.ds(2 * j + side, 1), :]
            delta = delta_ref[pl.ds(2 * j + side, 1), :]
            for i, (k, v, seg) in enumerate(sets):
                p_t = jnp.where(
                    seg[...] == seg_row[...], jnp.exp(dot_nt(k, q_head) - lse), 0.0
                )
                d_s = (p_t * (dot_nt(v, do_head) - delta)).astype(BF)
                total_v[i] = total_v[i] + dot(p_t.astype(BF), do_head)
                total_k[i] = total_k[i] + dot(d_s, q_head)
                total_q[side] = total_q[side] + dot(keys_t[i][side * HD : (side + 1) * HD, :], d_s)
        d_q[:, columns(0)] = jnp.transpose(jnp.concatenate(total_q, axis=0))
        d_k[:, columns(0)] = total_k[0]
        d_v[:, columns(0)] = total_v[0]
        give_k[:, columns(0)] = total_k[1].astype(BF)
        give_v[:, columns(0)] = total_v[1].astype(BF)

    def exchanges(i):
        cols = pl.ds(i * 4 * HD, 4 * HD)
        return (
            remote(give_k.at[:, cols], got_k.at[:, cols], kv_s.at[0, i], kv_r.at[0, i]),
            remote(give_v.at[:, cols], got_v.at[:, cols], kv_s.at[1, i], kv_r.at[1, i]),
        )

    for copy in loads[3:6]:
        copy.wait()
    nrm_t[...] = jnp.transpose(nrm[...])
    for i in range(PAIRS // 2):
        loop(2, lambda j, i=i: pair(2 * i + j))
        for copy in exchanges(i):
            copy.start()
        carry.step(i + 1)

    for copy in loads[6:]:
        copy.wait()
    acc[...] = jnp.zeros_like(acc)
    small_ref[...] = jnp.zeros_like(small_ref)

    def turned_back(dy, y):
        swapped = swap_pairs(dy)
        d_angle = y * swapped - swap_pairs(y) * dy
        small_ref[3:4, :] += jnp.sum(d_angle * pos[:, 0:1], axis=0, keepdims=True)
        small_ref[4:5, :] += jnp.sum(d_angle * pos[:, 1:2], axis=0, keepdims=True)
        return dy * cosines[...] - swapped * sines[...]

    for j in range(3):
        cols = slice(j * D, (j + 1) * D)
        if j == 0:
            dp[...] = turned_back(
                d_q[...] * HD ** (-0.5), qkv[:, :D].astype(F32) * HD**0.5
            )
        elif j == 1:
            for i in range(PAIRS // 2):
                for copy in exchanges(i):
                    copy.wait()
            dp[...] = turned_back(d_k[...] + got_k[...].astype(F32), qkv[:, D : 2 * D].astype(F32))
        else:
            dp[...] = d_v[...] + got_v[...].astype(F32)
        d_p = dp[...].astype(BF)
        dbin_ref[:, cols] = jnp.sum(dp[...], axis=0, keepdims=True)
        if j < 2:
            place = (0, (slice(None), cols))
        else:
            place = (1, (slice(0, HALF), slice(None)))
        part, at = place
        their[part][at] = dot(nrm_t[HALF:, :], d_p).astype(BF)
        copy = remote(their[part].at[at], core[part].at[at], core_s.at[j], core_r.at[j])
        copy.start()
        core_copies.append(copy)
        own[part][at] = dot(nrm_t[:HALF, :], d_p).astype(BF)
        if j == 1:
            carry.late_step()
        acc[:, :HALF] += dot_nt(d_p, w_in[0, :, cols])
        acc[:, HALF:] += dot_nt(d_p, w_in[1, :, cols])
    grad = g_ref[...].astype(F32)
    d_normed = turn_halves(acc[...], g)
    out, d_gain, d_shift = norm_backward(h[...].astype(F32), par[0:1, :], grad, d_normed)
    out_ref[...] = out.astype(BF)
    small_ref[0:1, :] = jnp.sum(grad, axis=0, keepdims=True)
    small_ref[1:2, :] = d_gain
    small_ref[2:3, :] = d_shift

    for copy in core_copies:
        copy.wait()
    saves = []
    if carry.last:
        for part in range(2):
            accumulate(own[part], core[part], own[part].shape[0])
        carry.conclude(dbin_ref, small_ref)
        return
    for part, target in enumerate((d_first, d_second)):
        accumulate(own[part], core[part], own[part].shape[0])
        copy = pltpu.make_async_copy(own[part], target, out_sem.at[part])
        copy.start()
        saves.append(copy)
    carry.end()
    for copy in saves:
        copy.wait()


def attention_back_call(
    s, weights, carry, carried, g, saved, seg_row, seg_m, seg_t, turns, pos, h, par, collective,
    streams=(), small=None,
):
    t = g.shape[0]
    qkv, nrm, kv_t, o, lse = saved
    hbm = pl.BlockSpec(memory_space=pl.ANY)
    vmem = pl.BlockSpec(memory_space=pltpu.VMEM)
    dma = pltpu.SemaphoreType.DMA
    halves = [grad_shape(s, 0), grad_shape(s, 1)]
    rows, wide = pltpu.VMEM((t, D), BF), pltpu.VMEM((t, D), F32)
    if carry.last:
        carry.tokens = t
    results = carry.results()
    scratch = [
        pltpu.VMEM((2, HALF, QKV), BF), pltpu.VMEM((2, HALF, D), BF), rows, wide, wide, wide,
        rows, rows, rows, rows,
        *[pltpu.VMEM(x, BF) for x in halves * 3],
        wide, wide, pltpu.VMEM((16, t), F32), pltpu.VMEM((D, t), BF),
        dma((11,)), dma((2, 3)), dma((2, 3)), dma((4,)), dma((4,)), dma((2,)),
        rows, pltpu.VMEM((t, QKV), BF), pltpu.VMEM((t, 2 * D), BF), rows, wide, wide, rows,
    ] + carry.scratch()
    extra, extra_specs = (), []
    out_shape, out_specs = [sds(x, BF) for x in halves] + results, [hbm] * (2 + len(results))
    if carry.last:
        extra, extra_specs = (*streams, small), [hbm] * 3 + [vmem]
        out_shape, out_specs = results, [hbm] * 5 + [vmem]
    out = pl.pallas_call(
        partial(attention_back_kernel, s, carry),
        out_shape=out_shape
        + [sds((1, QKV), F32), sds((8, D), F32), sds((t, D), BF)],
        in_specs=[hbm] * (4 + len(carried) + 7) + [vmem] * 7 + extra_specs,
        out_specs=out_specs + [vmem] * 3,
        scratch_shapes=scratch,
        compiler_params=pltpu.CompilerParams(
            collective_id=collective, has_side_effects=True, vmem_limit_bytes=63 * 1024 * 1024
        ),
        name="attention_back_carry",
    )(*weights, *carried, o, qkv, kv_t, nrm, *turns, h, g, lse, seg_row, seg_m, seg_t, pos, par, *extra)
    if carry.last:
        return out[:6]
    return out[:2], out[2:-3], out[-3:]


def in_place(x):
    return x.reshape(-1, x.shape[-1])


CHUNKS = 6


START = (0, 0, 0, 0)
RING = 4
GROUP = (1, 1, 1, 1)
SPAN = 6
BESIDE = (None, None, None)


def chunk_of(ref, part, k):
    size = ref.shape[0 if part else 1] // CHUNKS
    at = pl.ds(pl.multiple_of(k * size, size), size)
    return ref.at[at, :] if part else ref.at[:, at]


def ring_place(chip):
    return 2 * (chip // 2) + (chip % 2 + chip // 2) % 2


def ring_chip(place):
    return 2 * (place // 2) + (place % 2 + place // 2) % 2


CLOCKWISE = ((True, False), (True, False), (False, True), (True, False))


def forward_kernel(*refs):
    w_in, w_out, h0, small, pos, seg_col, seg_m, seg_t = refs[:8]
    refs = refs[8:]
    keep = [refs[4 * s : 4 * s + 4] for s in range(4)]
    acts, slopes = refs[16:18], refs[18:20]
    results = refs[20:38]
    refs = refs[38:]
    work, refs = refs[:18], refs[18:]
    qkvs, kv_ts, os, lses = work[0:2], work[2:4], work[4:6], work[6:8]
    nrms, hs = work[8:12], [work[12].at[s] for s in range(4)]
    turns, pars = (work[13:15], work[15:17]), work[17]
    held = [refs[4 * s : 4 * s + 4] for s in range(4)]
    acc, stage_a, stage_s, lse_scr, smalls, b_in, b_out, freqs = refs[16:24]
    own_sem, ring_s, ring_r, z_s, z_r, core_s, core_r, kv_sem, save_sem, stage_sem = refs[24:34]
    small_s, small_r, result_sem = refs[34:]

    def kept(i):
        return pltpu.make_async_copy(work[i], results[i], result_sem.at[i])

    c = lax.axis_index("section")
    g = lax.axis_index("group")
    z = lax.axis_index("dp")
    parity = z % 2
    place = ring_place(c)
    ahead, behind = ring_chip((place + 1) % 4), ring_chip((place + 3) % 4)
    partner = {"group": 1 - g}
    tokens = h0.shape[0]

    def remote(src, dst, ssem, rsem, device):
        return pltpu.make_async_remote_copy(
            src_ref=src, dst_ref=dst, send_sem=ssem, recv_sem=rsem, device_id=device,
            device_id_type=MESH,
        )

    greet(True, True)

    def small_copies():
        slot = smalls.at[2 * c + g]
        out = []
        for bit in range(4):
            for core in range(2):
                if bit or core:
                    target = {"section": flip(c, bit) if bit else c, "group": (g + core) % 2}
                    out.append(remote(small, slot, small_s.at[2 * bit + core], small_r.at[2 * c + g], target))
        return out

    for copy in small_copies():
        copy.start()
    smalls[2 * c + g] = small[...]

    def mine(s, part):
        return held[s][2 * part]

    def theirs(s, part):
        return held[s][2 * part + 1]

    def distance(s, part):
        d = place - ring_place(s)
        return (d + 4) % 4 if CLOCKWISE[s][part] else (4 - d) % 4

    def own_copies(s):
        first = pltpu.make_async_copy(
            w_in.at[:, : QKV] if s % 2 == 0 else w_in, mine(s, 0), own_sem.at[0]
        )
        source = w_out.at[:HALF, :] if s % 2 == 0 else w_out
        second = pltpu.make_async_copy(source, mine(s, 1), own_sem.at[1])
        over = remote(w_out.at[HALF:D, :], mine(s, 1), own_sem.at[2], own_sem.at[3], partner)
        return first, second, over

    for s in range(4):

        @pl.when(c == s)
        def _(s=s):
            first, second, over = own_copies(s)
            first.start()
            if s % 2:
                second.start()
            else:

                @pl.when(g == 0)
                def _():
                    second.start()
                    over.start()

    for s in range(4):

        @pl.when(c == s)
        def _(s=s):
            first, second, over = own_copies(s)
            first.wait()
            if s % 2:
                second.wait()
            else:

                @pl.when(g == 0)
                def _():
                    second.wait()
                    over.wait_send()

                @pl.when(g == 1)
                def _():
                    over.wait_recv()

    def ring_copy(s, part, k):
        ref = chunk_of(mine(s, part), part, jnp.where(k < 2, 2 * parity + k, k + 2))
        target = ahead if CLOCKWISE[s][part] else behind
        u = 2 * s + part
        return remote(ref, ref, ring_s.at[u, k], ring_r.at[u, k], {"section": target})

    def z_copy(s, part, j, sending):
        ref = chunk_of(mine(s, part), part, 2 * (parity if sending else 1 - parity) + j)
        u = 2 * s + part
        return remote(ref, ref, z_s.at[u, j], z_r.at[u, j], {"dp": z + 1 - 2 * parity})

    def core_copy(s, part, k):
        u = 2 * s + part
        return remote(
            chunk_of(mine(s, part), part, k), chunk_of(theirs(s, part), part, k),
            core_s.at[u, k], core_r.at[u, k], partner,
        )

    def event(s, part, k):
        p = distance(s, part)
        copy = ring_copy(s, part, k)
        pl.when(p > 0)(copy.wait_recv)
        pl.when(p < 3)(copy.start)

        @pl.when((k < 2) & (p > 0))
        def _():
            z_copy(s, part, jnp.minimum(k, 1), True).start()

        core_copy(s, part, jnp.where(k < 2, 2 * parity + k, k + 2)).start()

        @pl.when(k >= 2)
        def _():
            j = jnp.maximum(k - 2, 0)
            pl.when(p > 0)(z_copy(s, part, j, False).wait_recv)
            core_copy(s, part, 2 * (1 - parity) + j).start()

    def slot(t, first, last):
        for s in range(4):
            if START[s] <= last and first <= START[s] + RING // GROUP[s] + 2:
                for part in range(2):
                    k = t - START[s] - distance(s, part)

                    @pl.when((k >= 0) & (k < RING // GROUP[s]))
                    def _(s=s, part=part, k=k):
                        k = jnp.clip(k, 0, RING // GROUP[s] - 1)
                        for i in range(GROUP[s]):
                            event(s, part, k * GROUP[s] + i)

    def slots(first, last):
        loop(last - first + 1, lambda i: slot(first + i, first, last))

    def arrived(s):
        def one(k):
            core_copy(s, 0, k).wait_recv()
            core_copy(s, 1, k).wait_recv()

        loop(CHUNKS, one)
        for i in range(4):
            pltpu.make_async_copy(held[s][i], keep[s][i], save_sem.at[4 * s + i]).start()

    def assemble():
        for i in range(8):
            slot = smalls.at[i]
            copy = remote(slot, slot, small_s.at[0], small_r.at[i], partner)
            pl.when(2 * c + g != i)(copy.wait_recv)
        for s in range(4):

            def both(first, width, s=s):
                at = slice(first, first + width)
                return jnp.concatenate([smalls[2 * s, :, at], smalls[2 * s + 1, :, at]], axis=1)

            half = FF // 2
            b_in[s] = both(0, half)
            b_out[s] = both(half, HALF)
            pars[s] = jnp.concatenate(
                [both(half + HALF, HALF), both(half + 2 * HALF, HALF), jnp.zeros((6, D), F32)], axis=0
            )
            if s % 2 == 0:
                freqs[s // 2] = jnp.concatenate(
                    [both(half + 3 * HALF, HALF), both(half + 4 * HALF, HALF)], axis=0
                )

    def turn_rows(i):
        rows = tokens // 2
        at = pl.ds(pl.multiple_of((i % 2) * rows, rows), rows)
        for layer in range(2):

            @pl.when(i // 2 == layer)
            def _(layer=layer):
                angles = (
                    pos[at, 0:1] * freqs[layer, 0:1, :] + pos[at, 1:2] * freqs[layer, 1:2, :]
                )
                lanes = lax.broadcasted_iota(jnp.int32, angles.shape, 1)
                sines = jnp.sin(angles)
                turns[layer][0][at, :] = jnp.cos(angles)
                turns[layer][1][at, :] = jnp.where((lanes % HD) < HD // 2, -sines, sines)

    def normed(s, h):
        xhat, _ = normalize(h[...].astype(F32))
        nrms[s][...] = turn_halves(
            xhat * pars[s, 0:1, :] + pars[s, 1:2, :], g
        ).astype(BF)

    def project(s, first, width):
        cols = pl.ds(first, width)
        return (
            dot(nrms[s][:, :HALF], mine(s, 0)[:, cols])
            + dot(nrms[s][:, HALF:], theirs(s, 0)[:, cols])
            + b_in[s, 0:1, cols]
        )

    def attention(s, h, out, beside):
        layer = s // 2
        qkv, kv_t, o_ref = qkvs[layer], kv_ts[layer], os[layer]
        cosines, sines = turns[layer]
        normed(s, h)
        exchange = []
        for j in (1, 2, 0):
            x = project(s, j * D, D)
            if j < 2:
                x = x * cosines[...] + swap_pairs(x) * sines[...]
            if j == 0:
                x = x * HD ** (-0.5)
            qkv[:, j * D : (j + 1) * D] = x.astype(BF)
            if j:
                copy = remote(
                    qkv.at[:, j * D : (j + 1) * D], kv_t.at[:, (j - 1) * D : j * D],
                    kv_sem.at[0, 2 * layer + j - 1], kv_sem.at[1, 2 * layer + j - 1], partner,
                )
                copy.start()
                exchange.append(copy)
        for copy in exchange:
            copy.wait()
        for i in (layer, 2 + layer, 8 + s):
            kept(i).start()
        lanes = lax.broadcasted_iota(jnp.int32, (tokens, 2 * HD), 1)

        def pair(j):
            if beside is not None:
                pl.when(beside[0] + j <= beside[1])(lambda: slot(beside[0] + j, *beside))

            def columns(ref, first):
                return ref[:, pl.ds(pl.multiple_of(first + j * 2 * HD, 2 * HD), 2 * HD)]

            q = columns(qkv, 0)
            km, vm = columns(qkv, D), columns(qkv, 2 * D)
            kt, vt = columns(kv_t, 0), columns(kv_t, D)
            same_m = seg_col[...] == seg_m[...]
            same_t = seg_col[...] == seg_t[...]
            found = []
            for side in range(2):
                head = (lanes >= HD) if side else (lanes < HD)
                q_head = jnp.where(head, q, jnp.zeros_like(q))
                s_m = jnp.where(same_m, dot_nt(q_head, km), -1e9)
                s_t = jnp.where(same_t, dot_nt(q_head, kt), -1e9)
                top = jnp.maximum(
                    jnp.max(s_m, axis=-1, keepdims=True), jnp.max(s_t, axis=-1, keepdims=True)
                )
                p_m = jnp.exp(s_m - top)
                p_t = jnp.exp(s_t - top)
                total = jnp.sum(p_m, axis=-1, keepdims=True) + jnp.sum(
                    p_t, axis=-1, keepdims=True
                )
                o = dot(p_m.astype(BF), vm) + dot(p_t.astype(BF), vt)
                found.append(o / total)
                lse_scr[...] = jnp.where(
                    lanes == 2 * j + side, top + jnp.log(total), lse_scr[...]
                )
            o_ref[:, pl.ds(pl.multiple_of(j * 2 * HD, 2 * HD), 2 * HD)] = jnp.where(
                lanes < HD, found[0], found[1]
            ).astype(BF)

        loop(PAIRS, pair)
        lses[layer][...] = jnp.transpose(lse_scr[...])[:16, :]
        turned = turn_halves(o_ref[...].astype(F32), g).astype(BF)
        y = dot(turned[:, :HALF], mine(s, 1)[...]) + dot(turned[:, HALF:], theirs(s, 1)[...])
        out[...] = (h[...].astype(F32) + y + b_out[s, 0:1, :]).astype(BF)
        for i in (4 + layer, 6 + layer):
            kept(i).start()

    def feed(s, h, out, beside):
        layer = s // 2
        width = FF // CHUNKS
        normed(s, h)
        kept(8 + s).start()
        acc[...] = h[...].astype(F32) + b_out[s, 0:1, :]

        def staged(j, i):
            turn = j % 2
            cols = pl.ds(pl.multiple_of(j * width, width), width)
            source, target = ((stage_a, acts[layer]), (stage_s, slopes[layer]))[i]
            return pltpu.make_async_copy(source.at[turn], target.at[:, cols], stage_sem.at[i, turn])

        def block(j):
            if beside is not None:
                pl.when(beside[0] + j <= beside[1])(lambda: slot(beside[0] + j, *beside))
            turn = j % 2

            @pl.when(j >= 2)
            def _():
                staged(j - 2, 0).wait()
                staged(j - 2, 1).wait()

            b = (j + g * (CHUNKS // 2)) % CHUNKS
            u = project(s, pl.multiple_of(b * width, width), width)
            cdf = 0.5 + 0.5 * lax.erf(u * (0.5**0.5))
            act = (u * cdf).astype(BF)
            stage_a[turn] = act
            pdf = jnp.exp(u * u * -0.5) * 0.3989422804014327
            stage_s[turn] = (cdf + u * pdf).astype(BF)
            staged(j, 0).start()
            staged(j, 1).start()
            for half in range(2):

                @pl.when(j // (CHUNKS // 2) == half)
                def _(half=half):
                    rows = pl.ds(pl.multiple_of((j % (CHUNKS // 2)) * width, width), width)
                    acc[...] += dot(act, held[s][2 + half][rows, :])

        loop(CHUNKS, block)
        for j in (CHUNKS - 2, CHUNKS - 1):
            staged(j, 0).wait()
            staged(j, 1).wait()
        out[...] = acc[...].astype(BF)

    slots(0, 0)
    assemble()

    def wait_and_turn(i):
        slot(1 + i, 1, SPAN)
        pl.when(i < 4)(lambda: turn_rows(i))

    loop(SPAN, wait_and_turn)
    for i in range(13, 18):
        kept(i).start()
    arrived(0)
    attention(0, h0, hs[0], BESIDE[0])
    arrived(1)
    feed(1, hs[0], hs[1], BESIDE[1])
    arrived(2)
    attention(2, hs[1], hs[2], BESIDE[2])
    arrived(3)
    feed(3, hs[2], hs[3], None)

    kept(12).start()

    for copy in small_copies():
        copy.wait_send()
    for i in range(18):
        kept(i).wait()
    for s in range(4):
        for part in range(2):
            p = distance(s, part)

            def sent_out(k, s=s, part=part, p=p):
                core_copy(s, part, k).wait_send()
                pl.when((k < 4) & (p < 3))(ring_copy(s, part, jnp.minimum(k, 3)).wait_send)
                pl.when((k < 2) & (p > 0))(z_copy(s, part, jnp.minimum(k, 1), True).wait_send)

            loop(CHUNKS, sent_out)
        for i in range(4):
            pltpu.make_async_copy(held[s][i], keep[s][i], save_sem.at[4 * s + i]).wait()


def forward_call(w_in, w_out, h, small, pos, seg_col, seg_m, seg_t):
    t = h.shape[0]
    hbm = pl.BlockSpec(memory_space=pl.ANY)
    vmem = pl.BlockSpec(memory_space=pltpu.VMEM)
    weights = []
    for s in range(4):
        (a, b), (d, e) = unit_shape(s, 0), unit_shape(s, 1)
        weights += [(a, b), (a, b), (d, e), (d, e)]
    rows = sds((t, D), BF)
    out_shape = (
        [sds(w, BF) for w in weights]
        + [sds((t, FF), BF)] * 4
        + [sds((t, QKV), BF)] * 2
        + [sds((t, 2 * D), BF)] * 2
        + [rows] * 2
        + [sds((16, t), F32)] * 2
        + [rows] * 4
        + [sds((4, t, D), BF)]
        + [sds((t, D), F32)] * 4
        + [sds((4, 8, D), F32)]
    )
    dma = pltpu.SemaphoreType.DMA
    scratch = [pltpu.VMEM(x.shape, x.dtype) for x in out_shape[20:]]
    scratch += [pltpu.VMEM(w, BF) for w in weights] + [
        pltpu.VMEM((t, D), F32),
        pltpu.VMEM((2, t, FF // CHUNKS), BF),
        pltpu.VMEM((2, t, FF // CHUNKS), BF),
        pltpu.VMEM((t, 2 * HD), F32),
        pltpu.VMEM((8,) + small.shape, F32),
        pltpu.VMEM((4, 1, FF), F32),
        pltpu.VMEM((4, 1, D), F32),
        pltpu.VMEM((2, 2, D), F32),
        dma((4,)), dma((8, 4)), dma((8, 4)), dma((8, 2)), dma((8, 2)), dma((8, 6)), dma((8, 6)),
        dma((2, 4)), dma((16,)), dma((2, 2)), dma((8,)), dma((8,)), dma((18,)),
    ]
    out = pl.pallas_call(
        forward_kernel,
        out_shape=out_shape,
        in_specs=[hbm, hbm] + [vmem] * 6,
        out_specs=[hbm] * 38,
        scratch_shapes=scratch,
        compiler_params=pltpu.CompilerParams(
            collective_id=2, has_side_effects=True, vmem_limit_bytes=63 * 1024 * 1024
        ),
        name="forward",
    )(w_in, w_out, h, small, pos, seg_col, seg_m, seg_t)
    weights = [out[4 * s : 4 * s + 4] for s in range(4)]
    acts, slopes, qkvs, kv_ts, os, lses = (out[16 + 2 * i : 18 + 2 * i] for i in range(6))
    nrms, hs = out[28:32], out[32]
    saved = []
    for s in range(4):
        i = s // 2
        if s % 2 == 0:
            saved.append((qkvs[i], nrms[s], kv_ts[i], os[i], lses[i]))
        else:
            saved.append((acts[i], slopes[i], nrms[s]))
    return weights, saved, hs, (out[33:35], out[35:37]), out[37]


def small_rows(dbin, rest):
    first = jnp.pad(dbin.reshape(-1), (0, FF - dbin.size)).reshape(4, D)
    return jnp.concatenate([first, rest[:5], jnp.zeros((SMALL[0] - 9, D), F32)])


def carried_passes(weight_in, weight_out, h, g, small, freq, pos, seg_m, seg_t):
    section, core = lax.axis_index("section"), lax.axis_index("group")
    wide = jnp.concatenate([freq.reshape(2, PAIRS, HD // 2)] * 2, axis=2).reshape(-1)
    small = jnp.concatenate([*small, wide]).astype(F32)[None]
    weights, saved, streams, turns, pars = forward_call(
        weight_in[0], weight_out[0], h, small, pos, seg_m[:, None], seg_m[None], seg_t[None]
    )
    smalls, grads, in_grads = [None] * 4, [None] * 4, [None] * 4
    rows = (seg_m[None], seg_m[:, None], seg_t[:, None])

    def feed_back(s, g, carry, carried, leaving):
        act, slope, nrm = saved[s]
        grads[s], results, (dbin, rest, in_grads[s]) = feed_back_call(
            s, weights[s], act, slope, streams, g, nrm, pars[s], carry, carried, leaving, 3 + s
        )
        smalls[s] = small_rows(dbin, rest)
        return results

    def attention_back(s, g, carry, carried):
        grads[s], results, (dbin, rest, in_grads[s]) = attention_back_call(
            s, weights[s], carry, carried, g, saved[s], *rows, turns[s // 2], pos,
            streams if s else h, pars[s], 3 + s,
        )
        smalls[s] = small_rows(dbin, rest)
        return results

    (outputs,) = feed_back(3, g, None, (), ())
    quarters3 = attention_back(2, in_grads[3], Carry(3, (), ()), grads[3])
    early, *quarters2, first3, second3 = feed_back(
        1, in_grads[2], Carry(2, ((3, 0), (3, 1)), ()), (*grads[2], *quarters3),
        (in_grads[3], in_grads[2]),
    )
    *sums, input_grads, small_sum = attention_back_call(
        0, weights[0], Finish(), (*grads[1], *quarters2, first3, second3), in_grads[1], saved[0],
        *rows, turns[0], pos, h, pars[0], 3, in_grads[1:], jnp.stack(smalls[1:]),
    )
    first_rows = jnp.where(section >= 2, early, input_grads[:, :, : early.shape[2]])
    input_grads = jnp.concatenate([first_rows, input_grads[:, :, early.shape[2] :]], axis=2)
    first_a, second_a, first_f, second_f = sums
    second_a = in_place(second_a)
    in_a = jnp.concatenate([in_place(first_a), second_a[:HALF]], axis=1)
    both = jnp.concatenate([second_a[HALF:], flipped(second_a[HALF:], "group", 1)], axis=0)
    both = jnp.where(core == 0, jnp.pad(both, ((0, FF // 2 - D), (0, 0))), jnp.zeros((), BF))
    attends = section % 2 == 0
    in_f = in_place(first_f)
    out_in = jnp.where(attends, jnp.pad(in_a, ((0, 0), (0, FF - QKV))), in_f).astype(F32)
    out_out = jnp.where(attends, both, in_place(second_f)).astype(F32)
    return outputs.reshape(-1, D), input_grads.reshape(-1, D), out_in, out_out, small_sum


def plain_passes(weight_in, weight_out, h, g, small, freq, pos, seg_m, seg_t):
    section, group = lax.axis_index("section"), lax.axis_index("group")
    groups = lax.axis_size("group")
    small = jnp.concatenate([*small, freq.reshape(-1)])
    small = lax.all_gather(small, ("section", "group")).reshape(4, groups, -1).astype(F32)
    widths = [FF // groups, D // groups, D // groups, D // groups, D // groups]
    starts = [sum(widths[:i]) for i in range(5)]
    b_in, b_out, gain, shift, freq = (
        small[:, :, a : a + w] for a, w in zip(starts, widths)
    )
    b_in, b_out, gain, shift = (x.reshape(4, 1, -1) for x in (b_in, b_out, gain, shift))
    freq = freq.reshape(4, groups, 2, -1).transpose(0, 2, 1, 3).reshape(4, 2, D // 2)
    pars = [
        jnp.concatenate([gain[s], shift[s], jnp.zeros((6, D), F32)], axis=0) for s in range(4)
    ]
    turns = [turning(freq[s], pos) for s in (0, 2)]

    core = group % 2
    rot = jnp.zeros((1,), jnp.int32)
    all_in = lax.all_gather(weight_in, "group", axis=1, tiled=True)
    all_out = lax.all_gather(weight_out, "group", axis=1, tiled=True)
    all_in = lax.all_gather(all_in, "section", axis=0, tiled=True)
    all_out = lax.all_gather(all_out, "section", axis=0, tiled=True)
    weights, saved, streams = [], [], [h]
    for s in range(4):
        cols, rows = (QKV, D) if s % 2 == 0 else (FF, FF)
        w_in, w_out = all_in[s, :, :cols], all_out[s, :rows]
        weights.append((w_in[:HALF], w_in[HALF:], w_out[: rows // 2], w_out[rows // 2 :]))
        wia, wib, woa, wob = weights[s]
        if s % 2 == 0:
            cosines, sines = turns[s // 2]
            qkv, nrm = qkv_call(rot, h, pars[s], wia, wib, b_in[s, :, :QKV], cosines, sines)
            kv_t = flipped(qkv[:, D:], "group", 1)
            o, lse, h = attend_call(
                rot, qkv, kv_t, seg_m[:, None], seg_m[None], seg_t[None], h, woa, wob, b_out[s]
            )
            saved.append((qkv, nrm, kv_t, o, lse))
        else:
            act, slope, nrm, h = ff_call(rot, h, pars[s], wia, wib, b_in[s], woa, wob, b_out[s])
            saved.append((act, slope, nrm))
        streams.append(h)
    outputs = to_owners(streams[1:], section, core)
    smalls, grads, in_grads = [None] * 4, [None] * 4, [None] * 4
    for s in (3, 2, 1, 0):
        wia, wib, woa, wob = weights[s]
        if s % 2 == 0:
            qkv, nrm, kv_t, o, lse = saved[s]
            cosines, sines = turns[s // 2]
            dmix, delta, doa, dob = mix_back_call(rot, g, o, woa, wob)
            dq, dkm, dvm, dkt, dvt = attend_back_call(
                qkv, kv_t, dmix, lse, delta, seg_m[None], seg_m[:, None], seg_t[:, None]
            )
            dkr, dvr = flipped(dkt, "group", 1), flipped(dvt, "group", 1)
            dia, dib, dbin, rest, g = qkv_back_call(
                rot, dq, dkm, dvm, dkr, dvr, qkv, cosines, sines, pos, nrm, wia, wib,
                streams[s], pars[s], g,
            )
        else:
            act, slope, nrm = saved[s]
            dia, dib, doa, dob, dbin, rest, g = ff_back_call(
                rot, g, act, slope, nrm, wia, wib, woa, wob, streams[s], pars[s]
            )
        in_grads[s] = g
        grads[s] = (
            jnp.pad(jnp.concatenate([dia, dib]), ((0, 0), (0, FF - dia.shape[1]))),
            jnp.pad(jnp.concatenate([doa, dob]), ((0, FF - 2 * doa.shape[0]), (0, 0))),
        )
        smalls[s] = small_rows(dbin, rest)
    input_grads = to_owners(in_grads, section, core)
    small_sum = lax.psum(jnp.stack(smalls), ("section", "group", "dp"))[section]

    def owned(x):
        x = lax.psum_scatter(x, "section", scatter_dimension=0, tiled=True)[0]
        x = lax.psum_scatter(x, "group", scatter_dimension=0, tiled=True)
        return lax.psum(x, "dp").astype(F32)

    out_in = owned(jnp.stack([x[0] for x in grads]))
    out_out = owned(jnp.stack([x[1] for x in grads]))
    return outputs, input_grads, out_in, out_out, small_sum


def body(
    activations, weight_in, weight_out, bias_in, bias_out, norm_gain, norm_shift, rope_freq,
    image_sides, cotangent,
):
    sections = lax.axis_size("section")
    groups = lax.axis_size("group")
    section = lax.axis_index("section")
    group = lax.axis_index("group")
    core = group % 2
    micro = image_sides.shape[0]
    capacity = activations.shape[0] // micro
    tokens = capacity // 2
    assert sections == 4 and groups % 2 == 0 and 2 * micro == sections
    fast = groups == 2 and lax.axis_size("dp") == 4

    here = (section // 2) == core
    local = section % 2

    def take(x):
        own = lax.dynamic_index_in_dim(x.reshape(micro, capacity, D), local, 0, keepdims=False)
        give = lax.dynamic_slice_in_dim(own, (1 - core) * tokens, tokens, 0)
        keep = lax.dynamic_slice_in_dim(own, core * tokens, tokens, 0)
        return jnp.where(here, keep, flipped(give, "group", 1))

    h = take(activations)
    own_sides = lax.dynamic_index_in_dim(image_sides, local, 0, keepdims=False)
    sides = jnp.where(here, own_sides, flipped(own_sides, "group", 1))
    segment, patch_row, patch_col, is_valid = layout(sides, capacity)
    pos_all = jnp.stack([patch_col, patch_row], axis=1).astype(F32)

    def half_of(x, which):
        return lax.dynamic_slice_in_dim(x, which * tokens, tokens, 0)

    pos = half_of(pos_all, core)
    seg_m, seg_t = half_of(segment, core), half_of(segment, 1 - core)
    valid = half_of(is_valid, core)
    g = take(cotangent) * valid[:, None].astype(BF)

    passes = carried_passes if fast else plain_passes
    outputs, input_grads, out_in, out_out, small_sum = passes(
        weight_in, weight_out, h, g, (bias_in[0], bias_out[0], norm_gain[0], norm_shift[0]),
        rope_freq[0], pos, seg_m, seg_t,
    )

    first_bias = small_sum[:4].reshape(-1)
    d_freq = small_sum[7:9].reshape(2, HEADS, HD)[:, :, : HD // 2].reshape(2, D // 2)

    def piece(x):
        w = x.shape[-1] // groups
        return lax.dynamic_slice_in_dim(x, group * w, w, x.ndim - 1)[None]

    return (
        outputs[None],
        input_grads[None],
        out_in[None],
        out_out[None],
        piece(first_bias),
        piece(small_sum[4]),
        piece(small_sum[5]),
        piece(small_sum[6]),
        piece(d_freq),
    )


def solution(mesh):
    placed = (
        P(("group", "dp"), None),
        P("section", "group", None),
        P("section", "group", None),
        P("section", "group"),
        P("section", "group"),
        P("section", "group"),
        P("section", "group"),
        P("section", None, "group"),
        P(("group", "dp"), None),
        P(("group", "dp"), None),
    )
    return jax.shard_map(
        body,
        mesh=mesh,
        in_specs=placed,
        out_specs=(
            P("section", ("group", "dp"), None),
            P("section", ("group", "dp"), None),
            P("section", "group", None),
            P("section", "group", None),
            P("section", "group"),
            P("section", "group"),
            P("section", "group"),
            P("section", "group"),
            P("section", None, "group"),
        ),
        check_vma=False,
    )
```

```python
from functools import partial

import jax
import jax.numpy as jnp
from jax import lax
from jax.experimental import pallas as pl
from jax.experimental.pallas import tpu as pltpu
from jax.sharding import PartitionSpec as P

D = 768
HEADS = 12
HD = 64
FF = 3072
HALF = D // 2
PAIRS = HEADS // 2
QKV = 3 * D
EPSILON = 1e-06
BF = jnp.bfloat16
F32 = jnp.float32
NT = (((1,), (1,)), ((), ()))
TN = (((0,), (0,)), ((), ()))
VMEM_BYTES = 52 * 1024 * 1024


def dot(a, b):
    return jnp.dot(a, b, preferred_element_type=F32)


def dot_nt(a, b):
    return lax.dot_general(a, b, NT, preferred_element_type=F32)


def dot_tn(a, b):
    return lax.dot_general(a, b, TN, preferred_element_type=F32)


def normalize(h):
    average = jnp.mean(h, axis=-1, keepdims=True)
    centered = h - average
    variance = jnp.mean(centered * centered, axis=-1, keepdims=True)
    scale = lax.rsqrt(variance + EPSILON)
    return centered * scale, scale


def turn_halves(x, rot):
    return jnp.where(rot == 0, x, jnp.concatenate([x[:, HALF:], x[:, :HALF]], axis=1))


def swap_pairs(x):
    lanes = lax.broadcasted_iota(jnp.int32, x.shape, 1)
    low = (lanes % HD) < HD // 2
    return jnp.where(
        low, pltpu.roll(x, x.shape[1] - HD // 2, 1), pltpu.roll(x, HD // 2, 1)
    )


def norm_backward(h, gain, grad, d_normed):
    xhat, scale = normalize(h)
    e = d_normed * gain
    mean_e = jnp.mean(e, axis=-1, keepdims=True)
    mean_ex = jnp.mean(e * xhat, axis=-1, keepdims=True)
    g = grad + scale * (e - mean_e - xhat * mean_ex)
    d_gain = jnp.sum(d_normed * xhat, axis=0, keepdims=True)
    d_shift = jnp.sum(d_normed, axis=0, keepdims=True)
    return g, d_gain, d_shift


def qkv_kernel(rot_ref, h_ref, par_ref, wa_ref, wb_ref, bias_ref, cos_ref, sin_ref, out_ref, nrm_ref):
    j = pl.program_id(0)

    @pl.when(j == 0)
    def _():
        xhat, _ = normalize(h_ref[...].astype(F32))
        normed = xhat * par_ref[0:1, :] + par_ref[1:2, :]
        nrm_ref[...] = turn_halves(normed, rot_ref[0]).astype(BF)

    x = dot(nrm_ref[:, :HALF], wa_ref[...]) + dot(nrm_ref[:, HALF:], wb_ref[...]) + bias_ref[...]

    @pl.when(j < 2)
    def _():
        y = x * cos_ref[...] + swap_pairs(x) * sin_ref[...]
        out_ref[...] = (y * jnp.where(j == 0, HD ** (-0.5), 1.0)).astype(BF)

    @pl.when(j == 2)
    def _():
        out_ref[...] = x.astype(BF)


def attend_kernel(
    rot_ref, q_ref, km_ref, vm_ref, kt_ref, vt_ref, segq_ref, segm_ref, segt_ref, h_ref,
    woa_ref, wob_ref, bias_ref, o_ref, lse_ref, out_ref, lse_scr,
):
    j = pl.program_id(0)
    rows = q_ref.shape[0]
    lanes = lax.broadcasted_iota(jnp.int32, (rows, 2 * HD), 1)
    q = q_ref[...]
    same_m = segq_ref[...] == segm_ref[...]
    same_t = segq_ref[...] == segt_ref[...]
    outs = []
    for side in range(2):
        mine = (lanes >= HD) if side else (lanes < HD)
        q_head = jnp.where(mine, q, jnp.zeros_like(q))
        s_m = jnp.where(same_m, dot_nt(q_head, km_ref[...]), -1e9)
        s_t = jnp.where(same_t, dot_nt(q_head, kt_ref[...]), -1e9)
        top = jnp.maximum(
            jnp.max(s_m, axis=-1, keepdims=True), jnp.max(s_t, axis=-1, keepdims=True)
        )
        p_m = jnp.exp(s_m - top)
        p_t = jnp.exp(s_t - top)
        total = jnp.sum(p_m, axis=-1, keepdims=True) + jnp.sum(p_t, axis=-1, keepdims=True)
        o = dot(p_m.astype(BF), vm_ref[...]) + dot(p_t.astype(BF), vt_ref[...])
        outs.append(o / total)
        lse_scr[...] = jnp.where(lanes == 2 * j + side, top + jnp.log(total), lse_scr[...])
    o_ref[:, pl.ds(pl.multiple_of(j * 2 * HD, 2 * HD), 2 * HD)] = jnp.where(
        lanes < HD, outs[0], outs[1]
    ).astype(BF)

    @pl.when(j == PAIRS - 1)
    def _():
        lse_ref[...] = jnp.transpose(lse_scr[...])[:16, :]
        o_all = turn_halves(o_ref[...].astype(F32), rot_ref[0]).astype(BF)
        y = dot(o_all[:, :HALF], woa_ref[...]) + dot(o_all[:, HALF:], wob_ref[...])
        out_ref[...] = (h_ref[...].astype(F32) + y + bias_ref[...]).astype(BF)


def ff_kernel(
    rot_ref, h_ref, par_ref, wia_ref, wib_ref, bias_ref, woa_ref, wob_ref, bout_ref,
    act_ref, slope_ref, nrm_ref, out_ref, acc_ref,
):
    j = pl.program_id(0)
    n = pl.num_programs(0)

    @pl.when(j == 0)
    def _():
        xhat, _ = normalize(h_ref[...].astype(F32))
        normed = xhat * par_ref[0:1, :] + par_ref[1:2, :]
        nrm_ref[...] = turn_halves(normed, rot_ref[0]).astype(BF)
        acc_ref[...] = h_ref[...].astype(F32) + bout_ref[...]

    u = dot(nrm_ref[:, :HALF], wia_ref[...]) + dot(nrm_ref[:, HALF:], wib_ref[...]) + bias_ref[...]
    cdf = 0.5 + 0.5 * lax.erf(u * (0.5**0.5))
    act = (u * cdf).astype(BF)
    act_ref[...] = act
    pdf = jnp.exp(u * u * -0.5) * 0.3989422804014327
    slope_ref[...] = (cdf + u * pdf).astype(BF)

    @pl.when(j < n // 2)
    def _():
        acc_ref[...] += dot(act, woa_ref[...])

    @pl.when(j >= n // 2)
    def _():
        acc_ref[...] += dot(act, wob_ref[...])

    @pl.when(j == n - 1)
    def _():
        out_ref[...] = acc_ref[...].astype(BF)


def ff_back_kernel(
    rot_ref, g_ref, act_ref, slope_ref, nrm_ref, wia_ref, wib_ref, woa_ref, wob_ref, h_ref, par_ref,
    dia_ref, dib_ref, doa_ref, dob_ref, dbin_ref, small_ref, out_ref, acc_ref,
):
    j = pl.program_id(0)
    n = pl.num_programs(0)

    @pl.when(j == 0)
    def _():
        acc_ref[...] = jnp.zeros_like(acc_ref)

    def step(wo_ref, do_ref):
        g = g_ref[...]
        d_up_f = dot_nt(g, wo_ref[...]) * slope_ref[...].astype(F32)
        d_up = d_up_f.astype(BF)
        do_ref[...] = dot_tn(act_ref[...], g).astype(BF)
        dbin_ref[...] = jnp.sum(d_up_f, axis=0, keepdims=True)
        dia_ref[...] = dot_tn(nrm_ref[:, :HALF], d_up).astype(BF)
        dib_ref[...] = dot_tn(nrm_ref[:, HALF:], d_up).astype(BF)
        acc_ref[:, :HALF] += dot_nt(d_up, wia_ref[...])
        acc_ref[:, HALF:] += dot_nt(d_up, wib_ref[...])

    @pl.when(j < n // 2)
    def _():
        step(woa_ref, doa_ref)

    @pl.when(j >= n // 2)
    def _():
        step(wob_ref, dob_ref)

    @pl.when(j == n - 1)
    def _():
        g = g_ref[...].astype(F32)
        d_normed = turn_halves(acc_ref[...], rot_ref[0])
        out, d_gain, d_shift = norm_backward(h_ref[...].astype(F32), par_ref[0:1, :], g, d_normed)
        out_ref[...] = out.astype(BF)
        small_ref[0:1, :] = jnp.sum(g, axis=0, keepdims=True)
        small_ref[1:2, :] = d_gain
        small_ref[2:3, :] = d_shift
        small_ref[3:8, :] = jnp.zeros((5, D), F32)


def mix_back_kernel(rot_ref, g_ref, o_ref, woa_ref, wob_ref, dmix_ref, delta_ref, doa_ref, dob_ref):
    g = g_ref[...]
    rot = rot_ref[0]
    d_mix = jnp.concatenate([dot_nt(g, woa_ref[...]), dot_nt(g, wob_ref[...])], axis=1)
    d_mix = turn_halves(d_mix, rot).astype(BF)
    dmix_ref[...] = d_mix
    o = o_ref[...].astype(F32)
    product = d_mix.astype(F32) * o
    head = lax.broadcasted_iota(jnp.int32, (16, D), 0)
    lanes = lax.broadcasted_iota(jnp.int32, (16, D), 1)
    chosen = jnp.where(lanes // HD == head, 1.0, 0.0)
    delta_ref[...] = lax.dot_general(
        chosen, product, NT, preferred_element_type=F32, precision=lax.Precision.HIGHEST
    )
    turned = turn_halves(o, rot).astype(BF)
    doa_ref[...] = dot_tn(turned[:, :HALF], g).astype(BF)
    dob_ref[...] = dot_tn(turned[:, HALF:], g).astype(BF)


def attend_back_kernel(
    q_ref, km_ref, vm_ref, kt_ref, vt_ref, do_ref, lse_ref, delta_ref, segq_ref, segm_ref, segt_ref,
    dq_ref, dkm_ref, dvm_ref, dkt_ref, dvt_ref,
):
    j = pl.program_id(0)
    rows = q_ref.shape[0]
    lanes = lax.broadcasted_iota(jnp.int32, (rows, 2 * HD), 1)
    q = q_ref[...]
    do = do_ref[...]
    zero = jnp.zeros_like(q)
    d_q = jnp.zeros((rows, 2 * HD), F32)
    sets = ((km_ref, vm_ref, segm_ref), (kt_ref, vt_ref, segt_ref))
    d_k = [0.0, 0.0]
    d_v = [0.0, 0.0]
    for side in range(2):
        mine = (lanes >= HD) if side else (lanes < HD)
        q_head = jnp.where(mine, q, zero)
        do_head = jnp.where(mine, do, zero)
        lse = lse_ref[pl.ds(2 * j + side, 1), :]
        delta = delta_ref[pl.ds(2 * j + side, 1), :]
        for i, (k_ref, v_ref, seg_ref) in enumerate(sets):
            k = k_ref[...]
            s_t = dot_nt(k, q_head)
            p_t = jnp.where(seg_ref[...] == segq_ref[...], jnp.exp(s_t - lse), 0.0)
            d_p = dot_nt(v_ref[...], do_head)
            d_s = (p_t * (d_p - delta)).astype(BF)
            d_v[i] += dot(p_t.astype(BF), do_head)
            d_k[i] += dot(d_s, q_head)
            d_q += dot_tn(d_s, jnp.where(mine, k, zero))
    dq_ref[...] = d_q
    dkm_ref[...] = d_k[0]
    dvm_ref[...] = d_v[0]
    dkt_ref[...] = d_k[1].astype(BF)
    dvt_ref[...] = d_v[1].astype(BF)


def qkv_back_kernel(
    rot_ref, dq_ref, dkm_ref, dvm_ref, dkr_ref, dvr_ref, qkv_ref, cos_ref, sin_ref, pos_ref,
    nrm_ref, wa_ref, wb_ref, h_ref, par_ref, g_ref,
    dia_ref, dib_ref, dbin_ref, small_ref, out_ref, acc_ref, dp_ref,
):
    j = pl.program_id(0)
    n = pl.num_programs(0)

    @pl.when(j == 0)
    def _():
        acc_ref[...] = jnp.zeros_like(acc_ref)
        small_ref[...] = jnp.zeros_like(small_ref)

    def turned_back(dy, y):
        swapped = swap_pairs(dy)
        d_angle = y * swapped - swap_pairs(y) * dy
        small_ref[3:4, :] += jnp.sum(d_angle * pos_ref[:, 0:1], axis=0, keepdims=True)
        small_ref[4:5, :] += jnp.sum(d_angle * pos_ref[:, 1:2], axis=0, keepdims=True)
        return dy * cos_ref[...] - swapped * sin_ref[...]

    @pl.when(j == 0)
    def _():
        d_y = dq_ref[...] * HD ** (-0.5)
        y = qkv_ref[...].astype(F32) * HD**0.5
        dp_ref[...] = turned_back(d_y, y)

    @pl.when(j == 1)
    def _():
        d_y = dkm_ref[...] + dkr_ref[...].astype(F32)
        dp_ref[...] = turned_back(d_y, qkv_ref[...].astype(F32))

    @pl.when(j == 2)
    def _():
        dp_ref[...] = dvm_ref[...] + dvr_ref[...].astype(F32)

    d_f = dp_ref[...]
    d_p = d_f.astype(BF)
    dbin_ref[...] = jnp.sum(d_f, axis=0, keepdims=True)
    dia_ref[...] = dot_tn(nrm_ref[:, :HALF], d_p).astype(BF)
    dib_ref[...] = dot_tn(nrm_ref[:, HALF:], d_p).astype(BF)
    acc_ref[:, :HALF] += dot_nt(d_p, wa_ref[...])
    acc_ref[:, HALF:] += dot_nt(d_p, wb_ref[...])

    @pl.when(j == n - 1)
    def _():
        g = g_ref[...].astype(F32)
        d_normed = turn_halves(acc_ref[...], rot_ref[0])
        out, d_gain, d_shift = norm_backward(h_ref[...].astype(F32), par_ref[0:1, :], g, d_normed)
        out_ref[...] = out.astype(BF)
        small_ref[0:1, :] = jnp.sum(g, axis=0, keepdims=True)
        small_ref[1:2, :] = d_gain
        small_ref[2:3, :] = d_shift


def params_of(n=1):
    return pltpu.CompilerParams(
        dimension_semantics=("arbitrary",) * n, vmem_limit_bytes=VMEM_BYTES
    )


def whole(shape):
    return pl.BlockSpec(shape, lambda *_: (0,) * len(shape))


def sds(shape, dtype):
    return jax.ShapeDtypeStruct(shape, dtype)


def cost(flops, nbytes, trans=0):
    return pl.CostEstimate(flops=flops, bytes_accessed=nbytes, transcendentals=trans)


def qkv_call(rot, h, par, wa, wb, bias, cosines, sines):
    t = h.shape[0]
    return pl.pallas_call(
        qkv_kernel,
        out_shape=(sds((t, QKV), BF), sds((t, D), BF)),
        grid_spec=pltpu.PrefetchScalarGridSpec(
            num_scalar_prefetch=1,
            grid=(3,),
            in_specs=[
                whole((t, D)), whole((8, D)),
                pl.BlockSpec((HALF, D), lambda j, r: (0, j)),
                pl.BlockSpec((HALF, D), lambda j, r: (0, j)),
                pl.BlockSpec((1, D), lambda j, r: (0, j)),
                whole((t, D)), whole((t, D)),
            ],
            out_specs=[pl.BlockSpec((t, D), lambda j, r: (0, j)), whole((t, D))],
        ),
        compiler_params=params_of(),
        cost_estimate=cost(2 * t * D * QKV, 2 * D * QKV + 8 * t * D + 2 * t * QKV),
        name="qkv",
    )(rot, h, par, wa, wb, bias, cosines, sines)


def attend_call(rot, qkv, kv_t, seg_col, seg_m, seg_t, h, woa, wob, bias):
    t = h.shape[0]
    w = 2 * HD
    return pl.pallas_call(
        attend_kernel,
        out_shape=(sds((t, D), BF), sds((16, t), F32), sds((t, D), BF)),
        grid_spec=pltpu.PrefetchScalarGridSpec(
            num_scalar_prefetch=1,
            grid=(PAIRS,),
            in_specs=[
                pl.BlockSpec((t, w), lambda j, r: (0, j)),
                pl.BlockSpec((t, w), lambda j, r: (0, j + PAIRS)),
                pl.BlockSpec((t, w), lambda j, r: (0, j + 2 * PAIRS)),
                pl.BlockSpec((t, w), lambda j, r: (0, j)),
                pl.BlockSpec((t, w), lambda j, r: (0, j + PAIRS)),
                whole((t, 1)), whole((1, t)), whole((1, t)), whole((t, D)),
                whole((HALF, D)), whole((HALF, D)), whole((1, D)),
            ],
            out_specs=[whole((t, D)), whole((16, t)), whole((t, D))],
            scratch_shapes=[pltpu.VMEM((t, w), F32)],
        ),
        compiler_params=params_of(),
        cost_estimate=cost(8 * t * t * D * 4, 16 * t * D, 2 * t * t * HEADS),
        name="attend",
    )(rot, qkv, qkv, qkv, kv_t, kv_t, seg_col, seg_m, seg_t, h, woa, wob, bias)


def ff_specs(t, blocks):
    width = FF // blocks
    half = blocks // 2
    w_in = pl.BlockSpec((HALF, width), lambda j, r: (0, (j + half * r[0]) % blocks))
    b_in = pl.BlockSpec((1, width), lambda j, r: (0, (j + half * r[0]) % blocks))
    w_a = pl.BlockSpec((width, D), lambda j, r: (jnp.minimum(j, half - 1), 0))
    w_b = pl.BlockSpec((width, D), lambda j, r: (jnp.maximum(j - half, 0), 0))
    hid = pl.BlockSpec((t, width), lambda j, r: (0, j))
    return w_in, b_in, w_a, w_b, hid


def ff_call(rot, h, par, wia, wib, bias, woa, wob, bout):
    t = h.shape[0]
    blocks = 6
    w_in, b_in, w_a, w_b, hid = ff_specs(t, blocks)
    return pl.pallas_call(
        ff_kernel,
        out_shape=(sds((t, FF), BF), sds((t, FF), BF), sds((t, D), BF), sds((t, D), BF)),
        grid_spec=pltpu.PrefetchScalarGridSpec(
            num_scalar_prefetch=1,
            grid=(blocks,),
            in_specs=[whole((t, D)), whole((8, D)), w_in, w_in, b_in, w_a, w_b, whole((1, D))],
            out_specs=[hid, hid, whole((t, D)), whole((t, D))],
            scratch_shapes=[pltpu.VMEM((t, D), F32)],
        ),
        compiler_params=params_of(),
        cost_estimate=cost(4 * t * D * FF, 4 * D * FF + 4 * t * FF, 2 * t * FF),
        name="feed",
    )(rot, h, par, wia, wib, bias, woa, wob, bout)


def ff_back_call(rot, g, act, slope, nrm, wia, wib, woa, wob, h, par):
    t = h.shape[0]
    blocks = 6
    w_in, b_in, w_a, w_b, hid = ff_specs(t, blocks)
    return pl.pallas_call(
        ff_back_kernel,
        out_shape=(
            sds((HALF, FF), BF), sds((HALF, FF), BF), sds((FF // 2, D), BF), sds((FF // 2, D), BF),
            sds((1, FF), F32), sds((8, D), F32), sds((t, D), BF),
        ),
        grid_spec=pltpu.PrefetchScalarGridSpec(
            num_scalar_prefetch=1,
            grid=(blocks,),
            in_specs=[
                whole((t, D)), hid, hid, whole((t, D)), w_in, w_in, w_a, w_b, whole((t, D)),
                whole((8, D)),
            ],
            out_specs=[w_in, w_in, w_a, w_b, b_in, whole((8, D)), whole((t, D))],
            scratch_shapes=[pltpu.VMEM((t, D), F32)],
        ),
        compiler_params=params_of(),
        cost_estimate=cost(8 * t * D * FF, 8 * D * FF + 4 * t * FF),
        name="feed_back",
    )(rot, g, act, slope, nrm, wia, wib, woa, wob, h, par)


def mix_back_call(rot, g, o, woa, wob):
    t = g.shape[0]
    return pl.pallas_call(
        mix_back_kernel,
        out_shape=(sds((t, D), BF), sds((16, t), F32), sds((HALF, D), BF), sds((HALF, D), BF)),
        grid_spec=pltpu.PrefetchScalarGridSpec(
            num_scalar_prefetch=1,
            grid=(1,),
            in_specs=[whole((t, D)), whole((t, D)), whole((HALF, D)), whole((HALF, D))],
            out_specs=[whole((t, D)), whole((16, t)), whole((HALF, D)), whole((HALF, D))],
        ),
        compiler_params=params_of(),
        cost_estimate=cost(4 * t * D * D, 4 * D * D + 6 * t * D),
        name="mix_back",
    )(rot, g, o, woa, wob)


def attend_back_call(qkv, kv_t, dmix, lse, delta, seg_row, seg_m, seg_t):
    t = dmix.shape[0]
    w = 2 * HD
    col = pl.BlockSpec((t, w), lambda j: (0, j))
    return pl.pallas_call(
        attend_back_kernel,
        out_shape=(sds((t, D), F32), sds((t, D), F32), sds((t, D), F32), sds((t, D), BF), sds((t, D), BF)),
        grid=(PAIRS,),
        in_specs=[
            col,
            pl.BlockSpec((t, w), lambda j: (0, j + PAIRS)),
            pl.BlockSpec((t, w), lambda j: (0, j + 2 * PAIRS)),
            col,
            pl.BlockSpec((t, w), lambda j: (0, j + PAIRS)),
            col, whole((16, t)), whole((16, t)), whole((1, t)), whole((t, 1)), whole((t, 1)),
        ],
        out_specs=[col] * 5,
        compiler_params=params_of(),
        cost_estimate=cost(20 * t * t * D * 4, 30 * t * D, 2 * t * t * HEADS),
        name="attend_back",
    )(qkv, qkv, qkv, kv_t, kv_t, dmix, lse, delta, seg_row, seg_m, seg_t)


def qkv_back_call(rot, dq, dkm, dvm, dkr, dvr, qkv, cosines, sines, pos, nrm, wa, wb, h, par, g):
    t = h.shape[0]
    w_in = pl.BlockSpec((HALF, D), lambda j, r: (0, j))
    rows = whole((t, D))
    return pl.pallas_call(
        qkv_back_kernel,
        out_shape=(
            sds((HALF, QKV), BF), sds((HALF, QKV), BF), sds((1, QKV), F32), sds((8, D), F32),
            sds((t, D), BF),
        ),
        grid_spec=pltpu.PrefetchScalarGridSpec(
            num_scalar_prefetch=1,
            grid=(3,),
            in_specs=[
                rows, rows, rows, rows, rows, pl.BlockSpec((t, D), lambda j, r: (0, j)), rows, rows,
                whole((t, 2)), rows, w_in, w_in, rows, whole((8, D)), rows,
            ],
            out_specs=[w_in, w_in, pl.BlockSpec((1, D), lambda j, r: (0, j)), whole((8, D)), rows],
            scratch_shapes=[pltpu.VMEM((t, D), F32), pltpu.VMEM((t, D), F32)],
        ),
        compiler_params=params_of(),
        cost_estimate=cost(4 * t * D * QKV, 4 * D * QKV + 30 * t * D),
        name="qkv_back",
    )(rot, dq, dkm, dvm, dkr, dvr, qkv, cosines, sines, pos, nrm, wa, wb, h, par, g)


def layout(image_sides, capacity):
    counts = image_sides * image_sides
    end_pos = jnp.cumsum(counts)
    start_pos = end_pos - counts
    positions = jnp.arange(capacity, dtype=jnp.int32)
    segment = jnp.sum((positions[:, None] >= end_pos[None, :]).astype(jnp.int32), axis=1)
    slot_ids = jnp.arange(image_sides.shape[-1], dtype=jnp.int32)
    one_hot = (segment[:, None] == slot_ids[None, :]).astype(jnp.int32)
    start_tok = jnp.sum(one_hot * start_pos[None, :], axis=1)
    side_len = jnp.maximum(jnp.sum(one_hot * image_sides[None, :], axis=1), 1)
    local_idx = positions - start_tok
    is_valid = segment < image_sides.shape[-1]
    patch_row = jnp.where(is_valid, local_idx // side_len, 0)
    patch_col = jnp.where(is_valid, local_idx % side_len, 0)
    return segment, patch_row, patch_col, is_valid


def turning(freq, pos):
    wide = jnp.concatenate([freq.reshape(2, HEADS, HD // 2)] * 2, axis=2).reshape(2, D)
    angles = pos[:, 0:1] * wide[0][None, :] + pos[:, 1:2] * wide[1][None, :]
    low = (jnp.arange(D) % HD) < HD // 2
    sines = jnp.sin(angles)
    return jnp.cos(angles), jnp.where(low[None, :], -sines, sines)


def flipped(x, axis, bit):
    return lax.ppermute(x, axis, [(i, i ^ bit) for i in range(lax.axis_size(axis))])


def to_owners(blocks, section, core):
    stacked = jnp.stack(blocks)
    got = [stacked[section]] + [flipped(stacked[section ^ d], "section", d) for d in (1, 2, 3)]
    here = (section // 2) == core
    near = jnp.stack(got[:2])
    away = jnp.stack(got[2:])
    mine = jnp.where(here, near, away)
    other = flipped(jnp.where(here, away, near), "group", 1)

    def in_order(pair):
        return jnp.where(section % 2 == 0, pair, pair[::-1])

    mine, other = in_order(mine), in_order(other)
    first = jnp.where(core == 0, mine, other)
    second = jnp.where(core == 0, other, mine)
    return jnp.concatenate([first, second], axis=1).reshape(-1, D)


MESH = pl.DeviceIdType.MESH
SMALL = (16, D)
SEMS = 20
LINE = 4


def unit_shape(s, part):
    if s % 2:
        return (FF // 2, D) if part else (HALF, FF)
    return (HALF, D) if part else (HALF, QKV)


def grad_shape(s, part):
    if s % 2:
        return (FF // 2, D) if part else (HALF, FF)
    return (D, D) if part else (HALF, 2 * D)


def piece_shape(s, part):
    r, w = grad_shape(s, part)
    return (r // 8, w // 2)


def held_shape(s, part):
    r, w = grad_shape(s, part)
    return (4, 2, r // 8, w)


def columns_of(k, width):
    return pl.ds(pl.multiple_of((k % 2) * width, width), width)


def flip(v, bit):
    if bit == 1:
        return v + 1 - 2 * (v % 2)
    if bit == 2:
        return (v + 2) % 4
    return 3 - v


def here():
    return lax.axis_index("section"), lax.axis_index("group"), lax.axis_index("dp")


def loop(n, body):
    def one(i, carried):
        body(i)
        return carried

    lax.fori_loop(0, n, one, 0)


def greet(plane, line):
    c, g, z = here()
    barrier = pltpu.get_barrier_semaphore()
    pl.semaphore_signal(barrier, inc=1, device_id={"group": 1 - g}, device_id_type=MESH)
    count = 1
    for bit in (1, 2, 3):
        if plane:
            for core in (g, 1 - g):
                pl.semaphore_signal(
                    barrier, inc=1, device_id={"section": flip(c, bit), "group": core},
                    device_id_type=MESH,
                )
                count += 1
        if line:
            pl.semaphore_signal(barrier, inc=1, device_id={"dp": flip(z, bit)}, device_id_type=MESH)
            count += 1
    pl.semaphore_wait(barrier, count)


def guarded(cond, act):
    if cond is None:
        act()
    else:
        pl.when(cond)(act)


def accumulate(into, term, rows):
    strip = 32 if rows % 32 == 0 else 16

    def one(i):
        at = pl.ds(pl.multiple_of(i * strip, strip), strip)
        into[at, :] = (into[at, :].astype(F32) + term[at, :].astype(F32)).astype(BF)

    loop(rows // strip, one)


class Unit:
    def __init__(
        self, s, part, send, recv, own=None, quarter=None, final=None, plane=None, line=None,
        held=None, whole=None,
    ):
        self.s, self.part, self.own, self.quarter_ref, self.final = s, part, own, quarter, final
        self.send, self.recv = send, recv
        self.whole = whole
        self.rows, self.cols = grad_shape(s, part)
        self.plane1, self.plane2 = plane or (None, None)
        self.up_in, self.down_in = line or (None, None)
        self.held = held
        self.pending = []

    def push(self, cond, src, dst, k, device):
        copy = pltpu.make_async_remote_copy(
            src_ref=src, dst_ref=dst, send_sem=self.send.at[k], recv_sem=self.recv.at[k],
            device_id=device, device_id_type=MESH,
        )
        guarded(cond, copy.start)
        self.pending.append((cond, copy))

    def landed(self, cond, dst, k):
        copy = pltpu.make_async_remote_copy(
            src_ref=dst, dst_ref=dst, send_sem=self.send.at[k], recv_sem=self.recv.at[k],
            device_id={"group": 1 - lax.axis_index("group")}, device_id_type=MESH,
        )
        guarded(cond, copy.wait_recv)

    def finish(self):
        for cond, copy in self.pending:
            guarded(cond, copy.wait_send)

    def quarter(self, q):
        rows = self.rows // 4
        return self.own.at[pl.ds(pl.multiple_of(q * rows, rows), rows), :]

    def mine(self):
        if self.quarter_ref is not None:
            return self.quarter_ref
        return self.quarter(lax.axis_index("section"))

    def piece(self, k):
        rows, cols = self.rows // 8, self.cols // 2
        return self.mine().at[
            pl.ds(pl.multiple_of((k // 2) * rows, rows), rows),
            pl.ds(pl.multiple_of((k % 2) * cols, cols), cols),
        ]

    def first_step(self):
        c, _, _ = here()
        x, y = c % 2, c // 2
        other = {"section": flip(c, 2 if self.part else 1)}
        for b in range(2):
            q = 2 * (1 - y) + b if self.part else 2 * b + 1 - x
            self.push(None, self.quarter(q), self.plane1.at[b], 1 + b, other)

    def second_step(self):
        c, _, _ = here()
        x, y = c % 2, c // 2
        rows = self.rows // 4
        other = {"section": flip(c, 1 if self.part else 2)}
        for b in range(2):
            self.landed(None, self.plane1.at[b], 1 + b)
        b = (1 - x) if self.part else (1 - y)
        q = (2 * y + 1 - x) if self.part else (2 * (1 - y) + x)
        accumulate(self.quarter(q), self.plane1.at[b], rows)
        self.push(None, self.quarter(q), self.plane2, 3, other)
        accumulate(self.mine(), self.plane1.at[1 - b], rows)

    def third_step(self):
        self.landed(None, self.plane2, 3)
        accumulate(self.mine(), self.plane2, self.rows // 4)

    def line_step(self, t):
        _, _, z = here()
        n = LINE
        rows = self.rows // 8
        up = (z < n - 1) & (z <= t)
        down = (z > 0) & (z >= n - 1 - t)
        k_up = jnp.minimum(n - 1 - t + z, n - 1)
        k_down = jnp.maximum(z - (n - 1) + t, 0)
        if t > 0:

            @pl.when(up & (z > 0))
            def _():
                self.landed(None, self.up_in.at[t - 1], 4 + t - 1)
                accumulate(self.piece(k_up), self.up_in.at[t - 1], rows)

            @pl.when(down & (z < n - 1))
            def _():
                self.landed(None, self.down_in.at[t - 1], 7 + t - 1)
                accumulate(self.piece(k_down), self.down_in.at[t - 1], rows)

        self.push(up, self.piece(k_up), self.up_in.at[t], 4 + t, {"dp": jnp.minimum(z + 1, n - 1)})
        self.push(down, self.piece(k_down), self.down_in.at[t], 7 + t, {"dp": jnp.maximum(z - 1, 0)})

    def line_end(self):
        _, _, z = here()
        n = LINE
        rows = self.rows // 8

        @pl.when(z > 0)
        def _():
            self.landed(None, self.up_in.at[n - 2], 4 + n - 2)
            accumulate(self.piece(z), self.up_in.at[n - 2], rows)

        @pl.when(z < n - 1)
        def _():
            self.landed(None, self.down_in.at[n - 2], 7 + n - 2)
            accumulate(self.piece(z), self.down_in.at[n - 2], rows)

    def held_at(self, k, q=None):
        cols = columns_of(k, self.cols // 2)
        return self.held.at[:, k // 2, :, cols] if q is None else self.held.at[q, k // 2, :, cols]

    def whole_at(self, k):
        return self.whole.at[k // 2, :, columns_of(k, self.cols // 2)]

    def last_piece(self):
        return self.final if self.final is not None else self.piece(here()[2])

    def own_piece(self):
        _, _, z = here()
        return pltpu.make_async_copy(
            self.last_piece(), self.held_at(z, self.s), self.send.at[10 + self.s]
        )

    def gather(self):
        c, _, z = here()
        for q in range(4):
            if q == self.s:
                pl.when(c == q)(self.own_piece().start)
            else:
                self.push(
                    c == q, self.last_piece(), self.held_at(z, q), 10 + q, {"section": self.s}
                )

    def share_step(self, t):
        _, _, z = here()
        n = LINE
        whole = self.whole_at
        if t == 0:
            copy = pltpu.make_async_copy(self.last_piece(), whole(z), self.send.at[0])
            copy.start()
            copy.wait()
        else:
            self.landed(z >= t, whole(jnp.maximum(z - t, 0)), 14 + t - 1)
            self.landed(z + t < n, whole(jnp.minimum(z + t, n - 1)), 17 + t - 1)
        if t < n - 1:
            low, high = jnp.maximum(z - t, 0), jnp.minimum(z + t, n - 1)
            self.push(
                (z >= t) & (z < n - 1), whole(low), whole(low), 14 + t,
                {"dp": jnp.minimum(z + 1, n - 1)},
            )
            self.push(
                (z + t < n) & (z > 0), whole(high), whole(high), 17 + t,
                {"dp": jnp.maximum(z - 1, 0)},
            )

    def whole_copy(self):
        return pltpu.make_async_copy(self.whole, self.held.at[self.s], self.send.at[10 + self.s])

    def whole_gather(self):
        c, _, _ = here()
        for q in range(4):
            if q == self.s:
                pl.when(c == q)(self.whole_copy().start)
            else:
                self.push(c == q, self.whole, self.held.at[q], 10 + q, {"section": self.s})

    def whole_end(self):
        c, _, _ = here()
        for q in range(4):
            if q == self.s:
                pl.when(c == q)(self.whole_copy().wait)
            else:
                self.landed(c == self.s, self.held.at[q], 10 + q)

    def out_step(self, t):
        c, _, z = here()
        n = LINE
        mine = c == self.s
        held = self.held_at
        if t == 0:
            for q in range(4):
                if q == self.s:
                    pl.when(mine)(self.own_piece().wait)
                else:
                    self.landed(mine, held(z, q), 10 + q)
        else:
            self.landed(mine & (z >= t), held(jnp.maximum(z - t, 0)), 14 + t - 1)
            self.landed(mine & (z + t < n), held(jnp.minimum(z + t, n - 1)), 17 + t - 1)
        if t < n - 1:
            low, high = jnp.maximum(z - t, 0), jnp.minimum(z + t, n - 1)
            self.push(
                mine & (z >= t) & (z < n - 1), held(low), held(low), 14 + t,
                {"dp": jnp.minimum(z + 1, n - 1)},
            )
            self.push(
                mine & (z + t < n) & (z > 0), held(high), held(high), 17 + t,
                {"dp": jnp.maximum(z - 1, 0)},
            )


class Delivery:
    def __init__(self, sources, parts, out, send, recv):
        self.sources, self.parts, self.out, self.send, self.recv = sources, parts, out, send, recv

    def rows(self, block):
        size = self.sources[self.parts[0][0]].shape[0] // 2
        return pl.ds(block * size, size)

    def copies(self, s, block):
        c, g, _ = here()
        slot = self.out.at[c % 2, g, self.rows(block), :]
        source = self.sources[s].at[self.rows(block), :]
        near = pltpu.make_async_copy(source, slot, self.send.at[s, block])
        far = pltpu.make_async_remote_copy(
            src_ref=source, dst_ref=slot, send_sem=self.send.at[s, block],
            recv_sem=self.recv.at[(c % 2) * 2 + g, block],
            device_id={"section": s, "group": c // 2}, device_id_type=MESH,
        )
        return near, far, (c == s) & (g == c // 2)

    def start(self, parts):
        for part in parts:
            near, far, stays = self.copies(*part)
            pl.when(stays)(near.start)
            pl.when(jnp.logical_not(stays))(far.start)

    def finish(self):
        c, g, _ = here()
        for s, block in self.parts:
            near, far, stays = self.copies(s, block)
            pl.when(stays)(near.wait)
            pl.when(jnp.logical_not(stays))(far.wait_send)
            for m in range(2):
                for half in range(2):
                    slot = self.out.at[m, half, self.rows(block), :]
                    copy = pltpu.make_async_remote_copy(
                        src_ref=slot, dst_ref=slot, send_sem=self.send.at[0, 0],
                        recv_sem=self.recv.at[2 * m + half, block], device_id={"group": 1 - g},
                        device_id_type=MESH,
                    )
                    arrives = (c == s) & jnp.logical_not((2 * g + m == c) & (g == half))
                    pl.when(arrives)(copy.wait_recv)


ALL = tuple((s, block) for block in range(2) for s in range(4))


def feed_back_kernel(s, carry, *refs):
    delivers = carry is None
    wim, wit, wom, wot, act_in, slope_in, streams = refs[:7]
    refs = refs[7:]
    count = 0 if delivers else len(carry.all)
    carried, refs = refs[:count], refs[count:]
    g_ref, nrm, par = refs[:3]
    d_in, d_out = refs[3:5]
    refs = refs[5:]
    if delivers:
        delivered, refs = refs[0], refs[1:]
    results, refs = refs[:count], refs[count:]
    dbin_ref, small_ref, out_ref = refs[:3]
    w_in, w_out, act, slope, h, own_i, own_o, their_i, their_o, core_i, core_o, acc, nrm_t = refs[3:16]
    load_sem, core_s, core_r, out_sem = refs[16:20]
    refs = refs[20:]
    _, g, _ = here()
    partner = {"group": 1 - g}
    width = FF // CHUNKS
    third = CHUNKS // 2

    def column(j):
        b = (j + g * third) % CHUNKS
        return pl.ds(pl.multiple_of(b * width, width), width)

    def line_of(j):
        return pl.ds(pl.multiple_of(j * width, width), width)

    def loads(j):
        cols, rows = column(j), line_of(j % third)
        first = j < third
        return (
            (None, pltpu.make_async_copy(wim.at[:, cols], w_in.at[0, :, cols], load_sem.at[j, 0])),
            (None, pltpu.make_async_copy(wit.at[:, cols], w_in.at[1, :, cols], load_sem.at[j, 1])),
            (first, pltpu.make_async_copy(wom.at[rows, :], w_out.at[line_of(j), :], load_sem.at[j, 2])),
            (
                jnp.logical_not(first),
                pltpu.make_async_copy(wot.at[rows, :], w_out.at[line_of(j), :], load_sem.at[j, 2]),
            ),
            (None, pltpu.make_async_copy(act_in.at[:, line_of(j)], act.at[:, line_of(j)], load_sem.at[j, 3])),
            (None, pltpu.make_async_copy(slope_in.at[:, line_of(j)], slope.at[:, line_of(j)], load_sem.at[j, 4])),
        )

    def load(j):
        for cond, copy in loads(j):
            guarded(cond, copy.start)

    def core_copies(j):
        cols, rows = column(j), line_of(j % third)
        return (
            pltpu.make_async_remote_copy(
                src_ref=their_i.at[:, cols], dst_ref=core_i.at[:, cols], send_sem=core_s.at[j, 0],
                recv_sem=core_r.at[j, 0], device_id=partner, device_id_type=MESH,
            ),
            pltpu.make_async_remote_copy(
                src_ref=their_o.at[rows, :], dst_ref=core_o.at[rows, :], send_sem=core_s.at[j, 1],
                recv_sem=core_r.at[j, 1], device_id=partner, device_id_type=MESH,
            ),
        )

    loop(CHUNKS, load)
    stream_copy = pltpu.make_async_copy(streams.at[s - 1], h, out_sem.at[2])
    stream_copy.start()
    if not delivers:
        carry.load(carried, results, refs)
    greet(True, not delivers)
    if delivers:
        delivery = Delivery([streams.at[i] for i in range(4)], ALL, delivered, *refs)
        delivery.start(ALL)
    else:
        carry.begin()
    acc[...] = jnp.zeros_like(acc)
    nrm_t[...] = jnp.transpose(nrm[...])

    def block(j):
        for cond, copy in loads(j):
            guarded(cond, copy.wait)
        cols, rows = column(j), line_of(j)
        grad = g_ref[...]
        d_up_f = dot_nt(grad, w_out[rows, :]) * slope[:, rows].astype(F32)
        d_up = d_up_f.astype(BF)
        d_o = dot_tn(act[:, rows], grad).astype(BF)
        dbin_ref[:, cols] = jnp.sum(d_up_f, axis=0, keepdims=True)
        their_i[:, cols] = dot(nrm_t[HALF:, :], d_up).astype(BF)
        inward, outward = core_copies(j)
        inward.start()

        @pl.when(j >= third)
        def _():
            their_o[line_of(j % third), :] = d_o
            outward.start()

        @pl.when(j < third)
        def _():
            own_o[line_of(j % third), :] = d_o

        own_i[:, cols] = dot(nrm_t[:HALF, :], d_up).astype(BF)
        acc[:, :HALF] += dot_nt(d_up, w_in[0, :, cols])
        acc[:, HALF:] += dot_nt(d_up, w_in[1, :, cols])

    if delivers:
        loop(CHUNKS, block)
    else:
        for i in range(3):
            loop(CHUNKS // 3, lambda j, i=i: block(j + CHUNKS // 3 * i))
            carry.step(i + 1)
    stream_copy.wait()
    grad = g_ref[...].astype(F32)
    d_normed = turn_halves(acc[...], g)
    out, d_gain, d_shift = norm_backward(h[...].astype(F32), par[0:1, :], grad, d_normed)
    out_ref[...] = out.astype(BF)
    small_ref[0:1, :] = jnp.sum(grad, axis=0, keepdims=True)
    small_ref[1:2, :] = d_gain
    small_ref[2:3, :] = d_shift
    small_ref[3:8, :] = jnp.zeros((5, D), F32)

    def ended(j):
        inward, outward = core_copies(j)
        inward.wait()
        pl.when(j >= third)(outward.wait)

    loop(CHUNKS, ended)
    accumulate(own_i, core_i, HALF)
    saves = [pltpu.make_async_copy(own_i, d_in, out_sem.at[0])]
    saves[0].start()
    accumulate(own_o, core_o, FF // 2)
    saves.append(pltpu.make_async_copy(own_o, d_out, out_sem.at[1]))
    saves[1].start()
    if delivers:
        delivery.finish()
    else:
        carry.end()
    for copy in saves:
        copy.wait()


def every(units, act, *args):
    for unit in units:
        getattr(unit, act)(*args)


class Carry:
    last = False

    def __init__(self, plane, line, hold):
        self.planes = [(plane, 0), (plane, 1)]
        self.line, self.hold = line, hold
        self.all = self.planes + list(line) + list(hold)

    def results(self):
        out = []
        for u in self.planes:
            r, w = grad_shape(*u)
            out.append(sds((r // 4, w), BF))
        out += [sds(piece_shape(*u), BF) for u in self.line]
        return out + [sds(held_shape(*u), BF) for u in self.hold]

    def scratch(self):
        out = []
        for u in self.planes:
            r, w = grad_shape(*u)
            out += [pltpu.VMEM((r, w), BF), pltpu.VMEM((2, r // 4, w), BF), pltpu.VMEM((r // 4, w), BF)]
        for u in self.line:
            r, w = grad_shape(*u)
            out += [pltpu.VMEM((r // 4, w), BF)] + [pltpu.VMEM((3,) + piece_shape(*u), BF)] * 2
        out += [pltpu.VMEM(piece_shape(*u), BF) for u in self.hold]
        dma = pltpu.SemaphoreType.DMA
        return out + [dma((len(self.all), SEMS)), dma((len(self.all), SEMS))]

    def load(self, sources, results, refs):
        send, recv = refs[-2:]
        refs = list(refs[:-2])
        self.units, self.loads, self.targets = [], [], results
        for i, u in enumerate(self.all):
            sems = (send.at[i], recv.at[i])
            if i < 2:
                own, first, second = refs.pop(0), refs.pop(0), refs.pop(0)
                unit = Unit(*u, *sems, own=own, plane=(first, second))
            elif i < 2 + len(self.line):
                own, up, down = refs.pop(0), refs.pop(0), refs.pop(0)
                unit = Unit(*u, *sems, quarter=own, line=(up, down))
            else:
                own = refs.pop(0)
                unit = Unit(*u, *sems, final=own, held=results[i])
            copy = pltpu.make_async_copy(sources[i], own, sems[0].at[0])
            copy.start()
            self.units.append(unit)
            self.loads.append(copy)
        n = 2 + len(self.line)
        self.plane_units, self.line_units, self.hold_units = (
            self.units[:2], self.units[2:n], self.units[n:],
        )

    def begin(self):
        for copy in self.loads:
            copy.wait()
        for unit in self.hold_units:
            unit.gather()
        for unit in self.line_units:
            unit.line_step(0)
        for unit in self.plane_units:
            unit.first_step()

    def step(self, i):
        for unit in self.line_units:
            if i < LINE - 1:
                unit.line_step(i)
            else:
                unit.line_end()
        if i == 3:
            for unit in self.plane_units:
                unit.second_step()
        for unit in self.hold_units:
            if i < 3:
                unit.out_step(i - 1)

    def late_step(self):
        for unit in self.hold_units:
            unit.out_step(LINE - 2)

    def end(self):
        saves = [
            pltpu.make_async_copy(unit.last_piece(), target, unit.send.at[0])
            for unit, target in zip(self.line_units, self.targets[2:])
        ]
        for copy in saves:
            copy.start()
        for unit, target in zip(self.plane_units, self.targets):
            unit.third_step()
            copy = pltpu.make_async_copy(unit.mine(), target, unit.send.at[0])
            copy.start()
            saves.append(copy)
        for unit in self.hold_units:
            unit.out_step(LINE - 1)
        for copy in saves:
            copy.wait()
        for unit in self.units:
            unit.finish()


class Finish:
    all = ((1, 0), (1, 1), (2, 0), (2, 1), (3, 0), (3, 1))
    own_units = ((0, 0), (0, 1))
    last = True

    def results(self):
        held = [sds(held_shape(s, part), BF) for s in (0, 1) for part in (0, 1)]
        return held + [sds((2, 2, self.tokens, D), BF), sds(SMALL, F32)]

    def scratch(self):
        out = []
        for u in self.all[:2]:
            r, w = grad_shape(*u)
            out += [pltpu.VMEM((r, w), BF), pltpu.VMEM((2, r // 4, w), BF), pltpu.VMEM((r // 4, w), BF)]
        for u in self.all[2:4]:
            r, w = grad_shape(*u)
            out.append(pltpu.VMEM((r // 4, w), BF))
        out += [pltpu.VMEM(piece_shape(*u), BF) for u in self.all[4:]]
        for u in self.own_units:
            r, w = grad_shape(*u)
            out += [pltpu.VMEM((2, r // 4, w), BF), pltpu.VMEM((r // 4, w), BF)]
        for u in self.all[:4] + self.own_units:
            out += [pltpu.VMEM((3,) + piece_shape(*u), BF)] * 2
        out += [pltpu.VMEM(held_shape(*u)[1:], BF) for u in ((1, 1), (0, 1))]
        dma = pltpu.SemaphoreType.DMA
        small = [pltpu.VMEM((n,) + SMALL, F32) for n in (4, 4, 4, 2, 3, 4)]
        return out + small + [
            dma((8, SEMS)), dma((8, SEMS)), dma((7,)), dma((7,)), dma((4, 2)), dma((4, 2)),
        ]

    def load(self, sources, results, refs, own, streams, small_in):
        refs = list(refs)

        def take(n):
            out = refs[:n]
            del refs[:n]
            return out

        halves = [take(3), take(3)]
        quarters, finals = take(2), take(2)
        planes = [take(2), take(2)]
        lines = [take(2) for _ in range(6)]
        wholes = take(2)
        self.sm, self.sm_core, self.sm_x, self.sm_got, self.sm_y, self.sm_z = take(6)
        send, recv, self.sm_send, self.sm_recv, del_send, del_recv = refs
        held, delivered, self.small_out = results[:4], results[4], results[5]
        self.small_in = small_in

        def unit(i, u, **more):
            return Unit(*u, send.at[i], recv.at[i], held=held[2 * (u[0] % 2) + u[1]], **more)

        self.f1 = [
            unit(i, self.all[i], own=halves[i][0], plane=halves[i][1:], line=lines[i],
                 whole=wholes[0] if i else None)
            for i in range(2)
        ]
        self.a2 = [unit(2 + i, self.all[2 + i], quarter=quarters[i], line=lines[2 + i]) for i in range(2)]
        self.f3 = [unit(4 + i, self.all[4 + i], final=finals[i]) for i in range(2)]
        self.a0 = [
            unit(6 + i, self.own_units[i], own=own[i], plane=planes[i], line=lines[4 + i],
                 whole=wholes[1] if i else None)
            for i in range(2)
        ]
        self.units = self.f1 + self.a2 + self.f3 + self.a0
        self.delivery = Delivery(streams, ALL, delivered, del_send, del_recv)
        self.loads = [
            pltpu.make_async_copy(source, target, send.at[i, 0])
            for i, (source, target) in enumerate(
                zip(sources, [halves[0][0], halves[1][0], *quarters, *finals])
            )
        ]
        for copy in self.loads:
            copy.start()
        self.pending = []

    def begin(self):
        for copy in self.loads:
            copy.wait()
        every(self.f3, "gather")
        every(self.a2, "line_step", 0)
        every(self.f1, "first_step")

    def step(self, i):
        if i < 3:
            every(self.a2, "line_step", i)
            self.f3[0].out_step(i - 1)
        else:
            every(self.a2, "line_end")
            every(self.a2, "gather")
            every(self.f1, "second_step")

    def late_step(self):
        pass

    def small_push(self, src, dst, k, device):
        copy = pltpu.make_async_remote_copy(
            src_ref=src, dst_ref=dst, send_sem=self.sm_send.at[k], recv_sem=self.sm_recv.at[k],
            device_id=device, device_id_type=MESH,
        )
        copy.start()
        self.pending.append(copy)

    def small_landed(self, dst, k):
        pltpu.make_async_remote_copy(
            src_ref=dst, dst_ref=dst, send_sem=self.sm_send.at[k], recv_sem=self.sm_recv.at[k],
            device_id={"group": 1 - lax.axis_index("group")}, device_id_type=MESH,
        ).wait_recv()

    def small_step(self, k):
        c, g, z = here()
        x, y = c % 2, c // 2
        if k == 0:
            self.small_push(self.sm, self.sm_core, 0, {"group": 1 - g})
        elif k == 1:
            self.small_landed(self.sm_core, 0)
            self.sm_x[...] = self.sm[...] + self.sm_core[...]
            for b in range(2):
                self.small_push(
                    self.sm_x.at[2 * b + 1 - x], self.sm_got.at[b], 1 + b, {"section": flip(c, 1)}
                )
        elif k == 2:
            for b in range(2):
                self.small_landed(self.sm_got.at[b], 1 + b)
                self.sm_y[b] = self.sm_x[2 * b + x] + self.sm_got[b]
            self.small_push(self.sm_y.at[1 - y], self.sm_y.at[2], 3, {"section": flip(c, 2)})
        elif k == 3:
            self.small_landed(self.sm_y.at[2], 3)
            self.sm_z[z] = self.sm_y[y] + self.sm_y[2]
            for bit in (1, 2, 3):
                self.small_push(self.sm_z.at[z], self.sm_z.at[z], 3 + bit, {"dp": flip(z, bit)})
        else:
            for bit in (1, 2, 3):
                self.small_landed(self.sm_z.at[flip(z, bit)], 3 + bit)
            self.small_out[...] = self.sm_z[0] + self.sm_z[1] + self.sm_z[2] + self.sm_z[3]

    def conclude(self, dbin, rest):
        f1, a2, f3, a0 = self.f1, self.a2, self.f3, self.a0
        (held_a, shared_a), (held_f, shared_f) = a0, f1
        every(a0, "first_step")
        every(f1, "third_step")
        every(f1, "line_step", 0)
        f3[0].out_step(2)
        self.sm[1:4] = self.small_in[...]
        self.sm[0] = jnp.zeros(SMALL, F32)
        for i in range(3):
            self.sm[0, i : i + 1, :] = dbin[:, i * D : (i + 1) * D]
        self.sm[0, 4:9, :] = rest[0:5, :]
        self.small_step(0)
        every(f1, "line_step", 1)
        self.small_step(1)
        every(a0, "second_step")
        every(f1, "line_step", 2)
        self.small_step(2)
        every(f1, "line_end")
        held_f.gather()
        shared_f.share_step(0)
        f3[0].out_step(3)
        every(a0, "third_step")
        every(a0, "line_step", 0)
        self.small_step(3)
        self.delivery.start(ALL[:4])
        shared_f.share_step(1)
        every(a0, "line_step", 1)
        shared_f.share_step(2)
        every(a0, "line_step", 2)
        self.small_step(4)
        shared_f.share_step(3)
        shared_f.whole_gather()
        every(a0, "line_end")
        held_a.gather()
        shared_a.share_step(0)
        slabs = [*a2, held_f, f3[1]]
        shared_a.share_step(1)
        shared_a.share_step(2)
        held_a.out_step(0)
        shared_a.share_step(3)
        shared_a.whole_gather()
        every(slabs, "out_step", 0)
        self.delivery.start(ALL[4:])
        every(slabs, "out_step", 1)
        held_a.out_step(1)
        every(slabs, "out_step", 2)
        held_a.out_step(2)
        every(slabs, "out_step", 3)
        held_a.out_step(3)
        shared_f.whole_end()
        shared_a.whole_end()
        self.delivery.finish()
        for unit in self.units:
            unit.finish()
        for copy in self.pending:
            copy.wait_send()


def feed_back_call(s, weights, act, slope, streams, g, nrm, par, carry, carried, collective):
    t = g.shape[0]
    hbm = pl.BlockSpec(memory_space=pl.ANY)
    vmem = pl.BlockSpec(memory_space=pltpu.VMEM)
    delivers = carry is None
    dma = pltpu.SemaphoreType.DMA
    half_i, half_o = grad_shape(s, 0), grad_shape(s, 1)
    results = [sds((2, 2, t, D), BF)] if delivers else carry.results()
    scratch = [
        pltpu.VMEM((2, HALF, FF), BF), pltpu.VMEM((FF, D), BF), pltpu.VMEM((t, FF), BF),
        pltpu.VMEM((t, FF), BF), pltpu.VMEM((t, D), BF),
        pltpu.VMEM(half_i, BF), pltpu.VMEM(half_o, BF), pltpu.VMEM(half_i, BF),
        pltpu.VMEM(half_o, BF), pltpu.VMEM(half_i, BF), pltpu.VMEM(half_o, BF),
        pltpu.VMEM((t, D), F32), pltpu.VMEM((D, t), BF),
        dma((CHUNKS, 5)), dma((CHUNKS, 2)), dma((CHUNKS, 2)), dma((3,)),
    ] + ([dma((4, 2)), dma((4, 2))] if delivers else carry.scratch())
    out = pl.pallas_call(
        partial(feed_back_kernel, s, carry),
        out_shape=[sds(half_i, BF), sds(half_o, BF)] + results
        + [sds((1, FF), F32), sds((8, D), F32), sds((t, D), BF)],
        in_specs=[hbm] * (7 + len(carried)) + [vmem] * 3,
        out_specs=[hbm] * (2 + len(results)) + [vmem] * 3,
        scratch_shapes=scratch,
        compiler_params=pltpu.CompilerParams(
            collective_id=collective, has_side_effects=True, vmem_limit_bytes=62 * 1024 * 1024
        ),
        name="feed_back_carry",
    )(*weights, act, slope, streams, *carried, g, nrm, par)
    return out[:2], out[2 : 2 + len(results)], out[2 + len(results) :]


def attention_back_kernel(s, carry, *refs):
    wim, wit, wom, wot = refs[:4]
    count = len(carry.all)
    carried = refs[4 : 4 + count]
    refs = refs[4 + count :]
    large, (g_ref, lse_ref, seg_row, seg_m, seg_t, pos, par) = refs[:7], refs[7:14]
    refs = refs[14:]
    if carry.last:
        streams, small_in, results, refs = refs[:3], refs[3], refs[4:10], refs[10:]
    else:
        d_first, d_second = refs[:2]
        results, refs = refs[2 : 2 + count], refs[2 + count :]
    dbin_ref, small_ref, out_ref = refs[:3]
    w_in, w_out, dmix, d_q, d_k, d_v, give_k, give_v, got_k, got_v = refs[3:13]
    own, their, core = refs[13:15], refs[15:17], refs[17:19]
    acc, dp, delta_ref, nrm_t = refs[19:23]
    load_sem, kv_s, kv_r, core_s, core_r, out_sem = refs[23:29]
    o_ref, qkv, kv_t, nrm, cosines, sines, h = refs[29:36]
    if carry.last:
        streams = {0: out_ref, **{i + 1: streams[i] for i in range(3)}}
        carry.load(carried, results, refs[36:], own, streams, small_in)
    else:
        carry.load(carried, results, refs[36:])
    if s:
        large = large[:6] + (large[6].at[s - 1],)
    _, g, _ = here()
    partner = {"group": 1 - g}
    tokens = g_ref.shape[0]

    def remote(src, dst, ssem, rsem):
        return pltpu.make_async_remote_copy(
            src_ref=src, dst_ref=dst, send_sem=ssem, recv_sem=rsem, device_id=partner,
            device_id_type=MESH,
        )

    pairs = [(wom, w_out.at[0]), (wot, w_out.at[1])]
    pairs += list(zip(large[:4], (o_ref, qkv, kv_t, nrm)))
    pairs += [(wim, w_in.at[0]), (wit, w_in.at[1])]
    pairs += list(zip(large[4:], (cosines, sines, h)))
    loads = [
        pltpu.make_async_copy(src, dst, load_sem.at[i]) for i, (src, dst) in enumerate(pairs)
    ]
    for copy in loads:
        copy.start()
    greet(True, True)
    carry.begin()

    for copy in loads[:3]:
        copy.wait()
    grad = g_ref[...]
    d_mix = jnp.concatenate([dot_nt(grad, w_out[0]), dot_nt(grad, w_out[1])], axis=1)
    dmix[...] = turn_halves(d_mix, g).astype(BF)
    o = o_ref[...].astype(F32)
    head = lax.broadcasted_iota(jnp.int32, (16, D), 0)
    lane = lax.broadcasted_iota(jnp.int32, (16, D), 1)
    delta_ref[...] = lax.dot_general(
        jnp.where(lane // HD == head, 1.0, 0.0), dmix[...].astype(F32) * o, NT,
        preferred_element_type=F32, precision=lax.Precision.HIGHEST,
    )
    turned = turn_halves(o, g).astype(BF)
    turned_t = jnp.transpose(turned)
    their[1][HALF:, :] = dot(turned_t[HALF:, :], grad).astype(BF)
    core_copies = [remote(their[1].at[HALF:, :], core[1].at[HALF:, :], core_s.at[3], core_r.at[3])]
    core_copies[0].start()
    own[1][HALF:, :] = dot(turned_t[:HALF, :], grad).astype(BF)

    lanes = lax.broadcasted_iota(jnp.int32, (tokens, 2 * HD), 1)

    def pair(j):
        def columns(first):
            return pl.ds(pl.multiple_of(first + j * 2 * HD, 2 * HD), 2 * HD)

        q = qkv[:, columns(0)]
        do = dmix[:, columns(0)]
        zero = jnp.zeros_like(q)
        sets = (
            (qkv[:, columns(D)], qkv[:, columns(2 * D)], seg_m),
            (kv_t[:, columns(0)], kv_t[:, columns(D)], seg_t),
        )
        total_q = [0.0, 0.0]
        keys_t = [jnp.transpose(sets[i][0]) for i in range(2)]
        total_k = [jnp.zeros((tokens, 2 * HD), F32)] * 2
        total_v = [jnp.zeros((tokens, 2 * HD), F32)] * 2
        for side in range(2):
            mine = (lanes >= HD) if side else (lanes < HD)
            q_head = jnp.where(mine, q, zero)
            do_head = jnp.where(mine, do, zero)
            lse = lse_ref[pl.ds(2 * j + side, 1), :]
            delta = delta_ref[pl.ds(2 * j + side, 1), :]
            for i, (k, v, seg) in enumerate(sets):
                p_t = jnp.where(
                    seg[...] == seg_row[...], jnp.exp(dot_nt(k, q_head) - lse), 0.0
                )
                d_s = (p_t * (dot_nt(v, do_head) - delta)).astype(BF)
                total_v[i] = total_v[i] + dot(p_t.astype(BF), do_head)
                total_k[i] = total_k[i] + dot(d_s, q_head)
                total_q[side] = total_q[side] + dot(keys_t[i][side * HD : (side + 1) * HD, :], d_s)
        d_q[:, columns(0)] = jnp.transpose(jnp.concatenate(total_q, axis=0))
        d_k[:, columns(0)] = total_k[0]
        d_v[:, columns(0)] = total_v[0]
        give_k[:, columns(0)] = total_k[1].astype(BF)
        give_v[:, columns(0)] = total_v[1].astype(BF)

    def exchanges(i):
        cols = pl.ds(i * 4 * HD, 4 * HD)
        return (
            remote(give_k.at[:, cols], got_k.at[:, cols], kv_s.at[0, i], kv_r.at[0, i]),
            remote(give_v.at[:, cols], got_v.at[:, cols], kv_s.at[1, i], kv_r.at[1, i]),
        )

    for copy in loads[3:6]:
        copy.wait()
    nrm_t[...] = jnp.transpose(nrm[...])
    for i in range(PAIRS // 2):
        loop(2, lambda j, i=i: pair(2 * i + j))
        for copy in exchanges(i):
            copy.start()
        carry.step(i + 1)

    for copy in loads[6:]:
        copy.wait()
    acc[...] = jnp.zeros_like(acc)
    small_ref[...] = jnp.zeros_like(small_ref)

    def turned_back(dy, y):
        swapped = swap_pairs(dy)
        d_angle = y * swapped - swap_pairs(y) * dy
        small_ref[3:4, :] += jnp.sum(d_angle * pos[:, 0:1], axis=0, keepdims=True)
        small_ref[4:5, :] += jnp.sum(d_angle * pos[:, 1:2], axis=0, keepdims=True)
        return dy * cosines[...] - swapped * sines[...]

    for j in range(3):
        cols = slice(j * D, (j + 1) * D)
        if j == 0:
            dp[...] = turned_back(
                d_q[...] * HD ** (-0.5), qkv[:, :D].astype(F32) * HD**0.5
            )
        elif j == 1:
            for i in range(PAIRS // 2):
                for copy in exchanges(i):
                    copy.wait()
            dp[...] = turned_back(d_k[...] + got_k[...].astype(F32), qkv[:, D : 2 * D].astype(F32))
        else:
            dp[...] = d_v[...] + got_v[...].astype(F32)
        d_p = dp[...].astype(BF)
        dbin_ref[:, cols] = jnp.sum(dp[...], axis=0, keepdims=True)
        if j < 2:
            place = (0, (slice(None), cols))
        else:
            place = (1, (slice(0, HALF), slice(None)))
        part, at = place
        their[part][at] = dot(nrm_t[HALF:, :], d_p).astype(BF)
        copy = remote(their[part].at[at], core[part].at[at], core_s.at[j], core_r.at[j])
        copy.start()
        core_copies.append(copy)
        own[part][at] = dot(nrm_t[:HALF, :], d_p).astype(BF)
        if j == 1:
            carry.late_step()
        acc[:, :HALF] += dot_nt(d_p, w_in[0, :, cols])
        acc[:, HALF:] += dot_nt(d_p, w_in[1, :, cols])
    grad = g_ref[...].astype(F32)
    d_normed = turn_halves(acc[...], g)
    out, d_gain, d_shift = norm_backward(h[...].astype(F32), par[0:1, :], grad, d_normed)
    out_ref[...] = out.astype(BF)
    small_ref[0:1, :] = jnp.sum(grad, axis=0, keepdims=True)
    small_ref[1:2, :] = d_gain
    small_ref[2:3, :] = d_shift

    for copy in core_copies:
        copy.wait()
    saves = []
    if carry.last:
        for part in range(2):
            accumulate(own[part], core[part], own[part].shape[0])
        carry.conclude(dbin_ref, small_ref)
        return
    for part, target in enumerate((d_first, d_second)):
        accumulate(own[part], core[part], own[part].shape[0])
        copy = pltpu.make_async_copy(own[part], target, out_sem.at[part])
        copy.start()
        saves.append(copy)
    carry.end()
    for copy in saves:
        copy.wait()


def attention_back_call(
    s, weights, carry, carried, g, saved, seg_row, seg_m, seg_t, turns, pos, h, par, collective,
    streams=(), small=None,
):
    t = g.shape[0]
    qkv, nrm, kv_t, o, lse = saved
    hbm = pl.BlockSpec(memory_space=pl.ANY)
    vmem = pl.BlockSpec(memory_space=pltpu.VMEM)
    dma = pltpu.SemaphoreType.DMA
    halves = [grad_shape(s, 0), grad_shape(s, 1)]
    rows, wide = pltpu.VMEM((t, D), BF), pltpu.VMEM((t, D), F32)
    if carry.last:
        carry.tokens = t
    results = carry.results()
    scratch = [
        pltpu.VMEM((2, HALF, QKV), BF), pltpu.VMEM((2, HALF, D), BF), rows, wide, wide, wide,
        rows, rows, rows, rows,
        *[pltpu.VMEM(x, BF) for x in halves * 3],
        wide, wide, pltpu.VMEM((16, t), F32), pltpu.VMEM((D, t), BF),
        dma((11,)), dma((2, 3)), dma((2, 3)), dma((4,)), dma((4,)), dma((2,)),
        rows, pltpu.VMEM((t, QKV), BF), pltpu.VMEM((t, 2 * D), BF), rows, wide, wide, rows,
    ] + carry.scratch()
    extra, extra_specs = (), []
    out_shape, out_specs = [sds(x, BF) for x in halves] + results, [hbm] * (2 + len(results))
    if carry.last:
        extra, extra_specs = (*streams, small), [hbm] * 3 + [vmem]
        out_shape, out_specs = results, [hbm] * 5 + [vmem]
    out = pl.pallas_call(
        partial(attention_back_kernel, s, carry),
        out_shape=out_shape
        + [sds((1, QKV), F32), sds((8, D), F32), sds((t, D), BF)],
        in_specs=[hbm] * (4 + len(carried) + 7) + [vmem] * 7 + extra_specs,
        out_specs=out_specs + [vmem] * 3,
        scratch_shapes=scratch,
        compiler_params=pltpu.CompilerParams(
            collective_id=collective, has_side_effects=True, vmem_limit_bytes=63 * 1024 * 1024
        ),
        name="attention_back_carry",
    )(*weights, *carried, o, qkv, kv_t, nrm, *turns, h, g, lse, seg_row, seg_m, seg_t, pos, par, *extra)
    if carry.last:
        return out[:6]
    return out[:2], out[2:-3], out[-3:]


def in_place(x):
    return x.reshape(-1, x.shape[-1])


CHUNKS = 6


START = (0, 0, 0, 0)
RING = 4
GROUP = (1, 1, 1, 1)
SPAN = 6
BESIDE = (None, None, None)


def chunk_of(ref, part, k):
    size = ref.shape[0 if part else 1] // CHUNKS
    at = pl.ds(pl.multiple_of(k * size, size), size)
    return ref.at[at, :] if part else ref.at[:, at]


def ring_place(chip):
    return 2 * (chip // 2) + (chip % 2 + chip // 2) % 2


def ring_chip(place):
    return 2 * (place // 2) + (place % 2 + place // 2) % 2


CLOCKWISE = ((True, False), (True, False), (False, True), (True, False))


def forward_kernel(*refs):
    w_in, w_out, h0, small, pos, seg_col, seg_m, seg_t = refs[:8]
    refs = refs[8:]
    keep = [refs[4 * s : 4 * s + 4] for s in range(4)]
    acts, slopes = refs[16:18], refs[18:20]
    results = refs[20:38]
    refs = refs[38:]
    work, refs = refs[:18], refs[18:]
    qkvs, kv_ts, os, lses = work[0:2], work[2:4], work[4:6], work[6:8]
    nrms, hs = work[8:12], [work[12].at[s] for s in range(4)]
    turns, pars = (work[13:15], work[15:17]), work[17]
    held = [refs[4 * s : 4 * s + 4] for s in range(4)]
    acc, stage_a, stage_s, lse_scr, smalls, b_in, b_out, freqs = refs[16:24]
    own_sem, ring_s, ring_r, z_s, z_r, core_s, core_r, kv_sem, save_sem, stage_sem = refs[24:34]
    small_s, small_r, result_sem = refs[34:]

    def kept(i):
        return pltpu.make_async_copy(work[i], results[i], result_sem.at[i])

    c = lax.axis_index("section")
    g = lax.axis_index("group")
    z = lax.axis_index("dp")
    parity = z % 2
    place = ring_place(c)
    ahead, behind = ring_chip((place + 1) % 4), ring_chip((place + 3) % 4)
    partner = {"group": 1 - g}
    tokens = h0.shape[0]

    def remote(src, dst, ssem, rsem, device):
        return pltpu.make_async_remote_copy(
            src_ref=src, dst_ref=dst, send_sem=ssem, recv_sem=rsem, device_id=device,
            device_id_type=MESH,
        )

    greet(True, True)

    def small_copies():
        slot = smalls.at[2 * c + g]
        out = []
        for bit in range(4):
            for core in range(2):
                if bit or core:
                    target = {"section": flip(c, bit) if bit else c, "group": (g + core) % 2}
                    out.append(remote(small, slot, small_s.at[2 * bit + core], small_r.at[2 * c + g], target))
        return out

    for copy in small_copies():
        copy.start()
    smalls[2 * c + g] = small[...]

    def mine(s, part):
        return held[s][2 * part]

    def theirs(s, part):
        return held[s][2 * part + 1]

    def distance(s, part):
        d = place - ring_place(s)
        return (d + 4) % 4 if CLOCKWISE[s][part] else (4 - d) % 4

    def own_copies(s):
        first = pltpu.make_async_copy(
            w_in.at[:, : QKV] if s % 2 == 0 else w_in, mine(s, 0), own_sem.at[0]
        )
        source = w_out.at[:HALF, :] if s % 2 == 0 else w_out
        second = pltpu.make_async_copy(source, mine(s, 1), own_sem.at[1])
        over = remote(w_out.at[HALF:D, :], mine(s, 1), own_sem.at[2], own_sem.at[3], partner)
        return first, second, over

    for s in range(4):

        @pl.when(c == s)
        def _(s=s):
            first, second, over = own_copies(s)
            first.start()
            if s % 2:
                second.start()
            else:

                @pl.when(g == 0)
                def _():
                    second.start()
                    over.start()

    for s in range(4):

        @pl.when(c == s)
        def _(s=s):
            first, second, over = own_copies(s)
            first.wait()
            if s % 2:
                second.wait()
            else:

                @pl.when(g == 0)
                def _():
                    second.wait()
                    over.wait_send()

                @pl.when(g == 1)
                def _():
                    over.wait_recv()

    def ring_copy(s, part, k):
        ref = chunk_of(mine(s, part), part, jnp.where(k < 2, 2 * parity + k, k + 2))
        target = ahead if CLOCKWISE[s][part] else behind
        u = 2 * s + part
        return remote(ref, ref, ring_s.at[u, k], ring_r.at[u, k], {"section": target})

    def z_copy(s, part, j, sending):
        ref = chunk_of(mine(s, part), part, 2 * (parity if sending else 1 - parity) + j)
        u = 2 * s + part
        return remote(ref, ref, z_s.at[u, j], z_r.at[u, j], {"dp": z + 1 - 2 * parity})

    def core_copy(s, part, k):
        u = 2 * s + part
        return remote(
            chunk_of(mine(s, part), part, k), chunk_of(theirs(s, part), part, k),
            core_s.at[u, k], core_r.at[u, k], partner,
        )

    def event(s, part, k):
        p = distance(s, part)
        copy = ring_copy(s, part, k)
        pl.when(p > 0)(copy.wait_recv)
        pl.when(p < 3)(copy.start)

        @pl.when((k < 2) & (p > 0))
        def _():
            z_copy(s, part, jnp.minimum(k, 1), True).start()

        core_copy(s, part, jnp.where(k < 2, 2 * parity + k, k + 2)).start()

        @pl.when(k >= 2)
        def _():
            j = jnp.maximum(k - 2, 0)
            pl.when(p > 0)(z_copy(s, part, j, False).wait_recv)
            core_copy(s, part, 2 * (1 - parity) + j).start()

    def slot(t, first, last):
        for s in range(4):
            if START[s] <= last and first <= START[s] + RING // GROUP[s] + 2:
                for part in range(2):
                    k = t - START[s] - distance(s, part)

                    @pl.when((k >= 0) & (k < RING // GROUP[s]))
                    def _(s=s, part=part, k=k):
                        k = jnp.clip(k, 0, RING // GROUP[s] - 1)
                        for i in range(GROUP[s]):
                            event(s, part, k * GROUP[s] + i)

    def slots(first, last):
        loop(last - first + 1, lambda i: slot(first + i, first, last))

    def arrived(s):
        def one(k):
            core_copy(s, 0, k).wait_recv()
            core_copy(s, 1, k).wait_recv()

        loop(CHUNKS, one)
        for i in range(4):
            pltpu.make_async_copy(held[s][i], keep[s][i], save_sem.at[4 * s + i]).start()

    def assemble():
        for i in range(8):
            slot = smalls.at[i]
            copy = remote(slot, slot, small_s.at[0], small_r.at[i], partner)
            pl.when(2 * c + g != i)(copy.wait_recv)
        for s in range(4):

            def both(first, width, s=s):
                at = slice(first, first + width)
                return jnp.concatenate([smalls[2 * s, :, at], smalls[2 * s + 1, :, at]], axis=1)

            half = FF // 2
            b_in[s] = both(0, half)
            b_out[s] = both(half, HALF)
            pars[s] = jnp.concatenate(
                [both(half + HALF, HALF), both(half + 2 * HALF, HALF), jnp.zeros((6, D), F32)], axis=0
            )
            if s % 2 == 0:
                freqs[s // 2] = jnp.concatenate(
                    [both(half + 3 * HALF, HALF), both(half + 4 * HALF, HALF)], axis=0
                )

    def turn_rows(i):
        rows = tokens // 2
        at = pl.ds(pl.multiple_of((i % 2) * rows, rows), rows)
        for layer in range(2):

            @pl.when(i // 2 == layer)
            def _(layer=layer):
                angles = (
                    pos[at, 0:1] * freqs[layer, 0:1, :] + pos[at, 1:2] * freqs[layer, 1:2, :]
                )
                lanes = lax.broadcasted_iota(jnp.int32, angles.shape, 1)
                sines = jnp.sin(angles)
                turns[layer][0][at, :] = jnp.cos(angles)
                turns[layer][1][at, :] = jnp.where((lanes % HD) < HD // 2, -sines, sines)

    def normed(s, h):
        xhat, _ = normalize(h[...].astype(F32))
        nrms[s][...] = turn_halves(
            xhat * pars[s, 0:1, :] + pars[s, 1:2, :], g
        ).astype(BF)

    def project(s, first, width):
        cols = pl.ds(first, width)
        return (
            dot(nrms[s][:, :HALF], mine(s, 0)[:, cols])
            + dot(nrms[s][:, HALF:], theirs(s, 0)[:, cols])
            + b_in[s, 0:1, cols]
        )

    def attention(s, h, out, beside):
        layer = s // 2
        qkv, kv_t, o_ref = qkvs[layer], kv_ts[layer], os[layer]
        cosines, sines = turns[layer]
        normed(s, h)
        exchange = []
        for j in (1, 2, 0):
            x = project(s, j * D, D)
            if j < 2:
                x = x * cosines[...] + swap_pairs(x) * sines[...]
            if j == 0:
                x = x * HD ** (-0.5)
            qkv[:, j * D : (j + 1) * D] = x.astype(BF)
            if j:
                copy = remote(
                    qkv.at[:, j * D : (j + 1) * D], kv_t.at[:, (j - 1) * D : j * D],
                    kv_sem.at[0, 2 * layer + j - 1], kv_sem.at[1, 2 * layer + j - 1], partner,
                )
                copy.start()
                exchange.append(copy)
        for copy in exchange:
            copy.wait()
        for i in (layer, 2 + layer, 8 + s):
            kept(i).start()
        lanes = lax.broadcasted_iota(jnp.int32, (tokens, 2 * HD), 1)

        def pair(j):
            if beside is not None:
                pl.when(beside[0] + j <= beside[1])(lambda: slot(beside[0] + j, *beside))

            def columns(ref, first):
                return ref[:, pl.ds(pl.multiple_of(first + j * 2 * HD, 2 * HD), 2 * HD)]

            q = columns(qkv, 0)
            km, vm = columns(qkv, D), columns(qkv, 2 * D)
            kt, vt = columns(kv_t, 0), columns(kv_t, D)
            same_m = seg_col[...] == seg_m[...]
            same_t = seg_col[...] == seg_t[...]
            found = []
            for side in range(2):
                head = (lanes >= HD) if side else (lanes < HD)
                q_head = jnp.where(head, q, jnp.zeros_like(q))
                s_m = jnp.where(same_m, dot_nt(q_head, km), -1e9)
                s_t = jnp.where(same_t, dot_nt(q_head, kt), -1e9)
                top = jnp.maximum(
                    jnp.max(s_m, axis=-1, keepdims=True), jnp.max(s_t, axis=-1, keepdims=True)
                )
                p_m = jnp.exp(s_m - top)
                p_t = jnp.exp(s_t - top)
                total = jnp.sum(p_m, axis=-1, keepdims=True) + jnp.sum(
                    p_t, axis=-1, keepdims=True
                )
                o = dot(p_m.astype(BF), vm) + dot(p_t.astype(BF), vt)
                found.append(o / total)
                lse_scr[...] = jnp.where(
                    lanes == 2 * j + side, top + jnp.log(total), lse_scr[...]
                )
            o_ref[:, pl.ds(pl.multiple_of(j * 2 * HD, 2 * HD), 2 * HD)] = jnp.where(
                lanes < HD, found[0], found[1]
            ).astype(BF)

        loop(PAIRS, pair)
        lses[layer][...] = jnp.transpose(lse_scr[...])[:16, :]
        turned = turn_halves(o_ref[...].astype(F32), g).astype(BF)
        y = dot(turned[:, :HALF], mine(s, 1)[...]) + dot(turned[:, HALF:], theirs(s, 1)[...])
        out[...] = (h[...].astype(F32) + y + b_out[s, 0:1, :]).astype(BF)
        for i in (4 + layer, 6 + layer):
            kept(i).start()

    def feed(s, h, out, beside):
        layer = s // 2
        width = FF // CHUNKS
        normed(s, h)
        kept(8 + s).start()
        acc[...] = h[...].astype(F32) + b_out[s, 0:1, :]

        def staged(j, i):
            turn = j % 2
            cols = pl.ds(pl.multiple_of(j * width, width), width)
            source, target = ((stage_a, acts[layer]), (stage_s, slopes[layer]))[i]
            return pltpu.make_async_copy(source.at[turn], target.at[:, cols], stage_sem.at[i, turn])

        def block(j):
            if beside is not None:
                pl.when(beside[0] + j <= beside[1])(lambda: slot(beside[0] + j, *beside))
            turn = j % 2

            @pl.when(j >= 2)
            def _():
                staged(j - 2, 0).wait()
                staged(j - 2, 1).wait()

            b = (j + g * (CHUNKS // 2)) % CHUNKS
            u = project(s, pl.multiple_of(b * width, width), width)
            cdf = 0.5 + 0.5 * lax.erf(u * (0.5**0.5))
            act = (u * cdf).astype(BF)
            stage_a[turn] = act
            pdf = jnp.exp(u * u * -0.5) * 0.3989422804014327
            stage_s[turn] = (cdf + u * pdf).astype(BF)
            staged(j, 0).start()
            staged(j, 1).start()
            for half in range(2):

                @pl.when(j // (CHUNKS // 2) == half)
                def _(half=half):
                    rows = pl.ds(pl.multiple_of((j % (CHUNKS // 2)) * width, width), width)
                    acc[...] += dot(act, held[s][2 + half][rows, :])

        loop(CHUNKS, block)
        for j in (CHUNKS - 2, CHUNKS - 1):
            staged(j, 0).wait()
            staged(j, 1).wait()
        out[...] = acc[...].astype(BF)

    slots(0, 0)
    assemble()

    def wait_and_turn(i):
        slot(1 + i, 1, SPAN)
        pl.when(i < 4)(lambda: turn_rows(i))

    loop(SPAN, wait_and_turn)
    for i in range(13, 18):
        kept(i).start()
    arrived(0)
    attention(0, h0, hs[0], BESIDE[0])
    arrived(1)
    feed(1, hs[0], hs[1], BESIDE[1])
    arrived(2)
    attention(2, hs[1], hs[2], BESIDE[2])
    arrived(3)
    feed(3, hs[2], hs[3], None)

    kept(12).start()

    for copy in small_copies():
        copy.wait_send()
    for i in range(18):
        kept(i).wait()
    for s in range(4):
        for part in range(2):
            p = distance(s, part)

            def sent_out(k, s=s, part=part, p=p):
                core_copy(s, part, k).wait_send()
                pl.when((k < 4) & (p < 3))(ring_copy(s, part, jnp.minimum(k, 3)).wait_send)
                pl.when((k < 2) & (p > 0))(z_copy(s, part, jnp.minimum(k, 1), True).wait_send)

            loop(CHUNKS, sent_out)
        for i in range(4):
            pltpu.make_async_copy(held[s][i], keep[s][i], save_sem.at[4 * s + i]).wait()


def forward_call(w_in, w_out, h, small, pos, seg_col, seg_m, seg_t):
    t = h.shape[0]
    hbm = pl.BlockSpec(memory_space=pl.ANY)
    vmem = pl.BlockSpec(memory_space=pltpu.VMEM)
    weights = []
    for s in range(4):
        (a, b), (d, e) = unit_shape(s, 0), unit_shape(s, 1)
        weights += [(a, b), (a, b), (d, e), (d, e)]
    rows = sds((t, D), BF)
    out_shape = (
        [sds(w, BF) for w in weights]
        + [sds((t, FF), BF)] * 4
        + [sds((t, QKV), BF)] * 2
        + [sds((t, 2 * D), BF)] * 2
        + [rows] * 2
        + [sds((16, t), F32)] * 2
        + [rows] * 4
        + [sds((4, t, D), BF)]
        + [sds((t, D), F32)] * 4
        + [sds((4, 8, D), F32)]
    )
    dma = pltpu.SemaphoreType.DMA
    scratch = [pltpu.VMEM(x.shape, x.dtype) for x in out_shape[20:]]
    scratch += [pltpu.VMEM(w, BF) for w in weights] + [
        pltpu.VMEM((t, D), F32),
        pltpu.VMEM((2, t, FF // CHUNKS), BF),
        pltpu.VMEM((2, t, FF // CHUNKS), BF),
        pltpu.VMEM((t, 2 * HD), F32),
        pltpu.VMEM((8,) + small.shape, F32),
        pltpu.VMEM((4, 1, FF), F32),
        pltpu.VMEM((4, 1, D), F32),
        pltpu.VMEM((2, 2, D), F32),
        dma((4,)), dma((8, 4)), dma((8, 4)), dma((8, 2)), dma((8, 2)), dma((8, 6)), dma((8, 6)),
        dma((2, 4)), dma((16,)), dma((2, 2)), dma((8,)), dma((8,)), dma((18,)),
    ]
    out = pl.pallas_call(
        forward_kernel,
        out_shape=out_shape,
        in_specs=[hbm, hbm] + [vmem] * 6,
        out_specs=[hbm] * 38,
        scratch_shapes=scratch,
        compiler_params=pltpu.CompilerParams(
            collective_id=2, has_side_effects=True, vmem_limit_bytes=63 * 1024 * 1024
        ),
        name="forward",
    )(w_in, w_out, h, small, pos, seg_col, seg_m, seg_t)
    weights = [out[4 * s : 4 * s + 4] for s in range(4)]
    acts, slopes, qkvs, kv_ts, os, lses = (out[16 + 2 * i : 18 + 2 * i] for i in range(6))
    nrms, hs = out[28:32], out[32]
    saved = []
    for s in range(4):
        i = s // 2
        if s % 2 == 0:
            saved.append((qkvs[i], nrms[s], kv_ts[i], os[i], lses[i]))
        else:
            saved.append((acts[i], slopes[i], nrms[s]))
    return weights, saved, hs, (out[33:35], out[35:37]), out[37]


def small_rows(dbin, rest):
    first = jnp.pad(dbin.reshape(-1), (0, FF - dbin.size)).reshape(4, D)
    return jnp.concatenate([first, rest[:5], jnp.zeros((SMALL[0] - 9, D), F32)])


def carried_passes(weight_in, weight_out, h, g, small, freq, pos, seg_m, seg_t):
    section, core = lax.axis_index("section"), lax.axis_index("group")
    wide = jnp.concatenate([freq.reshape(2, PAIRS, HD // 2)] * 2, axis=2).reshape(-1)
    small = jnp.concatenate([*small, wide]).astype(F32)[None]
    weights, saved, streams, turns, pars = forward_call(
        weight_in[0], weight_out[0], h, small, pos, seg_m[:, None], seg_m[None], seg_t[None]
    )
    smalls, grads, in_grads = [None] * 4, [None] * 4, [None] * 4
    rows = (seg_m[None], seg_m[:, None], seg_t[:, None])

    def feed_back(s, g, carry, carried):
        act, slope, nrm = saved[s]
        grads[s], results, (dbin, rest, in_grads[s]) = feed_back_call(
            s, weights[s], act, slope, streams, g, nrm, pars[s], carry, carried, 3 + s
        )
        smalls[s] = small_rows(dbin, rest)
        return results

    def attention_back(s, g, carry, carried):
        grads[s], results, (dbin, rest, in_grads[s]) = attention_back_call(
            s, weights[s], carry, carried, g, saved[s], *rows, turns[s // 2], pos,
            streams if s else h, pars[s], 3 + s,
        )
        smalls[s] = small_rows(dbin, rest)
        return results

    (outputs,) = feed_back(3, g, None, ())
    quarters3 = attention_back(2, in_grads[3], Carry(3, (), ()), grads[3])
    *quarters2, first3, second3 = feed_back(
        1, in_grads[2], Carry(2, ((3, 0), (3, 1)), ()), (*grads[2], *quarters3)
    )
    *sums, input_grads, small_sum = attention_back_call(
        0, weights[0], Finish(), (*grads[1], *quarters2, first3, second3), in_grads[1], saved[0],
        *rows, turns[0], pos, h, pars[0], 3, in_grads[1:], jnp.stack(smalls[1:]),
    )
    first_a, second_a, first_f, second_f = sums
    second_a = in_place(second_a)
    in_a = jnp.concatenate([in_place(first_a), second_a[:HALF]], axis=1)
    both = jnp.concatenate([second_a[HALF:], flipped(second_a[HALF:], "group", 1)], axis=0)
    both = jnp.where(core == 0, jnp.pad(both, ((0, FF // 2 - D), (0, 0))), jnp.zeros((), BF))
    attends = section % 2 == 0
    in_f = in_place(first_f)
    out_in = jnp.where(attends, jnp.pad(in_a, ((0, 0), (0, FF - QKV))), in_f).astype(F32)
    out_out = jnp.where(attends, both, in_place(second_f)).astype(F32)
    return outputs.reshape(-1, D), input_grads.reshape(-1, D), out_in, out_out, small_sum


def plain_passes(weight_in, weight_out, h, g, small, freq, pos, seg_m, seg_t):
    section, group = lax.axis_index("section"), lax.axis_index("group")
    groups = lax.axis_size("group")
    small = jnp.concatenate([*small, freq.reshape(-1)])
    small = lax.all_gather(small, ("section", "group")).reshape(4, groups, -1).astype(F32)
    widths = [FF // groups, D // groups, D // groups, D // groups, D // groups]
    starts = [sum(widths[:i]) for i in range(5)]
    b_in, b_out, gain, shift, freq = (
        small[:, :, a : a + w] for a, w in zip(starts, widths)
    )
    b_in, b_out, gain, shift = (x.reshape(4, 1, -1) for x in (b_in, b_out, gain, shift))
    freq = freq.reshape(4, groups, 2, -1).transpose(0, 2, 1, 3).reshape(4, 2, D // 2)
    pars = [
        jnp.concatenate([gain[s], shift[s], jnp.zeros((6, D), F32)], axis=0) for s in range(4)
    ]
    turns = [turning(freq[s], pos) for s in (0, 2)]

    core = group % 2
    rot = jnp.zeros((1,), jnp.int32)
    all_in = lax.all_gather(weight_in, "group", axis=1, tiled=True)
    all_out = lax.all_gather(weight_out, "group", axis=1, tiled=True)
    all_in = lax.all_gather(all_in, "section", axis=0, tiled=True)
    all_out = lax.all_gather(all_out, "section", axis=0, tiled=True)
    weights, saved, streams = [], [], [h]
    for s in range(4):
        cols, rows = (QKV, D) if s % 2 == 0 else (FF, FF)
        w_in, w_out = all_in[s, :, :cols], all_out[s, :rows]
        weights.append((w_in[:HALF], w_in[HALF:], w_out[: rows // 2], w_out[rows // 2 :]))
        wia, wib, woa, wob = weights[s]
        if s % 2 == 0:
            cosines, sines = turns[s // 2]
            qkv, nrm = qkv_call(rot, h, pars[s], wia, wib, b_in[s, :, :QKV], cosines, sines)
            kv_t = flipped(qkv[:, D:], "group", 1)
            o, lse, h = attend_call(
                rot, qkv, kv_t, seg_m[:, None], seg_m[None], seg_t[None], h, woa, wob, b_out[s]
            )
            saved.append((qkv, nrm, kv_t, o, lse))
        else:
            act, slope, nrm, h = ff_call(rot, h, pars[s], wia, wib, b_in[s], woa, wob, b_out[s])
            saved.append((act, slope, nrm))
        streams.append(h)
    outputs = to_owners(streams[1:], section, core)
    smalls, grads, in_grads = [None] * 4, [None] * 4, [None] * 4
    for s in (3, 2, 1, 0):
        wia, wib, woa, wob = weights[s]
        if s % 2 == 0:
            qkv, nrm, kv_t, o, lse = saved[s]
            cosines, sines = turns[s // 2]
            dmix, delta, doa, dob = mix_back_call(rot, g, o, woa, wob)
            dq, dkm, dvm, dkt, dvt = attend_back_call(
                qkv, kv_t, dmix, lse, delta, seg_m[None], seg_m[:, None], seg_t[:, None]
            )
            dkr, dvr = flipped(dkt, "group", 1), flipped(dvt, "group", 1)
            dia, dib, dbin, rest, g = qkv_back_call(
                rot, dq, dkm, dvm, dkr, dvr, qkv, cosines, sines, pos, nrm, wia, wib,
                streams[s], pars[s], g,
            )
        else:
            act, slope, nrm = saved[s]
            dia, dib, doa, dob, dbin, rest, g = ff_back_call(
                rot, g, act, slope, nrm, wia, wib, woa, wob, streams[s], pars[s]
            )
        in_grads[s] = g
        grads[s] = (
            jnp.pad(jnp.concatenate([dia, dib]), ((0, 0), (0, FF - dia.shape[1]))),
            jnp.pad(jnp.concatenate([doa, dob]), ((0, FF - 2 * doa.shape[0]), (0, 0))),
        )
        smalls[s] = small_rows(dbin, rest)
    input_grads = to_owners(in_grads, section, core)
    small_sum = lax.psum(jnp.stack(smalls), ("section", "group", "dp"))[section]

    def owned(x):
        x = lax.psum_scatter(x, "section", scatter_dimension=0, tiled=True)[0]
        x = lax.psum_scatter(x, "group", scatter_dimension=0, tiled=True)
        return lax.psum(x, "dp").astype(F32)

    out_in = owned(jnp.stack([x[0] for x in grads]))
    out_out = owned(jnp.stack([x[1] for x in grads]))
    return outputs, input_grads, out_in, out_out, small_sum


def body(
    activations, weight_in, weight_out, bias_in, bias_out, norm_gain, norm_shift, rope_freq,
    image_sides, cotangent,
):
    sections = lax.axis_size("section")
    groups = lax.axis_size("group")
    section = lax.axis_index("section")
    group = lax.axis_index("group")
    core = group % 2
    micro = image_sides.shape[0]
    capacity = activations.shape[0] // micro
    tokens = capacity // 2
    assert sections == 4 and groups % 2 == 0 and 2 * micro == sections
    fast = groups == 2 and lax.axis_size("dp") == 4

    here = (section // 2) == core
    local = section % 2

    def take(x):
        own = lax.dynamic_index_in_dim(x.reshape(micro, capacity, D), local, 0, keepdims=False)
        give = lax.dynamic_slice_in_dim(own, (1 - core) * tokens, tokens, 0)
        keep = lax.dynamic_slice_in_dim(own, core * tokens, tokens, 0)
        return jnp.where(here, keep, flipped(give, "group", 1))

    h = take(activations)
    own_sides = lax.dynamic_index_in_dim(image_sides, local, 0, keepdims=False)
    sides = jnp.where(here, own_sides, flipped(own_sides, "group", 1))
    segment, patch_row, patch_col, is_valid = layout(sides, capacity)
    pos_all = jnp.stack([patch_col, patch_row], axis=1).astype(F32)

    def half_of(x, which):
        return lax.dynamic_slice_in_dim(x, which * tokens, tokens, 0)

    pos = half_of(pos_all, core)
    seg_m, seg_t = half_of(segment, core), half_of(segment, 1 - core)
    valid = half_of(is_valid, core)
    g = take(cotangent) * valid[:, None].astype(BF)

    passes = carried_passes if fast else plain_passes
    outputs, input_grads, out_in, out_out, small_sum = passes(
        weight_in, weight_out, h, g, (bias_in[0], bias_out[0], norm_gain[0], norm_shift[0]),
        rope_freq[0], pos, seg_m, seg_t,
    )

    first_bias = small_sum[:4].reshape(-1)
    d_freq = small_sum[7:9].reshape(2, HEADS, HD)[:, :, : HD // 2].reshape(2, D // 2)

    def piece(x):
        w = x.shape[-1] // groups
        return lax.dynamic_slice_in_dim(x, group * w, w, x.ndim - 1)[None]

    return (
        outputs[None],
        input_grads[None],
        out_in[None],
        out_out[None],
        piece(first_bias),
        piece(small_sum[4]),
        piece(small_sum[5]),
        piece(small_sum[6]),
        piece(d_freq),
    )


def solution(mesh):
    placed = (
        P(("group", "dp"), None),
        P("section", "group", None),
        P("section", "group", None),
        P("section", "group"),
        P("section", "group"),
        P("section", "group"),
        P("section", "group"),
        P("section", None, "group"),
        P(("group", "dp"), None),
        P(("group", "dp"), None),
    )
    return jax.shard_map(
        body,
        mesh=mesh,
        in_specs=placed,
        out_specs=(
            P("section", ("group", "dp"), None),
            P("section", ("group", "dp"), None),
            P("section", "group", None),
            P("section", "group", None),
            P("section", "group"),
            P("section", "group"),
            P("section", "group"),
            P("section", "group"),
            P("section", None, "group"),
        ),
        check_vma=False,
    )
```

```python
from functools import partial

import jax
import jax.numpy as jnp
from jax import lax
from jax.experimental import pallas as pl
from jax.experimental.pallas import tpu as pltpu
from jax.sharding import PartitionSpec as P

D = 768
HEADS = 12
HD = 64
FF = 3072
HALF = D // 2
PAIRS = HEADS // 2
QKV = 3 * D
EPSILON = 1e-06
BF = jnp.bfloat16
F32 = jnp.float32
NT = (((1,), (1,)), ((), ()))
TN = (((0,), (0,)), ((), ()))
VMEM_BYTES = 52 * 1024 * 1024


def dot(a, b):
    return jnp.dot(a, b, preferred_element_type=F32)


def dot_nt(a, b):
    return lax.dot_general(a, b, NT, preferred_element_type=F32)


def dot_tn(a, b):
    return lax.dot_general(a, b, TN, preferred_element_type=F32)


def normalize(h):
    average = jnp.mean(h, axis=-1, keepdims=True)
    centered = h - average
    variance = jnp.mean(centered * centered, axis=-1, keepdims=True)
    scale = lax.rsqrt(variance + EPSILON)
    return centered * scale, scale


def turn_halves(x, rot):
    return jnp.where(rot == 0, x, jnp.concatenate([x[:, HALF:], x[:, :HALF]], axis=1))


def swap_pairs(x):
    lanes = lax.broadcasted_iota(jnp.int32, x.shape, 1)
    low = (lanes % HD) < HD // 2
    return jnp.where(
        low, pltpu.roll(x, x.shape[1] - HD // 2, 1), pltpu.roll(x, HD // 2, 1)
    )


def norm_backward(h, gain, grad, d_normed):
    xhat, scale = normalize(h)
    e = d_normed * gain
    mean_e = jnp.mean(e, axis=-1, keepdims=True)
    mean_ex = jnp.mean(e * xhat, axis=-1, keepdims=True)
    g = grad + scale * (e - mean_e - xhat * mean_ex)
    d_gain = jnp.sum(d_normed * xhat, axis=0, keepdims=True)
    d_shift = jnp.sum(d_normed, axis=0, keepdims=True)
    return g, d_gain, d_shift


def qkv_kernel(rot_ref, h_ref, par_ref, wa_ref, wb_ref, bias_ref, cos_ref, sin_ref, out_ref, nrm_ref):
    j = pl.program_id(0)

    @pl.when(j == 0)
    def _():
        xhat, _ = normalize(h_ref[...].astype(F32))
        normed = xhat * par_ref[0:1, :] + par_ref[1:2, :]
        nrm_ref[...] = turn_halves(normed, rot_ref[0]).astype(BF)

    x = dot(nrm_ref[:, :HALF], wa_ref[...]) + dot(nrm_ref[:, HALF:], wb_ref[...]) + bias_ref[...]

    @pl.when(j < 2)
    def _():
        y = x * cos_ref[...] + swap_pairs(x) * sin_ref[...]
        out_ref[...] = (y * jnp.where(j == 0, HD ** (-0.5), 1.0)).astype(BF)

    @pl.when(j == 2)
    def _():
        out_ref[...] = x.astype(BF)


def attend_kernel(
    rot_ref, q_ref, km_ref, vm_ref, kt_ref, vt_ref, segq_ref, segm_ref, segt_ref, h_ref,
    woa_ref, wob_ref, bias_ref, o_ref, lse_ref, out_ref, lse_scr,
):
    j = pl.program_id(0)
    rows = q_ref.shape[0]
    lanes = lax.broadcasted_iota(jnp.int32, (rows, 2 * HD), 1)
    q = q_ref[...]
    same_m = segq_ref[...] == segm_ref[...]
    same_t = segq_ref[...] == segt_ref[...]
    outs = []
    for side in range(2):
        mine = (lanes >= HD) if side else (lanes < HD)
        q_head = jnp.where(mine, q, jnp.zeros_like(q))
        s_m = jnp.where(same_m, dot_nt(q_head, km_ref[...]), -1e9)
        s_t = jnp.where(same_t, dot_nt(q_head, kt_ref[...]), -1e9)
        top = jnp.maximum(
            jnp.max(s_m, axis=-1, keepdims=True), jnp.max(s_t, axis=-1, keepdims=True)
        )
        p_m = jnp.exp(s_m - top)
        p_t = jnp.exp(s_t - top)
        total = jnp.sum(p_m, axis=-1, keepdims=True) + jnp.sum(p_t, axis=-1, keepdims=True)
        o = dot(p_m.astype(BF), vm_ref[...]) + dot(p_t.astype(BF), vt_ref[...])
        outs.append(o / total)
        lse_scr[...] = jnp.where(lanes == 2 * j + side, top + jnp.log(total), lse_scr[...])
    o_ref[:, pl.ds(pl.multiple_of(j * 2 * HD, 2 * HD), 2 * HD)] = jnp.where(
        lanes < HD, outs[0], outs[1]
    ).astype(BF)

    @pl.when(j == PAIRS - 1)
    def _():
        lse_ref[...] = jnp.transpose(lse_scr[...])[:16, :]
        o_all = turn_halves(o_ref[...].astype(F32), rot_ref[0]).astype(BF)
        y = dot(o_all[:, :HALF], woa_ref[...]) + dot(o_all[:, HALF:], wob_ref[...])
        out_ref[...] = (h_ref[...].astype(F32) + y + bias_ref[...]).astype(BF)


def ff_kernel(
    rot_ref, h_ref, par_ref, wia_ref, wib_ref, bias_ref, woa_ref, wob_ref, bout_ref,
    act_ref, slope_ref, nrm_ref, out_ref, acc_ref,
):
    j = pl.program_id(0)
    n = pl.num_programs(0)

    @pl.when(j == 0)
    def _():
        xhat, _ = normalize(h_ref[...].astype(F32))
        normed = xhat * par_ref[0:1, :] + par_ref[1:2, :]
        nrm_ref[...] = turn_halves(normed, rot_ref[0]).astype(BF)
        acc_ref[...] = h_ref[...].astype(F32) + bout_ref[...]

    u = dot(nrm_ref[:, :HALF], wia_ref[...]) + dot(nrm_ref[:, HALF:], wib_ref[...]) + bias_ref[...]
    cdf = 0.5 + 0.5 * lax.erf(u * (0.5**0.5))
    act = (u * cdf).astype(BF)
    act_ref[...] = act
    pdf = jnp.exp(u * u * -0.5) * 0.3989422804014327
    slope_ref[...] = (cdf + u * pdf).astype(BF)

    @pl.when(j < n // 2)
    def _():
        acc_ref[...] += dot(act, woa_ref[...])

    @pl.when(j >= n // 2)
    def _():
        acc_ref[...] += dot(act, wob_ref[...])

    @pl.when(j == n - 1)
    def _():
        out_ref[...] = acc_ref[...].astype(BF)


def ff_back_kernel(
    rot_ref, g_ref, act_ref, slope_ref, nrm_ref, wia_ref, wib_ref, woa_ref, wob_ref, h_ref, par_ref,
    dia_ref, dib_ref, doa_ref, dob_ref, dbin_ref, small_ref, out_ref, acc_ref,
):
    j = pl.program_id(0)
    n = pl.num_programs(0)

    @pl.when(j == 0)
    def _():
        acc_ref[...] = jnp.zeros_like(acc_ref)

    def step(wo_ref, do_ref):
        g = g_ref[...]
        d_up_f = dot_nt(g, wo_ref[...]) * slope_ref[...].astype(F32)
        d_up = d_up_f.astype(BF)
        do_ref[...] = dot_tn(act_ref[...], g).astype(BF)
        dbin_ref[...] = jnp.sum(d_up_f, axis=0, keepdims=True)
        dia_ref[...] = dot_tn(nrm_ref[:, :HALF], d_up).astype(BF)
        dib_ref[...] = dot_tn(nrm_ref[:, HALF:], d_up).astype(BF)
        acc_ref[:, :HALF] += dot_nt(d_up, wia_ref[...])
        acc_ref[:, HALF:] += dot_nt(d_up, wib_ref[...])

    @pl.when(j < n // 2)
    def _():
        step(woa_ref, doa_ref)

    @pl.when(j >= n // 2)
    def _():
        step(wob_ref, dob_ref)

    @pl.when(j == n - 1)
    def _():
        g = g_ref[...].astype(F32)
        d_normed = turn_halves(acc_ref[...], rot_ref[0])
        out, d_gain, d_shift = norm_backward(h_ref[...].astype(F32), par_ref[0:1, :], g, d_normed)
        out_ref[...] = out.astype(BF)
        small_ref[0:1, :] = jnp.sum(g, axis=0, keepdims=True)
        small_ref[1:2, :] = d_gain
        small_ref[2:3, :] = d_shift
        small_ref[3:8, :] = jnp.zeros((5, D), F32)


def mix_back_kernel(rot_ref, g_ref, o_ref, woa_ref, wob_ref, dmix_ref, delta_ref, doa_ref, dob_ref):
    g = g_ref[...]
    rot = rot_ref[0]
    d_mix = jnp.concatenate([dot_nt(g, woa_ref[...]), dot_nt(g, wob_ref[...])], axis=1)
    d_mix = turn_halves(d_mix, rot).astype(BF)
    dmix_ref[...] = d_mix
    o = o_ref[...].astype(F32)
    product = d_mix.astype(F32) * o
    head = lax.broadcasted_iota(jnp.int32, (16, D), 0)
    lanes = lax.broadcasted_iota(jnp.int32, (16, D), 1)
    chosen = jnp.where(lanes // HD == head, 1.0, 0.0)
    delta_ref[...] = lax.dot_general(
        chosen, product, NT, preferred_element_type=F32, precision=lax.Precision.HIGHEST
    )
    turned = turn_halves(o, rot).astype(BF)
    doa_ref[...] = dot_tn(turned[:, :HALF], g).astype(BF)
    dob_ref[...] = dot_tn(turned[:, HALF:], g).astype(BF)


def attend_back_kernel(
    q_ref, km_ref, vm_ref, kt_ref, vt_ref, do_ref, lse_ref, delta_ref, segq_ref, segm_ref, segt_ref,
    dq_ref, dkm_ref, dvm_ref, dkt_ref, dvt_ref,
):
    j = pl.program_id(0)
    rows = q_ref.shape[0]
    lanes = lax.broadcasted_iota(jnp.int32, (rows, 2 * HD), 1)
    q = q_ref[...]
    do = do_ref[...]
    zero = jnp.zeros_like(q)
    d_q = jnp.zeros((rows, 2 * HD), F32)
    sets = ((km_ref, vm_ref, segm_ref), (kt_ref, vt_ref, segt_ref))
    d_k = [0.0, 0.0]
    d_v = [0.0, 0.0]
    for side in range(2):
        mine = (lanes >= HD) if side else (lanes < HD)
        q_head = jnp.where(mine, q, zero)
        do_head = jnp.where(mine, do, zero)
        lse = lse_ref[pl.ds(2 * j + side, 1), :]
        delta = delta_ref[pl.ds(2 * j + side, 1), :]
        for i, (k_ref, v_ref, seg_ref) in enumerate(sets):
            k = k_ref[...]
            s_t = dot_nt(k, q_head)
            p_t = jnp.where(seg_ref[...] == segq_ref[...], jnp.exp(s_t - lse), 0.0)
            d_p = dot_nt(v_ref[...], do_head)
            d_s = (p_t * (d_p - delta)).astype(BF)
            d_v[i] += dot(p_t.astype(BF), do_head)
            d_k[i] += dot(d_s, q_head)
            d_q += dot_tn(d_s, jnp.where(mine, k, zero))
    dq_ref[...] = d_q
    dkm_ref[...] = d_k[0]
    dvm_ref[...] = d_v[0]
    dkt_ref[...] = d_k[1].astype(BF)
    dvt_ref[...] = d_v[1].astype(BF)


def qkv_back_kernel(
    rot_ref, dq_ref, dkm_ref, dvm_ref, dkr_ref, dvr_ref, qkv_ref, cos_ref, sin_ref, pos_ref,
    nrm_ref, wa_ref, wb_ref, h_ref, par_ref, g_ref,
    dia_ref, dib_ref, dbin_ref, small_ref, out_ref, acc_ref, dp_ref,
):
    j = pl.program_id(0)
    n = pl.num_programs(0)

    @pl.when(j == 0)
    def _():
        acc_ref[...] = jnp.zeros_like(acc_ref)
        small_ref[...] = jnp.zeros_like(small_ref)

    def turned_back(dy, y):
        swapped = swap_pairs(dy)
        d_angle = y * swapped - swap_pairs(y) * dy
        small_ref[3:4, :] += jnp.sum(d_angle * pos_ref[:, 0:1], axis=0, keepdims=True)
        small_ref[4:5, :] += jnp.sum(d_angle * pos_ref[:, 1:2], axis=0, keepdims=True)
        return dy * cos_ref[...] - swapped * sin_ref[...]

    @pl.when(j == 0)
    def _():
        d_y = dq_ref[...] * HD ** (-0.5)
        y = qkv_ref[...].astype(F32) * HD**0.5
        dp_ref[...] = turned_back(d_y, y)

    @pl.when(j == 1)
    def _():
        d_y = dkm_ref[...] + dkr_ref[...].astype(F32)
        dp_ref[...] = turned_back(d_y, qkv_ref[...].astype(F32))

    @pl.when(j == 2)
    def _():
        dp_ref[...] = dvm_ref[...] + dvr_ref[...].astype(F32)

    d_f = dp_ref[...]
    d_p = d_f.astype(BF)
    dbin_ref[...] = jnp.sum(d_f, axis=0, keepdims=True)
    dia_ref[...] = dot_tn(nrm_ref[:, :HALF], d_p).astype(BF)
    dib_ref[...] = dot_tn(nrm_ref[:, HALF:], d_p).astype(BF)
    acc_ref[:, :HALF] += dot_nt(d_p, wa_ref[...])
    acc_ref[:, HALF:] += dot_nt(d_p, wb_ref[...])

    @pl.when(j == n - 1)
    def _():
        g = g_ref[...].astype(F32)
        d_normed = turn_halves(acc_ref[...], rot_ref[0])
        out, d_gain, d_shift = norm_backward(h_ref[...].astype(F32), par_ref[0:1, :], g, d_normed)
        out_ref[...] = out.astype(BF)
        small_ref[0:1, :] = jnp.sum(g, axis=0, keepdims=True)
        small_ref[1:2, :] = d_gain
        small_ref[2:3, :] = d_shift


def params_of(n=1):
    return pltpu.CompilerParams(
        dimension_semantics=("arbitrary",) * n, vmem_limit_bytes=VMEM_BYTES
    )


def whole(shape):
    return pl.BlockSpec(shape, lambda *_: (0,) * len(shape))


def sds(shape, dtype):
    return jax.ShapeDtypeStruct(shape, dtype)


def cost(flops, nbytes, trans=0):
    return pl.CostEstimate(flops=flops, bytes_accessed=nbytes, transcendentals=trans)


def qkv_call(rot, h, par, wa, wb, bias, cosines, sines):
    t = h.shape[0]
    return pl.pallas_call(
        qkv_kernel,
        out_shape=(sds((t, QKV), BF), sds((t, D), BF)),
        grid_spec=pltpu.PrefetchScalarGridSpec(
            num_scalar_prefetch=1,
            grid=(3,),
            in_specs=[
                whole((t, D)), whole((8, D)),
                pl.BlockSpec((HALF, D), lambda j, r: (0, j)),
                pl.BlockSpec((HALF, D), lambda j, r: (0, j)),
                pl.BlockSpec((1, D), lambda j, r: (0, j)),
                whole((t, D)), whole((t, D)),
            ],
            out_specs=[pl.BlockSpec((t, D), lambda j, r: (0, j)), whole((t, D))],
        ),
        compiler_params=params_of(),
        cost_estimate=cost(2 * t * D * QKV, 2 * D * QKV + 8 * t * D + 2 * t * QKV),
        name="qkv",
    )(rot, h, par, wa, wb, bias, cosines, sines)


def attend_call(rot, qkv, kv_t, seg_col, seg_m, seg_t, h, woa, wob, bias):
    t = h.shape[0]
    w = 2 * HD
    return pl.pallas_call(
        attend_kernel,
        out_shape=(sds((t, D), BF), sds((16, t), F32), sds((t, D), BF)),
        grid_spec=pltpu.PrefetchScalarGridSpec(
            num_scalar_prefetch=1,
            grid=(PAIRS,),
            in_specs=[
                pl.BlockSpec((t, w), lambda j, r: (0, j)),
                pl.BlockSpec((t, w), lambda j, r: (0, j + PAIRS)),
                pl.BlockSpec((t, w), lambda j, r: (0, j + 2 * PAIRS)),
                pl.BlockSpec((t, w), lambda j, r: (0, j)),
                pl.BlockSpec((t, w), lambda j, r: (0, j + PAIRS)),
                whole((t, 1)), whole((1, t)), whole((1, t)), whole((t, D)),
                whole((HALF, D)), whole((HALF, D)), whole((1, D)),
            ],
            out_specs=[whole((t, D)), whole((16, t)), whole((t, D))],
            scratch_shapes=[pltpu.VMEM((t, w), F32)],
        ),
        compiler_params=params_of(),
        cost_estimate=cost(8 * t * t * D * 4, 16 * t * D, 2 * t * t * HEADS),
        name="attend",
    )(rot, qkv, qkv, qkv, kv_t, kv_t, seg_col, seg_m, seg_t, h, woa, wob, bias)


def ff_specs(t, blocks):
    width = FF // blocks
    half = blocks // 2
    w_in = pl.BlockSpec((HALF, width), lambda j, r: (0, (j + half * r[0]) % blocks))
    b_in = pl.BlockSpec((1, width), lambda j, r: (0, (j + half * r[0]) % blocks))
    w_a = pl.BlockSpec((width, D), lambda j, r: (jnp.minimum(j, half - 1), 0))
    w_b = pl.BlockSpec((width, D), lambda j, r: (jnp.maximum(j - half, 0), 0))
    hid = pl.BlockSpec((t, width), lambda j, r: (0, j))
    return w_in, b_in, w_a, w_b, hid


def ff_call(rot, h, par, wia, wib, bias, woa, wob, bout):
    t = h.shape[0]
    blocks = 6
    w_in, b_in, w_a, w_b, hid = ff_specs(t, blocks)
    return pl.pallas_call(
        ff_kernel,
        out_shape=(sds((t, FF), BF), sds((t, FF), BF), sds((t, D), BF), sds((t, D), BF)),
        grid_spec=pltpu.PrefetchScalarGridSpec(
            num_scalar_prefetch=1,
            grid=(blocks,),
            in_specs=[whole((t, D)), whole((8, D)), w_in, w_in, b_in, w_a, w_b, whole((1, D))],
            out_specs=[hid, hid, whole((t, D)), whole((t, D))],
            scratch_shapes=[pltpu.VMEM((t, D), F32)],
        ),
        compiler_params=params_of(),
        cost_estimate=cost(4 * t * D * FF, 4 * D * FF + 4 * t * FF, 2 * t * FF),
        name="feed",
    )(rot, h, par, wia, wib, bias, woa, wob, bout)


def ff_back_call(rot, g, act, slope, nrm, wia, wib, woa, wob, h, par):
    t = h.shape[0]
    blocks = 6
    w_in, b_in, w_a, w_b, hid = ff_specs(t, blocks)
    return pl.pallas_call(
        ff_back_kernel,
        out_shape=(
            sds((HALF, FF), BF), sds((HALF, FF), BF), sds((FF // 2, D), BF), sds((FF // 2, D), BF),
            sds((1, FF), F32), sds((8, D), F32), sds((t, D), BF),
        ),
        grid_spec=pltpu.PrefetchScalarGridSpec(
            num_scalar_prefetch=1,
            grid=(blocks,),
            in_specs=[
                whole((t, D)), hid, hid, whole((t, D)), w_in, w_in, w_a, w_b, whole((t, D)),
                whole((8, D)),
            ],
            out_specs=[w_in, w_in, w_a, w_b, b_in, whole((8, D)), whole((t, D))],
            scratch_shapes=[pltpu.VMEM((t, D), F32)],
        ),
        compiler_params=params_of(),
        cost_estimate=cost(8 * t * D * FF, 8 * D * FF + 4 * t * FF),
        name="feed_back",
    )(rot, g, act, slope, nrm, wia, wib, woa, wob, h, par)


def mix_back_call(rot, g, o, woa, wob):
    t = g.shape[0]
    return pl.pallas_call(
        mix_back_kernel,
        out_shape=(sds((t, D), BF), sds((16, t), F32), sds((HALF, D), BF), sds((HALF, D), BF)),
        grid_spec=pltpu.PrefetchScalarGridSpec(
            num_scalar_prefetch=1,
            grid=(1,),
            in_specs=[whole((t, D)), whole((t, D)), whole((HALF, D)), whole((HALF, D))],
            out_specs=[whole((t, D)), whole((16, t)), whole((HALF, D)), whole((HALF, D))],
        ),
        compiler_params=params_of(),
        cost_estimate=cost(4 * t * D * D, 4 * D * D + 6 * t * D),
        name="mix_back",
    )(rot, g, o, woa, wob)


def attend_back_call(qkv, kv_t, dmix, lse, delta, seg_row, seg_m, seg_t):
    t = dmix.shape[0]
    w = 2 * HD
    col = pl.BlockSpec((t, w), lambda j: (0, j))
    return pl.pallas_call(
        attend_back_kernel,
        out_shape=(sds((t, D), F32), sds((t, D), F32), sds((t, D), F32), sds((t, D), BF), sds((t, D), BF)),
        grid=(PAIRS,),
        in_specs=[
            col,
            pl.BlockSpec((t, w), lambda j: (0, j + PAIRS)),
            pl.BlockSpec((t, w), lambda j: (0, j + 2 * PAIRS)),
            col,
            pl.BlockSpec((t, w), lambda j: (0, j + PAIRS)),
            col, whole((16, t)), whole((16, t)), whole((1, t)), whole((t, 1)), whole((t, 1)),
        ],
        out_specs=[col] * 5,
        compiler_params=params_of(),
        cost_estimate=cost(20 * t * t * D * 4, 30 * t * D, 2 * t * t * HEADS),
        name="attend_back",
    )(qkv, qkv, qkv, kv_t, kv_t, dmix, lse, delta, seg_row, seg_m, seg_t)


def qkv_back_call(rot, dq, dkm, dvm, dkr, dvr, qkv, cosines, sines, pos, nrm, wa, wb, h, par, g):
    t = h.shape[0]
    w_in = pl.BlockSpec((HALF, D), lambda j, r: (0, j))
    rows = whole((t, D))
    return pl.pallas_call(
        qkv_back_kernel,
        out_shape=(
            sds((HALF, QKV), BF), sds((HALF, QKV), BF), sds((1, QKV), F32), sds((8, D), F32),
            sds((t, D), BF),
        ),
        grid_spec=pltpu.PrefetchScalarGridSpec(
            num_scalar_prefetch=1,
            grid=(3,),
            in_specs=[
                rows, rows, rows, rows, rows, pl.BlockSpec((t, D), lambda j, r: (0, j)), rows, rows,
                whole((t, 2)), rows, w_in, w_in, rows, whole((8, D)), rows,
            ],
            out_specs=[w_in, w_in, pl.BlockSpec((1, D), lambda j, r: (0, j)), whole((8, D)), rows],
            scratch_shapes=[pltpu.VMEM((t, D), F32), pltpu.VMEM((t, D), F32)],
        ),
        compiler_params=params_of(),
        cost_estimate=cost(4 * t * D * QKV, 4 * D * QKV + 30 * t * D),
        name="qkv_back",
    )(rot, dq, dkm, dvm, dkr, dvr, qkv, cosines, sines, pos, nrm, wa, wb, h, par, g)


def layout(image_sides, capacity):
    counts = image_sides * image_sides
    end_pos = jnp.cumsum(counts)
    start_pos = end_pos - counts
    positions = jnp.arange(capacity, dtype=jnp.int32)
    segment = jnp.sum((positions[:, None] >= end_pos[None, :]).astype(jnp.int32), axis=1)
    slot_ids = jnp.arange(image_sides.shape[-1], dtype=jnp.int32)
    one_hot = (segment[:, None] == slot_ids[None, :]).astype(jnp.int32)
    start_tok = jnp.sum(one_hot * start_pos[None, :], axis=1)
    side_len = jnp.maximum(jnp.sum(one_hot * image_sides[None, :], axis=1), 1)
    local_idx = positions - start_tok
    is_valid = segment < image_sides.shape[-1]
    patch_row = jnp.where(is_valid, local_idx // side_len, 0)
    patch_col = jnp.where(is_valid, local_idx % side_len, 0)
    return segment, patch_row, patch_col, is_valid


def turning(freq, pos):
    wide = jnp.concatenate([freq.reshape(2, HEADS, HD // 2)] * 2, axis=2).reshape(2, D)
    angles = pos[:, 0:1] * wide[0][None, :] + pos[:, 1:2] * wide[1][None, :]
    low = (jnp.arange(D) % HD) < HD // 2
    sines = jnp.sin(angles)
    return jnp.cos(angles), jnp.where(low[None, :], -sines, sines)


def flipped(x, axis, bit):
    return lax.ppermute(x, axis, [(i, i ^ bit) for i in range(lax.axis_size(axis))])


def to_owners(blocks, section, core):
    stacked = jnp.stack(blocks)
    got = [stacked[section]] + [flipped(stacked[section ^ d], "section", d) for d in (1, 2, 3)]
    here = (section // 2) == core
    near = jnp.stack(got[:2])
    away = jnp.stack(got[2:])
    mine = jnp.where(here, near, away)
    other = flipped(jnp.where(here, away, near), "group", 1)

    def in_order(pair):
        return jnp.where(section % 2 == 0, pair, pair[::-1])

    mine, other = in_order(mine), in_order(other)
    first = jnp.where(core == 0, mine, other)
    second = jnp.where(core == 0, other, mine)
    return jnp.concatenate([first, second], axis=1).reshape(-1, D)


MESH = pl.DeviceIdType.MESH
SMALL = (16, D)
SEMS = 20
LINE = 4


def unit_shape(s, part):
    if s % 2:
        return (FF // 2, D) if part else (HALF, FF)
    return (HALF, D) if part else (HALF, QKV)


def grad_shape(s, part):
    if s % 2:
        return (FF // 2, D) if part else (HALF, FF)
    return (D, D) if part else (HALF, 2 * D)


def piece_shape(s, part):
    r, w = grad_shape(s, part)
    return (r // 8, w // 2)


def held_shape(s, part):
    r, w = grad_shape(s, part)
    return (4, 2, r // 8, w)


def columns_of(k, width):
    return pl.ds(pl.multiple_of((k % 2) * width, width), width)


def flip(v, bit):
    if bit == 1:
        return v + 1 - 2 * (v % 2)
    if bit == 2:
        return (v + 2) % 4
    return 3 - v


def here():
    return lax.axis_index("section"), lax.axis_index("group"), lax.axis_index("dp")


def loop(n, body):
    def one(i, carried):
        body(i)
        return carried

    lax.fori_loop(0, n, one, 0)


def greet(plane, line):
    c, g, z = here()
    barrier = pltpu.get_barrier_semaphore()
    pl.semaphore_signal(barrier, inc=1, device_id={"group": 1 - g}, device_id_type=MESH)
    count = 1
    for bit in (1, 2, 3):
        if plane:
            for core in (g, 1 - g):
                pl.semaphore_signal(
                    barrier, inc=1, device_id={"section": flip(c, bit), "group": core},
                    device_id_type=MESH,
                )
                count += 1
        if line:
            pl.semaphore_signal(barrier, inc=1, device_id={"dp": flip(z, bit)}, device_id_type=MESH)
            count += 1
    pl.semaphore_wait(barrier, count)


def guarded(cond, act):
    if cond is None:
        act()
    else:
        pl.when(cond)(act)


def accumulate(into, term, rows):
    strip = 32 if rows % 32 == 0 else 16

    def one(i):
        at = pl.ds(pl.multiple_of(i * strip, strip), strip)
        into[at, :] = (into[at, :].astype(F32) + term[at, :].astype(F32)).astype(BF)

    loop(rows // strip, one)


class Unit:
    def __init__(
        self, s, part, send, recv, own=None, quarter=None, final=None, plane=None, line=None,
        held=None, whole=None,
    ):
        self.s, self.part, self.own, self.quarter_ref, self.final = s, part, own, quarter, final
        self.send, self.recv = send, recv
        self.whole = whole
        self.rows, self.cols = grad_shape(s, part)
        self.plane1, self.plane2 = plane or (None, None)
        self.up_in, self.down_in = line or (None, None)
        self.held = held
        self.pending = []

    def push(self, cond, src, dst, k, device):
        copy = pltpu.make_async_remote_copy(
            src_ref=src, dst_ref=dst, send_sem=self.send.at[k], recv_sem=self.recv.at[k],
            device_id=device, device_id_type=MESH,
        )
        guarded(cond, copy.start)
        self.pending.append((cond, copy))

    def landed(self, cond, dst, k):
        copy = pltpu.make_async_remote_copy(
            src_ref=dst, dst_ref=dst, send_sem=self.send.at[k], recv_sem=self.recv.at[k],
            device_id={"group": 1 - lax.axis_index("group")}, device_id_type=MESH,
        )
        guarded(cond, copy.wait_recv)

    def finish(self):
        for cond, copy in self.pending:
            guarded(cond, copy.wait_send)

    def quarter(self, q):
        rows = self.rows // 4
        return self.own.at[pl.ds(pl.multiple_of(q * rows, rows), rows), :]

    def mine(self):
        if self.quarter_ref is not None:
            return self.quarter_ref
        return self.quarter(lax.axis_index("section"))

    def piece(self, k):
        rows, cols = self.rows // 8, self.cols // 2
        return self.mine().at[
            pl.ds(pl.multiple_of((k // 2) * rows, rows), rows),
            pl.ds(pl.multiple_of((k % 2) * cols, cols), cols),
        ]

    def first_step(self):
        c, _, _ = here()
        x, y = c % 2, c // 2
        other = {"section": flip(c, 2 if self.part else 1)}
        bit = x if self.part else y
        for b in (1 - bit, bit):
            q = 2 * (1 - y) + b if self.part else 2 * b + 1 - x
            self.push(None, self.quarter(q), self.plane1.at[b], 1 + b, other)

    def second_step(self):
        c, _, _ = here()
        x, y = c % 2, c // 2
        b = (1 - x) if self.part else (1 - y)
        q = (2 * y + 1 - x) if self.part else (2 * (1 - y) + x)
        self.landed(None, self.plane1.at[b], 1 + b)
        accumulate(self.quarter(q), self.plane1.at[b], self.rows // 4)
        self.push(
            None, self.quarter(q), self.plane2, 3, {"section": flip(c, 1 if self.part else 2)}
        )

    def keep_step(self):
        c, _, _ = here()
        b = (c % 2) if self.part else (c // 2)
        self.landed(None, self.plane1.at[b], 1 + b)
        accumulate(self.mine(), self.plane1.at[b], self.rows // 4)

    def third_step(self):
        self.landed(None, self.plane2, 3)
        accumulate(self.mine(), self.plane2, self.rows // 4)

    def line_step(self, t):
        _, _, z = here()
        n = LINE
        rows = self.rows // 8
        up = (z < n - 1) & (z <= t)
        down = (z > 0) & (z >= n - 1 - t)
        k_up = jnp.minimum(n - 1 - t + z, n - 1)
        k_down = jnp.maximum(z - (n - 1) + t, 0)
        if t > 0:

            @pl.when(up & (z > 0))
            def _():
                self.landed(None, self.up_in.at[t - 1], 4 + t - 1)
                accumulate(self.piece(k_up), self.up_in.at[t - 1], rows)

            @pl.when(down & (z < n - 1))
            def _():
                self.landed(None, self.down_in.at[t - 1], 7 + t - 1)
                accumulate(self.piece(k_down), self.down_in.at[t - 1], rows)

        self.push(up, self.piece(k_up), self.up_in.at[t], 4 + t, {"dp": jnp.minimum(z + 1, n - 1)})
        self.push(down, self.piece(k_down), self.down_in.at[t], 7 + t, {"dp": jnp.maximum(z - 1, 0)})

    def line_end(self):
        _, _, z = here()
        n = LINE
        rows = self.rows // 8

        @pl.when(z > 0)
        def _():
            self.landed(None, self.up_in.at[n - 2], 4 + n - 2)
            accumulate(self.piece(z), self.up_in.at[n - 2], rows)

        @pl.when(z < n - 1)
        def _():
            self.landed(None, self.down_in.at[n - 2], 7 + n - 2)
            accumulate(self.piece(z), self.down_in.at[n - 2], rows)

    def held_at(self, k, q=None):
        cols = columns_of(k, self.cols // 2)
        return self.held.at[:, k // 2, :, cols] if q is None else self.held.at[q, k // 2, :, cols]

    def whole_at(self, k):
        return self.whole.at[k // 2, :, columns_of(k, self.cols // 2)]

    def last_piece(self):
        return self.final if self.final is not None else self.piece(here()[2])

    def own_piece(self):
        _, _, z = here()
        return pltpu.make_async_copy(
            self.last_piece(), self.held_at(z, self.s), self.send.at[10 + self.s]
        )

    def gather(self):
        c, _, z = here()
        for q in range(4):
            if q == self.s:
                pl.when(c == q)(self.own_piece().start)
            else:
                self.push(
                    c == q, self.last_piece(), self.held_at(z, q), 10 + q, {"section": self.s}
                )

    def share_step(self, t):
        _, _, z = here()
        n = LINE
        whole = self.whole_at
        if t == 0:
            copy = pltpu.make_async_copy(self.last_piece(), whole(z), self.send.at[0])
            copy.start()
            copy.wait()
        else:
            self.landed(z >= t, whole(jnp.maximum(z - t, 0)), 14 + t - 1)
            self.landed(z + t < n, whole(jnp.minimum(z + t, n - 1)), 17 + t - 1)
        if t < n - 1:
            low, high = jnp.maximum(z - t, 0), jnp.minimum(z + t, n - 1)
            self.push(
                (z >= t) & (z < n - 1), whole(low), whole(low), 14 + t,
                {"dp": jnp.minimum(z + 1, n - 1)},
            )
            self.push(
                (z + t < n) & (z > 0), whole(high), whole(high), 17 + t,
                {"dp": jnp.maximum(z - 1, 0)},
            )

    def whole_copy(self):
        return pltpu.make_async_copy(self.whole, self.held.at[self.s], self.send.at[10 + self.s])

    def whole_gather(self):
        c, _, _ = here()
        for q in range(4):
            if q == self.s:
                pl.when(c == q)(self.whole_copy().start)
            else:
                self.push(c == q, self.whole, self.held.at[q], 10 + q, {"section": self.s})

    def whole_end(self):
        c, _, _ = here()
        for q in range(4):
            if q == self.s:
                pl.when(c == q)(self.whole_copy().wait)
            else:
                self.landed(c == self.s, self.held.at[q], 10 + q)

    def out_step(self, t):
        c, _, z = here()
        n = LINE
        mine = c == self.s
        held = self.held_at
        if t == 0:
            for q in range(4):
                if q == self.s:
                    pl.when(mine)(self.own_piece().wait)
                else:
                    self.landed(mine, held(z, q), 10 + q)
        else:
            self.landed(mine & (z >= t), held(jnp.maximum(z - t, 0)), 14 + t - 1)
            self.landed(mine & (z + t < n), held(jnp.minimum(z + t, n - 1)), 17 + t - 1)
        if t < n - 1:
            low, high = jnp.maximum(z - t, 0), jnp.minimum(z + t, n - 1)
            self.push(
                mine & (z >= t) & (z < n - 1), held(low), held(low), 14 + t,
                {"dp": jnp.minimum(z + 1, n - 1)},
            )
            self.push(
                mine & (z + t < n) & (z > 0), held(high), held(high), 17 + t,
                {"dp": jnp.maximum(z - 1, 0)},
            )


class Delivery:
    def __init__(self, sources, parts, out, send, recv):
        self.sources, self.parts, self.out, self.send, self.recv = sources, parts, out, send, recv

    def rows(self, block):
        size = self.sources[self.parts[0][0]].shape[0] // 2
        return pl.ds(block * size, size)

    def copies(self, s, block):
        c, g, _ = here()
        slot = self.out.at[c % 2, g, self.rows(block), :]
        source = self.sources[s].at[self.rows(block), :]
        near = pltpu.make_async_copy(source, slot, self.send.at[s, block])
        far = pltpu.make_async_remote_copy(
            src_ref=source, dst_ref=slot, send_sem=self.send.at[s, block],
            recv_sem=self.recv.at[(c % 2) * 2 + g, block],
            device_id={"section": s, "group": c // 2}, device_id_type=MESH,
        )
        return near, far, (c == s) & (g == c // 2)

    def start(self, parts):
        for part in parts:
            near, far, stays = self.copies(*part)
            pl.when(stays)(near.start)
            pl.when(jnp.logical_not(stays))(far.start)

    def finish(self):
        c, g, _ = here()
        for s, block in self.parts:
            near, far, stays = self.copies(s, block)
            pl.when(stays)(near.wait)
            pl.when(jnp.logical_not(stays))(far.wait_send)
            for m in range(2):
                for half in range(2):
                    slot = self.out.at[m, half, self.rows(block), :]
                    copy = pltpu.make_async_remote_copy(
                        src_ref=slot, dst_ref=slot, send_sem=self.send.at[0, 0],
                        recv_sem=self.recv.at[2 * m + half, block], device_id={"group": 1 - g},
                        device_id_type=MESH,
                    )
                    arrives = (c == s) & jnp.logical_not((2 * g + m == c) & (g == half))
                    pl.when(arrives)(copy.wait_recv)


ALL = tuple((s, block) for block in range(2) for s in range(4))


def feed_back_kernel(s, carry, *refs):
    delivers = carry is None
    wim, wit, wom, wot, act_in, slope_in, streams = refs[:7]
    refs = refs[7:]
    count = 0 if delivers else len(carry.all)
    carried, refs = refs[:count], refs[count:]
    g_ref, nrm, par = refs[:3]
    d_in, d_out = refs[3:5]
    refs = refs[5:]
    if delivers:
        delivered, refs = refs[0], refs[1:]
    results, refs = refs[:count], refs[count:]
    dbin_ref, small_ref, out_ref = refs[:3]
    w_in, w_out, act, slope, h, own_i, own_o, their_i, their_o, core_i, core_o, acc, nrm_t = refs[3:16]
    load_sem, core_s, core_r, out_sem = refs[16:20]
    refs = refs[20:]
    _, g, _ = here()
    partner = {"group": 1 - g}
    width = FF // CHUNKS
    third = CHUNKS // 2

    def column(j):
        b = (j + g * third) % CHUNKS
        return pl.ds(pl.multiple_of(b * width, width), width)

    def line_of(j):
        return pl.ds(pl.multiple_of(j * width, width), width)

    def loads(j):
        cols, rows = column(j), line_of(j % third)
        first = j < third
        return (
            (None, pltpu.make_async_copy(wim.at[:, cols], w_in.at[0, :, cols], load_sem.at[j, 0])),
            (None, pltpu.make_async_copy(wit.at[:, cols], w_in.at[1, :, cols], load_sem.at[j, 1])),
            (first, pltpu.make_async_copy(wom.at[rows, :], w_out.at[line_of(j), :], load_sem.at[j, 2])),
            (
                jnp.logical_not(first),
                pltpu.make_async_copy(wot.at[rows, :], w_out.at[line_of(j), :], load_sem.at[j, 2]),
            ),
            (None, pltpu.make_async_copy(act_in.at[:, line_of(j)], act.at[:, line_of(j)], load_sem.at[j, 3])),
            (None, pltpu.make_async_copy(slope_in.at[:, line_of(j)], slope.at[:, line_of(j)], load_sem.at[j, 4])),
        )

    def load(j):
        for cond, copy in loads(j):
            guarded(cond, copy.start)

    def core_copies(j):
        cols, rows = column(j), line_of(j % third)
        return (
            pltpu.make_async_remote_copy(
                src_ref=their_i.at[:, cols], dst_ref=core_i.at[:, cols], send_sem=core_s.at[j, 0],
                recv_sem=core_r.at[j, 0], device_id=partner, device_id_type=MESH,
            ),
            pltpu.make_async_remote_copy(
                src_ref=their_o.at[rows, :], dst_ref=core_o.at[rows, :], send_sem=core_s.at[j, 1],
                recv_sem=core_r.at[j, 1], device_id=partner, device_id_type=MESH,
            ),
        )

    loop(CHUNKS, load)
    stream_copy = pltpu.make_async_copy(streams.at[s - 1], h, out_sem.at[2])
    stream_copy.start()
    if not delivers:
        carry.load(carried, results, refs)
    greet(True, not delivers)
    if delivers:
        delivery = Delivery([streams.at[i] for i in range(4)], ALL, delivered, *refs)
        delivery.start(ALL)
    else:
        carry.begin()
    acc[...] = jnp.zeros_like(acc)
    nrm_t[...] = jnp.transpose(nrm[...])

    def block(j):
        for cond, copy in loads(j):
            guarded(cond, copy.wait)
        cols, rows = column(j), line_of(j)
        grad = g_ref[...]
        d_up_f = dot_nt(grad, w_out[rows, :]) * slope[:, rows].astype(F32)
        d_up = d_up_f.astype(BF)
        d_o = dot_tn(act[:, rows], grad).astype(BF)
        dbin_ref[:, cols] = jnp.sum(d_up_f, axis=0, keepdims=True)
        their_i[:, cols] = dot(nrm_t[HALF:, :], d_up).astype(BF)
        inward, outward = core_copies(j)
        inward.start()

        @pl.when(j >= third)
        def _():
            their_o[line_of(j % third), :] = d_o
            outward.start()

        @pl.when(j < third)
        def _():
            own_o[line_of(j % third), :] = d_o

        own_i[:, cols] = dot(nrm_t[:HALF, :], d_up).astype(BF)
        acc[:, :HALF] += dot_nt(d_up, w_in[0, :, cols])
        acc[:, HALF:] += dot_nt(d_up, w_in[1, :, cols])

    if delivers:
        loop(CHUNKS, block)
    else:
        for i in range(3):
            loop(CHUNKS // 3, lambda j, i=i: block(j + CHUNKS // 3 * i))
            carry.step(i + 1)
    stream_copy.wait()
    grad = g_ref[...].astype(F32)
    d_normed = turn_halves(acc[...], g)
    out, d_gain, d_shift = norm_backward(h[...].astype(F32), par[0:1, :], grad, d_normed)
    out_ref[...] = out.astype(BF)
    small_ref[0:1, :] = jnp.sum(grad, axis=0, keepdims=True)
    small_ref[1:2, :] = d_gain
    small_ref[2:3, :] = d_shift
    small_ref[3:8, :] = jnp.zeros((5, D), F32)

    def ended(j):
        inward, outward = core_copies(j)
        inward.wait()
        pl.when(j >= third)(outward.wait)

    loop(CHUNKS, ended)
    accumulate(own_i, core_i, HALF)
    saves = [pltpu.make_async_copy(own_i, d_in, out_sem.at[0])]
    saves[0].start()
    accumulate(own_o, core_o, FF // 2)
    saves.append(pltpu.make_async_copy(own_o, d_out, out_sem.at[1]))
    saves[1].start()
    if delivers:
        delivery.finish()
    else:
        carry.end()
    for copy in saves:
        copy.wait()


def every(units, act, *args):
    for unit in units:
        getattr(unit, act)(*args)


class Carry:
    last = False

    def __init__(self, plane, line, hold):
        self.planes = [(plane, 0), (plane, 1)]
        self.line, self.hold = line, hold
        self.all = self.planes + list(line) + list(hold)

    def results(self):
        out = []
        for u in self.planes:
            r, w = grad_shape(*u)
            out.append(sds((r // 4, w), BF))
        out += [sds(piece_shape(*u), BF) for u in self.line]
        return out + [sds(held_shape(*u), BF) for u in self.hold]

    def scratch(self):
        out = []
        for u in self.planes:
            r, w = grad_shape(*u)
            out += [pltpu.VMEM((r, w), BF), pltpu.VMEM((2, r // 4, w), BF), pltpu.VMEM((r // 4, w), BF)]
        for u in self.line:
            r, w = grad_shape(*u)
            out += [pltpu.VMEM((r // 4, w), BF)] + [pltpu.VMEM((3,) + piece_shape(*u), BF)] * 2
        out += [pltpu.VMEM(piece_shape(*u), BF) for u in self.hold]
        dma = pltpu.SemaphoreType.DMA
        return out + [dma((len(self.all), SEMS)), dma((len(self.all), SEMS))]

    def load(self, sources, results, refs):
        send, recv = refs[-2:]
        refs = list(refs[:-2])
        self.units, self.loads, self.targets = [], [], results
        for i, u in enumerate(self.all):
            sems = (send.at[i], recv.at[i])
            if i < 2:
                own, first, second = refs.pop(0), refs.pop(0), refs.pop(0)
                unit = Unit(*u, *sems, own=own, plane=(first, second))
            elif i < 2 + len(self.line):
                own, up, down = refs.pop(0), refs.pop(0), refs.pop(0)
                unit = Unit(*u, *sems, quarter=own, line=(up, down))
            else:
                own = refs.pop(0)
                unit = Unit(*u, *sems, final=own, held=results[i])
            copy = pltpu.make_async_copy(sources[i], own, sems[0].at[0])
            copy.start()
            self.units.append(unit)
            self.loads.append(copy)
        n = 2 + len(self.line)
        self.plane_units, self.line_units, self.hold_units = (
            self.units[:2], self.units[2:n], self.units[n:],
        )

    def begin(self):
        for copy in self.loads:
            copy.wait()
        for unit in self.hold_units:
            unit.gather()
        for unit in self.line_units:
            unit.line_step(0)
        for unit in self.plane_units:
            unit.first_step()

    def step(self, i):
        for unit in self.line_units:
            if i < LINE - 1:
                unit.line_step(i)
            else:
                unit.line_end()
        if i > 1:
            every(self.plane_units, "second_step" if i == 2 else "keep_step")
        for unit in self.hold_units:
            if i < 3:
                unit.out_step(i - 1)

    def late_step(self):
        for unit in self.hold_units:
            unit.out_step(LINE - 2)

    def end(self):
        saves = [
            pltpu.make_async_copy(unit.last_piece(), target, unit.send.at[0])
            for unit, target in zip(self.line_units, self.targets[2:])
        ]
        for copy in saves:
            copy.start()
        for unit, target in zip(self.plane_units, self.targets):
            unit.third_step()
            copy = pltpu.make_async_copy(unit.mine(), target, unit.send.at[0])
            copy.start()
            saves.append(copy)
        for unit in self.hold_units:
            unit.out_step(LINE - 1)
        for copy in saves:
            copy.wait()
        for unit in self.units:
            unit.finish()


class Finish:
    all = ((1, 0), (1, 1), (2, 0), (2, 1), (3, 0), (3, 1))
    own_units = ((0, 0), (0, 1))
    last = True

    def results(self):
        held = [sds(held_shape(s, part), BF) for s in (0, 1) for part in (0, 1)]
        return held + [sds((2, 2, self.tokens, D), BF), sds(SMALL, F32)]

    def scratch(self):
        out = []
        for u in self.all[:2]:
            r, w = grad_shape(*u)
            out += [pltpu.VMEM((r, w), BF), pltpu.VMEM((2, r // 4, w), BF), pltpu.VMEM((r // 4, w), BF)]
        for u in self.all[2:4]:
            r, w = grad_shape(*u)
            out.append(pltpu.VMEM((r // 4, w), BF))
        out += [pltpu.VMEM(piece_shape(*u), BF) for u in self.all[4:]]
        for u in self.own_units:
            r, w = grad_shape(*u)
            out += [pltpu.VMEM((2, r // 4, w), BF), pltpu.VMEM((r // 4, w), BF)]
        for u in self.all[:4] + self.own_units:
            out += [pltpu.VMEM((3,) + piece_shape(*u), BF)] * 2
        out += [pltpu.VMEM(held_shape(*u)[1:], BF) for u in ((1, 1), (0, 1))]
        dma = pltpu.SemaphoreType.DMA
        small = [pltpu.VMEM((n,) + SMALL, F32) for n in (4, 4, 4, 2, 3, 4)]
        return out + small + [
            dma((8, SEMS)), dma((8, SEMS)), dma((7,)), dma((7,)), dma((4, 2)), dma((4, 2)),
        ]

    def load(self, sources, results, refs, own, streams, small_in):
        refs = list(refs)

        def take(n):
            out = refs[:n]
            del refs[:n]
            return out

        halves = [take(3), take(3)]
        quarters, finals = take(2), take(2)
        planes = [take(2), take(2)]
        lines = [take(2) for _ in range(6)]
        wholes = take(2)
        self.sm, self.sm_core, self.sm_x, self.sm_got, self.sm_y, self.sm_z = take(6)
        send, recv, self.sm_send, self.sm_recv, del_send, del_recv = refs
        held, delivered, self.small_out = results[:4], results[4], results[5]
        self.small_in = small_in

        def unit(i, u, **more):
            return Unit(*u, send.at[i], recv.at[i], held=held[2 * (u[0] % 2) + u[1]], **more)

        self.f1 = [
            unit(i, self.all[i], own=halves[i][0], plane=halves[i][1:], line=lines[i],
                 whole=wholes[0] if i else None)
            for i in range(2)
        ]
        self.a2 = [unit(2 + i, self.all[2 + i], quarter=quarters[i], line=lines[2 + i]) for i in range(2)]
        self.f3 = [unit(4 + i, self.all[4 + i], final=finals[i]) for i in range(2)]
        self.a0 = [
            unit(6 + i, self.own_units[i], own=own[i], plane=planes[i], line=lines[4 + i],
                 whole=wholes[1] if i else None)
            for i in range(2)
        ]
        self.units = self.f1 + self.a2 + self.f3 + self.a0
        self.delivery = Delivery(streams, ALL, delivered, del_send, del_recv)
        self.loads = [
            pltpu.make_async_copy(source, target, send.at[i, 0])
            for i, (source, target) in enumerate(
                zip(sources, [halves[0][0], halves[1][0], *quarters, *finals])
            )
        ]
        for copy in self.loads:
            copy.start()
        self.pending = []

    def begin(self):
        for copy in self.loads:
            copy.wait()
        every(self.f3, "gather")
        every(self.a2, "line_step", 0)
        every(self.f1, "first_step")

    def step(self, i):
        if i > 1:
            every(self.f1, "second_step" if i == 2 else "keep_step")
        if i < 3:
            every(self.a2, "line_step", i)
            self.f3[0].out_step(i - 1)
        else:
            every(self.a2, "line_end")
            every(self.a2, "gather")

    def late_step(self):
        pass

    def small_push(self, src, dst, k, device):
        copy = pltpu.make_async_remote_copy(
            src_ref=src, dst_ref=dst, send_sem=self.sm_send.at[k], recv_sem=self.sm_recv.at[k],
            device_id=device, device_id_type=MESH,
        )
        copy.start()
        self.pending.append(copy)

    def small_landed(self, dst, k):
        pltpu.make_async_remote_copy(
            src_ref=dst, dst_ref=dst, send_sem=self.sm_send.at[k], recv_sem=self.sm_recv.at[k],
            device_id={"group": 1 - lax.axis_index("group")}, device_id_type=MESH,
        ).wait_recv()

    def small_step(self, k):
        c, g, z = here()
        x, y = c % 2, c // 2
        if k == 0:
            self.small_push(self.sm, self.sm_core, 0, {"group": 1 - g})
        elif k == 1:
            self.small_landed(self.sm_core, 0)
            self.sm_x[...] = self.sm[...] + self.sm_core[...]
            for b in range(2):
                self.small_push(
                    self.sm_x.at[2 * b + 1 - x], self.sm_got.at[b], 1 + b, {"section": flip(c, 1)}
                )
        elif k == 2:
            for b in range(2):
                self.small_landed(self.sm_got.at[b], 1 + b)
                self.sm_y[b] = self.sm_x[2 * b + x] + self.sm_got[b]
            self.small_push(self.sm_y.at[1 - y], self.sm_y.at[2], 3, {"section": flip(c, 2)})
        elif k == 3:
            self.small_landed(self.sm_y.at[2], 3)
            self.sm_z[z] = self.sm_y[y] + self.sm_y[2]
            for bit in (1, 2, 3):
                self.small_push(self.sm_z.at[z], self.sm_z.at[z], 3 + bit, {"dp": flip(z, bit)})
        else:
            for bit in (1, 2, 3):
                self.small_landed(self.sm_z.at[flip(z, bit)], 3 + bit)
            self.small_out[...] = self.sm_z[0] + self.sm_z[1] + self.sm_z[2] + self.sm_z[3]

    def conclude(self, dbin, rest):
        f1, a2, f3, a0 = self.f1, self.a2, self.f3, self.a0
        (held_a, shared_a), (held_f, shared_f) = a0, f1
        every(a0, "first_step")
        every(f1, "third_step")
        every(f1, "line_step", 0)
        f3[0].out_step(2)
        self.sm[1:4] = self.small_in[...]
        self.sm[0] = jnp.zeros(SMALL, F32)
        for i in range(3):
            self.sm[0, i : i + 1, :] = dbin[:, i * D : (i + 1) * D]
        self.sm[0, 4:9, :] = rest[0:5, :]
        self.small_step(0)
        every(a0, "second_step")
        every(f1, "line_step", 1)
        self.small_step(1)
        every(a0, "keep_step")
        every(f1, "line_step", 2)
        self.small_step(2)
        every(f1, "line_end")
        held_f.gather()
        shared_f.share_step(0)
        f3[0].out_step(3)
        every(a0, "third_step")
        every(a0, "line_step", 0)
        self.small_step(3)
        self.delivery.start(ALL[:4])
        shared_f.share_step(1)
        every(a0, "line_step", 1)
        shared_f.share_step(2)
        every(a0, "line_step", 2)
        self.small_step(4)
        shared_f.share_step(3)
        shared_f.whole_gather()
        every(a0, "line_end")
        held_a.gather()
        shared_a.share_step(0)
        slabs = [*a2, held_f, f3[1]]
        shared_a.share_step(1)
        shared_a.share_step(2)
        held_a.out_step(0)
        shared_a.share_step(3)
        shared_a.whole_gather()
        every(slabs, "out_step", 0)
        self.delivery.start(ALL[4:])
        every(slabs, "out_step", 1)
        held_a.out_step(1)
        every(slabs, "out_step", 2)
        held_a.out_step(2)
        every(slabs, "out_step", 3)
        held_a.out_step(3)
        shared_f.whole_end()
        shared_a.whole_end()
        self.delivery.finish()
        for unit in self.units:
            unit.finish()
        for copy in self.pending:
            copy.wait_send()


def feed_back_call(s, weights, act, slope, streams, g, nrm, par, carry, carried, collective):
    t = g.shape[0]
    hbm = pl.BlockSpec(memory_space=pl.ANY)
    vmem = pl.BlockSpec(memory_space=pltpu.VMEM)
    delivers = carry is None
    dma = pltpu.SemaphoreType.DMA
    half_i, half_o = grad_shape(s, 0), grad_shape(s, 1)
    results = [sds((2, 2, t, D), BF)] if delivers else carry.results()
    scratch = [
        pltpu.VMEM((2, HALF, FF), BF), pltpu.VMEM((FF, D), BF), pltpu.VMEM((t, FF), BF),
        pltpu.VMEM((t, FF), BF), pltpu.VMEM((t, D), BF),
        pltpu.VMEM(half_i, BF), pltpu.VMEM(half_o, BF), pltpu.VMEM(half_i, BF),
        pltpu.VMEM(half_o, BF), pltpu.VMEM(half_i, BF), pltpu.VMEM(half_o, BF),
        pltpu.VMEM((t, D), F32), pltpu.VMEM((D, t), BF),
        dma((CHUNKS, 5)), dma((CHUNKS, 2)), dma((CHUNKS, 2)), dma((3,)),
    ] + ([dma((4, 2)), dma((4, 2))] if delivers else carry.scratch())
    out = pl.pallas_call(
        partial(feed_back_kernel, s, carry),
        out_shape=[sds(half_i, BF), sds(half_o, BF)] + results
        + [sds((1, FF), F32), sds((8, D), F32), sds((t, D), BF)],
        in_specs=[hbm] * (7 + len(carried)) + [vmem] * 3,
        out_specs=[hbm] * (2 + len(results)) + [vmem] * 3,
        scratch_shapes=scratch,
        compiler_params=pltpu.CompilerParams(
            collective_id=collective, has_side_effects=True, vmem_limit_bytes=62 * 1024 * 1024
        ),
        name="feed_back_carry",
    )(*weights, act, slope, streams, *carried, g, nrm, par)
    return out[:2], out[2 : 2 + len(results)], out[2 + len(results) :]


def attention_back_kernel(s, carry, *refs):
    wim, wit, wom, wot = refs[:4]
    count = len(carry.all)
    carried = refs[4 : 4 + count]
    refs = refs[4 + count :]
    large, (g_ref, lse_ref, seg_row, seg_m, seg_t, pos, par) = refs[:7], refs[7:14]
    refs = refs[14:]
    if carry.last:
        streams, small_in, results, refs = refs[:3], refs[3], refs[4:10], refs[10:]
    else:
        d_first, d_second = refs[:2]
        results, refs = refs[2 : 2 + count], refs[2 + count :]
    dbin_ref, small_ref, out_ref = refs[:3]
    w_in, w_out, dmix, d_q, d_k, d_v, give_k, give_v, got_k, got_v = refs[3:13]
    own, their, core = refs[13:15], refs[15:17], refs[17:19]
    acc, dp, delta_ref, nrm_t = refs[19:23]
    load_sem, kv_s, kv_r, core_s, core_r, out_sem = refs[23:29]
    o_ref, qkv, kv_t, nrm, cosines, sines, h = refs[29:36]
    if carry.last:
        streams = {0: out_ref, **{i + 1: streams[i] for i in range(3)}}
        carry.load(carried, results, refs[36:], own, streams, small_in)
    else:
        carry.load(carried, results, refs[36:])
    if s:
        large = large[:6] + (large[6].at[s - 1],)
    _, g, _ = here()
    partner = {"group": 1 - g}
    tokens = g_ref.shape[0]

    def remote(src, dst, ssem, rsem):
        return pltpu.make_async_remote_copy(
            src_ref=src, dst_ref=dst, send_sem=ssem, recv_sem=rsem, device_id=partner,
            device_id_type=MESH,
        )

    pairs = [(wom, w_out.at[0]), (wot, w_out.at[1])]
    pairs += list(zip(large[:4], (o_ref, qkv, kv_t, nrm)))
    pairs += [(wim, w_in.at[0]), (wit, w_in.at[1])]
    pairs += list(zip(large[4:], (cosines, sines, h)))
    loads = [
        pltpu.make_async_copy(src, dst, load_sem.at[i]) for i, (src, dst) in enumerate(pairs)
    ]
    for copy in loads:
        copy.start()
    greet(True, True)
    carry.begin()

    for copy in loads[:3]:
        copy.wait()
    grad = g_ref[...]
    d_mix = jnp.concatenate([dot_nt(grad, w_out[0]), dot_nt(grad, w_out[1])], axis=1)
    dmix[...] = turn_halves(d_mix, g).astype(BF)
    o = o_ref[...].astype(F32)
    head = lax.broadcasted_iota(jnp.int32, (16, D), 0)
    lane = lax.broadcasted_iota(jnp.int32, (16, D), 1)
    delta_ref[...] = lax.dot_general(
        jnp.where(lane // HD == head, 1.0, 0.0), dmix[...].astype(F32) * o, NT,
        preferred_element_type=F32, precision=lax.Precision.HIGHEST,
    )
    turned = turn_halves(o, g).astype(BF)
    turned_t = jnp.transpose(turned)
    their[1][HALF:, :] = dot(turned_t[HALF:, :], grad).astype(BF)
    core_copies = [remote(their[1].at[HALF:, :], core[1].at[HALF:, :], core_s.at[3], core_r.at[3])]
    core_copies[0].start()
    own[1][HALF:, :] = dot(turned_t[:HALF, :], grad).astype(BF)

    lanes = lax.broadcasted_iota(jnp.int32, (tokens, 2 * HD), 1)

    def pair(j):
        def columns(first):
            return pl.ds(pl.multiple_of(first + j * 2 * HD, 2 * HD), 2 * HD)

        q = qkv[:, columns(0)]
        do = dmix[:, columns(0)]
        zero = jnp.zeros_like(q)
        sets = (
            (qkv[:, columns(D)], qkv[:, columns(2 * D)], seg_m),
            (kv_t[:, columns(0)], kv_t[:, columns(D)], seg_t),
        )
        total_q = [0.0, 0.0]
        keys_t = [jnp.transpose(sets[i][0]) for i in range(2)]
        total_k = [jnp.zeros((tokens, 2 * HD), F32)] * 2
        total_v = [jnp.zeros((tokens, 2 * HD), F32)] * 2
        for side in range(2):
            mine = (lanes >= HD) if side else (lanes < HD)
            q_head = jnp.where(mine, q, zero)
            do_head = jnp.where(mine, do, zero)
            lse = lse_ref[pl.ds(2 * j + side, 1), :]
            delta = delta_ref[pl.ds(2 * j + side, 1), :]
            for i, (k, v, seg) in enumerate(sets):
                p_t = jnp.where(
                    seg[...] == seg_row[...], jnp.exp(dot_nt(k, q_head) - lse), 0.0
                )
                d_s = (p_t * (dot_nt(v, do_head) - delta)).astype(BF)
                total_v[i] = total_v[i] + dot(p_t.astype(BF), do_head)
                total_k[i] = total_k[i] + dot(d_s, q_head)
                total_q[side] = total_q[side] + dot(keys_t[i][side * HD : (side + 1) * HD, :], d_s)
        d_q[:, columns(0)] = jnp.transpose(jnp.concatenate(total_q, axis=0))
        d_k[:, columns(0)] = total_k[0]
        d_v[:, columns(0)] = total_v[0]
        give_k[:, columns(0)] = total_k[1].astype(BF)
        give_v[:, columns(0)] = total_v[1].astype(BF)

    def exchanges(i):
        cols = pl.ds(i * 4 * HD, 4 * HD)
        return (
            remote(give_k.at[:, cols], got_k.at[:, cols], kv_s.at[0, i], kv_r.at[0, i]),
            remote(give_v.at[:, cols], got_v.at[:, cols], kv_s.at[1, i], kv_r.at[1, i]),
        )

    for copy in loads[3:6]:
        copy.wait()
    nrm_t[...] = jnp.transpose(nrm[...])
    for i in range(PAIRS // 2):
        loop(2, lambda j, i=i: pair(2 * i + j))
        for copy in exchanges(i):
            copy.start()
        carry.step(i + 1)

    for copy in loads[6:]:
        copy.wait()
    acc[...] = jnp.zeros_like(acc)
    small_ref[...] = jnp.zeros_like(small_ref)

    def turned_back(dy, y):
        swapped = swap_pairs(dy)
        d_angle = y * swapped - swap_pairs(y) * dy
        small_ref[3:4, :] += jnp.sum(d_angle * pos[:, 0:1], axis=0, keepdims=True)
        small_ref[4:5, :] += jnp.sum(d_angle * pos[:, 1:2], axis=0, keepdims=True)
        return dy * cosines[...] - swapped * sines[...]

    for j in range(3):
        cols = slice(j * D, (j + 1) * D)
        if j == 0:
            dp[...] = turned_back(
                d_q[...] * HD ** (-0.5), qkv[:, :D].astype(F32) * HD**0.5
            )
        elif j == 1:
            for i in range(PAIRS // 2):
                for copy in exchanges(i):
                    copy.wait()
            dp[...] = turned_back(d_k[...] + got_k[...].astype(F32), qkv[:, D : 2 * D].astype(F32))
        else:
            dp[...] = d_v[...] + got_v[...].astype(F32)
        d_p = dp[...].astype(BF)
        dbin_ref[:, cols] = jnp.sum(dp[...], axis=0, keepdims=True)
        if j < 2:
            place = (0, (slice(None), cols))
        else:
            place = (1, (slice(0, HALF), slice(None)))
        part, at = place
        their[part][at] = dot(nrm_t[HALF:, :], d_p).astype(BF)
        copy = remote(their[part].at[at], core[part].at[at], core_s.at[j], core_r.at[j])
        copy.start()
        core_copies.append(copy)
        own[part][at] = dot(nrm_t[:HALF, :], d_p).astype(BF)
        if j == 1:
            carry.late_step()
        acc[:, :HALF] += dot_nt(d_p, w_in[0, :, cols])
        acc[:, HALF:] += dot_nt(d_p, w_in[1, :, cols])
    grad = g_ref[...].astype(F32)
    d_normed = turn_halves(acc[...], g)
    out, d_gain, d_shift = norm_backward(h[...].astype(F32), par[0:1, :], grad, d_normed)
    out_ref[...] = out.astype(BF)
    small_ref[0:1, :] = jnp.sum(grad, axis=0, keepdims=True)
    small_ref[1:2, :] = d_gain
    small_ref[2:3, :] = d_shift

    for copy in core_copies:
        copy.wait()
    saves = []
    if carry.last:
        for part in range(2):
            accumulate(own[part], core[part], own[part].shape[0])
        carry.conclude(dbin_ref, small_ref)
        return
    for part, target in enumerate((d_first, d_second)):
        accumulate(own[part], core[part], own[part].shape[0])
        copy = pltpu.make_async_copy(own[part], target, out_sem.at[part])
        copy.start()
        saves.append(copy)
    carry.end()
    for copy in saves:
        copy.wait()


def attention_back_call(
    s, weights, carry, carried, g, saved, seg_row, seg_m, seg_t, turns, pos, h, par, collective,
    streams=(), small=None,
):
    t = g.shape[0]
    qkv, nrm, kv_t, o, lse = saved
    hbm = pl.BlockSpec(memory_space=pl.ANY)
    vmem = pl.BlockSpec(memory_space=pltpu.VMEM)
    dma = pltpu.SemaphoreType.DMA
    halves = [grad_shape(s, 0), grad_shape(s, 1)]
    rows, wide = pltpu.VMEM((t, D), BF), pltpu.VMEM((t, D), F32)
    if carry.last:
        carry.tokens = t
    results = carry.results()
    scratch = [
        pltpu.VMEM((2, HALF, QKV), BF), pltpu.VMEM((2, HALF, D), BF), rows, wide, wide, wide,
        rows, rows, rows, rows,
        *[pltpu.VMEM(x, BF) for x in halves * 3],
        wide, wide, pltpu.VMEM((16, t), F32), pltpu.VMEM((D, t), BF),
        dma((11,)), dma((2, 3)), dma((2, 3)), dma((4,)), dma((4,)), dma((2,)),
        rows, pltpu.VMEM((t, QKV), BF), pltpu.VMEM((t, 2 * D), BF), rows, wide, wide, rows,
    ] + carry.scratch()
    extra, extra_specs = (), []
    out_shape, out_specs = [sds(x, BF) for x in halves] + results, [hbm] * (2 + len(results))
    if carry.last:
        extra, extra_specs = (*streams, small), [hbm] * 3 + [vmem]
        out_shape, out_specs = results, [hbm] * 5 + [vmem]
    out = pl.pallas_call(
        partial(attention_back_kernel, s, carry),
        out_shape=out_shape
        + [sds((1, QKV), F32), sds((8, D), F32), sds((t, D), BF)],
        in_specs=[hbm] * (4 + len(carried) + 7) + [vmem] * 7 + extra_specs,
        out_specs=out_specs + [vmem] * 3,
        scratch_shapes=scratch,
        compiler_params=pltpu.CompilerParams(
            collective_id=collective, has_side_effects=True, vmem_limit_bytes=63 * 1024 * 1024
        ),
        name="attention_back_carry",
    )(*weights, *carried, o, qkv, kv_t, nrm, *turns, h, g, lse, seg_row, seg_m, seg_t, pos, par, *extra)
    if carry.last:
        return out[:6]
    return out[:2], out[2:-3], out[-3:]


def in_place(x):
    return x.reshape(-1, x.shape[-1])


CHUNKS = 6


START = (0, 0, 0, 0)
RING = 4
GROUP = (1, 1, 1, 1)
SPAN = 6
BESIDE = (None, None, None)


def chunk_of(ref, part, k):
    size = ref.shape[0 if part else 1] // CHUNKS
    at = pl.ds(pl.multiple_of(k * size, size), size)
    return ref.at[at, :] if part else ref.at[:, at]


def ring_place(chip):
    return 2 * (chip // 2) + (chip % 2 + chip // 2) % 2


def ring_chip(place):
    return 2 * (place // 2) + (place % 2 + place // 2) % 2


CLOCKWISE = ((True, False), (True, False), (False, True), (True, False))


def forward_kernel(*refs):
    w_in, w_out, h0, small, pos, seg_col, seg_m, seg_t = refs[:8]
    refs = refs[8:]
    keep = [refs[4 * s : 4 * s + 4] for s in range(4)]
    acts, slopes = refs[16:18], refs[18:20]
    results = refs[20:38]
    refs = refs[38:]
    work, refs = refs[:18], refs[18:]
    qkvs, kv_ts, os, lses = work[0:2], work[2:4], work[4:6], work[6:8]
    nrms, hs = work[8:12], [work[12].at[s] for s in range(4)]
    turns, pars = (work[13:15], work[15:17]), work[17]
    held = [refs[4 * s : 4 * s + 4] for s in range(4)]
    acc, stage_a, stage_s, lse_scr, smalls, b_in, b_out, freqs = refs[16:24]
    own_sem, ring_s, ring_r, z_s, z_r, core_s, core_r, kv_sem, save_sem, stage_sem = refs[24:34]
    small_s, small_r, result_sem = refs[34:]

    def kept(i):
        return pltpu.make_async_copy(work[i], results[i], result_sem.at[i])

    c = lax.axis_index("section")
    g = lax.axis_index("group")
    z = lax.axis_index("dp")
    parity = z % 2
    place = ring_place(c)
    ahead, behind = ring_chip((place + 1) % 4), ring_chip((place + 3) % 4)
    partner = {"group": 1 - g}
    tokens = h0.shape[0]

    def remote(src, dst, ssem, rsem, device):
        return pltpu.make_async_remote_copy(
            src_ref=src, dst_ref=dst, send_sem=ssem, recv_sem=rsem, device_id=device,
            device_id_type=MESH,
        )

    greet(True, True)

    def small_copies():
        slot = smalls.at[2 * c + g]
        out = []
        for bit in range(4):
            for core in range(2):
                if bit or core:
                    target = {"section": flip(c, bit) if bit else c, "group": (g + core) % 2}
                    out.append(remote(small, slot, small_s.at[2 * bit + core], small_r.at[2 * c + g], target))
        return out

    for copy in small_copies():
        copy.start()
    smalls[2 * c + g] = small[...]

    def mine(s, part):
        return held[s][2 * part]

    def theirs(s, part):
        return held[s][2 * part + 1]

    def distance(s, part):
        d = place - ring_place(s)
        return (d + 4) % 4 if CLOCKWISE[s][part] else (4 - d) % 4

    def own_copies(s):
        first = pltpu.make_async_copy(
            w_in.at[:, : QKV] if s % 2 == 0 else w_in, mine(s, 0), own_sem.at[0]
        )
        source = w_out.at[:HALF, :] if s % 2 == 0 else w_out
        second = pltpu.make_async_copy(source, mine(s, 1), own_sem.at[1])
        over = remote(w_out.at[HALF:D, :], mine(s, 1), own_sem.at[2], own_sem.at[3], partner)
        return first, second, over

    for s in range(4):

        @pl.when(c == s)
        def _(s=s):
            first, second, over = own_copies(s)
            first.start()
            if s % 2:
                second.start()
            else:

                @pl.when(g == 0)
                def _():
                    second.start()
                    over.start()

    for s in range(4):

        @pl.when(c == s)
        def _(s=s):
            first, second, over = own_copies(s)
            first.wait()
            if s % 2:
                second.wait()
            else:

                @pl.when(g == 0)
                def _():
                    second.wait()
                    over.wait_send()

                @pl.when(g == 1)
                def _():
                    over.wait_recv()

    def ring_copy(s, part, k):
        ref = chunk_of(mine(s, part), part, jnp.where(k < 2, 2 * parity + k, k + 2))
        target = ahead if CLOCKWISE[s][part] else behind
        u = 2 * s + part
        return remote(ref, ref, ring_s.at[u, k], ring_r.at[u, k], {"section": target})

    def z_copy(s, part, j, sending):
        ref = chunk_of(mine(s, part), part, 2 * (parity if sending else 1 - parity) + j)
        u = 2 * s + part
        return remote(ref, ref, z_s.at[u, j], z_r.at[u, j], {"dp": z + 1 - 2 * parity})

    def core_copy(s, part, k):
        u = 2 * s + part
        return remote(
            chunk_of(mine(s, part), part, k), chunk_of(theirs(s, part), part, k),
            core_s.at[u, k], core_r.at[u, k], partner,
        )

    def event(s, part, k):
        p = distance(s, part)
        copy = ring_copy(s, part, k)
        pl.when(p > 0)(copy.wait_recv)
        pl.when(p < 3)(copy.start)

        @pl.when((k < 2) & (p > 0))
        def _():
            z_copy(s, part, jnp.minimum(k, 1), True).start()

        core_copy(s, part, jnp.where(k < 2, 2 * parity + k, k + 2)).start()

        @pl.when(k >= 2)
        def _():
            j = jnp.maximum(k - 2, 0)
            pl.when(p > 0)(z_copy(s, part, j, False).wait_recv)
            core_copy(s, part, 2 * (1 - parity) + j).start()

    def slot(t, first, last):
        for s in range(4):
            if START[s] <= last and first <= START[s] + RING // GROUP[s] + 2:
                for part in range(2):
                    k = t - START[s] - distance(s, part)

                    @pl.when((k >= 0) & (k < RING // GROUP[s]))
                    def _(s=s, part=part, k=k):
                        k = jnp.clip(k, 0, RING // GROUP[s] - 1)
                        for i in range(GROUP[s]):
                            event(s, part, k * GROUP[s] + i)

    def slots(first, last):
        loop(last - first + 1, lambda i: slot(first + i, first, last))

    def arrived(s):
        def one(k):
            core_copy(s, 0, k).wait_recv()
            core_copy(s, 1, k).wait_recv()

        loop(CHUNKS, one)
        for i in range(4):
            pltpu.make_async_copy(held[s][i], keep[s][i], save_sem.at[4 * s + i]).start()

    def assemble():
        for i in range(8):
            slot = smalls.at[i]
            copy = remote(slot, slot, small_s.at[0], small_r.at[i], partner)
            pl.when(2 * c + g != i)(copy.wait_recv)
        for s in range(4):

            def both(first, width, s=s):
                at = slice(first, first + width)
                return jnp.concatenate([smalls[2 * s, :, at], smalls[2 * s + 1, :, at]], axis=1)

            half = FF // 2
            b_in[s] = both(0, half)
            b_out[s] = both(half, HALF)
            pars[s] = jnp.concatenate(
                [both(half + HALF, HALF), both(half + 2 * HALF, HALF), jnp.zeros((6, D), F32)], axis=0
            )
            if s % 2 == 0:
                freqs[s // 2] = jnp.concatenate(
                    [both(half + 3 * HALF, HALF), both(half + 4 * HALF, HALF)], axis=0
                )

    def turn_rows(i):
        rows = tokens // 2
        at = pl.ds(pl.multiple_of((i % 2) * rows, rows), rows)
        for layer in range(2):

            @pl.when(i // 2 == layer)
            def _(layer=layer):
                angles = (
                    pos[at, 0:1] * freqs[layer, 0:1, :] + pos[at, 1:2] * freqs[layer, 1:2, :]
                )
                lanes = lax.broadcasted_iota(jnp.int32, angles.shape, 1)
                sines = jnp.sin(angles)
                turns[layer][0][at, :] = jnp.cos(angles)
                turns[layer][1][at, :] = jnp.where((lanes % HD) < HD // 2, -sines, sines)

    def normed(s, h):
        xhat, _ = normalize(h[...].astype(F32))
        nrms[s][...] = turn_halves(
            xhat * pars[s, 0:1, :] + pars[s, 1:2, :], g
        ).astype(BF)

    def project(s, first, width):
        cols = pl.ds(first, width)
        return (
            dot(nrms[s][:, :HALF], mine(s, 0)[:, cols])
            + dot(nrms[s][:, HALF:], theirs(s, 0)[:, cols])
            + b_in[s, 0:1, cols]
        )

    def attention(s, h, out, beside):
        layer = s // 2
        qkv, kv_t, o_ref = qkvs[layer], kv_ts[layer], os[layer]
        cosines, sines = turns[layer]
        normed(s, h)
        exchange = []
        for j in (1, 2, 0):
            x = project(s, j * D, D)
            if j < 2:
                x = x * cosines[...] + swap_pairs(x) * sines[...]
            if j == 0:
                x = x * HD ** (-0.5)
            qkv[:, j * D : (j + 1) * D] = x.astype(BF)
            if j:
                copy = remote(
                    qkv.at[:, j * D : (j + 1) * D], kv_t.at[:, (j - 1) * D : j * D],
                    kv_sem.at[0, 2 * layer + j - 1], kv_sem.at[1, 2 * layer + j - 1], partner,
                )
                copy.start()
                exchange.append(copy)
        for copy in exchange:
            copy.wait()
        for i in (layer, 2 + layer, 8 + s):
            kept(i).start()
        lanes = lax.broadcasted_iota(jnp.int32, (tokens, 2 * HD), 1)

        def pair(j):
            if beside is not None:
                pl.when(beside[0] + j <= beside[1])(lambda: slot(beside[0] + j, *beside))

            def columns(ref, first):
                return ref[:, pl.ds(pl.multiple_of(first + j * 2 * HD, 2 * HD), 2 * HD)]

            q = columns(qkv, 0)
            km, vm = columns(qkv, D), columns(qkv, 2 * D)
            kt, vt = columns(kv_t, 0), columns(kv_t, D)
            same_m = seg_col[...] == seg_m[...]
            same_t = seg_col[...] == seg_t[...]
            found = []
            for side in range(2):
                head = (lanes >= HD) if side else (lanes < HD)
                q_head = jnp.where(head, q, jnp.zeros_like(q))
                s_m = jnp.where(same_m, dot_nt(q_head, km), -1e9)
                s_t = jnp.where(same_t, dot_nt(q_head, kt), -1e9)
                top = jnp.maximum(
                    jnp.max(s_m, axis=-1, keepdims=True), jnp.max(s_t, axis=-1, keepdims=True)
                )
                p_m = jnp.exp(s_m - top)
                p_t = jnp.exp(s_t - top)
                total = jnp.sum(p_m, axis=-1, keepdims=True) + jnp.sum(
                    p_t, axis=-1, keepdims=True
                )
                o = dot(p_m.astype(BF), vm) + dot(p_t.astype(BF), vt)
                found.append(o / total)
                lse_scr[...] = jnp.where(
                    lanes == 2 * j + side, top + jnp.log(total), lse_scr[...]
                )
            o_ref[:, pl.ds(pl.multiple_of(j * 2 * HD, 2 * HD), 2 * HD)] = jnp.where(
                lanes < HD, found[0], found[1]
            ).astype(BF)

        loop(PAIRS, pair)
        lses[layer][...] = jnp.transpose(lse_scr[...])[:16, :]
        turned = turn_halves(o_ref[...].astype(F32), g).astype(BF)
        y = dot(turned[:, :HALF], mine(s, 1)[...]) + dot(turned[:, HALF:], theirs(s, 1)[...])
        out[...] = (h[...].astype(F32) + y + b_out[s, 0:1, :]).astype(BF)
        for i in (4 + layer, 6 + layer):
            kept(i).start()

    def feed(s, h, out, beside):
        layer = s // 2
        width = FF // CHUNKS
        normed(s, h)
        kept(8 + s).start()
        acc[...] = h[...].astype(F32) + b_out[s, 0:1, :]

        def staged(j, i):
            turn = j % 2
            cols = pl.ds(pl.multiple_of(j * width, width), width)
            source, target = ((stage_a, acts[layer]), (stage_s, slopes[layer]))[i]
            return pltpu.make_async_copy(source.at[turn], target.at[:, cols], stage_sem.at[i, turn])

        def block(j):
            if beside is not None:
                pl.when(beside[0] + j <= beside[1])(lambda: slot(beside[0] + j, *beside))
            turn = j % 2

            @pl.when(j >= 2)
            def _():
                staged(j - 2, 0).wait()
                staged(j - 2, 1).wait()

            b = (j + g * (CHUNKS // 2)) % CHUNKS
            u = project(s, pl.multiple_of(b * width, width), width)
            cdf = 0.5 + 0.5 * lax.erf(u * (0.5**0.5))
            act = (u * cdf).astype(BF)
            stage_a[turn] = act
            pdf = jnp.exp(u * u * -0.5) * 0.3989422804014327
            stage_s[turn] = (cdf + u * pdf).astype(BF)
            staged(j, 0).start()
            staged(j, 1).start()
            for half in range(2):

                @pl.when(j // (CHUNKS // 2) == half)
                def _(half=half):
                    rows = pl.ds(pl.multiple_of((j % (CHUNKS // 2)) * width, width), width)
                    acc[...] += dot(act, held[s][2 + half][rows, :])

        loop(CHUNKS, block)
        for j in (CHUNKS - 2, CHUNKS - 1):
            staged(j, 0).wait()
            staged(j, 1).wait()
        out[...] = acc[...].astype(BF)

    slots(0, 0)
    assemble()

    def wait_and_turn(i):
        slot(1 + i, 1, SPAN)
        pl.when(i < 4)(lambda: turn_rows(i))

    loop(SPAN, wait_and_turn)
    for i in range(13, 18):
        kept(i).start()
    arrived(0)
    attention(0, h0, hs[0], BESIDE[0])
    arrived(1)
    feed(1, hs[0], hs[1], BESIDE[1])
    arrived(2)
    attention(2, hs[1], hs[2], BESIDE[2])
    arrived(3)
    feed(3, hs[2], hs[3], None)

    kept(12).start()

    for copy in small_copies():
        copy.wait_send()
    for i in range(18):
        kept(i).wait()
    for s in range(4):
        for part in range(2):
            p = distance(s, part)

            def sent_out(k, s=s, part=part, p=p):
                core_copy(s, part, k).wait_send()
                pl.when((k < 4) & (p < 3))(ring_copy(s, part, jnp.minimum(k, 3)).wait_send)
                pl.when((k < 2) & (p > 0))(z_copy(s, part, jnp.minimum(k, 1), True).wait_send)

            loop(CHUNKS, sent_out)
        for i in range(4):
            pltpu.make_async_copy(held[s][i], keep[s][i], save_sem.at[4 * s + i]).wait()


def forward_call(w_in, w_out, h, small, pos, seg_col, seg_m, seg_t):
    t = h.shape[0]
    hbm = pl.BlockSpec(memory_space=pl.ANY)
    vmem = pl.BlockSpec(memory_space=pltpu.VMEM)
    weights = []
    for s in range(4):
        (a, b), (d, e) = unit_shape(s, 0), unit_shape(s, 1)
        weights += [(a, b), (a, b), (d, e), (d, e)]
    rows = sds((t, D), BF)
    out_shape = (
        [sds(w, BF) for w in weights]
        + [sds((t, FF), BF)] * 4
        + [sds((t, QKV), BF)] * 2
        + [sds((t, 2 * D), BF)] * 2
        + [rows] * 2
        + [sds((16, t), F32)] * 2
        + [rows] * 4
        + [sds((4, t, D), BF)]
        + [sds((t, D), F32)] * 4
        + [sds((4, 8, D), F32)]
    )
    dma = pltpu.SemaphoreType.DMA
    scratch = [pltpu.VMEM(x.shape, x.dtype) for x in out_shape[20:]]
    scratch += [pltpu.VMEM(w, BF) for w in weights] + [
        pltpu.VMEM((t, D), F32),
        pltpu.VMEM((2, t, FF // CHUNKS), BF),
        pltpu.VMEM((2, t, FF // CHUNKS), BF),
        pltpu.VMEM((t, 2 * HD), F32),
        pltpu.VMEM((8,) + small.shape, F32),
        pltpu.VMEM((4, 1, FF), F32),
        pltpu.VMEM((4, 1, D), F32),
        pltpu.VMEM((2, 2, D), F32),
        dma((4,)), dma((8, 4)), dma((8, 4)), dma((8, 2)), dma((8, 2)), dma((8, 6)), dma((8, 6)),
        dma((2, 4)), dma((16,)), dma((2, 2)), dma((8,)), dma((8,)), dma((18,)),
    ]
    out = pl.pallas_call(
        forward_kernel,
        out_shape=out_shape,
        in_specs=[hbm, hbm] + [vmem] * 6,
        out_specs=[hbm] * 38,
        scratch_shapes=scratch,
        compiler_params=pltpu.CompilerParams(
            collective_id=2, has_side_effects=True, vmem_limit_bytes=63 * 1024 * 1024
        ),
        name="forward",
    )(w_in, w_out, h, small, pos, seg_col, seg_m, seg_t)
    weights = [out[4 * s : 4 * s + 4] for s in range(4)]
    acts, slopes, qkvs, kv_ts, os, lses = (out[16 + 2 * i : 18 + 2 * i] for i in range(6))
    nrms, hs = out[28:32], out[32]
    saved = []
    for s in range(4):
        i = s // 2
        if s % 2 == 0:
            saved.append((qkvs[i], nrms[s], kv_ts[i], os[i], lses[i]))
        else:
            saved.append((acts[i], slopes[i], nrms[s]))
    return weights, saved, hs, (out[33:35], out[35:37]), out[37]


def small_rows(dbin, rest):
    first = jnp.pad(dbin.reshape(-1), (0, FF - dbin.size)).reshape(4, D)
    return jnp.concatenate([first, rest[:5], jnp.zeros((SMALL[0] - 9, D), F32)])


def carried_passes(weight_in, weight_out, h, g, small, freq, pos, seg_m, seg_t):
    section, core = lax.axis_index("section"), lax.axis_index("group")
    wide = jnp.concatenate([freq.reshape(2, PAIRS, HD // 2)] * 2, axis=2).reshape(-1)
    small = jnp.concatenate([*small, wide]).astype(F32)[None]
    weights, saved, streams, turns, pars = forward_call(
        weight_in[0], weight_out[0], h, small, pos, seg_m[:, None], seg_m[None], seg_t[None]
    )
    smalls, grads, in_grads = [None] * 4, [None] * 4, [None] * 4
    rows = (seg_m[None], seg_m[:, None], seg_t[:, None])

    def feed_back(s, g, carry, carried):
        act, slope, nrm = saved[s]
        grads[s], results, (dbin, rest, in_grads[s]) = feed_back_call(
            s, weights[s], act, slope, streams, g, nrm, pars[s], carry, carried, 3 + s
        )
        smalls[s] = small_rows(dbin, rest)
        return results

    def attention_back(s, g, carry, carried):
        grads[s], results, (dbin, rest, in_grads[s]) = attention_back_call(
            s, weights[s], carry, carried, g, saved[s], *rows, turns[s // 2], pos,
            streams if s else h, pars[s], 3 + s,
        )
        smalls[s] = small_rows(dbin, rest)
        return results

    (outputs,) = feed_back(3, g, None, ())
    quarters3 = attention_back(2, in_grads[3], Carry(3, (), ()), grads[3])
    *quarters2, first3, second3 = feed_back(
        1, in_grads[2], Carry(2, ((3, 0), (3, 1)), ()), (*grads[2], *quarters3)
    )
    *sums, input_grads, small_sum = attention_back_call(
        0, weights[0], Finish(), (*grads[1], *quarters2, first3, second3), in_grads[1], saved[0],
        *rows, turns[0], pos, h, pars[0], 3, in_grads[1:], jnp.stack(smalls[1:]),
    )
    first_a, second_a, first_f, second_f = sums
    second_a = in_place(second_a)
    in_a = jnp.concatenate([in_place(first_a), second_a[:HALF]], axis=1)
    both = jnp.concatenate([second_a[HALF:], flipped(second_a[HALF:], "group", 1)], axis=0)
    both = jnp.where(core == 0, jnp.pad(both, ((0, FF // 2 - D), (0, 0))), jnp.zeros((), BF))
    attends = section % 2 == 0
    in_f = in_place(first_f)
    out_in = jnp.where(attends, jnp.pad(in_a, ((0, 0), (0, FF - QKV))), in_f).astype(F32)
    out_out = jnp.where(attends, both, in_place(second_f)).astype(F32)
    return outputs.reshape(-1, D), input_grads.reshape(-1, D), out_in, out_out, small_sum


def plain_passes(weight_in, weight_out, h, g, small, freq, pos, seg_m, seg_t):
    section, group = lax.axis_index("section"), lax.axis_index("group")
    groups = lax.axis_size("group")
    small = jnp.concatenate([*small, freq.reshape(-1)])
    small = lax.all_gather(small, ("section", "group")).reshape(4, groups, -1).astype(F32)
    widths = [FF // groups, D // groups, D // groups, D // groups, D // groups]
    starts = [sum(widths[:i]) for i in range(5)]
    b_in, b_out, gain, shift, freq = (
        small[:, :, a : a + w] for a, w in zip(starts, widths)
    )
    b_in, b_out, gain, shift = (x.reshape(4, 1, -1) for x in (b_in, b_out, gain, shift))
    freq = freq.reshape(4, groups, 2, -1).transpose(0, 2, 1, 3).reshape(4, 2, D // 2)
    pars = [
        jnp.concatenate([gain[s], shift[s], jnp.zeros((6, D), F32)], axis=0) for s in range(4)
    ]
    turns = [turning(freq[s], pos) for s in (0, 2)]

    core = group % 2
    rot = jnp.zeros((1,), jnp.int32)
    all_in = lax.all_gather(weight_in, "group", axis=1, tiled=True)
    all_out = lax.all_gather(weight_out, "group", axis=1, tiled=True)
    all_in = lax.all_gather(all_in, "section", axis=0, tiled=True)
    all_out = lax.all_gather(all_out, "section", axis=0, tiled=True)
    weights, saved, streams = [], [], [h]
    for s in range(4):
        cols, rows = (QKV, D) if s % 2 == 0 else (FF, FF)
        w_in, w_out = all_in[s, :, :cols], all_out[s, :rows]
        weights.append((w_in[:HALF], w_in[HALF:], w_out[: rows // 2], w_out[rows // 2 :]))
        wia, wib, woa, wob = weights[s]
        if s % 2 == 0:
            cosines, sines = turns[s // 2]
            qkv, nrm = qkv_call(rot, h, pars[s], wia, wib, b_in[s, :, :QKV], cosines, sines)
            kv_t = flipped(qkv[:, D:], "group", 1)
            o, lse, h = attend_call(
                rot, qkv, kv_t, seg_m[:, None], seg_m[None], seg_t[None], h, woa, wob, b_out[s]
            )
            saved.append((qkv, nrm, kv_t, o, lse))
        else:
            act, slope, nrm, h = ff_call(rot, h, pars[s], wia, wib, b_in[s], woa, wob, b_out[s])
            saved.append((act, slope, nrm))
        streams.append(h)
    outputs = to_owners(streams[1:], section, core)
    smalls, grads, in_grads = [None] * 4, [None] * 4, [None] * 4
    for s in (3, 2, 1, 0):
        wia, wib, woa, wob = weights[s]
        if s % 2 == 0:
            qkv, nrm, kv_t, o, lse = saved[s]
            cosines, sines = turns[s // 2]
            dmix, delta, doa, dob = mix_back_call(rot, g, o, woa, wob)
            dq, dkm, dvm, dkt, dvt = attend_back_call(
                qkv, kv_t, dmix, lse, delta, seg_m[None], seg_m[:, None], seg_t[:, None]
            )
            dkr, dvr = flipped(dkt, "group", 1), flipped(dvt, "group", 1)
            dia, dib, dbin, rest, g = qkv_back_call(
                rot, dq, dkm, dvm, dkr, dvr, qkv, cosines, sines, pos, nrm, wia, wib,
                streams[s], pars[s], g,
            )
        else:
            act, slope, nrm = saved[s]
            dia, dib, doa, dob, dbin, rest, g = ff_back_call(
                rot, g, act, slope, nrm, wia, wib, woa, wob, streams[s], pars[s]
            )
        in_grads[s] = g
        grads[s] = (
            jnp.pad(jnp.concatenate([dia, dib]), ((0, 0), (0, FF - dia.shape[1]))),
            jnp.pad(jnp.concatenate([doa, dob]), ((0, FF - 2 * doa.shape[0]), (0, 0))),
        )
        smalls[s] = small_rows(dbin, rest)
    input_grads = to_owners(in_grads, section, core)
    small_sum = lax.psum(jnp.stack(smalls), ("section", "group", "dp"))[section]

    def owned(x):
        x = lax.psum_scatter(x, "section", scatter_dimension=0, tiled=True)[0]
        x = lax.psum_scatter(x, "group", scatter_dimension=0, tiled=True)
        return lax.psum(x, "dp").astype(F32)

    out_in = owned(jnp.stack([x[0] for x in grads]))
    out_out = owned(jnp.stack([x[1] for x in grads]))
    return outputs, input_grads, out_in, out_out, small_sum


def body(
    activations, weight_in, weight_out, bias_in, bias_out, norm_gain, norm_shift, rope_freq,
    image_sides, cotangent,
):
    sections = lax.axis_size("section")
    groups = lax.axis_size("group")
    section = lax.axis_index("section")
    group = lax.axis_index("group")
    core = group % 2
    micro = image_sides.shape[0]
    capacity = activations.shape[0] // micro
    tokens = capacity // 2
    assert sections == 4 and groups % 2 == 0 and 2 * micro == sections
    fast = groups == 2 and lax.axis_size("dp") == 4

    here = (section // 2) == core
    local = section % 2

    def take(x):
        own = lax.dynamic_index_in_dim(x.reshape(micro, capacity, D), local, 0, keepdims=False)
        give = lax.dynamic_slice_in_dim(own, (1 - core) * tokens, tokens, 0)
        keep = lax.dynamic_slice_in_dim(own, core * tokens, tokens, 0)
        return jnp.where(here, keep, flipped(give, "group", 1))

    h = take(activations)
    own_sides = lax.dynamic_index_in_dim(image_sides, local, 0, keepdims=False)
    sides = jnp.where(here, own_sides, flipped(own_sides, "group", 1))
    segment, patch_row, patch_col, is_valid = layout(sides, capacity)
    pos_all = jnp.stack([patch_col, patch_row], axis=1).astype(F32)

    def half_of(x, which):
        return lax.dynamic_slice_in_dim(x, which * tokens, tokens, 0)

    pos = half_of(pos_all, core)
    seg_m, seg_t = half_of(segment, core), half_of(segment, 1 - core)
    valid = half_of(is_valid, core)
    g = take(cotangent) * valid[:, None].astype(BF)

    passes = carried_passes if fast else plain_passes
    outputs, input_grads, out_in, out_out, small_sum = passes(
        weight_in, weight_out, h, g, (bias_in[0], bias_out[0], norm_gain[0], norm_shift[0]),
        rope_freq[0], pos, seg_m, seg_t,
    )

    first_bias = small_sum[:4].reshape(-1)
    d_freq = small_sum[7:9].reshape(2, HEADS, HD)[:, :, : HD // 2].reshape(2, D // 2)

    def piece(x):
        w = x.shape[-1] // groups
        return lax.dynamic_slice_in_dim(x, group * w, w, x.ndim - 1)[None]

    return (
        outputs[None],
        input_grads[None],
        out_in[None],
        out_out[None],
        piece(first_bias),
        piece(small_sum[4]),
        piece(small_sum[5]),
        piece(small_sum[6]),
        piece(d_freq),
    )


def solution(mesh):
    placed = (
        P(("group", "dp"), None),
        P("section", "group", None),
        P("section", "group", None),
        P("section", "group"),
        P("section", "group"),
        P("section", "group"),
        P("section", "group"),
        P("section", None, "group"),
        P(("group", "dp"), None),
        P(("group", "dp"), None),
    )
    return jax.shard_map(
        body,
        mesh=mesh,
        in_specs=placed,
        out_specs=(
            P("section", ("group", "dp"), None),
            P("section", ("group", "dp"), None),
            P("section", "group", None),
            P("section", "group", None),
            P("section", "group"),
            P("section", "group"),
            P("section", "group"),
            P("section", "group"),
            P("section", None, "group"),
        ),
        check_vma=False,
    )
```

```python
from functools import partial

import jax
import jax.numpy as jnp
from jax import lax
from jax.experimental import pallas as pl
from jax.experimental.pallas import tpu as pltpu
from jax.sharding import PartitionSpec as P

D = 768
HEADS = 12
HD = 64
FF = 3072
HALF = D // 2
PAIRS = HEADS // 2
QKV = 3 * D
EPSILON = 1e-06
BF = jnp.bfloat16
F32 = jnp.float32
NT = (((1,), (1,)), ((), ()))
TN = (((0,), (0,)), ((), ()))
VMEM_BYTES = 52 * 1024 * 1024


def dot(a, b):
    return jnp.dot(a, b, preferred_element_type=F32)


def dot_nt(a, b):
    return lax.dot_general(a, b, NT, preferred_element_type=F32)


def dot_tn(a, b):
    return lax.dot_general(a, b, TN, preferred_element_type=F32)


def normalize(h):
    average = jnp.mean(h, axis=-1, keepdims=True)
    centered = h - average
    variance = jnp.mean(centered * centered, axis=-1, keepdims=True)
    scale = lax.rsqrt(variance + EPSILON)
    return centered * scale, scale


def turn_halves(x, rot):
    return jnp.where(rot == 0, x, jnp.concatenate([x[:, HALF:], x[:, :HALF]], axis=1))


def swap_pairs(x):
    lanes = lax.broadcasted_iota(jnp.int32, x.shape, 1)
    low = (lanes % HD) < HD // 2
    return jnp.where(
        low, pltpu.roll(x, x.shape[1] - HD // 2, 1), pltpu.roll(x, HD // 2, 1)
    )


def norm_backward(h, gain, grad, d_normed):
    xhat, scale = normalize(h)
    e = d_normed * gain
    mean_e = jnp.mean(e, axis=-1, keepdims=True)
    mean_ex = jnp.mean(e * xhat, axis=-1, keepdims=True)
    g = grad + scale * (e - mean_e - xhat * mean_ex)
    d_gain = jnp.sum(d_normed * xhat, axis=0, keepdims=True)
    d_shift = jnp.sum(d_normed, axis=0, keepdims=True)
    return g, d_gain, d_shift


def qkv_kernel(rot_ref, h_ref, par_ref, wa_ref, wb_ref, bias_ref, cos_ref, sin_ref, out_ref, nrm_ref):
    j = pl.program_id(0)

    @pl.when(j == 0)
    def _():
        xhat, _ = normalize(h_ref[...].astype(F32))
        normed = xhat * par_ref[0:1, :] + par_ref[1:2, :]
        nrm_ref[...] = turn_halves(normed, rot_ref[0]).astype(BF)

    x = dot(nrm_ref[:, :HALF], wa_ref[...]) + dot(nrm_ref[:, HALF:], wb_ref[...]) + bias_ref[...]

    @pl.when(j < 2)
    def _():
        y = x * cos_ref[...] + swap_pairs(x) * sin_ref[...]
        out_ref[...] = (y * jnp.where(j == 0, HD ** (-0.5), 1.0)).astype(BF)

    @pl.when(j == 2)
    def _():
        out_ref[...] = x.astype(BF)


def attend_kernel(
    rot_ref, q_ref, km_ref, vm_ref, kt_ref, vt_ref, segq_ref, segm_ref, segt_ref, h_ref,
    woa_ref, wob_ref, bias_ref, o_ref, lse_ref, out_ref, lse_scr,
):
    j = pl.program_id(0)
    rows = q_ref.shape[0]
    lanes = lax.broadcasted_iota(jnp.int32, (rows, 2 * HD), 1)
    q = q_ref[...]
    same_m = segq_ref[...] == segm_ref[...]
    same_t = segq_ref[...] == segt_ref[...]
    outs = []
    for side in range(2):
        mine = (lanes >= HD) if side else (lanes < HD)
        q_head = jnp.where(mine, q, jnp.zeros_like(q))
        s_m = jnp.where(same_m, dot_nt(q_head, km_ref[...]), -1e9)
        s_t = jnp.where(same_t, dot_nt(q_head, kt_ref[...]), -1e9)
        top = jnp.maximum(
            jnp.max(s_m, axis=-1, keepdims=True), jnp.max(s_t, axis=-1, keepdims=True)
        )
        p_m = jnp.exp(s_m - top)
        p_t = jnp.exp(s_t - top)
        total = jnp.sum(p_m, axis=-1, keepdims=True) + jnp.sum(p_t, axis=-1, keepdims=True)
        o = dot(p_m.astype(BF), vm_ref[...]) + dot(p_t.astype(BF), vt_ref[...])
        outs.append(o / total)
        lse_scr[...] = jnp.where(lanes == 2 * j + side, top + jnp.log(total), lse_scr[...])
    o_ref[:, pl.ds(pl.multiple_of(j * 2 * HD, 2 * HD), 2 * HD)] = jnp.where(
        lanes < HD, outs[0], outs[1]
    ).astype(BF)

    @pl.when(j == PAIRS - 1)
    def _():
        lse_ref[...] = jnp.transpose(lse_scr[...])[:16, :]
        o_all = turn_halves(o_ref[...].astype(F32), rot_ref[0]).astype(BF)
        y = dot(o_all[:, :HALF], woa_ref[...]) + dot(o_all[:, HALF:], wob_ref[...])
        out_ref[...] = (h_ref[...].astype(F32) + y + bias_ref[...]).astype(BF)


def ff_kernel(
    rot_ref, h_ref, par_ref, wia_ref, wib_ref, bias_ref, woa_ref, wob_ref, bout_ref,
    act_ref, slope_ref, nrm_ref, out_ref, acc_ref,
):
    j = pl.program_id(0)
    n = pl.num_programs(0)

    @pl.when(j == 0)
    def _():
        xhat, _ = normalize(h_ref[...].astype(F32))
        normed = xhat * par_ref[0:1, :] + par_ref[1:2, :]
        nrm_ref[...] = turn_halves(normed, rot_ref[0]).astype(BF)
        acc_ref[...] = h_ref[...].astype(F32) + bout_ref[...]

    u = dot(nrm_ref[:, :HALF], wia_ref[...]) + dot(nrm_ref[:, HALF:], wib_ref[...]) + bias_ref[...]
    cdf = 0.5 + 0.5 * lax.erf(u * (0.5**0.5))
    act = (u * cdf).astype(BF)
    act_ref[...] = act
    pdf = jnp.exp(u * u * -0.5) * 0.3989422804014327
    slope_ref[...] = (cdf + u * pdf).astype(BF)

    @pl.when(j < n // 2)
    def _():
        acc_ref[...] += dot(act, woa_ref[...])

    @pl.when(j >= n // 2)
    def _():
        acc_ref[...] += dot(act, wob_ref[...])

    @pl.when(j == n - 1)
    def _():
        out_ref[...] = acc_ref[...].astype(BF)


def ff_back_kernel(
    rot_ref, g_ref, act_ref, slope_ref, nrm_ref, wia_ref, wib_ref, woa_ref, wob_ref, h_ref, par_ref,
    dia_ref, dib_ref, doa_ref, dob_ref, dbin_ref, small_ref, out_ref, acc_ref,
):
    j = pl.program_id(0)
    n = pl.num_programs(0)

    @pl.when(j == 0)
    def _():
        acc_ref[...] = jnp.zeros_like(acc_ref)

    def step(wo_ref, do_ref):
        g = g_ref[...]
        d_up_f = dot_nt(g, wo_ref[...]) * slope_ref[...].astype(F32)
        d_up = d_up_f.astype(BF)
        do_ref[...] = dot_tn(act_ref[...], g).astype(BF)
        dbin_ref[...] = jnp.sum(d_up_f, axis=0, keepdims=True)
        dia_ref[...] = dot_tn(nrm_ref[:, :HALF], d_up).astype(BF)
        dib_ref[...] = dot_tn(nrm_ref[:, HALF:], d_up).astype(BF)
        acc_ref[:, :HALF] += dot_nt(d_up, wia_ref[...])
        acc_ref[:, HALF:] += dot_nt(d_up, wib_ref[...])

    @pl.when(j < n // 2)
    def _():
        step(woa_ref, doa_ref)

    @pl.when(j >= n // 2)
    def _():
        step(wob_ref, dob_ref)

    @pl.when(j == n - 1)
    def _():
        g = g_ref[...].astype(F32)
        d_normed = turn_halves(acc_ref[...], rot_ref[0])
        out, d_gain, d_shift = norm_backward(h_ref[...].astype(F32), par_ref[0:1, :], g, d_normed)
        out_ref[...] = out.astype(BF)
        small_ref[0:1, :] = jnp.sum(g, axis=0, keepdims=True)
        small_ref[1:2, :] = d_gain
        small_ref[2:3, :] = d_shift
        small_ref[3:8, :] = jnp.zeros((5, D), F32)


def mix_back_kernel(rot_ref, g_ref, o_ref, woa_ref, wob_ref, dmix_ref, delta_ref, doa_ref, dob_ref):
    g = g_ref[...]
    rot = rot_ref[0]
    d_mix = jnp.concatenate([dot_nt(g, woa_ref[...]), dot_nt(g, wob_ref[...])], axis=1)
    d_mix = turn_halves(d_mix, rot).astype(BF)
    dmix_ref[...] = d_mix
    o = o_ref[...].astype(F32)
    product = d_mix.astype(F32) * o
    head = lax.broadcasted_iota(jnp.int32, (16, D), 0)
    lanes = lax.broadcasted_iota(jnp.int32, (16, D), 1)
    chosen = jnp.where(lanes // HD == head, 1.0, 0.0)
    delta_ref[...] = lax.dot_general(
        chosen, product, NT, preferred_element_type=F32, precision=lax.Precision.HIGHEST
    )
    turned = turn_halves(o, rot).astype(BF)
    doa_ref[...] = dot_tn(turned[:, :HALF], g).astype(BF)
    dob_ref[...] = dot_tn(turned[:, HALF:], g).astype(BF)


def attend_back_kernel(
    q_ref, km_ref, vm_ref, kt_ref, vt_ref, do_ref, lse_ref, delta_ref, segq_ref, segm_ref, segt_ref,
    dq_ref, dkm_ref, dvm_ref, dkt_ref, dvt_ref,
):
    j = pl.program_id(0)
    rows = q_ref.shape[0]
    lanes = lax.broadcasted_iota(jnp.int32, (rows, 2 * HD), 1)
    q = q_ref[...]
    do = do_ref[...]
    zero = jnp.zeros_like(q)
    d_q = jnp.zeros((rows, 2 * HD), F32)
    sets = ((km_ref, vm_ref, segm_ref), (kt_ref, vt_ref, segt_ref))
    d_k = [0.0, 0.0]
    d_v = [0.0, 0.0]
    for side in range(2):
        mine = (lanes >= HD) if side else (lanes < HD)
        q_head = jnp.where(mine, q, zero)
        do_head = jnp.where(mine, do, zero)
        lse = lse_ref[pl.ds(2 * j + side, 1), :]
        delta = delta_ref[pl.ds(2 * j + side, 1), :]
        for i, (k_ref, v_ref, seg_ref) in enumerate(sets):
            k = k_ref[...]
            s_t = dot_nt(k, q_head)
            p_t = jnp.where(seg_ref[...] == segq_ref[...], jnp.exp(s_t - lse), 0.0)
            d_p = dot_nt(v_ref[...], do_head)
            d_s = (p_t * (d_p - delta)).astype(BF)
            d_v[i] += dot(p_t.astype(BF), do_head)
            d_k[i] += dot(d_s, q_head)
            d_q += dot_tn(d_s, jnp.where(mine, k, zero))
    dq_ref[...] = d_q
    dkm_ref[...] = d_k[0]
    dvm_ref[...] = d_v[0]
    dkt_ref[...] = d_k[1].astype(BF)
    dvt_ref[...] = d_v[1].astype(BF)


def qkv_back_kernel(
    rot_ref, dq_ref, dkm_ref, dvm_ref, dkr_ref, dvr_ref, qkv_ref, cos_ref, sin_ref, pos_ref,
    nrm_ref, wa_ref, wb_ref, h_ref, par_ref, g_ref,
    dia_ref, dib_ref, dbin_ref, small_ref, out_ref, acc_ref, dp_ref,
):
    j = pl.program_id(0)
    n = pl.num_programs(0)

    @pl.when(j == 0)
    def _():
        acc_ref[...] = jnp.zeros_like(acc_ref)
        small_ref[...] = jnp.zeros_like(small_ref)

    def turned_back(dy, y):
        swapped = swap_pairs(dy)
        d_angle = y * swapped - swap_pairs(y) * dy
        small_ref[3:4, :] += jnp.sum(d_angle * pos_ref[:, 0:1], axis=0, keepdims=True)
        small_ref[4:5, :] += jnp.sum(d_angle * pos_ref[:, 1:2], axis=0, keepdims=True)
        return dy * cos_ref[...] - swapped * sin_ref[...]

    @pl.when(j == 0)
    def _():
        d_y = dq_ref[...] * HD ** (-0.5)
        y = qkv_ref[...].astype(F32) * HD**0.5
        dp_ref[...] = turned_back(d_y, y)

    @pl.when(j == 1)
    def _():
        d_y = dkm_ref[...] + dkr_ref[...].astype(F32)
        dp_ref[...] = turned_back(d_y, qkv_ref[...].astype(F32))

    @pl.when(j == 2)
    def _():
        dp_ref[...] = dvm_ref[...] + dvr_ref[...].astype(F32)

    d_f = dp_ref[...]
    d_p = d_f.astype(BF)
    dbin_ref[...] = jnp.sum(d_f, axis=0, keepdims=True)
    dia_ref[...] = dot_tn(nrm_ref[:, :HALF], d_p).astype(BF)
    dib_ref[...] = dot_tn(nrm_ref[:, HALF:], d_p).astype(BF)
    acc_ref[:, :HALF] += dot_nt(d_p, wa_ref[...])
    acc_ref[:, HALF:] += dot_nt(d_p, wb_ref[...])

    @pl.when(j == n - 1)
    def _():
        g = g_ref[...].astype(F32)
        d_normed = turn_halves(acc_ref[...], rot_ref[0])
        out, d_gain, d_shift = norm_backward(h_ref[...].astype(F32), par_ref[0:1, :], g, d_normed)
        out_ref[...] = out.astype(BF)
        small_ref[0:1, :] = jnp.sum(g, axis=0, keepdims=True)
        small_ref[1:2, :] = d_gain
        small_ref[2:3, :] = d_shift


def params_of(n=1):
    return pltpu.CompilerParams(
        dimension_semantics=("arbitrary",) * n, vmem_limit_bytes=VMEM_BYTES
    )


def whole(shape):
    return pl.BlockSpec(shape, lambda *_: (0,) * len(shape))


def sds(shape, dtype):
    return jax.ShapeDtypeStruct(shape, dtype)


def cost(flops, nbytes, trans=0):
    return pl.CostEstimate(flops=flops, bytes_accessed=nbytes, transcendentals=trans)


def qkv_call(rot, h, par, wa, wb, bias, cosines, sines):
    t = h.shape[0]
    return pl.pallas_call(
        qkv_kernel,
        out_shape=(sds((t, QKV), BF), sds((t, D), BF)),
        grid_spec=pltpu.PrefetchScalarGridSpec(
            num_scalar_prefetch=1,
            grid=(3,),
            in_specs=[
                whole((t, D)), whole((8, D)),
                pl.BlockSpec((HALF, D), lambda j, r: (0, j)),
                pl.BlockSpec((HALF, D), lambda j, r: (0, j)),
                pl.BlockSpec((1, D), lambda j, r: (0, j)),
                whole((t, D)), whole((t, D)),
            ],
            out_specs=[pl.BlockSpec((t, D), lambda j, r: (0, j)), whole((t, D))],
        ),
        compiler_params=params_of(),
        cost_estimate=cost(2 * t * D * QKV, 2 * D * QKV + 8 * t * D + 2 * t * QKV),
        name="qkv",
    )(rot, h, par, wa, wb, bias, cosines, sines)


def attend_call(rot, qkv, kv_t, seg_col, seg_m, seg_t, h, woa, wob, bias):
    t = h.shape[0]
    w = 2 * HD
    return pl.pallas_call(
        attend_kernel,
        out_shape=(sds((t, D), BF), sds((16, t), F32), sds((t, D), BF)),
        grid_spec=pltpu.PrefetchScalarGridSpec(
            num_scalar_prefetch=1,
            grid=(PAIRS,),
            in_specs=[
                pl.BlockSpec((t, w), lambda j, r: (0, j)),
                pl.BlockSpec((t, w), lambda j, r: (0, j + PAIRS)),
                pl.BlockSpec((t, w), lambda j, r: (0, j + 2 * PAIRS)),
                pl.BlockSpec((t, w), lambda j, r: (0, j)),
                pl.BlockSpec((t, w), lambda j, r: (0, j + PAIRS)),
                whole((t, 1)), whole((1, t)), whole((1, t)), whole((t, D)),
                whole((HALF, D)), whole((HALF, D)), whole((1, D)),
            ],
            out_specs=[whole((t, D)), whole((16, t)), whole((t, D))],
            scratch_shapes=[pltpu.VMEM((t, w), F32)],
        ),
        compiler_params=params_of(),
        cost_estimate=cost(8 * t * t * D * 4, 16 * t * D, 2 * t * t * HEADS),
        name="attend",
    )(rot, qkv, qkv, qkv, kv_t, kv_t, seg_col, seg_m, seg_t, h, woa, wob, bias)


def ff_specs(t, blocks):
    width = FF // blocks
    half = blocks // 2
    w_in = pl.BlockSpec((HALF, width), lambda j, r: (0, (j + half * r[0]) % blocks))
    b_in = pl.BlockSpec((1, width), lambda j, r: (0, (j + half * r[0]) % blocks))
    w_a = pl.BlockSpec((width, D), lambda j, r: (jnp.minimum(j, half - 1), 0))
    w_b = pl.BlockSpec((width, D), lambda j, r: (jnp.maximum(j - half, 0), 0))
    hid = pl.BlockSpec((t, width), lambda j, r: (0, j))
    return w_in, b_in, w_a, w_b, hid


def ff_call(rot, h, par, wia, wib, bias, woa, wob, bout):
    t = h.shape[0]
    blocks = 6
    w_in, b_in, w_a, w_b, hid = ff_specs(t, blocks)
    return pl.pallas_call(
        ff_kernel,
        out_shape=(sds((t, FF), BF), sds((t, FF), BF), sds((t, D), BF), sds((t, D), BF)),
        grid_spec=pltpu.PrefetchScalarGridSpec(
            num_scalar_prefetch=1,
            grid=(blocks,),
            in_specs=[whole((t, D)), whole((8, D)), w_in, w_in, b_in, w_a, w_b, whole((1, D))],
            out_specs=[hid, hid, whole((t, D)), whole((t, D))],
            scratch_shapes=[pltpu.VMEM((t, D), F32)],
        ),
        compiler_params=params_of(),
        cost_estimate=cost(4 * t * D * FF, 4 * D * FF + 4 * t * FF, 2 * t * FF),
        name="feed",
    )(rot, h, par, wia, wib, bias, woa, wob, bout)


def ff_back_call(rot, g, act, slope, nrm, wia, wib, woa, wob, h, par):
    t = h.shape[0]
    blocks = 6
    w_in, b_in, w_a, w_b, hid = ff_specs(t, blocks)
    return pl.pallas_call(
        ff_back_kernel,
        out_shape=(
            sds((HALF, FF), BF), sds((HALF, FF), BF), sds((FF // 2, D), BF), sds((FF // 2, D), BF),
            sds((1, FF), F32), sds((8, D), F32), sds((t, D), BF),
        ),
        grid_spec=pltpu.PrefetchScalarGridSpec(
            num_scalar_prefetch=1,
            grid=(blocks,),
            in_specs=[
                whole((t, D)), hid, hid, whole((t, D)), w_in, w_in, w_a, w_b, whole((t, D)),
                whole((8, D)),
            ],
            out_specs=[w_in, w_in, w_a, w_b, b_in, whole((8, D)), whole((t, D))],
            scratch_shapes=[pltpu.VMEM((t, D), F32)],
        ),
        compiler_params=params_of(),
        cost_estimate=cost(8 * t * D * FF, 8 * D * FF + 4 * t * FF),
        name="feed_back",
    )(rot, g, act, slope, nrm, wia, wib, woa, wob, h, par)


def mix_back_call(rot, g, o, woa, wob):
    t = g.shape[0]
    return pl.pallas_call(
        mix_back_kernel,
        out_shape=(sds((t, D), BF), sds((16, t), F32), sds((HALF, D), BF), sds((HALF, D), BF)),
        grid_spec=pltpu.PrefetchScalarGridSpec(
            num_scalar_prefetch=1,
            grid=(1,),
            in_specs=[whole((t, D)), whole((t, D)), whole((HALF, D)), whole((HALF, D))],
            out_specs=[whole((t, D)), whole((16, t)), whole((HALF, D)), whole((HALF, D))],
        ),
        compiler_params=params_of(),
        cost_estimate=cost(4 * t * D * D, 4 * D * D + 6 * t * D),
        name="mix_back",
    )(rot, g, o, woa, wob)


def attend_back_call(qkv, kv_t, dmix, lse, delta, seg_row, seg_m, seg_t):
    t = dmix.shape[0]
    w = 2 * HD
    col = pl.BlockSpec((t, w), lambda j: (0, j))
    return pl.pallas_call(
        attend_back_kernel,
        out_shape=(sds((t, D), F32), sds((t, D), F32), sds((t, D), F32), sds((t, D), BF), sds((t, D), BF)),
        grid=(PAIRS,),
        in_specs=[
            col,
            pl.BlockSpec((t, w), lambda j: (0, j + PAIRS)),
            pl.BlockSpec((t, w), lambda j: (0, j + 2 * PAIRS)),
            col,
            pl.BlockSpec((t, w), lambda j: (0, j + PAIRS)),
            col, whole((16, t)), whole((16, t)), whole((1, t)), whole((t, 1)), whole((t, 1)),
        ],
        out_specs=[col] * 5,
        compiler_params=params_of(),
        cost_estimate=cost(20 * t * t * D * 4, 30 * t * D, 2 * t * t * HEADS),
        name="attend_back",
    )(qkv, qkv, qkv, kv_t, kv_t, dmix, lse, delta, seg_row, seg_m, seg_t)


def qkv_back_call(rot, dq, dkm, dvm, dkr, dvr, qkv, cosines, sines, pos, nrm, wa, wb, h, par, g):
    t = h.shape[0]
    w_in = pl.BlockSpec((HALF, D), lambda j, r: (0, j))
    rows = whole((t, D))
    return pl.pallas_call(
        qkv_back_kernel,
        out_shape=(
            sds((HALF, QKV), BF), sds((HALF, QKV), BF), sds((1, QKV), F32), sds((8, D), F32),
            sds((t, D), BF),
        ),
        grid_spec=pltpu.PrefetchScalarGridSpec(
            num_scalar_prefetch=1,
            grid=(3,),
            in_specs=[
                rows, rows, rows, rows, rows, pl.BlockSpec((t, D), lambda j, r: (0, j)), rows, rows,
                whole((t, 2)), rows, w_in, w_in, rows, whole((8, D)), rows,
            ],
            out_specs=[w_in, w_in, pl.BlockSpec((1, D), lambda j, r: (0, j)), whole((8, D)), rows],
            scratch_shapes=[pltpu.VMEM((t, D), F32), pltpu.VMEM((t, D), F32)],
        ),
        compiler_params=params_of(),
        cost_estimate=cost(4 * t * D * QKV, 4 * D * QKV + 30 * t * D),
        name="qkv_back",
    )(rot, dq, dkm, dvm, dkr, dvr, qkv, cosines, sines, pos, nrm, wa, wb, h, par, g)


def layout(image_sides, capacity):
    counts = image_sides * image_sides
    end_pos = jnp.cumsum(counts)
    start_pos = end_pos - counts
    positions = jnp.arange(capacity, dtype=jnp.int32)
    segment = jnp.sum((positions[:, None] >= end_pos[None, :]).astype(jnp.int32), axis=1)
    slot_ids = jnp.arange(image_sides.shape[-1], dtype=jnp.int32)
    one_hot = (segment[:, None] == slot_ids[None, :]).astype(jnp.int32)
    start_tok = jnp.sum(one_hot * start_pos[None, :], axis=1)
    side_len = jnp.maximum(jnp.sum(one_hot * image_sides[None, :], axis=1), 1)
    local_idx = positions - start_tok
    is_valid = segment < image_sides.shape[-1]
    patch_row = jnp.where(is_valid, local_idx // side_len, 0)
    patch_col = jnp.where(is_valid, local_idx % side_len, 0)
    return segment, patch_row, patch_col, is_valid


def turning(freq, pos):
    wide = jnp.concatenate([freq.reshape(2, HEADS, HD // 2)] * 2, axis=2).reshape(2, D)
    angles = pos[:, 0:1] * wide[0][None, :] + pos[:, 1:2] * wide[1][None, :]
    low = (jnp.arange(D) % HD) < HD // 2
    sines = jnp.sin(angles)
    return jnp.cos(angles), jnp.where(low[None, :], -sines, sines)


def flipped(x, axis, bit):
    return lax.ppermute(x, axis, [(i, i ^ bit) for i in range(lax.axis_size(axis))])


def to_owners(blocks, section, core):
    stacked = jnp.stack(blocks)
    got = [stacked[section]] + [flipped(stacked[section ^ d], "section", d) for d in (1, 2, 3)]
    here = (section // 2) == core
    near = jnp.stack(got[:2])
    away = jnp.stack(got[2:])
    mine = jnp.where(here, near, away)
    other = flipped(jnp.where(here, away, near), "group", 1)

    def in_order(pair):
        return jnp.where(section % 2 == 0, pair, pair[::-1])

    mine, other = in_order(mine), in_order(other)
    first = jnp.where(core == 0, mine, other)
    second = jnp.where(core == 0, other, mine)
    return jnp.concatenate([first, second], axis=1).reshape(-1, D)


MESH = pl.DeviceIdType.MESH
SMALL = (16, D)
SEMS = 20
LINE = 4


def unit_shape(s, part):
    if s % 2:
        return (FF // 2, D) if part else (HALF, FF)
    return (HALF, D) if part else (HALF, QKV)


def grad_shape(s, part):
    if s % 2:
        return (FF // 2, D) if part else (HALF, FF)
    return (D, D) if part else (HALF, 2 * D)


def piece_shape(s, part):
    r, w = grad_shape(s, part)
    return (r // 8, w // 2)


def held_shape(s, part):
    r, w = grad_shape(s, part)
    return (4, 2, r // 8, w)


def columns_of(k, width):
    return pl.ds(pl.multiple_of((k % 2) * width, width), width)


def flip(v, bit):
    if bit == 1:
        return v + 1 - 2 * (v % 2)
    if bit == 2:
        return (v + 2) % 4
    return 3 - v


def here():
    return lax.axis_index("section"), lax.axis_index("group"), lax.axis_index("dp")


def loop(n, body):
    def one(i, carried):
        body(i)
        return carried

    lax.fori_loop(0, n, one, 0)


def greet(plane, line):
    c, g, z = here()
    barrier = pltpu.get_barrier_semaphore()
    pl.semaphore_signal(barrier, inc=1, device_id={"group": 1 - g}, device_id_type=MESH)
    count = 1
    for bit in (1, 2, 3):
        if plane:
            for core in (g, 1 - g):
                pl.semaphore_signal(
                    barrier, inc=1, device_id={"section": flip(c, bit), "group": core},
                    device_id_type=MESH,
                )
                count += 1
        if line:
            pl.semaphore_signal(barrier, inc=1, device_id={"dp": flip(z, bit)}, device_id_type=MESH)
            count += 1
    pl.semaphore_wait(barrier, count)


def guarded(cond, act):
    if cond is None:
        act()
    else:
        pl.when(cond)(act)


def accumulate(into, term, rows):
    strip = 32 if rows % 32 == 0 else 16

    def one(i):
        at = pl.ds(pl.multiple_of(i * strip, strip), strip)
        into[at, :] = (into[at, :].astype(F32) + term[at, :].astype(F32)).astype(BF)

    loop(rows // strip, one)


class Unit:
    def __init__(
        self, s, part, send, recv, own=None, quarter=None, final=None, plane=None, line=None,
        held=None, whole=None,
    ):
        self.s, self.part, self.own, self.quarter_ref, self.final = s, part, own, quarter, final
        self.send, self.recv = send, recv
        self.whole = whole
        self.rows, self.cols = grad_shape(s, part)
        self.plane1, self.plane2 = plane or (None, None)
        self.up_in, self.down_in = line or (None, None)
        self.held = held
        self.pending = []

    def push(self, cond, src, dst, k, device):
        copy = pltpu.make_async_remote_copy(
            src_ref=src, dst_ref=dst, send_sem=self.send.at[k], recv_sem=self.recv.at[k],
            device_id=device, device_id_type=MESH,
        )
        guarded(cond, copy.start)
        self.pending.append((cond, copy))

    def landed(self, cond, dst, k):
        copy = pltpu.make_async_remote_copy(
            src_ref=dst, dst_ref=dst, send_sem=self.send.at[k], recv_sem=self.recv.at[k],
            device_id={"group": 1 - lax.axis_index("group")}, device_id_type=MESH,
        )
        guarded(cond, copy.wait_recv)

    def finish(self):
        for cond, copy in self.pending:
            guarded(cond, copy.wait_send)

    def quarter(self, q):
        rows = self.rows // 4
        return self.own.at[pl.ds(pl.multiple_of(q * rows, rows), rows), :]

    def mine(self):
        if self.quarter_ref is not None:
            return self.quarter_ref
        return self.quarter(lax.axis_index("section"))

    def piece(self, k):
        rows, cols = self.rows // 8, self.cols // 2
        return self.mine().at[
            pl.ds(pl.multiple_of((k // 2) * rows, rows), rows),
            pl.ds(pl.multiple_of((k % 2) * cols, cols), cols),
        ]

    def first_step(self):
        c, _, _ = here()
        x, y = c % 2, c // 2
        other = {"section": flip(c, 2 if self.part else 1)}
        bit = x if self.part else y
        for b in (1 - bit, bit):
            q = 2 * (1 - y) + b if self.part else 2 * b + 1 - x
            self.push(None, self.quarter(q), self.plane1.at[b], 1 + b, other)

    def second_step(self):
        c, _, _ = here()
        x, y = c % 2, c // 2
        b = (1 - x) if self.part else (1 - y)
        q = (2 * y + 1 - x) if self.part else (2 * (1 - y) + x)
        self.landed(None, self.plane1.at[b], 1 + b)
        accumulate(self.quarter(q), self.plane1.at[b], self.rows // 4)
        self.push(
            None, self.quarter(q), self.plane2, 3, {"section": flip(c, 1 if self.part else 2)}
        )

    def keep_step(self):
        c, _, _ = here()
        b = (c % 2) if self.part else (c // 2)
        self.landed(None, self.plane1.at[b], 1 + b)
        accumulate(self.mine(), self.plane1.at[b], self.rows // 4)

    def third_step(self):
        self.landed(None, self.plane2, 3)
        accumulate(self.mine(), self.plane2, self.rows // 4)

    def line_step(self, t):
        _, _, z = here()
        n = LINE
        rows = self.rows // 8
        up = (z < n - 1) & (z <= t)
        down = (z > 0) & (z >= n - 1 - t)
        k_up = jnp.minimum(n - 1 - t + z, n - 1)
        k_down = jnp.maximum(z - (n - 1) + t, 0)
        if t > 0:

            @pl.when(up & (z > 0))
            def _():
                self.landed(None, self.up_in.at[t - 1], 4 + t - 1)
                accumulate(self.piece(k_up), self.up_in.at[t - 1], rows)

            @pl.when(down & (z < n - 1))
            def _():
                self.landed(None, self.down_in.at[t - 1], 7 + t - 1)
                accumulate(self.piece(k_down), self.down_in.at[t - 1], rows)

        self.push(up, self.piece(k_up), self.up_in.at[t], 4 + t, {"dp": jnp.minimum(z + 1, n - 1)})
        self.push(down, self.piece(k_down), self.down_in.at[t], 7 + t, {"dp": jnp.maximum(z - 1, 0)})

    def line_end(self):
        _, _, z = here()
        n = LINE
        rows = self.rows // 8

        @pl.when(z > 0)
        def _():
            self.landed(None, self.up_in.at[n - 2], 4 + n - 2)
            accumulate(self.piece(z), self.up_in.at[n - 2], rows)

        @pl.when(z < n - 1)
        def _():
            self.landed(None, self.down_in.at[n - 2], 7 + n - 2)
            accumulate(self.piece(z), self.down_in.at[n - 2], rows)

    def held_at(self, k, q=None):
        cols = columns_of(k, self.cols // 2)
        return self.held.at[:, k // 2, :, cols] if q is None else self.held.at[q, k // 2, :, cols]

    def whole_at(self, k):
        return self.whole.at[k // 2, :, columns_of(k, self.cols // 2)]

    def last_piece(self):
        return self.final if self.final is not None else self.piece(here()[2])

    def own_piece(self):
        _, _, z = here()
        return pltpu.make_async_copy(
            self.last_piece(), self.held_at(z, self.s), self.send.at[10 + self.s]
        )

    def gather(self):
        c, _, z = here()
        for q in range(4):
            if q == self.s:
                pl.when(c == q)(self.own_piece().start)
            else:
                self.push(
                    c == q, self.last_piece(), self.held_at(z, q), 10 + q, {"section": self.s}
                )

    def share_step(self, t):
        _, _, z = here()
        n = LINE
        whole = self.whole_at
        if t == 0:
            copy = pltpu.make_async_copy(self.last_piece(), whole(z), self.send.at[0])
            copy.start()
            copy.wait()
        else:
            self.landed(z >= t, whole(jnp.maximum(z - t, 0)), 14 + t - 1)
            self.landed(z + t < n, whole(jnp.minimum(z + t, n - 1)), 17 + t - 1)
        if t < n - 1:
            low, high = jnp.maximum(z - t, 0), jnp.minimum(z + t, n - 1)
            self.push(
                (z >= t) & (z < n - 1), whole(low), whole(low), 14 + t,
                {"dp": jnp.minimum(z + 1, n - 1)},
            )
            self.push(
                (z + t < n) & (z > 0), whole(high), whole(high), 17 + t,
                {"dp": jnp.maximum(z - 1, 0)},
            )

    def whole_copy(self):
        return pltpu.make_async_copy(self.whole, self.held.at[self.s], self.send.at[10 + self.s])

    def whole_gather(self):
        c, _, _ = here()
        for q in range(4):
            if q == self.s:
                pl.when(c == q)(self.whole_copy().start)
            else:
                self.push(c == q, self.whole, self.held.at[q], 10 + q, {"section": self.s})

    def whole_end(self):
        c, _, _ = here()
        for q in range(4):
            if q == self.s:
                pl.when(c == q)(self.whole_copy().wait)
            else:
                self.landed(c == self.s, self.held.at[q], 10 + q)

    def out_step(self, t):
        c, _, z = here()
        n = LINE
        mine = c == self.s
        held = self.held_at
        if t == 0:
            for q in range(4):
                if q == self.s:
                    pl.when(mine)(self.own_piece().wait)
                else:
                    self.landed(mine, held(z, q), 10 + q)
        else:
            self.landed(mine & (z >= t), held(jnp.maximum(z - t, 0)), 14 + t - 1)
            self.landed(mine & (z + t < n), held(jnp.minimum(z + t, n - 1)), 17 + t - 1)
        if t < n - 1:
            low, high = jnp.maximum(z - t, 0), jnp.minimum(z + t, n - 1)
            self.push(
                mine & (z >= t) & (z < n - 1), held(low), held(low), 14 + t,
                {"dp": jnp.minimum(z + 1, n - 1)},
            )
            self.push(
                mine & (z + t < n) & (z > 0), held(high), held(high), 17 + t,
                {"dp": jnp.maximum(z - 1, 0)},
            )


class Delivery:
    def __init__(self, sources, parts, out, send, recv):
        self.sources, self.parts, self.out, self.send, self.recv = sources, parts, out, send, recv

    def rows(self, block):
        size = self.sources[self.parts[0][0]].shape[0] // 2
        return pl.ds(block * size, size)

    def copies(self, s, block):
        c, g, _ = here()
        slot = self.out.at[c % 2, g, self.rows(block), :]
        source = self.sources[s].at[self.rows(block), :]
        near = pltpu.make_async_copy(source, slot, self.send.at[s, block])
        far = pltpu.make_async_remote_copy(
            src_ref=source, dst_ref=slot, send_sem=self.send.at[s, block],
            recv_sem=self.recv.at[(c % 2) * 2 + g, block],
            device_id={"section": s, "group": c // 2}, device_id_type=MESH,
        )
        return near, far, (c == s) & (g == c // 2)

    def start(self, parts):
        for part in parts:
            near, far, stays = self.copies(*part)
            pl.when(stays)(near.start)
            pl.when(jnp.logical_not(stays))(far.start)

    def finish(self):
        c, g, _ = here()
        for s, block in self.parts:
            near, far, stays = self.copies(s, block)
            pl.when(stays)(near.wait)
            pl.when(jnp.logical_not(stays))(far.wait_send)
            for m in range(2):
                for half in range(2):
                    slot = self.out.at[m, half, self.rows(block), :]
                    copy = pltpu.make_async_remote_copy(
                        src_ref=slot, dst_ref=slot, send_sem=self.send.at[0, 0],
                        recv_sem=self.recv.at[2 * m + half, block], device_id={"group": 1 - g},
                        device_id_type=MESH,
                    )
                    arrives = (c == s) & jnp.logical_not((2 * g + m == c) & (g == half))
                    pl.when(arrives)(copy.wait_recv)


ALL = tuple((s, block) for block in range(2) for s in range(4))


def feed_back_kernel(s, carry, *refs):
    delivers = carry is None
    wim, wit, wom, wot, act_in, slope_in, streams = refs[:7]
    refs = refs[7:]
    count = 0 if delivers else len(carry.all)
    carried, refs = refs[:count], refs[count:]
    g_ref, nrm, par = refs[:3]
    d_in, d_out = refs[3:5]
    refs = refs[5:]
    if delivers:
        delivered, refs = refs[0], refs[1:]
    results, refs = refs[:count], refs[count:]
    dbin_ref, small_ref, out_ref = refs[:3]
    w_in, w_out, act, slope, h, own_i, own_o, their_i, their_o, core_i, core_o, acc, nrm_t = refs[3:16]
    load_sem, core_s, core_r, out_sem = refs[16:20]
    refs = refs[20:]
    _, g, _ = here()
    partner = {"group": 1 - g}
    width = FF // CHUNKS
    third = CHUNKS // 2

    def column(j):
        b = (j + g * third) % CHUNKS
        return pl.ds(pl.multiple_of(b * width, width), width)

    def line_of(j):
        return pl.ds(pl.multiple_of(j * width, width), width)

    def loads(j):
        cols, rows = column(j), line_of(j % third)
        first = j < third
        return (
            (None, pltpu.make_async_copy(wim.at[:, cols], w_in.at[0, :, cols], load_sem.at[j, 0])),
            (None, pltpu.make_async_copy(wit.at[:, cols], w_in.at[1, :, cols], load_sem.at[j, 1])),
            (first, pltpu.make_async_copy(wom.at[rows, :], w_out.at[line_of(j), :], load_sem.at[j, 2])),
            (
                jnp.logical_not(first),
                pltpu.make_async_copy(wot.at[rows, :], w_out.at[line_of(j), :], load_sem.at[j, 2]),
            ),
            (None, pltpu.make_async_copy(act_in.at[:, line_of(j)], act.at[:, line_of(j)], load_sem.at[j, 3])),
            (None, pltpu.make_async_copy(slope_in.at[:, line_of(j)], slope.at[:, line_of(j)], load_sem.at[j, 4])),
        )

    def load(j):
        for cond, copy in loads(j):
            guarded(cond, copy.start)

    def core_copies(j):
        cols, rows = column(j), line_of(j % third)
        return (
            pltpu.make_async_remote_copy(
                src_ref=their_i.at[:, cols], dst_ref=core_i.at[:, cols], send_sem=core_s.at[j, 0],
                recv_sem=core_r.at[j, 0], device_id=partner, device_id_type=MESH,
            ),
            pltpu.make_async_remote_copy(
                src_ref=their_o.at[rows, :], dst_ref=core_o.at[rows, :], send_sem=core_s.at[j, 1],
                recv_sem=core_r.at[j, 1], device_id=partner, device_id_type=MESH,
            ),
        )

    loop(CHUNKS, load)
    stream_copy = pltpu.make_async_copy(streams.at[s - 1], h, out_sem.at[2])
    stream_copy.start()
    if not delivers:
        carry.load(carried, results, refs)
    greet(True, not delivers)
    if delivers:
        delivery = Delivery([streams.at[i] for i in range(4)], ALL, delivered, *refs)
        delivery.start(ALL)
    else:
        carry.begin()
    acc[...] = jnp.zeros_like(acc)
    nrm_t[...] = jnp.transpose(nrm[...])

    def block(j):
        for cond, copy in loads(j):
            guarded(cond, copy.wait)
        cols, rows = column(j), line_of(j)
        grad = g_ref[...]
        d_up_f = dot_nt(grad, w_out[rows, :]) * slope[:, rows].astype(F32)
        d_up = d_up_f.astype(BF)
        d_o = dot_tn(act[:, rows], grad).astype(BF)
        dbin_ref[:, cols] = jnp.sum(d_up_f, axis=0, keepdims=True)
        their_i[:, cols] = dot(nrm_t[HALF:, :], d_up).astype(BF)
        inward, outward = core_copies(j)
        inward.start()

        @pl.when(j >= third)
        def _():
            their_o[line_of(j % third), :] = d_o
            outward.start()

        @pl.when(j < third)
        def _():
            own_o[line_of(j % third), :] = d_o

        own_i[:, cols] = dot(nrm_t[:HALF, :], d_up).astype(BF)
        acc[:, :HALF] += dot_nt(d_up, w_in[0, :, cols])
        acc[:, HALF:] += dot_nt(d_up, w_in[1, :, cols])

    if delivers:
        loop(CHUNKS, block)
    else:
        for i in range(3):
            loop(CHUNKS // 3, lambda j, i=i: block(j + CHUNKS // 3 * i))
            carry.step(i + 1)
    stream_copy.wait()
    grad = g_ref[...].astype(F32)
    d_normed = turn_halves(acc[...], g)
    out, d_gain, d_shift = norm_backward(h[...].astype(F32), par[0:1, :], grad, d_normed)
    out_ref[...] = out.astype(BF)
    small_ref[0:1, :] = jnp.sum(grad, axis=0, keepdims=True)
    small_ref[1:2, :] = d_gain
    small_ref[2:3, :] = d_shift
    small_ref[3:8, :] = jnp.zeros((5, D), F32)

    def ended(j):
        inward, outward = core_copies(j)
        inward.wait()
        pl.when(j >= third)(outward.wait)

    loop(CHUNKS, ended)
    accumulate(own_i, core_i, HALF)
    saves = [pltpu.make_async_copy(own_i, d_in, out_sem.at[0])]
    saves[0].start()
    accumulate(own_o, core_o, FF // 2)
    saves.append(pltpu.make_async_copy(own_o, d_out, out_sem.at[1]))
    saves[1].start()
    if delivers:
        delivery.finish()
    else:
        carry.end()
    for copy in saves:
        copy.wait()


def every(units, act, *args):
    for unit in units:
        getattr(unit, act)(*args)


class Carry:
    last = False

    def __init__(self, plane, line, hold):
        self.planes = [(plane, 0), (plane, 1)]
        self.line, self.hold = line, hold
        self.all = self.planes + list(line) + list(hold)

    def results(self):
        out = []
        for u in self.planes:
            r, w = grad_shape(*u)
            out.append(sds((r // 4, w), BF))
        out += [sds(piece_shape(*u), BF) for u in self.line]
        return out + [sds(held_shape(*u), BF) for u in self.hold]

    def scratch(self):
        out = []
        for u in self.planes:
            r, w = grad_shape(*u)
            out += [pltpu.VMEM((r, w), BF), pltpu.VMEM((2, r // 4, w), BF), pltpu.VMEM((r // 4, w), BF)]
        for u in self.line:
            r, w = grad_shape(*u)
            out += [pltpu.VMEM((r // 4, w), BF)] + [pltpu.VMEM((3,) + piece_shape(*u), BF)] * 2
        out += [pltpu.VMEM(piece_shape(*u), BF) for u in self.hold]
        dma = pltpu.SemaphoreType.DMA
        return out + [dma((len(self.all), SEMS)), dma((len(self.all), SEMS))]

    def load(self, sources, results, refs):
        send, recv = refs[-2:]
        refs = list(refs[:-2])
        self.units, self.loads, self.targets = [], [], results
        for i, u in enumerate(self.all):
            sems = (send.at[i], recv.at[i])
            if i < 2:
                own, first, second = refs.pop(0), refs.pop(0), refs.pop(0)
                unit = Unit(*u, *sems, own=own, plane=(first, second))
            elif i < 2 + len(self.line):
                own, up, down = refs.pop(0), refs.pop(0), refs.pop(0)
                unit = Unit(*u, *sems, quarter=own, line=(up, down))
            else:
                own = refs.pop(0)
                unit = Unit(*u, *sems, final=own, held=results[i])
            copy = pltpu.make_async_copy(sources[i], own, sems[0].at[0])
            copy.start()
            self.units.append(unit)
            self.loads.append(copy)
        n = 2 + len(self.line)
        self.plane_units, self.line_units, self.hold_units = (
            self.units[:2], self.units[2:n], self.units[n:],
        )

    def begin(self):
        for copy in self.loads:
            copy.wait()
        for unit in self.hold_units:
            unit.gather()
        for unit in self.line_units:
            unit.line_step(0)
        for unit in self.plane_units:
            unit.first_step()

    def step(self, i):
        for unit in self.line_units:
            if i < LINE - 1:
                unit.line_step(i)
            else:
                unit.line_end()
        if i > 1:
            every(self.plane_units, "second_step" if i == 2 else "keep_step")
        for unit in self.hold_units:
            if i < 3:
                unit.out_step(i - 1)

    def late_step(self):
        for unit in self.hold_units:
            unit.out_step(LINE - 2)

    def end(self):
        saves = [
            pltpu.make_async_copy(unit.last_piece(), target, unit.send.at[0])
            for unit, target in zip(self.line_units, self.targets[2:])
        ]
        for copy in saves:
            copy.start()
        for unit, target in zip(self.plane_units, self.targets):
            unit.third_step()
            copy = pltpu.make_async_copy(unit.mine(), target, unit.send.at[0])
            copy.start()
            saves.append(copy)
        for unit in self.hold_units:
            unit.out_step(LINE - 1)
        for copy in saves:
            copy.wait()
        for unit in self.units:
            unit.finish()


class Finish:
    all = ((1, 0), (1, 1), (2, 0), (2, 1), (3, 0), (3, 1))
    own_units = ((0, 0), (0, 1))
    last = True

    def results(self):
        held = [sds(held_shape(s, part), BF) for s in (0, 1) for part in (0, 1)]
        return held + [sds((2, 2, self.tokens, D), BF), sds(SMALL, F32)]

    def scratch(self):
        out = []
        for u in self.all[:2]:
            r, w = grad_shape(*u)
            out += [pltpu.VMEM((r, w), BF), pltpu.VMEM((2, r // 4, w), BF), pltpu.VMEM((r // 4, w), BF)]
        for u in self.all[2:4]:
            r, w = grad_shape(*u)
            out.append(pltpu.VMEM((r // 4, w), BF))
        out += [pltpu.VMEM(piece_shape(*u), BF) for u in self.all[4:]]
        for u in self.own_units:
            r, w = grad_shape(*u)
            out += [pltpu.VMEM((2, r // 4, w), BF), pltpu.VMEM((r // 4, w), BF)]
        for u in self.all[:4] + self.own_units:
            out += [pltpu.VMEM((3,) + piece_shape(*u), BF)] * 2
        out += [pltpu.VMEM(held_shape(*u)[1:], BF) for u in ((1, 1), (0, 1))]
        dma = pltpu.SemaphoreType.DMA
        small = [pltpu.VMEM((n,) + SMALL, F32) for n in (4, 4, 4, 2, 3, 4)]
        return out + small + [
            dma((8, SEMS)), dma((8, SEMS)), dma((7,)), dma((7,)), dma((4, 2)), dma((4, 2)),
        ]

    def load(self, sources, results, refs, own, streams, small_in):
        refs = list(refs)

        def take(n):
            out = refs[:n]
            del refs[:n]
            return out

        halves = [take(3), take(3)]
        quarters, finals = take(2), take(2)
        planes = [take(2), take(2)]
        lines = [take(2) for _ in range(6)]
        wholes = take(2)
        self.sm, self.sm_core, self.sm_x, self.sm_got, self.sm_y, self.sm_z = take(6)
        send, recv, self.sm_send, self.sm_recv, del_send, del_recv = refs
        held, delivered, self.small_out = results[:4], results[4], results[5]
        self.small_in = small_in

        def unit(i, u, **more):
            return Unit(*u, send.at[i], recv.at[i], held=held[2 * (u[0] % 2) + u[1]], **more)

        self.f1 = [
            unit(i, self.all[i], own=halves[i][0], plane=halves[i][1:], line=lines[i],
                 whole=wholes[0] if i else None)
            for i in range(2)
        ]
        self.a2 = [unit(2 + i, self.all[2 + i], quarter=quarters[i], line=lines[2 + i]) for i in range(2)]
        self.f3 = [unit(4 + i, self.all[4 + i], final=finals[i]) for i in range(2)]
        self.a0 = [
            unit(6 + i, self.own_units[i], own=own[i], plane=planes[i], line=lines[4 + i],
                 whole=wholes[1] if i else None)
            for i in range(2)
        ]
        self.units = self.f1 + self.a2 + self.f3 + self.a0
        self.delivery = Delivery(streams, ALL, delivered, del_send, del_recv)
        self.loads = [
            pltpu.make_async_copy(source, target, send.at[i, 0])
            for i, (source, target) in enumerate(
                zip(sources, [halves[0][0], halves[1][0], *quarters, *finals])
            )
        ]
        for copy in self.loads:
            copy.start()
        self.pending = []

    def begin(self):
        for copy in self.loads:
            copy.wait()
        every(self.f3, "gather")
        every(self.a2, "line_step", 0)
        every(self.f1, "first_step")

    def step(self, i):
        if i > 1:
            every(self.f1, "second_step" if i == 2 else "keep_step")
        if i < 3:
            every(self.a2, "line_step", i)
            self.f3[0].out_step(i - 1)
        else:
            every(self.a2, "line_end")
            every(self.a2, "gather")

    def late_step(self):
        pass

    def small_push(self, src, dst, k, device):
        copy = pltpu.make_async_remote_copy(
            src_ref=src, dst_ref=dst, send_sem=self.sm_send.at[k], recv_sem=self.sm_recv.at[k],
            device_id=device, device_id_type=MESH,
        )
        copy.start()
        self.pending.append(copy)

    def small_landed(self, dst, k):
        pltpu.make_async_remote_copy(
            src_ref=dst, dst_ref=dst, send_sem=self.sm_send.at[k], recv_sem=self.sm_recv.at[k],
            device_id={"group": 1 - lax.axis_index("group")}, device_id_type=MESH,
        ).wait_recv()

    def small_step(self, k):
        c, g, z = here()
        x, y = c % 2, c // 2
        if k == 0:
            self.small_push(self.sm, self.sm_core, 0, {"group": 1 - g})
        elif k == 1:
            self.small_landed(self.sm_core, 0)
            self.sm_x[...] = self.sm[...] + self.sm_core[...]
            for b in range(2):
                self.small_push(
                    self.sm_x.at[2 * b + 1 - x], self.sm_got.at[b], 1 + b, {"section": flip(c, 1)}
                )
        elif k == 2:
            for b in range(2):
                self.small_landed(self.sm_got.at[b], 1 + b)
                self.sm_y[b] = self.sm_x[2 * b + x] + self.sm_got[b]
            self.small_push(self.sm_y.at[1 - y], self.sm_y.at[2], 3, {"section": flip(c, 2)})
        elif k == 3:
            self.small_landed(self.sm_y.at[2], 3)
            self.sm_z[z] = self.sm_y[y] + self.sm_y[2]
            for bit in (1, 2, 3):
                self.small_push(self.sm_z.at[z], self.sm_z.at[z], 3 + bit, {"dp": flip(z, bit)})
        else:
            for bit in (1, 2, 3):
                self.small_landed(self.sm_z.at[flip(z, bit)], 3 + bit)
            self.small_out[...] = self.sm_z[0] + self.sm_z[1] + self.sm_z[2] + self.sm_z[3]

    def conclude(self, dbin, rest):
        f1, a2, f3, a0 = self.f1, self.a2, self.f3, self.a0
        (held_a, shared_a), (held_f, shared_f) = a0, f1
        every(a0, "first_step")
        every(f1, "third_step")
        every(f1, "line_step", 0)
        f3[0].out_step(2)
        self.sm[...] = jnp.zeros_like(self.sm)
        pairs = (dbin, rest, *self.small_in)
        for s in range(4):
            first, others = pairs[2 * s : 2 * s + 2]
            for i in range(first.shape[1] // D):
                self.sm[s, i : i + 1, :] = first[:, i * D : (i + 1) * D]
            self.sm[s, 4:9, :] = others[0:5, :]
        self.small_step(0)
        every(a0, "second_step")
        every(f1, "line_step", 1)
        self.small_step(1)
        every(a0, "keep_step")
        every(f1, "line_step", 2)
        self.small_step(2)
        every(f1, "line_end")
        held_f.gather()
        shared_f.share_step(0)
        f3[0].out_step(3)
        every(a0, "third_step")
        every(a0, "line_step", 0)
        self.small_step(3)
        self.delivery.start(ALL[:4])
        shared_f.share_step(1)
        every(a0, "line_step", 1)
        shared_f.share_step(2)
        every(a0, "line_step", 2)
        self.small_step(4)
        shared_f.share_step(3)
        shared_f.whole_gather()
        every(a0, "line_end")
        held_a.gather()
        shared_a.share_step(0)
        slabs = [*a2, held_f, f3[1]]
        shared_a.share_step(1)
        shared_a.share_step(2)
        held_a.out_step(0)
        shared_a.share_step(3)
        shared_a.whole_gather()
        every(slabs, "out_step", 0)
        self.delivery.start(ALL[4:])
        every(slabs, "out_step", 1)
        held_a.out_step(1)
        every(slabs, "out_step", 2)
        held_a.out_step(2)
        every(slabs, "out_step", 3)
        held_a.out_step(3)
        shared_f.whole_end()
        shared_a.whole_end()
        self.delivery.finish()
        for unit in self.units:
            unit.finish()
        for copy in self.pending:
            copy.wait_send()


def feed_back_call(s, weights, act, slope, streams, g, nrm, par, carry, carried, collective):
    t = g.shape[0]
    hbm = pl.BlockSpec(memory_space=pl.ANY)
    vmem = pl.BlockSpec(memory_space=pltpu.VMEM)
    delivers = carry is None
    dma = pltpu.SemaphoreType.DMA
    half_i, half_o = grad_shape(s, 0), grad_shape(s, 1)
    results = [sds((2, 2, t, D), BF)] if delivers else carry.results()
    scratch = [
        pltpu.VMEM((2, HALF, FF), BF), pltpu.VMEM((FF, D), BF), pltpu.VMEM((t, FF), BF),
        pltpu.VMEM((t, FF), BF), pltpu.VMEM((t, D), BF),
        pltpu.VMEM(half_i, BF), pltpu.VMEM(half_o, BF), pltpu.VMEM(half_i, BF),
        pltpu.VMEM(half_o, BF), pltpu.VMEM(half_i, BF), pltpu.VMEM(half_o, BF),
        pltpu.VMEM((t, D), F32), pltpu.VMEM((D, t), BF),
        dma((CHUNKS, 5)), dma((CHUNKS, 2)), dma((CHUNKS, 2)), dma((3,)),
    ] + ([dma((4, 2)), dma((4, 2))] if delivers else carry.scratch())
    out = pl.pallas_call(
        partial(feed_back_kernel, s, carry),
        out_shape=[sds(half_i, BF), sds(half_o, BF)] + results
        + [sds((1, FF), F32), sds((8, D), F32), sds((t, D), BF)],
        in_specs=[hbm] * (7 + len(carried)) + [vmem] * 3,
        out_specs=[hbm] * (2 + len(results)) + [vmem] * 3,
        scratch_shapes=scratch,
        compiler_params=pltpu.CompilerParams(
            collective_id=collective, has_side_effects=True, vmem_limit_bytes=62 * 1024 * 1024
        ),
        name="feed_back_carry",
    )(*weights, act, slope, streams, *carried, g, nrm, par)
    return out[:2], out[2 : 2 + len(results)], out[2 + len(results) :]


def attention_back_kernel(s, carry, *refs):
    wim, wit, wom, wot = refs[:4]
    count = len(carry.all)
    carried = refs[4 : 4 + count]
    refs = refs[4 + count :]
    large, (g_ref, lse_ref, seg_row, seg_m, seg_t, pos, par) = refs[:7], refs[7:14]
    refs = refs[14:]
    if carry.last:
        streams, small_in, results, refs = refs[:3], refs[3:9], refs[9:15], refs[15:]
    else:
        d_first, d_second = refs[:2]
        results, refs = refs[2 : 2 + count], refs[2 + count :]
    dbin_ref, small_ref, out_ref = refs[:3]
    w_in, w_out, dmix, d_q, d_k, d_v, give_k, give_v, got_k, got_v = refs[3:13]
    own, their, core = refs[13:15], refs[15:17], refs[17:19]
    acc, dp, delta_ref, nrm_t = refs[19:23]
    load_sem, kv_s, kv_r, core_s, core_r, out_sem = refs[23:29]
    o_ref, qkv, kv_t, nrm, cosines, sines, h = refs[29:36]
    if carry.last:
        streams = {0: out_ref, **{i + 1: streams[i] for i in range(3)}}
        carry.load(carried, results, refs[36:], own, streams, small_in)
    else:
        carry.load(carried, results, refs[36:])
    if s:
        large = large[:6] + (large[6].at[s - 1],)
    _, g, _ = here()
    partner = {"group": 1 - g}
    tokens = g_ref.shape[0]

    def remote(src, dst, ssem, rsem):
        return pltpu.make_async_remote_copy(
            src_ref=src, dst_ref=dst, send_sem=ssem, recv_sem=rsem, device_id=partner,
            device_id_type=MESH,
        )

    pairs = [(wom, w_out.at[0]), (wot, w_out.at[1])]
    pairs += list(zip(large[:4], (o_ref, qkv, kv_t, nrm)))
    pairs += [(wim, w_in.at[0]), (wit, w_in.at[1])]
    pairs += list(zip(large[4:], (cosines, sines, h)))
    loads = [
        pltpu.make_async_copy(src, dst, load_sem.at[i]) for i, (src, dst) in enumerate(pairs)
    ]
    for copy in loads:
        copy.start()
    greet(True, True)
    carry.begin()

    for copy in loads[:3]:
        copy.wait()
    grad = g_ref[...]
    d_mix = jnp.concatenate([dot_nt(grad, w_out[0]), dot_nt(grad, w_out[1])], axis=1)
    dmix[...] = turn_halves(d_mix, g).astype(BF)
    o = o_ref[...].astype(F32)
    head = lax.broadcasted_iota(jnp.int32, (16, D), 0)
    lane = lax.broadcasted_iota(jnp.int32, (16, D), 1)
    delta_ref[...] = lax.dot_general(
        jnp.where(lane // HD == head, 1.0, 0.0), dmix[...].astype(F32) * o, NT,
        preferred_element_type=F32, precision=lax.Precision.HIGHEST,
    )
    turned = turn_halves(o, g).astype(BF)
    turned_t = jnp.transpose(turned)
    their[1][HALF:, :] = dot(turned_t[HALF:, :], grad).astype(BF)
    core_copies = [remote(their[1].at[HALF:, :], core[1].at[HALF:, :], core_s.at[3], core_r.at[3])]
    core_copies[0].start()
    own[1][HALF:, :] = dot(turned_t[:HALF, :], grad).astype(BF)

    lanes = lax.broadcasted_iota(jnp.int32, (tokens, 2 * HD), 1)

    def pair(j):
        def columns(first):
            return pl.ds(pl.multiple_of(first + j * 2 * HD, 2 * HD), 2 * HD)

        q = qkv[:, columns(0)]
        do = dmix[:, columns(0)]
        zero = jnp.zeros_like(q)
        sets = (
            (qkv[:, columns(D)], qkv[:, columns(2 * D)], seg_m),
            (kv_t[:, columns(0)], kv_t[:, columns(D)], seg_t),
        )
        total_q = [0.0, 0.0]
        keys_t = [jnp.transpose(sets[i][0]) for i in range(2)]
        total_k = [jnp.zeros((tokens, 2 * HD), F32)] * 2
        total_v = [jnp.zeros((tokens, 2 * HD), F32)] * 2
        for side in range(2):
            mine = (lanes >= HD) if side else (lanes < HD)
            q_head = jnp.where(mine, q, zero)
            do_head = jnp.where(mine, do, zero)
            lse = lse_ref[pl.ds(2 * j + side, 1), :]
            delta = delta_ref[pl.ds(2 * j + side, 1), :]
            for i, (k, v, seg) in enumerate(sets):
                p_t = jnp.where(
                    seg[...] == seg_row[...], jnp.exp(dot_nt(k, q_head) - lse), 0.0
                )
                d_s = (p_t * (dot_nt(v, do_head) - delta)).astype(BF)
                total_v[i] = total_v[i] + dot(p_t.astype(BF), do_head)
                total_k[i] = total_k[i] + dot(d_s, q_head)
                total_q[side] = total_q[side] + dot(keys_t[i][side * HD : (side + 1) * HD, :], d_s)
        d_q[:, columns(0)] = jnp.transpose(jnp.concatenate(total_q, axis=0))
        d_k[:, columns(0)] = total_k[0]
        d_v[:, columns(0)] = total_v[0]
        give_k[:, columns(0)] = total_k[1].astype(BF)
        give_v[:, columns(0)] = total_v[1].astype(BF)

    def exchanges(i):
        cols = pl.ds(i * 4 * HD, 4 * HD)
        return (
            remote(give_k.at[:, cols], got_k.at[:, cols], kv_s.at[0, i], kv_r.at[0, i]),
            remote(give_v.at[:, cols], got_v.at[:, cols], kv_s.at[1, i], kv_r.at[1, i]),
        )

    for copy in loads[3:6]:
        copy.wait()
    nrm_t[...] = jnp.transpose(nrm[...])
    for i in range(PAIRS // 2):
        loop(2, lambda j, i=i: pair(2 * i + j))
        for copy in exchanges(i):
            copy.start()
        carry.step(i + 1)

    for copy in loads[6:]:
        copy.wait()
    acc[...] = jnp.zeros_like(acc)
    small_ref[...] = jnp.zeros_like(small_ref)

    def turned_back(dy, y):
        swapped = swap_pairs(dy)
        d_angle = y * swapped - swap_pairs(y) * dy
        small_ref[3:4, :] += jnp.sum(d_angle * pos[:, 0:1], axis=0, keepdims=True)
        small_ref[4:5, :] += jnp.sum(d_angle * pos[:, 1:2], axis=0, keepdims=True)
        return dy * cosines[...] - swapped * sines[...]

    for j in range(3):
        cols = slice(j * D, (j + 1) * D)
        if j == 0:
            dp[...] = turned_back(
                d_q[...] * HD ** (-0.5), qkv[:, :D].astype(F32) * HD**0.5
            )
        elif j == 1:
            for i in range(PAIRS // 2):
                for copy in exchanges(i):
                    copy.wait()
            dp[...] = turned_back(d_k[...] + got_k[...].astype(F32), qkv[:, D : 2 * D].astype(F32))
        else:
            dp[...] = d_v[...] + got_v[...].astype(F32)
        d_p = dp[...].astype(BF)
        dbin_ref[:, cols] = jnp.sum(dp[...], axis=0, keepdims=True)
        if j < 2:
            place = (0, (slice(None), cols))
        else:
            place = (1, (slice(0, HALF), slice(None)))
        part, at = place
        their[part][at] = dot(nrm_t[HALF:, :], d_p).astype(BF)
        copy = remote(their[part].at[at], core[part].at[at], core_s.at[j], core_r.at[j])
        copy.start()
        core_copies.append(copy)
        own[part][at] = dot(nrm_t[:HALF, :], d_p).astype(BF)
        if j == 1:
            carry.late_step()
        acc[:, :HALF] += dot_nt(d_p, w_in[0, :, cols])
        acc[:, HALF:] += dot_nt(d_p, w_in[1, :, cols])
    grad = g_ref[...].astype(F32)
    d_normed = turn_halves(acc[...], g)
    out, d_gain, d_shift = norm_backward(h[...].astype(F32), par[0:1, :], grad, d_normed)
    out_ref[...] = out.astype(BF)
    small_ref[0:1, :] = jnp.sum(grad, axis=0, keepdims=True)
    small_ref[1:2, :] = d_gain
    small_ref[2:3, :] = d_shift

    for copy in core_copies:
        copy.wait()
    saves = []
    if carry.last:
        for part in range(2):
            accumulate(own[part], core[part], own[part].shape[0])
        carry.conclude(dbin_ref, small_ref)
        return
    for part, target in enumerate((d_first, d_second)):
        accumulate(own[part], core[part], own[part].shape[0])
        copy = pltpu.make_async_copy(own[part], target, out_sem.at[part])
        copy.start()
        saves.append(copy)
    carry.end()
    for copy in saves:
        copy.wait()


def attention_back_call(
    s, weights, carry, carried, g, saved, seg_row, seg_m, seg_t, turns, pos, h, par, collective,
    streams=(), small=None,
):
    t = g.shape[0]
    qkv, nrm, kv_t, o, lse = saved
    hbm = pl.BlockSpec(memory_space=pl.ANY)
    vmem = pl.BlockSpec(memory_space=pltpu.VMEM)
    dma = pltpu.SemaphoreType.DMA
    halves = [grad_shape(s, 0), grad_shape(s, 1)]
    rows, wide = pltpu.VMEM((t, D), BF), pltpu.VMEM((t, D), F32)
    if carry.last:
        carry.tokens = t
    results = carry.results()
    scratch = [
        pltpu.VMEM((2, HALF, QKV), BF), pltpu.VMEM((2, HALF, D), BF), rows, wide, wide, wide,
        rows, rows, rows, rows,
        *[pltpu.VMEM(x, BF) for x in halves * 3],
        wide, wide, pltpu.VMEM((16, t), F32), pltpu.VMEM((D, t), BF),
        dma((11,)), dma((2, 3)), dma((2, 3)), dma((4,)), dma((4,)), dma((2,)),
        rows, pltpu.VMEM((t, QKV), BF), pltpu.VMEM((t, 2 * D), BF), rows, wide, wide, rows,
    ] + carry.scratch()
    extra, extra_specs = (), []
    out_shape, out_specs = [sds(x, BF) for x in halves] + results, [hbm] * (2 + len(results))
    if carry.last:
        extra, extra_specs = (*streams, *small), [hbm] * 3 + [vmem] * 6
        out_shape, out_specs = results, [hbm] * 5 + [vmem]
    out = pl.pallas_call(
        partial(attention_back_kernel, s, carry),
        out_shape=out_shape
        + [sds((1, QKV), F32), sds((8, D), F32), sds((t, D), BF)],
        in_specs=[hbm] * (4 + len(carried) + 7) + [vmem] * 7 + extra_specs,
        out_specs=out_specs + [vmem] * 3,
        scratch_shapes=scratch,
        compiler_params=pltpu.CompilerParams(
            collective_id=collective, has_side_effects=True, vmem_limit_bytes=63 * 1024 * 1024
        ),
        name="attention_back_carry",
    )(*weights, *carried, o, qkv, kv_t, nrm, *turns, h, g, lse, seg_row, seg_m, seg_t, pos, par, *extra)
    if carry.last:
        return out[:6]
    return out[:2], out[2:-3], out[-3:]


def in_place(x):
    return x.reshape(-1, x.shape[-1])


CHUNKS = 6


START = (0, 0, 0, 0)
RING = 4
GROUP = (1, 1, 1, 1)
SPAN = 6
BESIDE = (None, None, None)


def chunk_of(ref, part, k):
    size = ref.shape[0 if part else 1] // CHUNKS
    at = pl.ds(pl.multiple_of(k * size, size), size)
    return ref.at[at, :] if part else ref.at[:, at]


def ring_place(chip):
    return 2 * (chip // 2) + (chip % 2 + chip // 2) % 2


def ring_chip(place):
    return 2 * (place // 2) + (place % 2 + place // 2) % 2


CLOCKWISE = ((True, False), (True, False), (False, True), (True, False))


def forward_kernel(*refs):
    w_in, w_out, h0, small, pos, seg_col, seg_m, seg_t = refs[:8]
    refs = refs[8:]
    keep = [refs[4 * s : 4 * s + 4] for s in range(4)]
    acts, slopes = refs[16:18], refs[18:20]
    results = refs[20:38]
    refs = refs[38:]
    work, refs = refs[:18], refs[18:]
    qkvs, kv_ts, os, lses = work[0:2], work[2:4], work[4:6], work[6:8]
    nrms, hs = work[8:12], [work[12].at[s] for s in range(4)]
    turns, pars = (work[13:15], work[15:17]), work[17]
    held = [refs[4 * s : 4 * s + 4] for s in range(4)]
    acc, stage_a, stage_s, lse_scr, smalls, b_in, b_out, freqs = refs[16:24]
    own_sem, ring_s, ring_r, z_s, z_r, core_s, core_r, kv_sem, save_sem, stage_sem = refs[24:34]
    small_s, small_r, result_sem = refs[34:]

    def kept(i):
        return pltpu.make_async_copy(work[i], results[i], result_sem.at[i])

    c = lax.axis_index("section")
    g = lax.axis_index("group")
    z = lax.axis_index("dp")
    parity = z % 2
    place = ring_place(c)
    ahead, behind = ring_chip((place + 1) % 4), ring_chip((place + 3) % 4)
    partner = {"group": 1 - g}
    tokens = h0.shape[0]

    def remote(src, dst, ssem, rsem, device):
        return pltpu.make_async_remote_copy(
            src_ref=src, dst_ref=dst, send_sem=ssem, recv_sem=rsem, device_id=device,
            device_id_type=MESH,
        )

    greet(True, True)

    def small_copies():
        slot = smalls.at[2 * c + g]
        out = []
        for bit in range(4):
            for core in range(2):
                if bit or core:
                    target = {"section": flip(c, bit) if bit else c, "group": (g + core) % 2}
                    out.append(remote(small, slot, small_s.at[2 * bit + core], small_r.at[2 * c + g], target))
        return out

    for copy in small_copies():
        copy.start()
    smalls[2 * c + g] = small[...]

    def mine(s, part):
        return held[s][2 * part]

    def theirs(s, part):
        return held[s][2 * part + 1]

    def distance(s, part):
        d = place - ring_place(s)
        return (d + 4) % 4 if CLOCKWISE[s][part] else (4 - d) % 4

    def own_copies(s):
        first = pltpu.make_async_copy(
            w_in.at[:, : QKV] if s % 2 == 0 else w_in, mine(s, 0), own_sem.at[0]
        )
        source = w_out.at[:HALF, :] if s % 2 == 0 else w_out
        second = pltpu.make_async_copy(source, mine(s, 1), own_sem.at[1])
        over = remote(w_out.at[HALF:D, :], mine(s, 1), own_sem.at[2], own_sem.at[3], partner)
        return first, second, over

    for s in range(4):

        @pl.when(c == s)
        def _(s=s):
            first, second, over = own_copies(s)
            first.start()
            if s % 2:
                second.start()
            else:

                @pl.when(g == 0)
                def _():
                    second.start()
                    over.start()

    for s in range(4):

        @pl.when(c == s)
        def _(s=s):
            first, second, over = own_copies(s)
            first.wait()
            if s % 2:
                second.wait()
            else:

                @pl.when(g == 0)
                def _():
                    second.wait()
                    over.wait_send()

                @pl.when(g == 1)
                def _():
                    over.wait_recv()

    def ring_copy(s, part, k):
        ref = chunk_of(mine(s, part), part, jnp.where(k < 2, 2 * parity + k, k + 2))
        target = ahead if CLOCKWISE[s][part] else behind
        u = 2 * s + part
        return remote(ref, ref, ring_s.at[u, k], ring_r.at[u, k], {"section": target})

    def z_copy(s, part, j, sending):
        ref = chunk_of(mine(s, part), part, 2 * (parity if sending else 1 - parity) + j)
        u = 2 * s + part
        return remote(ref, ref, z_s.at[u, j], z_r.at[u, j], {"dp": z + 1 - 2 * parity})

    def core_copy(s, part, k):
        u = 2 * s + part
        return remote(
            chunk_of(mine(s, part), part, k), chunk_of(theirs(s, part), part, k),
            core_s.at[u, k], core_r.at[u, k], partner,
        )

    def event(s, part, k):
        p = distance(s, part)
        copy = ring_copy(s, part, k)
        pl.when(p > 0)(copy.wait_recv)
        pl.when(p < 3)(copy.start)

        @pl.when((k < 2) & (p > 0))
        def _():
            z_copy(s, part, jnp.minimum(k, 1), True).start()

        core_copy(s, part, jnp.where(k < 2, 2 * parity + k, k + 2)).start()

        @pl.when(k >= 2)
        def _():
            j = jnp.maximum(k - 2, 0)
            pl.when(p > 0)(z_copy(s, part, j, False).wait_recv)
            core_copy(s, part, 2 * (1 - parity) + j).start()

    def slot(t, first, last):
        for s in range(4):
            if START[s] <= last and first <= START[s] + RING // GROUP[s] + 2:
                for part in range(2):
                    k = t - START[s] - distance(s, part)

                    @pl.when((k >= 0) & (k < RING // GROUP[s]))
                    def _(s=s, part=part, k=k):
                        k = jnp.clip(k, 0, RING // GROUP[s] - 1)
                        for i in range(GROUP[s]):
                            event(s, part, k * GROUP[s] + i)

    def slots(first, last):
        loop(last - first + 1, lambda i: slot(first + i, first, last))

    def arrived(s):
        def one(k):
            core_copy(s, 0, k).wait_recv()
            core_copy(s, 1, k).wait_recv()

        loop(CHUNKS, one)
        for i in range(4):
            pltpu.make_async_copy(held[s][i], keep[s][i], save_sem.at[4 * s + i]).start()

    def assemble():
        for i in range(8):
            slot = smalls.at[i]
            copy = remote(slot, slot, small_s.at[0], small_r.at[i], partner)
            pl.when(2 * c + g != i)(copy.wait_recv)
        for s in range(4):

            def both(first, width, s=s):
                at = slice(first, first + width)
                return jnp.concatenate([smalls[2 * s, :, at], smalls[2 * s + 1, :, at]], axis=1)

            half = FF // 2
            b_in[s] = both(0, half)
            b_out[s] = both(half, HALF)
            pars[s] = jnp.concatenate(
                [both(half + HALF, HALF), both(half + 2 * HALF, HALF), jnp.zeros((6, D), F32)], axis=0
            )
            if s % 2 == 0:
                freqs[s // 2] = jnp.concatenate(
                    [both(half + 3 * HALF, HALF), both(half + 4 * HALF, HALF)], axis=0
                )

    def turn_rows(i):
        rows = tokens // 2
        at = pl.ds(pl.multiple_of((i % 2) * rows, rows), rows)
        for layer in range(2):

            @pl.when(i // 2 == layer)
            def _(layer=layer):
                angles = (
                    pos[at, 0:1] * freqs[layer, 0:1, :] + pos[at, 1:2] * freqs[layer, 1:2, :]
                )
                lanes = lax.broadcasted_iota(jnp.int32, angles.shape, 1)
                sines = jnp.sin(angles)
                turns[layer][0][at, :] = jnp.cos(angles)
                turns[layer][1][at, :] = jnp.where((lanes % HD) < HD // 2, -sines, sines)

    def normed(s, h):
        xhat, _ = normalize(h[...].astype(F32))
        nrms[s][...] = turn_halves(
            xhat * pars[s, 0:1, :] + pars[s, 1:2, :], g
        ).astype(BF)

    def project(s, first, width):
        cols = pl.ds(first, width)
        return (
            dot(nrms[s][:, :HALF], mine(s, 0)[:, cols])
            + dot(nrms[s][:, HALF:], theirs(s, 0)[:, cols])
            + b_in[s, 0:1, cols]
        )

    def attention(s, h, out, beside):
        layer = s // 2
        qkv, kv_t, o_ref = qkvs[layer], kv_ts[layer], os[layer]
        cosines, sines = turns[layer]
        normed(s, h)
        exchange = []
        for j in (1, 2, 0):
            x = project(s, j * D, D)
            if j < 2:
                x = x * cosines[...] + swap_pairs(x) * sines[...]
            if j == 0:
                x = x * HD ** (-0.5)
            qkv[:, j * D : (j + 1) * D] = x.astype(BF)
            if j:
                copy = remote(
                    qkv.at[:, j * D : (j + 1) * D], kv_t.at[:, (j - 1) * D : j * D],
                    kv_sem.at[0, 2 * layer + j - 1], kv_sem.at[1, 2 * layer + j - 1], partner,
                )
                copy.start()
                exchange.append(copy)
        for copy in exchange:
            copy.wait()
        for i in (layer, 2 + layer, 8 + s):
            kept(i).start()
        lanes = lax.broadcasted_iota(jnp.int32, (tokens, 2 * HD), 1)

        def pair(j):
            if beside is not None:
                pl.when(beside[0] + j <= beside[1])(lambda: slot(beside[0] + j, *beside))

            def columns(ref, first):
                return ref[:, pl.ds(pl.multiple_of(first + j * 2 * HD, 2 * HD), 2 * HD)]

            q = columns(qkv, 0)
            km, vm = columns(qkv, D), columns(qkv, 2 * D)
            kt, vt = columns(kv_t, 0), columns(kv_t, D)
            same_m = seg_col[...] == seg_m[...]
            same_t = seg_col[...] == seg_t[...]
            found = []
            for side in range(2):
                head = (lanes >= HD) if side else (lanes < HD)
                q_head = jnp.where(head, q, jnp.zeros_like(q))
                s_m = jnp.where(same_m, dot_nt(q_head, km), -1e9)
                s_t = jnp.where(same_t, dot_nt(q_head, kt), -1e9)
                top = jnp.maximum(
                    jnp.max(s_m, axis=-1, keepdims=True), jnp.max(s_t, axis=-1, keepdims=True)
                )
                p_m = jnp.exp(s_m - top)
                p_t = jnp.exp(s_t - top)
                total = jnp.sum(p_m, axis=-1, keepdims=True) + jnp.sum(
                    p_t, axis=-1, keepdims=True
                )
                o = dot(p_m.astype(BF), vm) + dot(p_t.astype(BF), vt)
                found.append(o / total)
                lse_scr[...] = jnp.where(
                    lanes == 2 * j + side, top + jnp.log(total), lse_scr[...]
                )
            o_ref[:, pl.ds(pl.multiple_of(j * 2 * HD, 2 * HD), 2 * HD)] = jnp.where(
                lanes < HD, found[0], found[1]
            ).astype(BF)

        loop(PAIRS, pair)
        lses[layer][...] = jnp.transpose(lse_scr[...])[:16, :]
        turned = turn_halves(o_ref[...].astype(F32), g).astype(BF)
        y = dot(turned[:, :HALF], mine(s, 1)[...]) + dot(turned[:, HALF:], theirs(s, 1)[...])
        out[...] = (h[...].astype(F32) + y + b_out[s, 0:1, :]).astype(BF)
        for i in (4 + layer, 6 + layer):
            kept(i).start()

    def feed(s, h, out, beside):
        layer = s // 2
        width = FF // CHUNKS
        normed(s, h)
        kept(8 + s).start()
        acc[...] = h[...].astype(F32) + b_out[s, 0:1, :]

        def staged(j, i):
            turn = j % 2
            cols = pl.ds(pl.multiple_of(j * width, width), width)
            source, target = ((stage_a, acts[layer]), (stage_s, slopes[layer]))[i]
            return pltpu.make_async_copy(source.at[turn], target.at[:, cols], stage_sem.at[i, turn])

        def block(j):
            if beside is not None:
                pl.when(beside[0] + j <= beside[1])(lambda: slot(beside[0] + j, *beside))
            turn = j % 2

            @pl.when(j >= 2)
            def _():
                staged(j - 2, 0).wait()
                staged(j - 2, 1).wait()

            b = (j + g * (CHUNKS // 2)) % CHUNKS
            u = project(s, pl.multiple_of(b * width, width), width)
            cdf = 0.5 + 0.5 * lax.erf(u * (0.5**0.5))
            act = (u * cdf).astype(BF)
            stage_a[turn] = act
            pdf = jnp.exp(u * u * -0.5) * 0.3989422804014327
            stage_s[turn] = (cdf + u * pdf).astype(BF)
            staged(j, 0).start()
            staged(j, 1).start()
            for half in range(2):

                @pl.when(j // (CHUNKS // 2) == half)
                def _(half=half):
                    rows = pl.ds(pl.multiple_of((j % (CHUNKS // 2)) * width, width), width)
                    acc[...] += dot(act, held[s][2 + half][rows, :])

        loop(CHUNKS, block)
        for j in (CHUNKS - 2, CHUNKS - 1):
            staged(j, 0).wait()
            staged(j, 1).wait()
        out[...] = acc[...].astype(BF)

    slots(0, 0)
    assemble()

    def wait_and_turn(i):
        slot(1 + i, 1, SPAN)
        pl.when(i < 4)(lambda: turn_rows(i))

    loop(SPAN, wait_and_turn)
    for i in range(13, 18):
        kept(i).start()
    arrived(0)
    attention(0, h0, hs[0], BESIDE[0])
    arrived(1)
    feed(1, hs[0], hs[1], BESIDE[1])
    arrived(2)
    attention(2, hs[1], hs[2], BESIDE[2])
    arrived(3)
    feed(3, hs[2], hs[3], None)

    kept(12).start()

    for copy in small_copies():
        copy.wait_send()
    for i in range(18):
        kept(i).wait()
    for s in range(4):
        for part in range(2):
            p = distance(s, part)

            def sent_out(k, s=s, part=part, p=p):
                core_copy(s, part, k).wait_send()
                pl.when((k < 4) & (p < 3))(ring_copy(s, part, jnp.minimum(k, 3)).wait_send)
                pl.when((k < 2) & (p > 0))(z_copy(s, part, jnp.minimum(k, 1), True).wait_send)

            loop(CHUNKS, sent_out)
        for i in range(4):
            pltpu.make_async_copy(held[s][i], keep[s][i], save_sem.at[4 * s + i]).wait()


def forward_call(w_in, w_out, h, small, pos, seg_col, seg_m, seg_t):
    t = h.shape[0]
    hbm = pl.BlockSpec(memory_space=pl.ANY)
    vmem = pl.BlockSpec(memory_space=pltpu.VMEM)
    weights = []
    for s in range(4):
        (a, b), (d, e) = unit_shape(s, 0), unit_shape(s, 1)
        weights += [(a, b), (a, b), (d, e), (d, e)]
    rows = sds((t, D), BF)
    out_shape = (
        [sds(w, BF) for w in weights]
        + [sds((t, FF), BF)] * 4
        + [sds((t, QKV), BF)] * 2
        + [sds((t, 2 * D), BF)] * 2
        + [rows] * 2
        + [sds((16, t), F32)] * 2
        + [rows] * 4
        + [sds((4, t, D), BF)]
        + [sds((t, D), F32)] * 4
        + [sds((4, 8, D), F32)]
    )
    dma = pltpu.SemaphoreType.DMA
    scratch = [pltpu.VMEM(x.shape, x.dtype) for x in out_shape[20:]]
    scratch += [pltpu.VMEM(w, BF) for w in weights] + [
        pltpu.VMEM((t, D), F32),
        pltpu.VMEM((2, t, FF // CHUNKS), BF),
        pltpu.VMEM((2, t, FF // CHUNKS), BF),
        pltpu.VMEM((t, 2 * HD), F32),
        pltpu.VMEM((8,) + small.shape, F32),
        pltpu.VMEM((4, 1, FF), F32),
        pltpu.VMEM((4, 1, D), F32),
        pltpu.VMEM((2, 2, D), F32),
        dma((4,)), dma((8, 4)), dma((8, 4)), dma((8, 2)), dma((8, 2)), dma((8, 6)), dma((8, 6)),
        dma((2, 4)), dma((16,)), dma((2, 2)), dma((8,)), dma((8,)), dma((18,)),
    ]
    out = pl.pallas_call(
        forward_kernel,
        out_shape=out_shape,
        in_specs=[hbm, hbm] + [vmem] * 6,
        out_specs=[hbm] * 38,
        scratch_shapes=scratch,
        compiler_params=pltpu.CompilerParams(
            collective_id=2, has_side_effects=True, vmem_limit_bytes=63 * 1024 * 1024
        ),
        name="forward",
    )(w_in, w_out, h, small, pos, seg_col, seg_m, seg_t)
    weights = [out[4 * s : 4 * s + 4] for s in range(4)]
    acts, slopes, qkvs, kv_ts, os, lses = (out[16 + 2 * i : 18 + 2 * i] for i in range(6))
    nrms, hs = out[28:32], out[32]
    saved = []
    for s in range(4):
        i = s // 2
        if s % 2 == 0:
            saved.append((qkvs[i], nrms[s], kv_ts[i], os[i], lses[i]))
        else:
            saved.append((acts[i], slopes[i], nrms[s]))
    return weights, saved, hs, (out[33:35], out[35:37]), out[37]


def small_rows(dbin, rest):
    first = jnp.pad(dbin.reshape(-1), (0, FF - dbin.size)).reshape(4, D)
    return jnp.concatenate([first, rest[:5], jnp.zeros((SMALL[0] - 9, D), F32)])


def carried_passes(weight_in, weight_out, h, g, small, freq, pos, seg_m, seg_t):
    section, core = lax.axis_index("section"), lax.axis_index("group")
    wide = jnp.concatenate([freq.reshape(2, PAIRS, HD // 2)] * 2, axis=2).reshape(-1)
    small = jnp.concatenate([*small, wide]).astype(F32)[None]
    weights, saved, streams, turns, pars = forward_call(
        weight_in[0], weight_out[0], h, small, pos, seg_m[:, None], seg_m[None], seg_t[None]
    )
    smalls, grads, in_grads = [None] * 4, [None] * 4, [None] * 4
    rows = (seg_m[None], seg_m[:, None], seg_t[:, None])

    def feed_back(s, g, carry, carried):
        act, slope, nrm = saved[s]
        grads[s], results, (dbin, rest, in_grads[s]) = feed_back_call(
            s, weights[s], act, slope, streams, g, nrm, pars[s], carry, carried, 3 + s
        )
        smalls[s] = (dbin, rest)
        return results

    def attention_back(s, g, carry, carried):
        grads[s], results, (dbin, rest, in_grads[s]) = attention_back_call(
            s, weights[s], carry, carried, g, saved[s], *rows, turns[s // 2], pos,
            streams if s else h, pars[s], 3 + s,
        )
        smalls[s] = (dbin, rest)
        return results

    (outputs,) = feed_back(3, g, None, ())
    quarters3 = attention_back(2, in_grads[3], Carry(3, (), ()), grads[3])
    *quarters2, first3, second3 = feed_back(
        1, in_grads[2], Carry(2, ((3, 0), (3, 1)), ()), (*grads[2], *quarters3)
    )
    *sums, input_grads, small_sum = attention_back_call(
        0, weights[0], Finish(), (*grads[1], *quarters2, first3, second3), in_grads[1], saved[0],
        *rows, turns[0], pos, h, pars[0], 3, in_grads[1:], [x for pair in smalls[1:] for x in pair],
    )
    first_a, second_a, first_f, second_f = sums
    second_a = in_place(second_a)
    in_a = jnp.concatenate([in_place(first_a), second_a[:HALF]], axis=1)
    both = jnp.concatenate([second_a[HALF:], flipped(second_a[HALF:], "group", 1)], axis=0)
    both = jnp.where(core == 0, jnp.pad(both, ((0, FF // 2 - D), (0, 0))), jnp.zeros((), BF))
    attends = section % 2 == 0
    in_f = in_place(first_f)
    out_in = jnp.where(attends, jnp.pad(in_a, ((0, 0), (0, FF - QKV))), in_f).astype(F32)
    out_out = jnp.where(attends, both, in_place(second_f)).astype(F32)
    return outputs.reshape(-1, D), input_grads.reshape(-1, D), out_in, out_out, small_sum


def plain_passes(weight_in, weight_out, h, g, small, freq, pos, seg_m, seg_t):
    section, group = lax.axis_index("section"), lax.axis_index("group")
    groups = lax.axis_size("group")
    small = jnp.concatenate([*small, freq.reshape(-1)])
    small = lax.all_gather(small, ("section", "group")).reshape(4, groups, -1).astype(F32)
    widths = [FF // groups, D // groups, D // groups, D // groups, D // groups]
    starts = [sum(widths[:i]) for i in range(5)]
    b_in, b_out, gain, shift, freq = (
        small[:, :, a : a + w] for a, w in zip(starts, widths)
    )
    b_in, b_out, gain, shift = (x.reshape(4, 1, -1) for x in (b_in, b_out, gain, shift))
    freq = freq.reshape(4, groups, 2, -1).transpose(0, 2, 1, 3).reshape(4, 2, D // 2)
    pars = [
        jnp.concatenate([gain[s], shift[s], jnp.zeros((6, D), F32)], axis=0) for s in range(4)
    ]
    turns = [turning(freq[s], pos) for s in (0, 2)]

    core = group % 2
    rot = jnp.zeros((1,), jnp.int32)
    all_in = lax.all_gather(weight_in, "group", axis=1, tiled=True)
    all_out = lax.all_gather(weight_out, "group", axis=1, tiled=True)
    all_in = lax.all_gather(all_in, "section", axis=0, tiled=True)
    all_out = lax.all_gather(all_out, "section", axis=0, tiled=True)
    weights, saved, streams = [], [], [h]
    for s in range(4):
        cols, rows = (QKV, D) if s % 2 == 0 else (FF, FF)
        w_in, w_out = all_in[s, :, :cols], all_out[s, :rows]
        weights.append((w_in[:HALF], w_in[HALF:], w_out[: rows // 2], w_out[rows // 2 :]))
        wia, wib, woa, wob = weights[s]
        if s % 2 == 0:
            cosines, sines = turns[s // 2]
            qkv, nrm = qkv_call(rot, h, pars[s], wia, wib, b_in[s, :, :QKV], cosines, sines)
            kv_t = flipped(qkv[:, D:], "group", 1)
            o, lse, h = attend_call(
                rot, qkv, kv_t, seg_m[:, None], seg_m[None], seg_t[None], h, woa, wob, b_out[s]
            )
            saved.append((qkv, nrm, kv_t, o, lse))
        else:
            act, slope, nrm, h = ff_call(rot, h, pars[s], wia, wib, b_in[s], woa, wob, b_out[s])
            saved.append((act, slope, nrm))
        streams.append(h)
    outputs = to_owners(streams[1:], section, core)
    smalls, grads, in_grads = [None] * 4, [None] * 4, [None] * 4
    for s in (3, 2, 1, 0):
        wia, wib, woa, wob = weights[s]
        if s % 2 == 0:
            qkv, nrm, kv_t, o, lse = saved[s]
            cosines, sines = turns[s // 2]
            dmix, delta, doa, dob = mix_back_call(rot, g, o, woa, wob)
            dq, dkm, dvm, dkt, dvt = attend_back_call(
                qkv, kv_t, dmix, lse, delta, seg_m[None], seg_m[:, None], seg_t[:, None]
            )
            dkr, dvr = flipped(dkt, "group", 1), flipped(dvt, "group", 1)
            dia, dib, dbin, rest, g = qkv_back_call(
                rot, dq, dkm, dvm, dkr, dvr, qkv, cosines, sines, pos, nrm, wia, wib,
                streams[s], pars[s], g,
            )
        else:
            act, slope, nrm = saved[s]
            dia, dib, doa, dob, dbin, rest, g = ff_back_call(
                rot, g, act, slope, nrm, wia, wib, woa, wob, streams[s], pars[s]
            )
        in_grads[s] = g
        grads[s] = (
            jnp.pad(jnp.concatenate([dia, dib]), ((0, 0), (0, FF - dia.shape[1]))),
            jnp.pad(jnp.concatenate([doa, dob]), ((0, FF - 2 * doa.shape[0]), (0, 0))),
        )
        smalls[s] = small_rows(dbin, rest)
    input_grads = to_owners(in_grads, section, core)
    small_sum = lax.psum(jnp.stack(smalls), ("section", "group", "dp"))[section]

    def owned(x):
        x = lax.psum_scatter(x, "section", scatter_dimension=0, tiled=True)[0]
        x = lax.psum_scatter(x, "group", scatter_dimension=0, tiled=True)
        return lax.psum(x, "dp").astype(F32)

    out_in = owned(jnp.stack([x[0] for x in grads]))
    out_out = owned(jnp.stack([x[1] for x in grads]))
    return outputs, input_grads, out_in, out_out, small_sum


def body(
    activations, weight_in, weight_out, bias_in, bias_out, norm_gain, norm_shift, rope_freq,
    image_sides, cotangent,
):
    sections = lax.axis_size("section")
    groups = lax.axis_size("group")
    section = lax.axis_index("section")
    group = lax.axis_index("group")
    core = group % 2
    micro = image_sides.shape[0]
    capacity = activations.shape[0] // micro
    tokens = capacity // 2
    assert sections == 4 and groups % 2 == 0 and 2 * micro == sections
    fast = groups == 2 and lax.axis_size("dp") == 4

    here = (section // 2) == core
    local = section % 2

    def take(x):
        own = lax.dynamic_index_in_dim(x.reshape(micro, capacity, D), local, 0, keepdims=False)
        give = lax.dynamic_slice_in_dim(own, (1 - core) * tokens, tokens, 0)
        keep = lax.dynamic_slice_in_dim(own, core * tokens, tokens, 0)
        return jnp.where(here, keep, flipped(give, "group", 1))

    h = take(activations)
    own_sides = lax.dynamic_index_in_dim(image_sides, local, 0, keepdims=False)
    sides = jnp.where(here, own_sides, flipped(own_sides, "group", 1))
    segment, patch_row, patch_col, is_valid = layout(sides, capacity)
    pos_all = jnp.stack([patch_col, patch_row], axis=1).astype(F32)

    def half_of(x, which):
        return lax.dynamic_slice_in_dim(x, which * tokens, tokens, 0)

    pos = half_of(pos_all, core)
    seg_m, seg_t = half_of(segment, core), half_of(segment, 1 - core)
    valid = half_of(is_valid, core)
    g = take(cotangent) * valid[:, None].astype(BF)

    passes = carried_passes if fast else plain_passes
    outputs, input_grads, out_in, out_out, small_sum = passes(
        weight_in, weight_out, h, g, (bias_in[0], bias_out[0], norm_gain[0], norm_shift[0]),
        rope_freq[0], pos, seg_m, seg_t,
    )

    first_bias = small_sum[:4].reshape(-1)
    d_freq = small_sum[7:9].reshape(2, HEADS, HD)[:, :, : HD // 2].reshape(2, D // 2)

    def piece(x):
        w = x.shape[-1] // groups
        return lax.dynamic_slice_in_dim(x, group * w, w, x.ndim - 1)[None]

    return (
        outputs[None],
        input_grads[None],
        out_in[None],
        out_out[None],
        piece(first_bias),
        piece(small_sum[4]),
        piece(small_sum[5]),
        piece(small_sum[6]),
        piece(d_freq),
    )


def solution(mesh):
    placed = (
        P(("group", "dp"), None),
        P("section", "group", None),
        P("section", "group", None),
        P("section", "group"),
        P("section", "group"),
        P("section", "group"),
        P("section", "group"),
        P("section", None, "group"),
        P(("group", "dp"), None),
        P(("group", "dp"), None),
    )
    return jax.shard_map(
        body,
        mesh=mesh,
        in_specs=placed,
        out_specs=(
            P("section", ("group", "dp"), None),
            P("section", ("group", "dp"), None),
            P("section", "group", None),
            P("section", "group", None),
            P("section", "group"),
            P("section", "group"),
            P("section", "group"),
            P("section", "group"),
            P("section", None, "group"),
        ),
        check_vma=False,
    )
```
